32 devices in a mesh: dp: 2 (over x), expert: 16 (over z, y, core).
Axes of the slice: x: 2, y: 2, z: 4, core: 2. Of those that a mesh axis runs over, the one named last changes fastest.
Arguments:
- tokens: bfloat16 [4096, 2048], P(('dp', 'expert')), may hold values from -6 to 6
- cotangent: bfloat16 [4096, 2048], P(('dp', 'expert')), may hold values from -6 to 6
- segment_ids: int32 [2, 2048], P('dp'), may hold values from 0 to 2, as said below
- routes: int32 [4096, 6], P(('dp', 'expert')), may hold values from 0 to 15, all different within a row; in each aligned block of 128 rows (0 to 127, 128 to 255, ...) at most 72 rows name the same one
- attn_in: bfloat16 [2048, 6144], P(('dp', 'expert')), may hold values from -0.125 to 0.125
- attn_out: bfloat16 [2048, 2048], P(('dp', 'expert')), may hold values from -0.5 to 0.5
- gain_attn: bfloat16 [2048], P(('dp', 'expert')), may hold values from 0.099609375 to 1.8984375
- shared_in: bfloat16 [2048, 5632], P(('dp', 'expert')), may hold values from -0.125 to 0.125
- shared_out: bfloat16 [2816, 2048], P(('dp', 'expert')), may hold values from -0.15625 to 0.15625
- router: bfloat16 [2048, 16], P(('dp', 'expert')), may hold values from -0.0625 to 0.0625
- gain_ffn: bfloat16 [2048], P(('dp', 'expert')), may hold values from 0.099609375 to 1.8984375
- expert_in: bfloat16 [16, 2048, 2816], P('expert', 'dp'), may hold values from -0.125 to 0.125
- expert_out: bfloat16 [16, 1408, 2048], P('expert', 'dp'), may hold values from -0.3125 to 0.3125
Outputs:
- output: bfloat16 [4096, 2048], P(('dp', 'expert'))
- grad_tokens: bfloat16 [4096, 2048], P(('dp', 'expert'))
- grad_attn_in: float32 [2048, 6144], P(('dp', 'expert'))
- grad_attn_out: float32 [2048, 2048], P(('dp', 'expert'))
- grad_gain_attn: float32 [2048], P(('dp', 'expert'))
- grad_shared_in: float32 [2048, 5632], P(('dp', 'expert'))
- grad_shared_out: float32 [2816, 2048], P(('dp', 'expert'))
- grad_router: float32 [2048, 16], P(('dp', 'expert'))
- grad_gain_ffn: float32 [2048], P(('dp', 'expert'))
- grad_expert_in: float32 [16, 2048, 2816], P('expert', 'dp')
- grad_expert_out: float32 [16, 1408, 2048], P('expert', 'dp')
The draws below stay inside these ranges and needn't reach their ends.
Inputs may be any that keep to these rules, and one draw needn't show every extreme that they name: `routes`: in the rows of one device each expert is named by at most 72 rows, and by exactly 72 rows in some device's rows; a row names 6 different experts. `segment_ids`: ids never fall along a sequence; every sequence holds ids 0, 1 and 2; documents 0 and 2 hold 1 to 127 tokens each.
All inputs are finite; a program needn't handle non-finite values.
Results may differ from the reference program's by a relative error of at most 0.018.
Values may be sent and summed in bfloat16 or wider, within the bound.
No kernel may reach another device: no remote copies, remote signals or barrier semaphores. Data moves between devices by JAX's collectives and lax.ppermute only.
A program may use at most 384 MiB of HBM per device.

```python
import math
import jax
import jax.numpy as jnp
import numpy as np
from jax import lax

D = 2048
HEADS = 16
HEAD_DIM = 128
SH = 2816
FF = 1408
TOP = 6
TOK_DEV = 128
EXPERTS = 16
CAP = 72
SEQ_LEN = 2048
SEQS = 2
TOKENS = 4096


def draw_segment_ids(key, part):
    key = jax.random.fold_in(key, 7)
    head_key, tail_key = jax.random.split(key)
    head_len = jax.random.randint(head_key, (SEQS, 1), 1, TOK_DEV)
    tail_len = jax.random.randint(tail_key, (SEQS, 1), 1, TOK_DEV)
    places = jnp.arange(SEQ_LEN, dtype=jnp.int32)[None, :]
    return (places >= head_len).astype(jnp.int32) + (places >= SEQ_LEN - tail_len).astype(jnp.int32)


def steps_of(stream_key, extent, pieces, smallest, high):
    level = 1.0
    for dim, parts in pieces:
        steps = jax.random.uniform(jax.random.fold_in(jax.random.fold_in(stream_key, 6), dim), (parts,), jnp.float32, smallest / len(pieces), high / len(pieces))
        level = level * jnp.repeat(jnp.exp(steps), extent[dim] // parts).reshape((-1,) + (1,) * (len(extent) - 1 - dim))
    return level


def deal_out(own_key, own, number, rows, count, top, bound, lean):
    sequence = jax.random.permutation(own_key, count)
    packed, ordinary = portions_of(count, rows * top, bound, lean, True), portions_of(count, rows * top, bound, lean, False)
    places = jnp.arange(count)

    def named(tallies, turn):
        used = int((tallies > 0).sum())
        fixed = max(1, used // 4)
        shifted = fixed + (places - fixed + turn * (used - fixed)) % max(1, count - fixed)
        return jnp.zeros((count,), jnp.int32).at[sequence[jnp.where(places < fixed, places, shifted)]].set(jnp.asarray(tallies, jnp.int32))

    tallies = jnp.where(number % 4 == 0, named(packed, number // 4), named(ordinary, number - number // 4 - 1))
    mixed = jax.random.permutation(jax.random.fold_in(own, 3), count)
    donor, sink = mixed[0:count // 2 * 2:2], mixed[1:count // 2 * 2:2]
    margin = jnp.minimum(tallies[donor] - 1, bound - tallies[sink]) // 2
    margin = jnp.where((donor == sequence[0]) | (sink == sequence[0]) | (tallies[sink] == 0), 0, jnp.maximum(margin, 0))
    shifted = jax.random.randint(jax.random.fold_in(own, 4), (count // 2,), 0, 1 << 20) % (margin + 1)
    tallies = tallies.at[donor].add(-shifted).at[sink].add(shifted)
    members = jnp.searchsorted(jnp.cumsum(tallies), jnp.arange(rows * top), side="right").astype(jnp.int32)
    grid = members.reshape(top, rows).T
    grid = grid[jax.random.permutation(jax.random.fold_in(own, 1), rows)]
    turn = jax.random.randint(jax.random.fold_in(own, 2), (rows, 1), 0, top)
    return jnp.take_along_axis(grid, (jnp.arange(top)[None, :] + turn) % top, axis=1)


def portions_of(amount, total, most, skew, full):
    portions = [(1 << 20) // math.isqrt(standing ** skew) + 1 for standing in range(1, amount + 1)]
    largest = most if full else min(most, max(-(-total // amount), total * portions[0] // sum(portions)))
    least = 1 if total - largest >= amount - 1 else 0
    counts, surplus = [largest] + [least] * (amount - 1), total - largest - least * (amount - 1)
    while surplus > 0:
        free = [i for i in range(1, amount) if counts[i] < largest] or [i for i in range(1, amount) if counts[i] < most]
        pool, remaining = sum([portions[i] for i in free]), surplus
        for i in free:
            addition = min(most - counts[i], max(1, remaining * portions[i] // pool), surplus)
            counts[i] = counts[i] + addition
            surplus = surplus - addition
    return np.array(counts)


def gaussian(stream_key, dims, width, reach, pieces=(), kind=jnp.bfloat16):
    factor_of = steps_of(stream_key, dims, pieces, -0.22, 0.18) if pieces else 1.0
    entries = jax.random.normal(stream_key, dims, jnp.float32) * width * factor_of
    return jnp.minimum(jnp.maximum(entries, -reach), reach).astype(kind)


def setup_inputs(seed: int = 0) -> dict:
    keys = jax.random.split(jax.random.key(seed), 14)
    tokens = gaussian(keys[0], (TOKENS, D), 1.0, 6.0, ((0, 32),))
    cotangent = gaussian(keys[1], (TOKENS, D), 1.0, 6.0, ((0, 32),))
    segment_ids = draw_segment_ids(jax.random.fold_in(keys[13], 71), 0)
    routes_keys = jax.random.split(jax.random.fold_in(keys[3], 1), TOKENS // TOK_DEV)
    routes_turns = jax.random.permutation(jax.random.fold_in(keys[3], 3), TOKENS // TOK_DEV)
    routes = jax.vmap(lambda own, number: deal_out(jax.random.fold_in(keys[3], 2), own, number, TOK_DEV, EXPERTS, TOP, CAP, 1))(routes_keys, routes_turns).reshape((TOKENS, TOP))
    attn_in = gaussian(keys[4], (D, 3 * D), D ** -0.5, 0.125, ((0, 32),))
    attn_out = gaussian(keys[5], (D, D), (D // 16) ** -0.5, 0.5, ((0, 32),))
    gain_attn = jnp.clip(1.0 + 0.18 * jax.random.normal(keys[6], (D,), jnp.float32), 0.099609375, 1.8984375).astype(jnp.bfloat16)
    shared_in = gaussian(keys[7], (D, 2 * SH), D ** -0.5, 0.125, ((0, 32),))
    shared_out = gaussian(keys[8], (SH, D), (SH // 2) ** -0.5, 0.15625, ((0, 32),))
    router = gaussian(keys[9], (D, EXPERTS), (4 * D) ** -0.5, 0.0625, ((0, 32),))
    gain_ffn = jnp.clip(1.0 + 0.18 * jax.random.normal(keys[10], (D,), jnp.float32), 0.099609375, 1.8984375).astype(jnp.bfloat16)
    expert_in = gaussian(keys[11], (EXPERTS, D, 2 * FF), D ** -0.5, 0.125, ((0, 16), (1, 2)))
    expert_out = gaussian(keys[12], (EXPERTS, FF, D), (FF // 4) ** -0.5, 0.3125, ((0, 16), (1, 2)))
    return {"tokens": tokens, "cotangent": cotangent, "segment_ids": segment_ids, "routes": routes, "attn_in": attn_in, "attn_out": attn_out, "gain_attn": gain_attn, "shared_in": shared_in, "shared_out": shared_out, "router": router, "gain_ffn": gain_ffn, "expert_in": expert_in, "expert_out": expert_out}


EPS = 1e-06
THETA = 10000.0
NEG = -1e+30
HIGHEST = lax.Precision.HIGHEST

@jax.custom_vjp
def low(v):
    return lax.optimization_barrier(v.astype(jnp.bfloat16)).astype(jnp.float32)

@jax.custom_vjp
def low_back(v):
    return v

def low_keep(v):
    return (low(v), None)

def low_pass(kept, grad):
    return (grad,)

def back_keep(v):
    return (v, None)

def back_low(kept, grad):
    return (low(grad),)
low.defvjp(low_keep, low_pass)
low_back.defvjp(back_keep, back_low)

def matmul(left, right):
    return jnp.dot(left, right, precision=HIGHEST, preferred_element_type=jnp.float32)

def rms_norm(values, gain):
    return values * lax.rsqrt(lax.optimization_barrier(jnp.mean(values * values, axis=-1, keepdims=True)) + EPS) * gain

def rope_tables(segments):
    length = segments.shape[0]
    places = jnp.arange(length, dtype=jnp.int32)
    starts = jnp.concatenate([jnp.ones((1,), dtype=jnp.bool_), segments[1:] != segments[:-1]])
    first_place = lax.cummax(jnp.where(starts, places, 0), axis=0)
    offset = (places - first_place).astype(jnp.float32)
    half_dim = HEAD_DIM // 2
    freqs = jnp.exp(jnp.arange(half_dim, dtype=jnp.float32) * (-2.0 * math.log(THETA) / HEAD_DIM))
    angles = offset[:, None] * freqs[None, :]
    return (jnp.cos(angles)[:, None, :], jnp.sin(angles)[:, None, :])

def rotate(values, cos_table, sin_table):
    half_dim = values.shape[-1] // 2
    first_half = values[..., :half_dim]
    second_half = values[..., half_dim:]
    return jnp.concatenate([first_half * cos_table - second_half * sin_table, second_half * cos_table + first_half * sin_table], axis=-1)

def block_forward(params, hidden_in, segments, chosen_ids):
    attn_in, attn_out, gain_attn, shared_in, shared_out, router, gain_ffn, expert_in, expert_out = params
    length = hidden_in.shape[0]
    cos_table, sin_table = rope_tables(segments)
    norm_one = low(rms_norm(hidden_in, gain_attn))
    qkv_rows = low_back(matmul(norm_one, attn_in)).reshape(length, 3, HEADS, HEAD_DIM)
    query_rows = low(rotate(qkv_rows[:, 0], cos_table, sin_table))
    key_rows = low(rotate(qkv_rows[:, 1], cos_table, sin_table))
    value_rows = low(qkv_rows[:, 2])
    scores = low_back(jnp.einsum('qhd,khd->hqk', query_rows, key_rows, precision=HIGHEST) * HEAD_DIM ** (-0.5))
    places = jnp.arange(length)
    allowed = (places[:, None] >= places[None, :]) & (segments[:, None] == segments[None, :])
    scores = jnp.where(allowed[None], scores, NEG)
    probs = low(jax.nn.softmax(scores, axis=-1))
    mixed = jnp.einsum('hqk,khd->qhd', probs, value_rows, precision=HIGHEST).reshape(length, D)
    mixed = low(low_back(mixed))
    resid = hidden_in + low_back(matmul(mixed, attn_out))
    norm_two = low(rms_norm(resid, gain_ffn))
    logits = matmul(norm_two, router)
    picks = (chosen_ids[:, :, None] == jnp.arange(EXPERTS)[None, None, :]).astype(jnp.float32)
    gates = jax.nn.softmax(jnp.einsum('tke,te->tk', picks, logits, precision=HIGHEST), axis=-1)
    weights = jnp.einsum('tk,tke->et', gates, picks, precision=HIGHEST)
    shared_pre = low_back(matmul(norm_two, shared_in))
    shared_act = low(jax.nn.silu(shared_pre[:, :SH]) * shared_pre[:, SH:])
    shared_res = low_back(matmul(shared_act, shared_out))

    def one_expert(running, expert_item):
        weight_up, weight_down, column = expert_item
        expert_rows = low_back(norm_two)
        expert_pre = low_back(matmul(expert_rows, weight_up))
        expert_act = low(jax.nn.silu(expert_pre[:, :FF]) * expert_pre[:, FF:])
        result = low(low_back(matmul(expert_act, weight_down)))
        return (running + column[:, None] * result, None)
    routed, _ = lax.scan(jax.checkpoint(one_expert), jnp.zeros((length, D), jnp.float32), (expert_in, expert_out, weights))
    return resid + shared_res + routed

def reference(tokens, cotangent, segment_ids, routes, attn_in, attn_out, gain_attn, shared_in, shared_out, router, gain_ffn, expert_in, expert_out):
    params = tuple((weight.astype(jnp.float32) for weight in (attn_in, attn_out, gain_attn, shared_in, shared_out, router, gain_ffn, expert_in, expert_out)))
    seq_inputs = tokens.astype(jnp.float32).reshape(SEQS, SEQ_LEN, D)
    seq_cots = cotangent.astype(jnp.float32).reshape(SEQS, SEQ_LEN, D)
    seq_routes = routes.reshape(SEQS, SEQ_LEN, TOP)

    def seq_step(running, seq_item):
        seq_input, seq_cot, seq_segments, seq_ids = seq_item
        result, pullback = jax.vjp(lambda weights_now, inputs_now: block_forward(weights_now, inputs_now, seq_segments, seq_ids), params, seq_input)
        grad_params, grad_input = pullback(seq_cot)
        running = jax.tree.map(lambda left, right: left + right, running, grad_params)
        return (running, (result.astype(jnp.bfloat16), grad_input.astype(jnp.bfloat16)))
    starting = jax.tree.map(jnp.zeros_like, params)
    totals, (results, input_grads) = lax.scan(seq_step, starting, (seq_inputs, seq_cots, segment_ids, seq_routes))
    return (results.reshape(TOKENS, D), input_grads.reshape(TOKENS, D), totals[0], totals[1], totals[2], totals[3], totals[4], totals[5], totals[6], totals[7], totals[8])
```

```python
import math

import jax
import jax.numpy as jnp
from jax import lax
from jax.sharding import PartitionSpec as P

HEADS = 16
HEAD_DIM = 128
TOP = 6


EPS = 1e-06
THETA = 10000.0
NEG = -1e30
HIGHEST = lax.Precision.HIGHEST
BF16 = jnp.bfloat16
F32 = jnp.float32


def rope_tables(segments):
    length = segments.shape[0]
    places = jnp.arange(length, dtype=jnp.int32)
    starts = jnp.concatenate([jnp.ones((1,), dtype=jnp.bool_), segments[1:] != segments[:-1]])
    first_place = lax.cummax(jnp.where(starts, places, 0), axis=0)
    offset = (places - first_place).astype(jnp.float32)
    half_dim = HEAD_DIM // 2
    freqs = jnp.exp(jnp.arange(half_dim, dtype=jnp.float32) * (-2.0 * math.log(THETA) / HEAD_DIM))
    angles = offset[:, None] * freqs[None, :]
    return jnp.cos(angles), jnp.sin(angles)


def rotate(values, cos_table, sin_table):
    half_dim = values.shape[-1] // 2
    first_half = values[..., :half_dim]
    second_half = values[..., half_dim:]
    return jnp.concatenate(
        [
            first_half * cos_table - second_half * sin_table,
            second_half * cos_table + first_half * sin_table,
        ],
        axis=-1,
    )


def unrotate(grads, cos_table, sin_table):
    return rotate(grads, cos_table, -sin_table)


def silu_back(grad_act, gate_part, up_part):
    sigmoid_gate = jax.nn.sigmoid(gate_part)
    gate_grad = grad_act * up_part * sigmoid_gate * (1.0 + gate_part * (1.0 - sigmoid_gate))
    up_grad = grad_act * gate_part * sigmoid_gate
    return jnp.concatenate([gate_grad, up_grad], axis=-1)


def dot(left, right):
    return jnp.dot(left, right, preferred_element_type=F32)


def dot_tn(left, right):
    return lax.dot_general(left, right, (((0,), (0,)), ((), ())), preferred_element_type=F32)


def dot_nt(left, right):
    return lax.dot_general(left, right, (((1,), (1,)), ((), ())), preferred_element_type=F32)


def dp_gather(value):
    count = lax.axis_size("dp")
    if count == 1:
        return value[None]
    here = lax.axis_index("dp")
    parts = [value] + [
        lax.ppermute(value, "dp", [(i, (i - step) % count) for i in range(count)])
        for step in range(1, count)
    ]
    if count == 2:
        first = here == 0
        return jnp.stack(
            [jnp.where(first, parts[0], parts[1]), jnp.where(first, parts[1], parts[0])]
        )
    whole = jnp.zeros((count,) + value.shape, value.dtype)
    for step, part in enumerate(parts):
        whole = lax.dynamic_update_index_in_dim(whole, part, (here + step) % count, 0)
    return whole


def dp_scatter(value):
    count = lax.axis_size("dp")
    here = lax.axis_index("dp")
    total = lax.dynamic_index_in_dim(value, here, 0, keepdims=False)
    for step in range(1, count):
        block = lax.dynamic_index_in_dim(value, (here + step) % count, 0, keepdims=False)
        got = lax.ppermute(
            block.astype(BF16), "dp", [(i, (i + step) % count) for i in range(count)]
        )
        total = total + got.astype(F32)
    return total


def gather_rows(value):
    return lax.all_gather(value, "expert", axis=0, tiled=True)


def scatter_rows(value):
    return lax.psum_scatter(value, "expert", scatter_dimension=0, tiled=True)


def swap(value):
    return lax.all_to_all(value, "expert", split_axis=0, concat_axis=0, tiled=True)


def per_device(
    tokens,
    cotangent,
    segment_ids,
    routes,
    attn_in,
    attn_out,
    gain_attn,
    shared_in,
    shared_out,
    router,
    gain_ffn,
    expert_in,
    expert_out,
):
    n_dp, n_e = lax.axis_size("dp"), lax.axis_size("expert")
    me = lax.axis_index("expert")
    count, width = tokens.shape
    segments = segment_ids[0]
    length = segments.shape[0]
    rows = attn_in.shape[0]
    capacity = min(count, 3 * TOP * count // (2 * n_e))
    shared_rows = shared_out.shape[0]
    shared_width = shared_rows * n_dp
    expert_width = expert_out.shape[1] * n_dp
    score_scale = HEAD_DIM ** (-0.5)

    hidden_in = tokens.astype(F32)
    inverse_one = lax.rsqrt(jnp.mean(hidden_in * hidden_in, axis=-1, keepdims=True) + EPS)
    normed_one = hidden_in * inverse_one
    gain_rows = gain_attn.astype(F32)[:, None]
    head_w = (attn_in.astype(F32) * gain_rows).astype(BF16)
    head_w = head_w.reshape(rows, 3, n_e, HEAD_DIM).transpose(2, 0, 1, 3)
    head_w = swap(head_w.reshape(n_e, rows, 3 * HEAD_DIM))
    norm_all = gather_rows(normed_one.astype(BF16))
    head_w = dp_gather(head_w).reshape(width, 3 * HEAD_DIM)
    share_w = shared_in.reshape(rows, 2, n_dp, n_e, shared_rows).transpose(3, 0, 1, 2, 4)
    share_w = swap(share_w.reshape(n_e, rows, 2 * shared_width))
    share_w = dp_gather(share_w).reshape(width, 2 * shared_width)
    share_out = dp_gather(shared_out).reshape(shared_width, width)

    small = jnp.concatenate([router, gain_ffn[:, None]], axis=1)
    small = dp_gather(small).reshape(-1, router.shape[1] + 1)
    small_rows = small.shape[0]
    extra = jnp.zeros((count, 128), BF16)
    extra = extra.at[:small_rows, : small.shape[1]].set(small)
    extra = extra.at[:, 64 : 64 + TOP].set(routes.astype(BF16))
    cot_all = gather_rows(jnp.concatenate([cotangent, extra], axis=1))
    proj_all = lax.all_gather(attn_out, ("dp", "expert"), axis=0, tiled=True)
    extra_all = cot_all[:, width:]
    cot_all = cot_all[:, :width]
    small = extra_all.reshape(n_e, count, 128)[:, :small_rows, : router.shape[1] + 1]
    small = small.reshape(n_e, n_dp, rows, -1).transpose(1, 0, 2, 3).reshape(width, -1)
    router_full = small[:, : router.shape[1]]
    gain_second = small[:, router.shape[1]].astype(F32)
    routes_all = extra_all[:, 64 : 64 + TOP].astype(F32)

    cos_table, sin_table = rope_tables(segments)
    qkv = dot(norm_all, head_w)
    query = rotate(qkv[:, :HEAD_DIM], cos_table, sin_table).astype(BF16)
    key = rotate(qkv[:, HEAD_DIM : 2 * HEAD_DIM], cos_table, sin_table).astype(BF16)
    value = qkv[:, 2 * HEAD_DIM :].astype(BF16)
    places = jnp.arange(length, dtype=jnp.int32)
    allowed = (places[:, None] >= places[None, :]) & (segments[:, None] == segments[None, :])
    scores = jnp.where(allowed, dot_nt(query, key) * score_scale, NEG)
    row_max = jnp.max(scores, axis=-1, keepdims=True)
    shifted = jnp.exp(scores - row_max)
    row_total = jnp.sum(shifted, axis=-1, keepdims=True)
    log_total = row_max + jnp.log(row_total)
    probs_low = (shifted / row_total).astype(BF16)
    mixed = dot(probs_low, value).astype(BF16)
    mixed = swap(mixed.reshape(n_e, count, HEAD_DIM))
    mixed = mixed.transpose(1, 0, 2).reshape(count, width)
    resid = hidden_in + dot(mixed, proj_all)

    inverse_two = lax.rsqrt(jnp.mean(resid * resid, axis=-1, keepdims=True) + EPS)
    normed_two = resid * inverse_two
    norm_two = (normed_two * gain_second).astype(BF16)
    logits = dot(norm_two, router_full)
    picked = jnp.any(routes[:, :, None] == jnp.arange(n_e)[None, None, :], axis=1)
    chosen = jnp.where(picked, logits, NEG)
    chosen = jnp.where(picked, jnp.exp(chosen - jnp.max(chosen, axis=-1, keepdims=True)), 0.0)
    gates = chosen / jnp.sum(chosen, axis=-1, keepdims=True)
    gate_high = gates.astype(BF16)
    gate_low = (gates - gate_high.astype(F32)).astype(BF16)
    blank = jnp.zeros((count, 128 - 2 * n_e), BF16)
    payload = gather_rows(jnp.concatenate([norm_two, gate_high, gate_low, blank], axis=1))
    norm_two_all = payload[:, :width]
    mine = jnp.arange(n_e) == me
    gate_all = payload[:, width : width + 2 * n_e].astype(F32).reshape(length, 2, n_e)
    gate_all = jnp.sum(jnp.where(mine, gate_all, 0.0), axis=(1, 2))

    named = jnp.any(routes_all == me.astype(F32), axis=1).reshape(n_e, count)
    ranking = jnp.cumsum(named.astype(jnp.int32), axis=1) - 1
    select = (
        named[:, None, :]
        & (ranking[:, None, :] == jnp.arange(capacity, dtype=jnp.int32)[None, :, None])
    ).astype(BF16)
    arrived = jnp.einsum(
        "bct,btd->bcd",
        select,
        norm_two_all.reshape(n_e, count, width),
        preferred_element_type=F32,
    ).astype(BF16).reshape(n_e * capacity, width)
    cot_rows = jnp.einsum(
        "bct,btd->bcd", select, cot_all.reshape(n_e, count, width), preferred_element_type=F32
    ).reshape(n_e * capacity, width)
    gate_rows = jnp.sum(
        jnp.where(select != 0, gate_all.reshape(n_e, 1, count), 0.0), axis=-1
    ).reshape(n_e * capacity, 1)

    up_own, down_own, _ = lax.optimization_barrier((expert_in[0], expert_out[0], head_w))
    expert_up = dp_gather(up_own).reshape(width, 2 * expert_width)
    expert_down = dp_gather(down_own).reshape(expert_width, width)
    expert_pre = dot(arrived, expert_up)
    expert_act = (
        jax.nn.silu(expert_pre[:, :expert_width]) * expert_pre[:, expert_width:]
    ).astype(BF16)
    expert_res = dot(expert_act, expert_down).astype(BF16).astype(F32)
    gate_grad = jnp.sum(cot_rows * expert_res, axis=-1).reshape(n_e, capacity, 1)
    gate_grad = jnp.sum(jnp.where(select != 0, gate_grad, 0.0), axis=1)
    gate_grad = swap(gate_grad)
    weighted = (gate_rows * expert_res).astype(BF16).reshape(n_e, capacity, width)

    shared_pre = dot(norm_two_all, share_w)
    shared_act = (
        jax.nn.silu(shared_pre[:, :shared_width]) * shared_pre[:, shared_width:]
    ).astype(BF16)
    out_part = dot(shared_act, share_out) + jnp.einsum(
        "bct,bcd->btd", select, weighted, preferred_element_type=F32
    ).reshape(length, width)

    route_grad = (gate_rows * cot_rows).astype(BF16)
    act_grad = dot_nt(route_grad, expert_down)
    pre_grad = silu_back(
        act_grad, expert_pre[:, :expert_width], expert_pre[:, expert_width:]
    ).astype(BF16)
    row_grad = dot_nt(pre_grad, expert_up).astype(BF16).reshape(n_e, capacity, width)
    shared_act_grad = dot_nt(cot_all, share_out)
    shared_pre_grad = silu_back(
        shared_act_grad, shared_pre[:, :shared_width], shared_pre[:, shared_width:]
    ).astype(BF16)
    norm_two_part = dot_nt(shared_pre_grad, share_w) + jnp.einsum(
        "bct,bcd->btd", select, row_grad, preferred_element_type=F32
    ).reshape(length, width)
    norm_two_grad = scatter_rows(norm_two_part.astype(BF16)).astype(F32)

    down_grad = dot_tn(expert_act, route_grad)
    up_grad = dot_tn(arrived, pre_grad)
    expert_out_grad = dp_scatter(down_grad.reshape(n_dp, -1, width))[None]
    expert_in_grad = dp_scatter(up_grad.reshape(n_dp, -1, 2 * expert_width))[None]
    share_out_grad = dp_scatter(dot_tn(shared_act, cot_all).reshape(n_dp, shared_rows, width))
    share_in_grad = dot_tn(norm_two_all, shared_pre_grad)
    share_in_grad = dp_scatter(share_in_grad.reshape(n_dp, n_e, rows, 2 * shared_width))
    share_in_grad = swap(share_in_grad.astype(BF16)).astype(F32)
    share_in_grad = (
        share_in_grad.reshape(n_e, rows, 2, n_dp, shared_rows)
        .transpose(1, 2, 3, 0, 4)
        .reshape(rows, -1)
    )

    gate_grad = gate_grad.T
    logit_grad = gates * (gate_grad - jnp.sum(gates * gate_grad, axis=-1, keepdims=True))
    router_grad = jnp.dot(
        norm_two.astype(F32).T, logit_grad, precision=HIGHEST, preferred_element_type=F32
    )
    norm_two_grad = norm_two_grad + jnp.dot(
        logit_grad, router_full.astype(F32).T, precision=HIGHEST, preferred_element_type=F32
    )
    gain_two_grad = jnp.sum(norm_two_grad * normed_two, axis=0)
    upstream = cotangent.astype(F32)
    scaled_two = norm_two_grad * gain_second
    resid_grad = upstream + inverse_two * (
        scaled_two - normed_two * jnp.mean(scaled_two * normed_two, axis=-1, keepdims=True)
    )
    small_grad = jnp.concatenate([router_grad, gain_two_grad[:, None]], axis=1)
    small_grad = small_grad.reshape(n_dp * n_e, rows, n_e + 1)
    small_grad = lax.all_to_all(
        small_grad, ("dp", "expert"), split_axis=0, concat_axis=0, tiled=True
    )
    small_grad = jnp.sum(small_grad, axis=0)

    branch_cot = resid_grad.astype(BF16)
    mixed_grad = dot_nt(branch_cot, proj_all).astype(BF16)
    mixed_grad = swap(mixed_grad.reshape(count, n_e, HEAD_DIM).transpose(1, 0, 2))
    mixed_grad = mixed_grad.reshape(length, HEAD_DIM)
    proj_grad = dot_tn(mixed, branch_cot).astype(BF16)
    attn_out_grad = lax.psum_scatter(
        proj_grad, ("dp", "expert"), scatter_dimension=0, tiled=True
    ).astype(F32)
    scores_again = jnp.where(allowed, dot_nt(query, key) * score_scale, NEG)
    probs_now = jnp.exp(scores_again - log_total)
    probs_again = probs_now.astype(BF16)
    probs_grad = dot_nt(mixed_grad, value)
    value_grad = dot_tn(probs_again, mixed_grad)
    score_grad = (
        probs_now * (probs_grad - jnp.sum(probs_grad * probs_now, axis=-1, keepdims=True))
    ).astype(BF16)
    query_grad = dot(score_grad, key) * score_scale
    key_grad = dot_tn(score_grad, query) * score_scale
    qkv_grad = jnp.concatenate(
        [
            unrotate(query_grad, cos_table, sin_table),
            unrotate(key_grad, cos_table, sin_table),
            value_grad,
        ],
        axis=1,
    ).astype(BF16)
    scaled_one = scatter_rows(dot_nt(qkv_grad, head_w).astype(BF16)).astype(F32)
    input_grad = resid_grad + inverse_one * (
        scaled_one - normed_one * jnp.mean(scaled_one * normed_one, axis=-1, keepdims=True)
    )
    head_grad = dot_tn(norm_all, qkv_grad).reshape(n_dp, n_e, rows, 3 * HEAD_DIM)
    head_grad = swap(dp_scatter(head_grad).astype(BF16)).astype(F32)
    head_grad = (
        head_grad.reshape(n_e, rows, 3, HEAD_DIM).transpose(1, 2, 0, 3).reshape(rows, 3 * width)
    )
    gain_attn_grad = jnp.sum(head_grad * attn_in.astype(F32), axis=1)
    attn_in_grad = head_grad * gain_rows
    return (
        (resid + scatter_rows(out_part.astype(BF16)).astype(F32)).astype(BF16),
        input_grad.astype(BF16),
        attn_in_grad,
        attn_out_grad,
        gain_attn_grad,
        share_in_grad,
        share_out_grad,
        small_grad[:, :n_e],
        small_grad[:, n_e],
        expert_in_grad,
        expert_out_grad,
    )


def solution(mesh):
    return jax.shard_map(
        per_device,
        mesh=mesh,
        in_specs=(
            P(("dp", "expert"), None),
            P(("dp", "expert"), None),
            P("dp", None),
            P(("dp", "expert"), None),
            P(("dp", "expert"), None),
            P(("dp", "expert"), None),
            P(("dp", "expert")),
            P(("dp", "expert"), None),
            P(("dp", "expert"), None),
            P(("dp", "expert"), None),
            P(("dp", "expert")),
            P("expert", "dp", None),
            P("expert", "dp", None),
        ),
        out_specs=(
            P(("dp", "expert"), None),
            P(("dp", "expert"), None),
            P(("dp", "expert"), None),
            P(("dp", "expert"), None),
            P(("dp", "expert")),
            P(("dp", "expert"), None),
            P(("dp", "expert"), None),
            P(("dp", "expert"), None),
            P(("dp", "expert")),
            P("expert", "dp", None),
            P("expert", "dp", None),
        ),
        check_vma=False,
    )
```

```python
import functools
import math

import jax
import jax.numpy as jnp
from jax import lax
from jax.experimental import pallas as pl
from jax.experimental.pallas import tpu as pltpu
from jax.sharding import PartitionSpec as P

HEADS = 16
HEAD_DIM = 128
TOP = 6


EPS = 1e-06
THETA = 10000.0
NEG = -1e30
HIGHEST = lax.Precision.HIGHEST
BF16 = jnp.bfloat16
F32 = jnp.float32


def rope_tables(segments):
    length = segments.shape[0]
    places = jnp.arange(length, dtype=jnp.int32)
    starts = jnp.concatenate([jnp.ones((1,), dtype=jnp.bool_), segments[1:] != segments[:-1]])
    first_place = lax.cummax(jnp.where(starts, places, 0), axis=0)
    offset = (places - first_place).astype(jnp.float32)
    half_dim = HEAD_DIM // 2
    freqs = jnp.exp(jnp.arange(half_dim, dtype=jnp.float32) * (-2.0 * math.log(THETA) / HEAD_DIM))
    angles = offset[:, None] * freqs[None, :]
    return jnp.cos(angles), jnp.sin(angles)


def rotate(values, cos_table, sin_table):
    half_dim = values.shape[-1] // 2
    first_half = values[..., :half_dim]
    second_half = values[..., half_dim:]
    return jnp.concatenate(
        [
            first_half * cos_table - second_half * sin_table,
            second_half * cos_table + first_half * sin_table,
        ],
        axis=-1,
    )


def unrotate(grads, cos_table, sin_table):
    return rotate(grads, cos_table, -sin_table)


def silu_back(grad_act, gate_part, up_part):
    sigmoid_gate = jax.nn.sigmoid(gate_part)
    gate_grad = grad_act * up_part * sigmoid_gate * (1.0 + gate_part * (1.0 - sigmoid_gate))
    up_grad = grad_act * gate_part * sigmoid_gate
    return jnp.concatenate([gate_grad, up_grad], axis=-1)


def dot(left, right):
    return jnp.dot(left, right, preferred_element_type=F32)


def dot_tn(left, right):
    return lax.dot_general(left, right, (((0,), (0,)), ((), ())), preferred_element_type=F32)


def dot_nt(left, right):
    return lax.dot_general(left, right, (((1,), (1,)), ((), ())), preferred_element_type=F32)


def dp_gather(value):
    count = lax.axis_size("dp")
    if count == 1:
        return value[None]
    here = lax.axis_index("dp")
    parts = [value] + [
        lax.ppermute(value, "dp", [(i, (i - step) % count) for i in range(count)])
        for step in range(1, count)
    ]
    if count == 2:
        first = here == 0
        return jnp.stack(
            [jnp.where(first, parts[0], parts[1]), jnp.where(first, parts[1], parts[0])]
        )
    whole = jnp.zeros((count,) + value.shape, value.dtype)
    for step, part in enumerate(parts):
        whole = lax.dynamic_update_index_in_dim(whole, part, (here + step) % count, 0)
    return whole


def dp_scatter(value):
    count = lax.axis_size("dp")
    here = lax.axis_index("dp")
    total = lax.dynamic_index_in_dim(value, here, 0, keepdims=False)
    for step in range(1, count):
        block = lax.dynamic_index_in_dim(value, (here + step) % count, 0, keepdims=False)
        got = lax.ppermute(
            block.astype(BF16), "dp", [(i, (i + step) % count) for i in range(count)]
        )
        total = total + got.astype(F32)
    return total


def ring_order():
    pairs = lax.axis_size("expert") // 2
    return list(range(0, pairs, 2)) + list(range(pairs - 1, 0, -2))


def ring_shift(value, step):
    order = ring_order()
    pairs = len(order)
    perm = [
        (order[q] * 2 + c, order[(q + step) % pairs] * 2 + c) for q in range(pairs) for c in range(2)
    ]
    return lax.ppermute(value, "expert", perm)


def core_swap(value):
    count = lax.axis_size("expert")
    return lax.ppermute(value, "expert", [(i, i ^ 1) for i in range(count)])


def ring_block(offset):
    order = ring_order()
    pairs = len(order)
    me = lax.axis_index("expert")
    table = [0] * (2 * pairs)
    for q in range(pairs):
        for c in range(2):
            table[order[q] * 2 + c] = order[(q - offset) % pairs] * 2 + c
    return jnp.asarray(table, jnp.int32)[me]


def place_kernel(spans, widths, starts_ref, *refs):
    pieces, rest = refs[: len(spans)], refs[len(spans) :]
    outs, sems = rest[: len(widths)], rest[len(widths)]
    copies = []
    for n, (piece, size) in enumerate(zip(pieces, spans)):
        row = pl.multiple_of(starts_ref[n], 16)
        left = 0
        for m, (out, wide) in enumerate(zip(outs, widths)):
            copies.append(
                pltpu.make_async_copy(
                    piece.at[:, pl.ds(left, wide)], out.at[pl.ds(row, size), :], sems.at[n, m]
                )
            )
            left += wide
    for copy in copies:
        copy.start()
    for copy in copies:
        copy.wait()


def place(pieces, starts, length, widths):
    spans = tuple(piece.shape[0] for piece in pieces)
    return pl.pallas_call(
        functools.partial(place_kernel, spans, tuple(widths)),
        out_shape=[jax.ShapeDtypeStruct((length, wide), pieces[0].dtype) for wide in widths],
        in_specs=[pl.BlockSpec(memory_space=pltpu.SMEM)]
        + [pl.BlockSpec(memory_space=pl.ANY)] * len(pieces),
        out_specs=[pl.BlockSpec(memory_space=pl.ANY)] * len(widths),
        scratch_shapes=[pltpu.SemaphoreType.DMA((len(pieces), len(widths)))],
    )(jnp.stack(starts).astype(jnp.int32), *pieces)


def gather_rows(value, widths=None):
    rows = value.shape[0]
    half_rows = rows // 2
    half = lax.axis_size("expert") // 4
    pieces, starts = [], []

    def keep(piece, offset, shift):
        block = ring_block(offset)
        pieces.append(piece)
        starts.append(block * rows + shift)
        pieces.append(core_swap(piece))
        starts.append((block ^ 1) * rows + shift)

    keep(value, 0, 0)
    ahead = back = value
    for step in range(1, half):
        ahead, back = ring_shift(ahead, 1), ring_shift(back, -1)
        keep(ahead, step, 0)
        keep(back, -step, 0)
    keep(ring_shift(ahead[:half_rows], 1), half, 0)
    keep(ring_shift(back[half_rows:], -1), -half, half_rows)
    length = rows * lax.axis_size("expert")
    whole = place(pieces, starts, length, widths or [value.shape[1]])
    return whole if widths else whole[0]


def scatter_rows(value):
    count = lax.axis_size("expert")
    half = count // 4
    rows = value.shape[0] // count
    half_rows = rows // 2

    def mine(offset, shift, size):
        block = ring_block(offset)
        own = lax.dynamic_slice_in_dim(value, block * rows + shift, size, 0)
        other = lax.dynamic_slice_in_dim(value, (block ^ 1) * rows + shift, size, 0)
        return own.astype(F32) + core_swap(other).astype(F32)

    ahead = ring_shift(mine(-half, 0, half_rows).astype(BF16), 1)
    back = ring_shift(mine(half, half_rows, half_rows).astype(BF16), -1)
    for step in range(half - 1, 0, -1):
        onward = mine(-step, 0, rows)
        homeward = mine(step, 0, rows)
        if step == half - 1:
            blank = jnp.zeros((half_rows, value.shape[1]), F32)
            ahead = jnp.concatenate([ahead.astype(F32), blank], axis=0)
            back = jnp.concatenate([blank, back.astype(F32)], axis=0)
        ahead = ring_shift((onward + ahead.astype(F32)).astype(BF16), 1)
        back = ring_shift((homeward + back.astype(F32)).astype(BF16), -1)
    return mine(0, 0, rows) + ahead.astype(F32) + back.astype(F32)


def swap(value):
    return lax.all_to_all(value, "expert", split_axis=0, concat_axis=0, tiled=True)


def per_device(
    tokens,
    cotangent,
    segment_ids,
    routes,
    attn_in,
    attn_out,
    gain_attn,
    shared_in,
    shared_out,
    router,
    gain_ffn,
    expert_in,
    expert_out,
):
    n_dp, n_e = lax.axis_size("dp"), lax.axis_size("expert")
    me = lax.axis_index("expert")
    count, width = tokens.shape
    segments = segment_ids[0]
    length = segments.shape[0]
    rows = attn_in.shape[0]
    capacity = min(count, 3 * TOP * count // (2 * n_e))
    shared_rows = shared_out.shape[0]
    shared_width = shared_rows * n_dp
    expert_width = expert_out.shape[1] * n_dp
    score_scale = HEAD_DIM ** (-0.5)

    hidden_in = tokens.astype(F32)
    inverse_one = lax.rsqrt(jnp.mean(hidden_in * hidden_in, axis=-1, keepdims=True) + EPS)
    normed_one = hidden_in * inverse_one
    gain_rows = gain_attn.astype(F32)[:, None]
    head_w = (attn_in.astype(F32) * gain_rows).astype(BF16)
    head_w = head_w.reshape(rows, 3, n_e, HEAD_DIM).transpose(2, 0, 1, 3)
    head_w = swap(head_w.reshape(n_e, rows, 3 * HEAD_DIM))
    norm_all = gather_rows(normed_one.astype(BF16))
    head_w = dp_gather(head_w).reshape(width, 3 * HEAD_DIM)
    share_w = shared_in.reshape(rows, 2, n_dp, n_e, shared_rows).transpose(3, 0, 1, 2, 4)
    share_w = swap(share_w.reshape(n_e, rows, 2 * shared_width))
    share_w = dp_gather(share_w).reshape(width, 2 * shared_width)
    share_out = dp_gather(shared_out).reshape(shared_width, width)

    small = jnp.concatenate([router, gain_ffn[:, None]], axis=1)
    small = dp_gather(small).reshape(-1, router.shape[1] + 1)
    small_rows = small.shape[0]
    extra = jnp.zeros((count, 128), BF16)
    extra = extra.at[:small_rows, : small.shape[1]].set(small)
    extra = extra.at[:, 64 : 64 + TOP].set(routes.astype(BF16))
    cot_all, extra_all = gather_rows(jnp.concatenate([cotangent, extra], axis=1), [width, 128])
    proj_all = dp_gather(attn_out).reshape(n_dp * rows, width)
    proj_all = gather_rows(proj_all).reshape(n_e, n_dp, rows, width)
    proj_all = proj_all.transpose(1, 0, 2, 3).reshape(width, width)
    small = extra_all.reshape(n_e, count, 128)[:, :small_rows, : router.shape[1] + 1]
    small = small.reshape(n_e, n_dp, rows, -1).transpose(1, 0, 2, 3).reshape(width, -1)
    router_full = small[:, : router.shape[1]]
    gain_second = small[:, router.shape[1]].astype(F32)
    routes_all = extra_all[:, 64 : 64 + TOP].astype(F32)

    cos_table, sin_table = rope_tables(segments)
    qkv = dot(norm_all, head_w)
    query = rotate(qkv[:, :HEAD_DIM], cos_table, sin_table).astype(BF16)
    key = rotate(qkv[:, HEAD_DIM : 2 * HEAD_DIM], cos_table, sin_table).astype(BF16)
    value = qkv[:, 2 * HEAD_DIM :].astype(BF16)
    places = jnp.arange(length, dtype=jnp.int32)
    allowed = (places[:, None] >= places[None, :]) & (segments[:, None] == segments[None, :])
    scores = jnp.where(allowed, dot_nt(query, key) * score_scale, NEG)
    row_max = jnp.max(scores, axis=-1, keepdims=True)
    shifted = jnp.exp(scores - row_max)
    row_total = jnp.sum(shifted, axis=-1, keepdims=True)
    log_total = row_max + jnp.log(row_total)
    probs_low = (shifted / row_total).astype(BF16)
    mixed = dot(probs_low, value).astype(BF16)
    mixed = swap(mixed.reshape(n_e, count, HEAD_DIM))
    mixed = mixed.transpose(1, 0, 2).reshape(count, width)
    resid = hidden_in + dot(mixed, proj_all)

    inverse_two = lax.rsqrt(jnp.mean(resid * resid, axis=-1, keepdims=True) + EPS)
    normed_two = resid * inverse_two
    norm_two = (normed_two * gain_second).astype(BF16)
    logits = dot(norm_two, router_full)
    picked = jnp.any(routes[:, :, None] == jnp.arange(n_e)[None, None, :], axis=1)
    chosen = jnp.where(picked, logits, NEG)
    chosen = jnp.where(picked, jnp.exp(chosen - jnp.max(chosen, axis=-1, keepdims=True)), 0.0)
    gates = chosen / jnp.sum(chosen, axis=-1, keepdims=True)
    gate_high = gates.astype(BF16)
    gate_low = (gates - gate_high.astype(F32)).astype(BF16)
    blank = jnp.zeros((count, 128 - 2 * n_e), BF16)
    payload = jnp.concatenate([norm_two, gate_high, gate_low, blank], axis=1)
    norm_two_all, payload = gather_rows(payload, [width, 128])
    mine = jnp.arange(n_e) == me
    gate_all = payload[:, : 2 * n_e].astype(F32).reshape(length, 2, n_e)
    gate_all = jnp.sum(jnp.where(mine, gate_all, 0.0), axis=(1, 2))

    named = jnp.any(routes_all == me.astype(F32), axis=1).reshape(n_e, count)
    ranking = jnp.cumsum(named.astype(jnp.int32), axis=1) - 1
    select = (
        named[:, None, :]
        & (ranking[:, None, :] == jnp.arange(capacity, dtype=jnp.int32)[None, :, None])
    ).astype(BF16)
    arrived = jnp.einsum(
        "bct,btd->bcd",
        select,
        norm_two_all.reshape(n_e, count, width),
        preferred_element_type=F32,
    ).astype(BF16).reshape(n_e * capacity, width)
    cot_rows = jnp.einsum(
        "bct,btd->bcd", select, cot_all.reshape(n_e, count, width), preferred_element_type=F32
    ).reshape(n_e * capacity, width)
    gate_rows = jnp.sum(
        jnp.where(select != 0, gate_all.reshape(n_e, 1, count), 0.0), axis=-1
    ).reshape(n_e * capacity, 1)

    expert_up = lax.all_gather(expert_in, "dp", axis=1, tiled=True)[0]
    expert_down = lax.all_gather(expert_out, "dp", axis=1, tiled=True)[0]
    expert_pre = dot(arrived, expert_up)
    expert_act = (
        jax.nn.silu(expert_pre[:, :expert_width]) * expert_pre[:, expert_width:]
    ).astype(BF16)
    expert_res = dot(expert_act, expert_down).astype(BF16).astype(F32)
    gate_grad = jnp.sum(cot_rows * expert_res, axis=-1).reshape(n_e, capacity, 1)
    gate_grad = jnp.sum(jnp.where(select != 0, gate_grad, 0.0), axis=1)
    gate_grad = swap(gate_grad)
    weighted = (gate_rows * expert_res).astype(BF16).reshape(n_e, capacity, width)

    shared_pre = dot(norm_two_all, share_w)
    shared_act = (
        jax.nn.silu(shared_pre[:, :shared_width]) * shared_pre[:, shared_width:]
    ).astype(BF16)
    out_part = dot(shared_act, share_out) + jnp.einsum(
        "bct,bcd->btd", select, weighted, preferred_element_type=F32
    ).reshape(length, width)

    route_grad = (gate_rows * cot_rows).astype(BF16)
    act_grad = dot_nt(route_grad, expert_down)
    pre_grad = silu_back(
        act_grad, expert_pre[:, :expert_width], expert_pre[:, expert_width:]
    ).astype(BF16)
    row_grad = dot_nt(pre_grad, expert_up).astype(BF16).reshape(n_e, capacity, width)
    shared_act_grad = dot_nt(cot_all, share_out)
    shared_pre_grad = silu_back(
        shared_act_grad, shared_pre[:, :shared_width], shared_pre[:, shared_width:]
    ).astype(BF16)
    norm_two_part = dot_nt(shared_pre_grad, share_w) + jnp.einsum(
        "bct,bcd->btd", select, row_grad, preferred_element_type=F32
    ).reshape(length, width)
    norm_two_grad = scatter_rows(norm_two_part.astype(BF16))

    down_grad = dot_tn(expert_act, route_grad)
    up_grad = dot_tn(arrived, pre_grad)
    expert_out_grad = lax.psum_scatter(
        down_grad.astype(BF16), "dp", scatter_dimension=0, tiled=True
    ).astype(F32)[None]
    expert_in_grad = lax.psum_scatter(
        up_grad.astype(BF16), "dp", scatter_dimension=0, tiled=True
    ).astype(F32)[None]
    share_out_grad = dp_scatter(dot_tn(shared_act, cot_all).reshape(n_dp, shared_rows, width))
    share_in_grad = dot_tn(norm_two_all, shared_pre_grad)
    share_in_grad = dp_scatter(share_in_grad.reshape(n_dp, n_e, rows, 2 * shared_width))
    share_in_grad = swap(share_in_grad.astype(BF16)).astype(F32)
    share_in_grad = (
        share_in_grad.reshape(n_e, rows, 2, n_dp, shared_rows)
        .transpose(1, 2, 3, 0, 4)
        .reshape(rows, -1)
    )

    gate_grad = gate_grad.T
    logit_grad = gates * (gate_grad - jnp.sum(gates * gate_grad, axis=-1, keepdims=True))
    router_grad = jnp.dot(
        norm_two.astype(F32).T, logit_grad, precision=HIGHEST, preferred_element_type=F32
    )
    norm_two_grad = norm_two_grad + jnp.dot(
        logit_grad, router_full.astype(F32).T, precision=HIGHEST, preferred_element_type=F32
    )
    gain_two_grad = jnp.sum(norm_two_grad * normed_two, axis=0)
    upstream = cotangent.astype(F32)
    scaled_two = norm_two_grad * gain_second
    resid_grad = upstream + inverse_two * (
        scaled_two - normed_two * jnp.mean(scaled_two * normed_two, axis=-1, keepdims=True)
    )
    small_grad = jnp.concatenate([router_grad, gain_two_grad[:, None]], axis=1)
    small_grad = small_grad.reshape(n_dp * n_e, rows, n_e + 1)
    small_grad = lax.all_to_all(
        small_grad, ("dp", "expert"), split_axis=0, concat_axis=0, tiled=True
    )
    small_grad = jnp.sum(small_grad, axis=0)

    branch_cot = resid_grad.astype(BF16)
    mixed_grad = dot_nt(branch_cot, proj_all).astype(BF16)
    mixed_grad = swap(mixed_grad.reshape(count, n_e, HEAD_DIM).transpose(1, 0, 2))
    mixed_grad = mixed_grad.reshape(length, HEAD_DIM)
    proj_grad = dot_tn(mixed, branch_cot).astype(BF16)
    proj_grad = proj_grad.reshape(n_dp, n_e, rows, width).transpose(1, 0, 2, 3)
    proj_grad = scatter_rows(proj_grad.reshape(width, width))
    attn_out_grad = dp_scatter(proj_grad.reshape(n_dp, rows, width))
    scores_again = jnp.where(allowed, dot_nt(query, key) * score_scale, NEG)
    probs_now = jnp.exp(scores_again - log_total)
    probs_again = probs_now.astype(BF16)
    probs_grad = dot_nt(mixed_grad, value)
    value_grad = dot_tn(probs_again, mixed_grad)
    score_grad = (
        probs_now * (probs_grad - jnp.sum(probs_grad * probs_now, axis=-1, keepdims=True))
    ).astype(BF16)
    query_grad = dot(score_grad, key) * score_scale
    key_grad = dot_tn(score_grad, query) * score_scale
    qkv_grad = jnp.concatenate(
        [
            unrotate(query_grad, cos_table, sin_table),
            unrotate(key_grad, cos_table, sin_table),
            value_grad,
        ],
        axis=1,
    ).astype(BF16)
    scaled_one = scatter_rows(dot_nt(qkv_grad, head_w).astype(BF16))
    input_grad = resid_grad + inverse_one * (
        scaled_one - normed_one * jnp.mean(scaled_one * normed_one, axis=-1, keepdims=True)
    )
    head_grad = dot_tn(norm_all, qkv_grad).reshape(n_dp, n_e, rows, 3 * HEAD_DIM)
    head_grad = swap(dp_scatter(head_grad).astype(BF16)).astype(F32)
    head_grad = (
        head_grad.reshape(n_e, rows, 3, HEAD_DIM).transpose(1, 2, 0, 3).reshape(rows, 3 * width)
    )
    gain_attn_grad = jnp.sum(head_grad * attn_in.astype(F32), axis=1)
    attn_in_grad = head_grad * gain_rows
    return (
        (resid + scatter_rows(out_part.astype(BF16))).astype(BF16),
        input_grad.astype(BF16),
        attn_in_grad,
        attn_out_grad,
        gain_attn_grad,
        share_in_grad,
        share_out_grad,
        small_grad[:, :n_e],
        small_grad[:, n_e],
        expert_in_grad,
        expert_out_grad,
    )


def solution(mesh):
    return jax.shard_map(
        per_device,
        mesh=mesh,
        in_specs=(
            P(("dp", "expert"), None),
            P(("dp", "expert"), None),
            P("dp", None),
            P(("dp", "expert"), None),
            P(("dp", "expert"), None),
            P(("dp", "expert"), None),
            P(("dp", "expert")),
            P(("dp", "expert"), None),
            P(("dp", "expert"), None),
            P(("dp", "expert"), None),
            P(("dp", "expert")),
            P("expert", "dp", None),
            P("expert", "dp", None),
        ),
        out_specs=(
            P(("dp", "expert"), None),
            P(("dp", "expert"), None),
            P(("dp", "expert"), None),
            P(("dp", "expert"), None),
            P(("dp", "expert")),
            P(("dp", "expert"), None),
            P(("dp", "expert"), None),
            P(("dp", "expert"), None),
            P(("dp", "expert")),
            P("expert", "dp", None),
            P("expert", "dp", None),
        ),
        check_vma=False,
    )
```

```python
import functools
import math

import jax
import jax.numpy as jnp
from jax import lax
from jax.experimental import pallas as pl
from jax.experimental.pallas import tpu as pltpu
from jax.sharding import PartitionSpec as P

HEADS = 16
HEAD_DIM = 128
TOP = 6


EPS = 1e-06
THETA = 10000.0
NEG = -1e30
HIGHEST = lax.Precision.HIGHEST
BF16 = jnp.bfloat16
F32 = jnp.float32
LOG2E = math.log2(math.e)


def rope_tables(segments):
    length = segments.shape[0]
    places = jnp.arange(length, dtype=jnp.int32)
    starts = jnp.concatenate([jnp.ones((1,), dtype=jnp.bool_), segments[1:] != segments[:-1]])
    first_place = lax.cummax(jnp.where(starts, places, 0), axis=0)
    offset = (places - first_place).astype(jnp.float32)
    half_dim = HEAD_DIM // 2
    freqs = jnp.exp(jnp.arange(half_dim, dtype=jnp.float32) * (-2.0 * math.log(THETA) / HEAD_DIM))
    angles = offset[:, None] * freqs[None, :]
    cos_table, sin_table = jnp.cos(angles), jnp.sin(angles)
    return (
        jnp.concatenate([cos_table, cos_table], axis=1),
        jnp.concatenate([-sin_table, sin_table], axis=1),
        first_place[None, :],
    )


def silu_back(grad_act, gate_part, up_part):
    sigmoid_gate = jax.nn.sigmoid(gate_part)
    gate_grad = grad_act * up_part * sigmoid_gate * (1.0 + gate_part * (1.0 - sigmoid_gate))
    up_grad = grad_act * gate_part * sigmoid_gate
    return jnp.concatenate([gate_grad, up_grad], axis=-1)


def dot(left, right):
    return jnp.dot(left, right, preferred_element_type=F32)


def dot_tn(left, right):
    return lax.dot_general(left, right, (((0,), (0,)), ((), ())), preferred_element_type=F32)


def dot_nt(left, right):
    return lax.dot_general(left, right, (((1,), (1,)), ((), ())), preferred_element_type=F32)


def turn(values, cos_table, sin_table):
    return values * cos_table + pltpu.roll(values, HEAD_DIM // 2, 1) * sin_table


def attend_kernel(block, qkv_ref, cos_ref, sin_ref, start_ref, o_ref, q_ref, k_ref, v_ref, lse_ref, vt_ref):
    length = qkv_ref.shape[0]
    step = pl.program_id(0)
    factor = HEAD_DIM ** (-0.5) * LOG2E

    @pl.when(step == 0)
    def _():
        cos_table, sin_table = cos_ref[...], sin_ref[...]
        q_ref[...] = turn(qkv_ref[:, :HEAD_DIM], cos_table, sin_table).astype(BF16)
        k_ref[...] = turn(qkv_ref[:, HEAD_DIM : 2 * HEAD_DIM], cos_table, sin_table).astype(BF16)
        value = qkv_ref[:, 2 * HEAD_DIM :]
        v_ref[...] = value.astype(BF16)
        vt_ref[...] = value.T.astype(BF16)

    for i in range(length // block):

        @pl.when(step == i)
        def _(i=i):
            low, high = i * block, (i + 1) * block
            raw = dot_nt(k_ref[:high, :], q_ref[low:high, :])
            keys = lax.broadcasted_iota(jnp.int32, raw.shape, 0)
            queries = low + lax.broadcasted_iota(jnp.int32, raw.shape, 1)
            allowed = (keys <= queries) & (keys >= start_ref[:, low:high])
            raw = jnp.where(allowed, raw, NEG)
            top = jnp.max(raw, axis=0, keepdims=True)
            shifted = jnp.exp2((raw - top) * factor)
            total = jnp.sum(shifted, axis=0, keepdims=True)
            probs = (shifted * (1.0 / total)).astype(BF16)
            mixed = dot(vt_ref[:, :high], probs)
            o_ref[low:high, :] = mixed.T.astype(BF16)
            lse_ref[:, low:high] = top * factor + jnp.log2(total)


def attend(qkv, cos_table, sin_table, first_place):
    length = qkv.shape[0]
    block = min(256, length)
    whole = lambda shape: pl.BlockSpec(shape, lambda i: (0, 0))
    head = jax.ShapeDtypeStruct((length, HEAD_DIM), BF16)
    return pl.pallas_call(
        functools.partial(attend_kernel, block),
        grid=(length // block,),
        out_shape=[head, head, head, head, jax.ShapeDtypeStruct((1, length), F32)],
        in_specs=[
            whole((length, 3 * HEAD_DIM)),
            whole((length, HEAD_DIM)),
            whole((length, HEAD_DIM)),
            whole((1, length)),
        ],
        out_specs=[whole((length, HEAD_DIM))] * 4 + [whole((1, length))],
        scratch_shapes=[pltpu.VMEM((HEAD_DIM, length), BF16)],
        compiler_params=pltpu.CompilerParams(vmem_limit_bytes=48 * 2**20),
        name="attend",
    )(qkv, cos_table, sin_table, first_place)


def attend_back_kernel(
    block, q_ref, k_ref, v_ref, do_ref, lse_ref, start_ref, cos_ref, sin_ref, out_ref, kt_ref, dk_ref, dv_ref
):
    length = q_ref.shape[0]
    step = pl.program_id(0)
    scale = HEAD_DIM ** (-0.5)
    factor = scale * LOG2E
    count = length // block

    @pl.when(step == 0)
    def _():
        kt_ref[...] = k_ref[...].astype(F32).T.astype(BF16)
        dk_ref[...] = jnp.zeros_like(dk_ref)
        dv_ref[...] = jnp.zeros_like(dv_ref)

    for i in range(count):

        @pl.when(step == i)
        def _(i=i):
            low, high = i * block, (i + 1) * block
            query, grad = q_ref[low:high, :], do_ref[low:high, :]
            raw = dot_nt(k_ref[:high, :], query)
            keys = lax.broadcasted_iota(jnp.int32, raw.shape, 0)
            queries = low + lax.broadcasted_iota(jnp.int32, raw.shape, 1)
            allowed = (keys <= queries) & (keys >= start_ref[:, low:high])
            raw = jnp.where(allowed, raw * factor - lse_ref[:, low:high], NEG)
            probs = jnp.exp2(raw)
            probs_grad = dot_nt(v_ref[:high, :], grad)
            inner = jnp.sum(probs_grad * probs, axis=0, keepdims=True)
            score_grad = (probs * (probs_grad - inner)).astype(BF16)
            dv_ref[:high, :] += dot(probs.astype(BF16), grad)
            dk_ref[:high, :] += dot(score_grad, query)
            query_grad = dot(kt_ref[:, :high], score_grad).T * scale
            out_ref[low:high, :HEAD_DIM] = turn(
                query_grad, cos_ref[low:high, :], -sin_ref[low:high, :]
            ).astype(BF16)

    @pl.when(step == count - 1)
    def _():
        out_ref[:, HEAD_DIM : 2 * HEAD_DIM] = turn(
            dk_ref[...] * scale, cos_ref[...], -sin_ref[...]
        ).astype(BF16)
        out_ref[:, 2 * HEAD_DIM :] = dv_ref[...].astype(BF16)


def attend_back(query, key, value, grad, lse, first_place, cos_table, sin_table):
    length = query.shape[0]
    block = min(256, length)
    whole = lambda shape: pl.BlockSpec(shape, lambda i: (0, 0))
    head = whole((length, HEAD_DIM))
    return pl.pallas_call(
        functools.partial(attend_back_kernel, block),
        grid=(length // block,),
        out_shape=jax.ShapeDtypeStruct((length, 3 * HEAD_DIM), BF16),
        in_specs=[head] * 4 + [whole((1, length))] * 2 + [head] * 2,
        out_specs=whole((length, 3 * HEAD_DIM)),
        scratch_shapes=[
            pltpu.VMEM((HEAD_DIM, length), BF16),
            pltpu.VMEM((length, HEAD_DIM), F32),
            pltpu.VMEM((length, HEAD_DIM), F32),
        ],
        compiler_params=pltpu.CompilerParams(vmem_limit_bytes=48 * 2**20),
        name="attend_back",
    )(query, key, value, grad, lse, first_place, cos_table, sin_table)


def dp_gather(value):
    count = lax.axis_size("dp")
    if count == 1:
        return value[None]
    here = lax.axis_index("dp")
    parts = [value] + [
        lax.ppermute(value, "dp", [(i, (i - step) % count) for i in range(count)])
        for step in range(1, count)
    ]
    if count == 2:
        first = here == 0
        return jnp.stack(
            [jnp.where(first, parts[0], parts[1]), jnp.where(first, parts[1], parts[0])]
        )
    whole = jnp.zeros((count,) + value.shape, value.dtype)
    for step, part in enumerate(parts):
        whole = lax.dynamic_update_index_in_dim(whole, part, (here + step) % count, 0)
    return whole


def dp_scatter(value):
    count = lax.axis_size("dp")
    here = lax.axis_index("dp")
    total = lax.dynamic_index_in_dim(value, here, 0, keepdims=False)
    for step in range(1, count):
        block = lax.dynamic_index_in_dim(value, (here + step) % count, 0, keepdims=False)
        got = lax.ppermute(
            block.astype(BF16), "dp", [(i, (i + step) % count) for i in range(count)]
        )
        total = total + got.astype(F32)
    return total


def ring_order():
    pairs = lax.axis_size("expert") // 2
    return list(range(0, pairs, 2)) + list(range(pairs - 1, 0, -2))


def ring_shift(value, step):
    order = ring_order()
    pairs = len(order)
    perm = [
        (order[q] * 2 + c, order[(q + step) % pairs] * 2 + c) for q in range(pairs) for c in range(2)
    ]
    return lax.ppermute(value, "expert", perm)


def core_swap(value):
    count = lax.axis_size("expert")
    return lax.ppermute(value, "expert", [(i, i ^ 1) for i in range(count)])


def ring_block(offset):
    order = ring_order()
    pairs = len(order)
    me = lax.axis_index("expert")
    table = [0] * (2 * pairs)
    for q in range(pairs):
        for c in range(2):
            table[order[q] * 2 + c] = order[(q - offset) % pairs] * 2 + c
    return jnp.asarray(table, jnp.int32)[me]


def place_kernel(sources, widths, order_ref, *refs):
    pieces, outs = refs[: -len(widths)], refs[-len(widths) :]
    step = pl.program_id(0)
    for n, parts in enumerate(sources):

        @pl.when(step == n)
        def _(parts=parts):
            low = 0
            for part in parts:
                size = pieces[part].shape[0]
                left = 0
                for out, wide in zip(outs, widths):
                    out[low : low + size, :] = pieces[part][:, left : left + wide]
                    left += wide
                low += size


def place(pieces, sources, order, rows, widths):
    length = rows * len(sources)
    spec = pltpu.PrefetchScalarGridSpec(
        num_scalar_prefetch=1,
        grid=(len(sources),),
        in_specs=[pl.BlockSpec(piece.shape, lambda i, order: (0, 0)) for piece in pieces],
        out_specs=[pl.BlockSpec((rows, wide), lambda i, order: (order[i], 0)) for wide in widths],
    )
    return pl.pallas_call(
        functools.partial(place_kernel, sources, tuple(widths)),
        out_shape=[jax.ShapeDtypeStruct((length, wide), pieces[0].dtype) for wide in widths],
        grid_spec=spec,
        compiler_params=pltpu.CompilerParams(vmem_limit_bytes=48 * 2**20),
        name="place",
    )(jnp.stack(order).astype(jnp.int32), *pieces)


def gather_rows(value, widths=None, after=None):
    if after is not None:
        value, _ = lax.optimization_barrier((value, after))
    rows = value.shape[0]
    half_rows = rows // 2
    half = lax.axis_size("expert") // 4
    pieces, sources, order = [], [], []

    def keep(parts, offset):
        block = ring_block(offset)
        for group, place_of in ((parts, block), ([core_swap(p) for p in parts], block ^ 1)):
            sources.append(tuple(range(len(pieces), len(pieces) + len(group))))
            pieces.extend(group)
            order.append(place_of)

    keep([value], 0)
    ahead = back = value
    for step in range(1, half):
        ahead, back = ring_shift(ahead, 1), ring_shift(back, -1)
        keep([ahead], step)
        keep([back], -step)
    last = [ring_shift(ahead[:half_rows], 1), ring_shift(back[half_rows:], -1)]
    keep(last, half)
    whole = place(pieces, sources, order, rows, widths or [value.shape[1]])
    return whole, [part[:1, :1] for part in last]


def scatter_rows(value):
    count = lax.axis_size("expert")
    half = count // 4
    rows = value.shape[0] // count
    half_rows = rows // 2

    def mine(offset, shift, size):
        block = ring_block(offset)
        own = lax.dynamic_slice_in_dim(value, block * rows + shift, size, 0)
        other = lax.dynamic_slice_in_dim(value, (block ^ 1) * rows + shift, size, 0)
        return own.astype(F32) + core_swap(other).astype(F32)

    ahead = ring_shift(mine(-half, 0, half_rows).astype(BF16), 1)
    back = ring_shift(mine(half, half_rows, half_rows).astype(BF16), -1)
    for step in range(half - 1, 0, -1):
        onward = mine(-step, 0, rows)
        homeward = mine(step, 0, rows)
        if step == half - 1:
            blank = jnp.zeros((half_rows, value.shape[1]), F32)
            ahead = jnp.concatenate([ahead.astype(F32), blank], axis=0)
            back = jnp.concatenate([blank, back.astype(F32)], axis=0)
        ahead = ring_shift((onward + ahead.astype(F32)).astype(BF16), 1)
        back = ring_shift((homeward + back.astype(F32)).astype(BF16), -1)
    return mine(0, 0, rows) + ahead.astype(F32) + back.astype(F32)


def swap(value):
    return lax.all_to_all(value, "expert", split_axis=0, concat_axis=0, tiled=True)


def per_device(
    tokens,
    cotangent,
    segment_ids,
    routes,
    attn_in,
    attn_out,
    gain_attn,
    shared_in,
    shared_out,
    router,
    gain_ffn,
    expert_in,
    expert_out,
):
    n_dp, n_e = lax.axis_size("dp"), lax.axis_size("expert")
    me = lax.axis_index("expert")
    count, width = tokens.shape
    segments = segment_ids[0]
    length = segments.shape[0]
    rows = attn_in.shape[0]
    capacity = min(count, 3 * TOP * count // (2 * n_e))
    shared_rows = shared_out.shape[0]
    shared_width = shared_rows * n_dp
    expert_width = expert_out.shape[1] * n_dp

    hidden_in = tokens.astype(F32)
    inverse_one = lax.rsqrt(jnp.mean(hidden_in * hidden_in, axis=-1, keepdims=True) + EPS)
    normed_one = hidden_in * inverse_one
    gain_rows = gain_attn.astype(F32)[:, None]
    head_w = (attn_in.astype(F32) * gain_rows).astype(BF16)
    head_w = head_w.reshape(rows, 3, n_e, HEAD_DIM).transpose(2, 0, 1, 3)
    head_w = swap(head_w.reshape(n_e, rows, 3 * HEAD_DIM))
    head_w = dp_gather(head_w).reshape(width, 3 * HEAD_DIM)
    (norm_all,), done_one = gather_rows(normed_one.astype(BF16))

    small = jnp.concatenate([router, gain_ffn[:, None]], axis=1)
    small = dp_gather(small).reshape(-1, router.shape[1] + 1)
    small_rows = small.shape[0]
    extra = jnp.zeros((count, 128), BF16)
    extra = extra.at[:small_rows, : small.shape[1]].set(small)
    extra = extra.at[:, 64 : 64 + TOP].set(routes.astype(BF16))
    proj_all = dp_gather(attn_out).reshape(n_dp * rows, width)
    (proj_all, extra_all), done_two = gather_rows(
        jnp.concatenate([proj_all, extra], axis=1), [width, 128], done_one
    )
    proj_all = proj_all.reshape(n_e, n_dp, rows, width).transpose(1, 0, 2, 3).reshape(width, width)
    small = extra_all.reshape(n_e, count, 128)[:, :small_rows, : router.shape[1] + 1]
    small = small.reshape(n_e, n_dp, rows, -1).transpose(1, 0, 2, 3).reshape(width, -1)
    router_full = small[:, : router.shape[1]]
    gain_second = small[:, router.shape[1]].astype(F32)
    routes_all = extra_all[:, 64 : 64 + TOP].astype(F32)

    expert_in, expert_out, _ = lax.optimization_barrier((expert_in, expert_out, head_w))
    expert_up = lax.all_gather(expert_in, "dp", axis=1, tiled=True)[0]
    expert_down = lax.all_gather(expert_out, "dp", axis=1, tiled=True)[0]
    shared_in, _ = lax.optimization_barrier((shared_in, done_one))
    share_w = shared_in.reshape(rows, 2, n_dp, n_e, shared_rows).transpose(3, 0, 1, 2, 4)
    share_w = swap(share_w.reshape(n_e, rows, 2 * shared_width))
    share_w = dp_gather(share_w).reshape(width, 2 * shared_width)
    share_out = dp_gather(shared_out).reshape(shared_width, width)

    cos_table, sin_table, first_place = rope_tables(segments)
    qkv = dot(norm_all, head_w)
    mixed, query, key, value, lse = attend(qkv, cos_table, sin_table, first_place)
    mixed = swap(mixed.reshape(n_e, count, HEAD_DIM))
    mixed = mixed.transpose(1, 0, 2).reshape(count, width)
    resid = hidden_in + dot(mixed, proj_all)

    inverse_two = lax.rsqrt(jnp.mean(resid * resid, axis=-1, keepdims=True) + EPS)
    normed_two = resid * inverse_two
    norm_two = (normed_two * gain_second).astype(BF16)
    logits = dot(norm_two, router_full)
    picked = jnp.any(routes[:, :, None] == jnp.arange(n_e)[None, None, :], axis=1)
    chosen = jnp.where(picked, logits, NEG)
    chosen = jnp.where(picked, jnp.exp(chosen - jnp.max(chosen, axis=-1, keepdims=True)), 0.0)
    gates = chosen / jnp.sum(chosen, axis=-1, keepdims=True)
    gate_high = gates.astype(BF16)
    gate_low = (gates - gate_high.astype(F32)).astype(BF16)
    blank = jnp.zeros((count, 128 - 2 * n_e), BF16)
    payload = jnp.concatenate([norm_two, gate_high, gate_low, blank], axis=1)
    (norm_two_all, payload), done_three = gather_rows(payload, [width, 128])
    (cot_all,), _ = gather_rows(cotangent, None, done_three)
    mine = jnp.arange(n_e) == me
    gate_all = payload[:, : 2 * n_e].astype(F32).reshape(length, 2, n_e)
    gate_all = jnp.sum(jnp.where(mine, gate_all, 0.0), axis=(1, 2))

    named = jnp.any(routes_all == me.astype(F32), axis=1).reshape(n_e, count)
    ranking = jnp.cumsum(named.astype(jnp.int32), axis=1) - 1
    select = (
        named[:, None, :]
        & (ranking[:, None, :] == jnp.arange(capacity, dtype=jnp.int32)[None, :, None])
    ).astype(BF16)
    arrived = jnp.einsum(
        "bct,btd->bcd",
        select,
        norm_two_all.reshape(n_e, count, width),
        preferred_element_type=F32,
    ).astype(BF16).reshape(n_e * capacity, width)
    cot_rows = jnp.einsum(
        "bct,btd->bcd", select, cot_all.reshape(n_e, count, width), preferred_element_type=F32
    ).reshape(n_e * capacity, width)
    gate_rows = jnp.sum(
        jnp.where(select != 0, gate_all.reshape(n_e, 1, count), 0.0), axis=-1
    ).reshape(n_e * capacity, 1)

    expert_pre = dot(arrived, expert_up)
    expert_act = (
        jax.nn.silu(expert_pre[:, :expert_width]) * expert_pre[:, expert_width:]
    ).astype(BF16)
    expert_res = dot(expert_act, expert_down).astype(BF16).astype(F32)
    gate_grad = jnp.sum(cot_rows * expert_res, axis=-1).reshape(n_e, capacity, 1)
    gate_grad = jnp.sum(jnp.where(select != 0, gate_grad, 0.0), axis=1)
    gate_grad = swap(gate_grad)
    weighted = (gate_rows * expert_res).astype(BF16).reshape(n_e, capacity, width)

    shared_pre = dot(norm_two_all, share_w)
    shared_act = (
        jax.nn.silu(shared_pre[:, :shared_width]) * shared_pre[:, shared_width:]
    ).astype(BF16)
    out_part = dot(shared_act, share_out) + jnp.einsum(
        "bct,bcd->btd", select, weighted, preferred_element_type=F32
    ).reshape(length, width)

    route_grad = (gate_rows * cot_rows).astype(BF16)
    act_grad = dot_nt(route_grad, expert_down)
    pre_grad = silu_back(
        act_grad, expert_pre[:, :expert_width], expert_pre[:, expert_width:]
    ).astype(BF16)
    row_grad = dot_nt(pre_grad, expert_up).astype(BF16).reshape(n_e, capacity, width)
    shared_act_grad = dot_nt(cot_all, share_out)
    shared_pre_grad = silu_back(
        shared_act_grad, shared_pre[:, :shared_width], shared_pre[:, shared_width:]
    ).astype(BF16)
    norm_two_part = dot_nt(shared_pre_grad, share_w) + jnp.einsum(
        "bct,bcd->btd", select, row_grad, preferred_element_type=F32
    ).reshape(length, width)
    norm_two_grad = scatter_rows(norm_two_part.astype(BF16))

    down_grad = dot_tn(expert_act, route_grad)
    up_grad = dot_tn(arrived, pre_grad)
    expert_out_grad = lax.psum_scatter(
        down_grad.astype(BF16), "dp", scatter_dimension=0, tiled=True
    ).astype(F32)[None]
    expert_in_grad = lax.psum_scatter(
        up_grad.astype(BF16), "dp", scatter_dimension=0, tiled=True
    ).astype(F32)[None]
    share_out_grad = dp_scatter(dot_tn(shared_act, cot_all).reshape(n_dp, shared_rows, width))
    share_in_grad = dot_tn(norm_two_all, shared_pre_grad)
    share_in_grad = dp_scatter(share_in_grad.reshape(n_dp, n_e, rows, 2 * shared_width))
    share_in_grad = swap(share_in_grad.astype(BF16)).astype(F32)
    share_in_grad = (
        share_in_grad.reshape(n_e, rows, 2, n_dp, shared_rows)
        .transpose(1, 2, 3, 0, 4)
        .reshape(rows, -1)
    )

    gate_grad = gate_grad.T
    logit_grad = gates * (gate_grad - jnp.sum(gates * gate_grad, axis=-1, keepdims=True))
    router_grad = jnp.dot(
        norm_two.astype(F32).T, logit_grad, precision=HIGHEST, preferred_element_type=F32
    )
    norm_two_grad = norm_two_grad + jnp.dot(
        logit_grad, router_full.astype(F32).T, precision=HIGHEST, preferred_element_type=F32
    )
    gain_two_grad = jnp.sum(norm_two_grad * normed_two, axis=0)
    upstream = cotangent.astype(F32)
    scaled_two = norm_two_grad * gain_second
    resid_grad = upstream + inverse_two * (
        scaled_two - normed_two * jnp.mean(scaled_two * normed_two, axis=-1, keepdims=True)
    )
    small_grad = jnp.concatenate([router_grad, gain_two_grad[:, None]], axis=1)
    small_grad = small_grad.reshape(n_dp * n_e, rows, n_e + 1)
    small_grad = lax.all_to_all(
        small_grad, ("dp", "expert"), split_axis=0, concat_axis=0, tiled=True
    )
    small_grad = jnp.sum(small_grad, axis=0)

    branch_cot = resid_grad.astype(BF16)
    mixed_grad = dot_nt(branch_cot, proj_all).astype(BF16)
    mixed_grad = swap(mixed_grad.reshape(count, n_e, HEAD_DIM).transpose(1, 0, 2))
    mixed_grad = mixed_grad.reshape(length, HEAD_DIM)
    proj_grad = dot_tn(mixed, branch_cot).astype(BF16)
    proj_grad = proj_grad.reshape(n_dp, n_e, rows, width).transpose(1, 0, 2, 3)
    proj_grad = scatter_rows(proj_grad.reshape(width, width))
    attn_out_grad = dp_scatter(proj_grad.reshape(n_dp, rows, width))
    qkv_grad = attend_back(
        query, key, value, mixed_grad, lse, first_place, cos_table, sin_table
    )
    scaled_one = scatter_rows(dot_nt(qkv_grad, head_w).astype(BF16))
    input_grad = resid_grad + inverse_one * (
        scaled_one - normed_one * jnp.mean(scaled_one * normed_one, axis=-1, keepdims=True)
    )
    head_grad = dot_tn(norm_all, qkv_grad).reshape(n_dp, n_e, rows, 3 * HEAD_DIM)
    head_grad = swap(dp_scatter(head_grad).astype(BF16)).astype(F32)
    head_grad = (
        head_grad.reshape(n_e, rows, 3, HEAD_DIM).transpose(1, 2, 0, 3).reshape(rows, 3 * width)
    )
    gain_attn_grad = jnp.sum(head_grad * attn_in.astype(F32), axis=1)
    attn_in_grad = head_grad * gain_rows
    return (
        (resid + scatter_rows(out_part.astype(BF16))).astype(BF16),
        input_grad.astype(BF16),
        attn_in_grad,
        attn_out_grad,
        gain_attn_grad,
        share_in_grad,
        share_out_grad,
        small_grad[:, :n_e],
        small_grad[:, n_e],
        expert_in_grad,
        expert_out_grad,
    )


def solution(mesh):
    return jax.shard_map(
        per_device,
        mesh=mesh,
        in_specs=(
            P(("dp", "expert"), None),
            P(("dp", "expert"), None),
            P("dp", None),
            P(("dp", "expert"), None),
            P(("dp", "expert"), None),
            P(("dp", "expert"), None),
            P(("dp", "expert")),
            P(("dp", "expert"), None),
            P(("dp", "expert"), None),
            P(("dp", "expert"), None),
            P(("dp", "expert")),
            P("expert", "dp", None),
            P("expert", "dp", None),
        ),
        out_specs=(
            P(("dp", "expert"), None),
            P(("dp", "expert"), None),
            P(("dp", "expert"), None),
            P(("dp", "expert"), None),
            P(("dp", "expert")),
            P(("dp", "expert"), None),
            P(("dp", "expert"), None),
            P(("dp", "expert"), None),
            P(("dp", "expert")),
            P("expert", "dp", None),
            P("expert", "dp", None),
        ),
        check_vma=False,
    )
```

```python
import functools
import math

import jax
import jax.numpy as jnp
from jax import lax
from jax.experimental import pallas as pl
from jax.experimental.pallas import tpu as pltpu
from jax.sharding import PartitionSpec as P

HEADS = 16
HEAD_DIM = 128
TOP = 6


EPS = 1e-06
THETA = 10000.0
NEG = -1e30
HIGHEST = lax.Precision.HIGHEST
BF16 = jnp.bfloat16
F32 = jnp.float32
LOG2E = math.log2(math.e)


def rope_tables(segments):
    length = segments.shape[0]
    places = jnp.arange(length, dtype=jnp.int32)
    starts = jnp.concatenate([jnp.ones((1,), dtype=jnp.bool_), segments[1:] != segments[:-1]])
    first_place = lax.cummax(jnp.where(starts, places, 0), axis=0)
    offset = (places - first_place).astype(jnp.float32)
    half_dim = HEAD_DIM // 2
    freqs = jnp.exp(jnp.arange(half_dim, dtype=jnp.float32) * (-2.0 * math.log(THETA) / HEAD_DIM))
    angles = offset[:, None] * freqs[None, :]
    cos_table, sin_table = jnp.cos(angles), jnp.sin(angles)
    return (
        jnp.concatenate([cos_table, cos_table], axis=1),
        jnp.concatenate([-sin_table, sin_table], axis=1),
        first_place[None, :],
    )


def silu_back(grad_act, gate_part, up_part):
    sigmoid_gate = jax.nn.sigmoid(gate_part)
    gate_grad = grad_act * up_part * sigmoid_gate * (1.0 + gate_part * (1.0 - sigmoid_gate))
    up_grad = grad_act * gate_part * sigmoid_gate
    return jnp.concatenate([gate_grad, up_grad], axis=-1)


def dot(left, right):
    return jnp.dot(left, right, preferred_element_type=F32)


def dot_tn(left, right):
    return lax.dot_general(left, right, (((0,), (0,)), ((), ())), preferred_element_type=F32)


def dot_nt(left, right):
    return lax.dot_general(left, right, (((1,), (1,)), ((), ())), preferred_element_type=F32)


def turn(values, cos_table, sin_table):
    return values * cos_table + pltpu.roll(values, HEAD_DIM // 2, 1) * sin_table


def attend_kernel(sources, block, order_ref, *refs):
    pieces = refs[: sources[-1][-1] + 1]
    weight_ref, cos_ref, sin_ref, start_ref = refs[len(pieces) : len(pieces) + 4]
    o_ref, q_ref, k_ref, v_ref, lse_ref, rows_ref, vt_ref = refs[len(pieces) + 4 :]
    step = pl.program_id(0)
    length = q_ref.shape[0]
    factor = HEAD_DIM ** (-0.5) * LOG2E
    rows = rows_ref.shape[0]

    for n, parts in enumerate(sources):

        @pl.when(step == n)
        def _(parts=parts):
            low = 0
            for part in parts:
                size = pieces[part].shape[0]
                rows_ref[low : low + size, :] = pieces[part][...]
                low += size

    @pl.when(step < len(sources))
    def _():
        qkv = dot(rows_ref[...], weight_ref[...])
        at = pl.ds(pl.multiple_of(order_ref[step] * rows, rows), rows)
        cos_table, sin_table = cos_ref[at, :], sin_ref[at, :]
        q_ref[at, :] = turn(qkv[:, :HEAD_DIM], cos_table, sin_table).astype(BF16)
        k_ref[at, :] = turn(qkv[:, HEAD_DIM : 2 * HEAD_DIM], cos_table, sin_table).astype(BF16)
        value = qkv[:, 2 * HEAD_DIM :]
        v_ref[at, :] = value.astype(BF16)
        vt_ref[:, at] = value.T.astype(BF16)

    for i in range(length // block):

        @pl.when(step == len(sources) + i)
        def _(i=i):
            low, high = i * block, (i + 1) * block
            raw = dot_nt(k_ref[:high, :], q_ref[low:high, :])
            keys = lax.broadcasted_iota(jnp.int32, raw.shape, 0)
            queries = low + lax.broadcasted_iota(jnp.int32, raw.shape, 1)
            allowed = (keys <= queries) & (keys >= start_ref[:, low:high])
            raw = jnp.where(allowed, raw, NEG)
            top = jnp.max(raw, axis=0, keepdims=True)
            shifted = jnp.exp2((raw - top) * factor)
            total = jnp.sum(shifted, axis=0, keepdims=True)
            probs = (shifted * (1.0 / total)).astype(BF16)
            mixed = dot(vt_ref[:, :high], probs)
            o_ref[low:high, :] = mixed.T.astype(BF16)
            lse_ref[:, low:high] = top * factor + jnp.log2(total)


def attend(blocks, order, weight, cos_table, sin_table, first_place):
    pieces, sources = flatten(blocks)
    length = cos_table.shape[0]
    rows = length // len(sources)
    width = weight.shape[0]
    block = min(256, length)
    last = len(sources) - 1
    whole = lambda shape: pl.BlockSpec(shape, lambda i, order: (0, 0))
    head = jax.ShapeDtypeStruct((length, HEAD_DIM), BF16)
    return pl.pallas_call(
        functools.partial(attend_kernel, sources, block),
        out_shape=[head] * 4
        + [jax.ShapeDtypeStruct((1, length), F32), jax.ShapeDtypeStruct((length, width), BF16)],
        grid_spec=pltpu.PrefetchScalarGridSpec(
            num_scalar_prefetch=1,
            grid=(len(sources) + length // block,),
            in_specs=[whole(piece.shape) for piece in pieces]
            + [
                whole(weight.shape),
                whole((length, HEAD_DIM)),
                whole((length, HEAD_DIM)),
                whole((1, length)),
            ],
            out_specs=[whole((length, HEAD_DIM))] * 4
            + [
                whole((1, length)),
                pl.BlockSpec((rows, width), lambda i, order: (jnp.minimum(i, last), 0)),
            ],
            scratch_shapes=[pltpu.VMEM((HEAD_DIM, length), BF16)],
        ),
        compiler_params=pltpu.CompilerParams(vmem_limit_bytes=52 * 2**20),
        name="attend",
    )(order, *pieces, weight, cos_table, sin_table, first_place)


def attend_back_kernel(
    block, rows, order_ref, q_ref, k_ref, v_ref, do_ref, lse_ref, start_ref, cos_ref, sin_ref, out_ref, kt_ref, dq_ref, dk_ref, dv_ref
):
    length = q_ref.shape[0]
    step = pl.program_id(0)
    scale = HEAD_DIM ** (-0.5)
    factor = scale * LOG2E
    count = length // block

    @pl.when(step == 0)
    def _():
        kt_ref[...] = k_ref[...].astype(F32).T.astype(BF16)
        dk_ref[...] = jnp.zeros_like(dk_ref)
        dv_ref[...] = jnp.zeros_like(dv_ref)

    for i in range(count):

        @pl.when(step == i)
        def _(i=i):
            low, high = i * block, (i + 1) * block
            query, grad = q_ref[low:high, :], do_ref[low:high, :]
            raw = dot_nt(k_ref[:high, :], query)
            keys = lax.broadcasted_iota(jnp.int32, raw.shape, 0)
            queries = low + lax.broadcasted_iota(jnp.int32, raw.shape, 1)
            allowed = (keys <= queries) & (keys >= start_ref[:, low:high])
            raw = jnp.where(allowed, raw * factor - lse_ref[:, low:high], NEG)
            probs = jnp.exp2(raw)
            probs_grad = dot_nt(v_ref[:high, :], grad)
            inner = jnp.sum(probs_grad * probs, axis=0, keepdims=True)
            score_grad = (probs * (probs_grad - inner)).astype(BF16)
            dv_ref[:high, :] += dot(probs.astype(BF16), grad)
            dk_ref[:high, :] += dot(score_grad, query)
            dq_ref[low:high, :] = dot(kt_ref[:, :high], score_grad).T

    @pl.when(step == count - 1)
    def _():
        for n in range(length // rows):
            at = pl.ds(pl.multiple_of(order_ref[n] * rows, rows), rows)
            to = slice(n * rows, (n + 1) * rows)
            cos_table, sin_table = cos_ref[at, :], -sin_ref[at, :]
            out_ref[to, :HEAD_DIM] = turn(dq_ref[at, :] * scale, cos_table, sin_table).astype(BF16)
            out_ref[to, HEAD_DIM : 2 * HEAD_DIM] = turn(
                dk_ref[at, :] * scale, cos_table, sin_table
            ).astype(BF16)
            out_ref[to, 2 * HEAD_DIM :] = dv_ref[at, :].astype(BF16)


def attend_back(query, key, value, grad, lse, first_place, cos_table, sin_table, order):
    length = query.shape[0]
    block = min(256, length)
    whole = lambda shape: pl.BlockSpec(shape, lambda i, order: (0, 0))
    head = whole((length, HEAD_DIM))
    return pl.pallas_call(
        functools.partial(attend_back_kernel, block, length // order.shape[0]),
        out_shape=jax.ShapeDtypeStruct((length, 3 * HEAD_DIM), BF16),
        grid_spec=pltpu.PrefetchScalarGridSpec(
            num_scalar_prefetch=1,
            grid=(length // block,),
            in_specs=[head] * 4 + [whole((1, length))] * 2 + [head] * 2,
            out_specs=whole((length, 3 * HEAD_DIM)),
            scratch_shapes=[pltpu.VMEM((HEAD_DIM, length), BF16)]
            + [pltpu.VMEM((length, HEAD_DIM), F32)] * 3,
        ),
        compiler_params=pltpu.CompilerParams(vmem_limit_bytes=48 * 2**20),
        name="attend_back",
    )(order, query, key, value, grad, lse, first_place, cos_table, sin_table)


def dp_gather(value):
    count = lax.axis_size("dp")
    if count == 1:
        return value[None]
    here = lax.axis_index("dp")
    parts = [value] + [
        lax.ppermute(value, "dp", [(i, (i - step) % count) for i in range(count)])
        for step in range(1, count)
    ]
    if count == 2:
        first = here == 0
        return jnp.stack(
            [jnp.where(first, parts[0], parts[1]), jnp.where(first, parts[1], parts[0])]
        )
    whole = jnp.zeros((count,) + value.shape, value.dtype)
    for step, part in enumerate(parts):
        whole = lax.dynamic_update_index_in_dim(whole, part, (here + step) % count, 0)
    return whole


def dp_scatter(value):
    count = lax.axis_size("dp")
    here = lax.axis_index("dp")
    total = lax.dynamic_index_in_dim(value, here, 0, keepdims=False)
    for step in range(1, count):
        block = lax.dynamic_index_in_dim(value, (here + step) % count, 0, keepdims=False)
        got = lax.ppermute(
            block.astype(BF16), "dp", [(i, (i + step) % count) for i in range(count)]
        )
        total = total + got.astype(F32)
    return total


def ring_order():
    pairs = lax.axis_size("expert") // 2
    return list(range(0, pairs, 2)) + list(range(pairs - 1, 0, -2))


def ring_shift(value, step):
    order = ring_order()
    pairs = len(order)
    perm = [
        (order[q] * 2 + c, order[(q + step) % pairs] * 2 + c) for q in range(pairs) for c in range(2)
    ]
    return lax.ppermute(value, "expert", perm)


def core_swap(value):
    count = lax.axis_size("expert")
    return lax.ppermute(value, "expert", [(i, i ^ 1) for i in range(count)])


def ring_offsets():
    half = lax.axis_size("expert") // 4
    return [0] + [o for step in range(1, half) for o in (step, -step)] + [half]


def ring_blocks():
    order = ring_order()
    pairs = len(order)
    table = [[0] * (2 * pairs) for _ in range(2 * pairs)]
    for q in range(pairs):
        for c in range(2):
            for j, offset in enumerate(ring_offsets()):
                for other in range(2):
                    table[order[q] * 2 + c][2 * j + other] = (
                        order[(q - offset) % pairs] * 2 + (c ^ other)
                    )
    return lax.dynamic_index_in_dim(
        jnp.asarray(table, jnp.int32), lax.axis_index("expert"), 0, keepdims=False
    )


def tied(value, *tokens):
    token = sum(t.astype(F32).reshape(-1)[0] for t in tokens) * 0.0
    return (value.astype(F32) * (1.0 + token)).astype(value.dtype)


def ring_gather(value, gate=None):
    half_rows = value.shape[0] // 2
    half = lax.axis_size("expert") // 4
    blocks = {}

    def keep(parts, offset):
        blocks[offset] = (parts, [core_swap(part) for part in parts])

    keep([value], 0)
    ahead = back = value
    for step in range(1, half):
        ahead, back = ring_shift(ahead, 1), ring_shift(back, -1)
        if step == 1 and gate is not None:
            ahead, back = tied(ahead, gate), tied(back, gate)
        keep([ahead], step)
        keep([back], -step)
    last = [ring_shift(ahead[:half_rows], 1), ring_shift(back[half_rows:], -1)]
    keep(last, half)
    return [parts for offset in ring_offsets() for parts in blocks[offset]]


def flatten(blocks):
    pieces = [piece for parts in blocks for piece in parts]
    sources, n = [], 0
    for parts in blocks:
        sources.append(tuple(range(n, n + len(parts))))
        n += len(parts)
    return pieces, tuple(sources)


def place_kernel(sources, widths, order_ref, *refs):
    pieces, outs = refs[: -len(widths)], refs[-len(widths) :]
    step = pl.program_id(0)
    for n, parts in enumerate(sources):

        @pl.when(step == n)
        def _(parts=parts):
            low = 0
            for part in parts:
                size = pieces[part].shape[0]
                left = 0
                for out, wide in zip(outs, widths):
                    block = pieces[part][:, left : left + wide]
                    if len(out.shape) == 3:
                        groups, rows, _ = out.shape
                        rows = min(rows, size)
                        per = size // rows
                        for g in range(per):
                            at = low + g * rows
                            out[at // out.shape[1], at % out.shape[1] : at % out.shape[1] + rows, :] = block[
                                g * rows : (g + 1) * rows
                            ]
                    else:
                        out[low : low + size, :] = block
                    left += wide
                low += size


def place(blocks, order, widths, groups=1):
    pieces, sources = flatten(blocks)
    rows = sum(pieces[part].shape[0] for part in sources[0])
    length = rows * len(blocks)
    shapes = [jax.ShapeDtypeStruct((length, wide), pieces[0].dtype) for wide in widths]
    specs = [pl.BlockSpec((rows, wide), lambda i, order: (order[i], 0)) for wide in widths]
    if groups > 1:
        shapes[0] = jax.ShapeDtypeStruct((groups, length // groups, widths[0]), pieces[0].dtype)
        specs[0] = pl.BlockSpec((groups, rows // groups, widths[0]), lambda i, order: (0, order[i], 0))
    return pl.pallas_call(
        functools.partial(place_kernel, sources, tuple(widths)),
        out_shape=shapes,
        grid_spec=pltpu.PrefetchScalarGridSpec(
            num_scalar_prefetch=1,
            grid=(len(blocks),),
            in_specs=[pl.BlockSpec(piece.shape, lambda i, order: (0, 0)) for piece in pieces],
            out_specs=specs,
        ),
        compiler_params=pltpu.CompilerParams(vmem_limit_bytes=48 * 2**20),
        name="place",
    )(order, *pieces)


def ring_scatter(block):
    half = lax.axis_size("expert") // 4
    offsets = ring_offsets()
    spare = {}

    def mine(offset):
        if offset not in spare:
            j = offsets.index(offset)
            spare[offset] = block(2 * j).astype(F32) + core_swap(block(2 * j + 1)).astype(F32)
        return spare[offset]

    far = mine(half).astype(BF16)
    half_rows = far.shape[0] // 2
    ahead = ring_shift(far[:half_rows], 1)
    back = ring_shift(far[half_rows:], -1)
    for step in range(half - 1, 0, -1):
        onward, homeward = mine(-step), mine(step)
        if step == half - 1:
            onward = jnp.concatenate(
                [onward[:half_rows] + ahead.astype(F32), onward[half_rows:]], axis=0
            )
            homeward = jnp.concatenate(
                [homeward[:half_rows], homeward[half_rows:] + back.astype(F32)], axis=0
            )
        else:
            onward = onward + ahead.astype(F32)
            homeward = homeward + back.astype(F32)
        ahead = ring_shift(onward.astype(BF16), 1)
        back = ring_shift(homeward.astype(BF16), -1)
    return mine(0) + ahead.astype(F32) + back.astype(F32)


def combine_kernel(turned, select_ref, rows_ref, act_ref, weight_ref, out_ref):
    mul = dot_nt if turned else dot
    out_ref[...] = (
        dot_tn(select_ref[0], rows_ref[0]) + mul(act_ref[...], weight_ref[...])
    ).astype(BF16)


def combine(select, rows, act, weight, turned):
    blocks, capacity, count = select.shape
    width = rows.shape[-1]
    return pl.pallas_call(
        functools.partial(combine_kernel, turned),
        grid=(blocks,),
        out_shape=jax.ShapeDtypeStruct((blocks * count, width), BF16),
        in_specs=[
            pl.BlockSpec((1, capacity, count), lambda i: (i, 0, 0)),
            pl.BlockSpec((1, capacity, width), lambda i: (i, 0, 0)),
            pl.BlockSpec((count, act.shape[1]), lambda i: (i, 0)),
            pl.BlockSpec(weight.shape, lambda i: (0, 0)),
        ],
        out_specs=pl.BlockSpec((count, width), lambda i: (i, 0)),
        compiler_params=pltpu.CompilerParams(vmem_limit_bytes=32 * 2**20),
        name="combine",
    )(select, rows, act, weight)


def swap(value):
    return lax.all_to_all(value, "expert", split_axis=0, concat_axis=0, tiled=True)


def per_device(
    tokens,
    cotangent,
    segment_ids,
    routes,
    attn_in,
    attn_out,
    gain_attn,
    shared_in,
    shared_out,
    router,
    gain_ffn,
    expert_in,
    expert_out,
):
    n_dp, n_e = lax.axis_size("dp"), lax.axis_size("expert")
    me = lax.axis_index("expert")
    count, width = tokens.shape
    segments = segment_ids[0]
    length = segments.shape[0]
    rows = attn_in.shape[0]
    capacity = min(count, 3 * TOP * count // (2 * n_e))
    shared_rows = shared_out.shape[0]
    shared_width = shared_rows * n_dp
    expert_width = expert_out.shape[1] * n_dp

    order = ring_blocks()
    steady = jnp.arange(n_e, dtype=jnp.int32)
    hidden_in = tokens.astype(F32)
    inverse_one = lax.rsqrt(jnp.mean(hidden_in * hidden_in, axis=-1, keepdims=True) + EPS)
    normed_one = hidden_in * inverse_one
    norm_blocks = ring_gather(normed_one.astype(BF16))
    gain_rows = gain_attn.astype(F32)[:, None]
    head_w = (attn_in.astype(F32) * tied(gain_rows, norm_blocks[2][0])).astype(BF16)
    head_w = head_w.reshape(rows, 3, n_e, HEAD_DIM).transpose(2, 0, 1, 3)
    head_w = swap(head_w.reshape(n_e, rows, 3 * HEAD_DIM))
    head_w = dp_gather(head_w).reshape(width, 3 * HEAD_DIM)

    cos_table, sin_table, first_place = rope_tables(segments)
    mixed, query, key, value, lse, norm_all = attend(
        norm_blocks, order, head_w, cos_table, sin_table, first_place
    )
    mixed = swap(mixed.reshape(n_e, count, HEAD_DIM))
    mixed = mixed.transpose(1, 0, 2).reshape(count, width)

    small = jnp.concatenate([router, gain_ffn[:, None]], axis=1)
    small = dp_gather(small).reshape(-1, router.shape[1] + 1)
    small_rows = small.shape[0]
    extra = jnp.zeros((count, 128), BF16)
    extra = extra.at[:small_rows, : small.shape[1]].set(small)
    extra = extra.at[:, 64 : 64 + TOP].set(routes.astype(BF16))
    proj_all = jnp.concatenate([dp_gather(attn_out).reshape(n_dp * rows, width), extra], axis=1)
    proj_all = ring_gather(tied(proj_all, norm_blocks[-1][0], norm_blocks[-1][-1]), lse)
    proj_all, extra_all = place(proj_all, order, [width, 128], n_dp)
    proj_all = proj_all.reshape(width, width)
    small = extra_all.reshape(n_e, count, 128)[:, :small_rows, : router.shape[1] + 1]
    small = small.reshape(n_e, n_dp, rows, -1).transpose(1, 0, 2, 3).reshape(width, -1)
    router_full = small[:, : router.shape[1]]
    gain_second = small[:, router.shape[1]].astype(F32)
    routes_all = extra_all[:, 64 : 64 + TOP].astype(F32)

    expert_up = lax.all_gather(expert_in, "dp", axis=1, tiled=True)[0]
    down_parts = jnp.split(expert_out[0], 2, axis=0)
    down_parts = [dp_gather(part) for part in down_parts]
    expert_down = jnp.concatenate(down_parts, axis=1).reshape(expert_width, width)
    share_w = shared_in.reshape(rows, 2, n_dp, n_e, shared_rows).transpose(3, 0, 1, 2, 4)
    share_w = share_w.reshape(n_e, rows, 2 * shared_width)
    share_w = swap(tied(share_w, norm_blocks[-1][0], norm_blocks[-1][-1]))
    share_w = dp_gather(share_w).reshape(width, 2 * shared_width)
    share_out = dp_gather(shared_out).reshape(shared_width, width)
    resid = tied(hidden_in, down_parts[0][0], down_parts[0][-1]) + dot(mixed, proj_all)

    inverse_two = lax.rsqrt(jnp.mean(resid * resid, axis=-1, keepdims=True) + EPS)
    normed_two = resid * inverse_two
    norm_two = (normed_two * gain_second).astype(BF16)
    logits = dot(norm_two, router_full)
    picked = jnp.any(routes[:, :, None] == jnp.arange(n_e)[None, None, :], axis=1)
    chosen = jnp.where(picked, logits, NEG)
    chosen = jnp.where(picked, jnp.exp(chosen - jnp.max(chosen, axis=-1, keepdims=True)), 0.0)
    gates = chosen / jnp.sum(chosen, axis=-1, keepdims=True)
    gate_high = gates.astype(BF16)
    gate_low = (gates - gate_high.astype(F32)).astype(BF16)
    blank = jnp.zeros((count, 128 - 2 * n_e), BF16)
    payload = jnp.concatenate([norm_two, gate_high, gate_low, blank], axis=1)
    payload = ring_gather(payload)
    cot_all = tied(cotangent, payload[-1][0], payload[-1][-1], down_parts[1][0], down_parts[1][-1])
    norm_two_all, payload = place(payload, steady, [width, 128])
    (cot_all,) = place(ring_gather(cot_all), steady, [width])
    mine = jnp.arange(n_e) == me
    gate_all = payload[:, : 2 * n_e].astype(F32).reshape(length, 2, n_e)
    gate_all = jnp.sum(jnp.where(mine, gate_all, 0.0), axis=(1, 2))

    named = jnp.any(routes_all == me.astype(F32), axis=1).reshape(n_e, count)
    named = jnp.take(named, order, axis=0)
    ranking = jnp.cumsum(named.astype(jnp.int32), axis=1) - 1
    select = (
        named[:, None, :]
        & (ranking[:, None, :] == jnp.arange(capacity, dtype=jnp.int32)[None, :, None])
    ).astype(BF16)
    arrived = jnp.einsum(
        "bct,btd->bcd",
        select,
        norm_two_all.reshape(n_e, count, width),
        preferred_element_type=F32,
    ).astype(BF16).reshape(n_e * capacity, width)
    cot_rows = jnp.einsum(
        "bct,btd->bcd", select, cot_all.reshape(n_e, count, width), preferred_element_type=F32
    ).reshape(n_e * capacity, width)
    gate_rows = jnp.sum(
        jnp.where(select != 0, gate_all.reshape(n_e, 1, count), 0.0), axis=-1
    ).reshape(n_e * capacity, 1)

    expert_pre = dot(arrived, expert_up)
    expert_act = (
        jax.nn.silu(expert_pre[:, :expert_width]) * expert_pre[:, expert_width:]
    ).astype(BF16)
    expert_res = dot(expert_act, expert_down).astype(BF16).astype(F32)
    gate_grad = jnp.sum(cot_rows * expert_res, axis=-1).reshape(n_e, capacity, 1)
    gate_grad = jnp.sum(jnp.where(select != 0, gate_grad, 0.0), axis=1)
    gate_grad = jnp.sum(
        jnp.where(order[:, None, None] == steady[None, :, None], gate_grad[:, None, :], 0.0), axis=0
    )
    gate_grad = swap(gate_grad)
    weighted = (gate_rows * expert_res).astype(BF16).reshape(n_e, capacity, width)

    shared_pre = dot(norm_two_all, share_w)
    shared_act = (
        jax.nn.silu(shared_pre[:, :shared_width]) * shared_pre[:, shared_width:]
    ).astype(BF16)
    out_part = combine(select, weighted, shared_act, share_out, False)
    routed_out = ring_scatter(lambda n: out_part[n * count : (n + 1) * count])

    route_grad = (gate_rows * cot_rows).astype(BF16)
    act_grad = dot_nt(route_grad, expert_down)
    pre_grad = silu_back(
        act_grad, expert_pre[:, :expert_width], expert_pre[:, expert_width:]
    ).astype(BF16)
    row_grad = dot_nt(pre_grad, expert_up).astype(BF16).reshape(n_e, capacity, width)
    shared_act_grad = dot_nt(cot_all, share_out)
    shared_pre_grad = silu_back(
        shared_act_grad, shared_pre[:, :shared_width], shared_pre[:, shared_width:]
    ).astype(BF16)
    norm_two_part = combine(select, row_grad, shared_pre_grad, share_w, True)
    norm_two_grad = ring_scatter(lambda n: norm_two_part[n * count : (n + 1) * count])

    down_grad = dot_tn(expert_act, route_grad)
    up_grad = dot_tn(arrived, pre_grad)
    expert_out_grad = lax.psum_scatter(
        down_grad.astype(BF16), "dp", scatter_dimension=0, tiled=True
    ).astype(F32)[None]
    expert_in_grad = lax.psum_scatter(
        up_grad.astype(BF16), "dp", scatter_dimension=0, tiled=True
    ).astype(F32)[None]
    share_out_grad = dp_scatter(dot_tn(shared_act, cot_all).reshape(n_dp, shared_rows, width))
    share_in_grad = dot_tn(norm_two_all, shared_pre_grad)
    share_in_grad = dp_scatter(share_in_grad.reshape(n_dp, n_e, rows, 2 * shared_width))
    share_in_grad = swap(share_in_grad.astype(BF16)).astype(F32)
    share_in_grad = (
        share_in_grad.reshape(n_e, rows, 2, n_dp, shared_rows)
        .transpose(1, 2, 3, 0, 4)
        .reshape(rows, -1)
    )

    gate_grad = gate_grad.T
    logit_grad = gates * (gate_grad - jnp.sum(gates * gate_grad, axis=-1, keepdims=True))
    router_grad = jnp.dot(
        logit_grad.T, norm_two.astype(F32), precision=HIGHEST, preferred_element_type=F32
    )
    norm_two_grad = norm_two_grad + jnp.dot(
        logit_grad, router_full.astype(F32).T, precision=HIGHEST, preferred_element_type=F32
    )
    gain_two_grad = jnp.sum(norm_two_grad * normed_two, axis=0)
    upstream = cotangent.astype(F32)
    scaled_two = norm_two_grad * gain_second
    resid_grad = upstream + inverse_two * (
        scaled_two - normed_two * jnp.mean(scaled_two * normed_two, axis=-1, keepdims=True)
    )
    small_grad = jnp.concatenate([router_grad, gain_two_grad[None]], axis=0)

    branch_cot = resid_grad.astype(BF16)
    mixed_grad = dot_nt(branch_cot, proj_all).astype(BF16)
    mixed_grad = swap(mixed_grad.reshape(count, n_e, HEAD_DIM).transpose(1, 0, 2))
    mixed_grad = mixed_grad.reshape(length, HEAD_DIM)
    proj_grad = dot_tn(mixed, branch_cot).astype(BF16)
    proj_grad = proj_grad.reshape(n_dp, n_e, rows, width)
    proj_grad = ring_scatter(
        lambda n: lax.dynamic_index_in_dim(proj_grad, order[n], 1, False).reshape(-1, width)
    )
    attn_out_grad = dp_scatter(proj_grad.reshape(n_dp, rows, width))
    qkv_grad = attend_back(
        query, key, value, mixed_grad, lse, first_place, cos_table, sin_table, order
    )
    small_grad = tied(small_grad, qkv_grad).reshape(n_e + 1, n_dp * n_e, rows).transpose(1, 0, 2)
    small_grad = lax.all_to_all(
        small_grad, ("dp", "expert"), split_axis=0, concat_axis=0, tiled=True
    )
    small_grad = jnp.sum(small_grad, axis=0)
    norm_one_part = dot_nt(qkv_grad, head_w).astype(BF16)
    scaled_one = ring_scatter(lambda n: norm_one_part[n * count : (n + 1) * count])
    input_grad = resid_grad + inverse_one * (
        scaled_one - normed_one * jnp.mean(scaled_one * normed_one, axis=-1, keepdims=True)
    )
    head_grad = dot_tn(norm_all, qkv_grad).reshape(n_dp, n_e, rows, 3 * HEAD_DIM)
    head_grad = swap(dp_scatter(head_grad).astype(BF16)).astype(F32)
    head_grad = (
        head_grad.reshape(n_e, rows, 3, HEAD_DIM).transpose(1, 2, 0, 3).reshape(rows, 3 * width)
    )
    gain_attn_grad = jnp.sum(head_grad * attn_in.astype(F32), axis=1)
    attn_in_grad = head_grad * gain_rows
    return (
        (resid + routed_out).astype(BF16),
        input_grad.astype(BF16),
        attn_in_grad,
        attn_out_grad,
        gain_attn_grad,
        share_in_grad,
        share_out_grad,
        small_grad[:n_e].T,
        small_grad[n_e],
        expert_in_grad,
        expert_out_grad,
    )


def solution(mesh):
    return jax.shard_map(
        per_device,
        mesh=mesh,
        in_specs=(
            P(("dp", "expert"), None),
            P(("dp", "expert"), None),
            P("dp", None),
            P(("dp", "expert"), None),
            P(("dp", "expert"), None),
            P(("dp", "expert"), None),
            P(("dp", "expert")),
            P(("dp", "expert"), None),
            P(("dp", "expert"), None),
            P(("dp", "expert"), None),
            P(("dp", "expert")),
            P("expert", "dp", None),
            P("expert", "dp", None),
        ),
        out_specs=(
            P(("dp", "expert"), None),
            P(("dp", "expert"), None),
            P(("dp", "expert"), None),
            P(("dp", "expert"), None),
            P(("dp", "expert")),
            P(("dp", "expert"), None),
            P(("dp", "expert"), None),
            P(("dp", "expert"), None),
            P(("dp", "expert")),
            P("expert", "dp", None),
            P("expert", "dp", None),
        ),
        check_vma=False,
    )
```

```python
import functools
import math

import jax
import jax.numpy as jnp
from jax import lax
from jax.experimental import pallas as pl
from jax.experimental.pallas import tpu as pltpu
from jax.sharding import PartitionSpec as P

HEADS = 16
HEAD_DIM = 128
TOP = 6


EPS = 1e-06
THETA = 10000.0
NEG = -1e30
HIGHEST = lax.Precision.HIGHEST
BF16 = jnp.bfloat16
F32 = jnp.float32
LOG2E = math.log2(math.e)


def rope_tables(segments):
    length = segments.shape[0]
    places = jnp.arange(length, dtype=jnp.int32)
    starts = jnp.concatenate([jnp.ones((1,), dtype=jnp.bool_), segments[1:] != segments[:-1]])
    first_place = lax.cummax(jnp.where(starts, places, 0), axis=0)
    offset = (places - first_place).astype(jnp.float32)
    half_dim = HEAD_DIM // 2
    freqs = jnp.exp(jnp.arange(half_dim, dtype=jnp.float32) * (-2.0 * math.log(THETA) / HEAD_DIM))
    angles = offset[:, None] * freqs[None, :]
    cos_table, sin_table = jnp.cos(angles), jnp.sin(angles)
    return (
        jnp.concatenate([cos_table, cos_table], axis=1),
        jnp.concatenate([-sin_table, sin_table], axis=1),
        first_place[None, :],
    )


def silu_back(grad_act, gate_part, up_part):
    sigmoid_gate = jax.nn.sigmoid(gate_part)
    gate_grad = grad_act * up_part * sigmoid_gate * (1.0 + gate_part * (1.0 - sigmoid_gate))
    up_grad = grad_act * gate_part * sigmoid_gate
    return jnp.concatenate([gate_grad, up_grad], axis=-1)


def dot(left, right):
    return jnp.dot(left, right, preferred_element_type=F32)


def dot_tn(left, right):
    return lax.dot_general(left, right, (((0,), (0,)), ((), ())), preferred_element_type=F32)


def dot_nt(left, right):
    return lax.dot_general(left, right, (((1,), (1,)), ((), ())), preferred_element_type=F32)


def turn(values, cos_table, sin_table):
    return values * cos_table + pltpu.roll(values, HEAD_DIM // 2, 1) * sin_table


def attend_kernel(sources, block, order_ref, *refs):
    pieces = refs[: sources[-1][-1] + 1]
    weight_ref, cos_ref, sin_ref, start_ref = refs[len(pieces) : len(pieces) + 4]
    o_ref, q_ref, k_ref, v_ref, lse_ref, rows_ref, vt_ref = refs[len(pieces) + 4 :]
    step = pl.program_id(0)
    length = q_ref.shape[0]
    factor = HEAD_DIM ** (-0.5) * LOG2E
    rows = rows_ref.shape[0]

    for n, parts in enumerate(sources):

        @pl.when(step == n)
        def _(parts=parts):
            low = 0
            for part in parts:
                size = pieces[part].shape[0]
                rows_ref[low : low + size, :] = pieces[part][...]
                low += size

    @pl.when(step < len(sources))
    def _():
        qkv = dot(rows_ref[...], weight_ref[...])
        at = pl.ds(pl.multiple_of(order_ref[step] * rows, rows), rows)
        cos_table, sin_table = cos_ref[at, :], sin_ref[at, :]
        q_ref[at, :] = turn(qkv[:, :HEAD_DIM], cos_table, sin_table).astype(BF16)
        k_ref[at, :] = turn(qkv[:, HEAD_DIM : 2 * HEAD_DIM], cos_table, sin_table).astype(BF16)
        value = qkv[:, 2 * HEAD_DIM :]
        v_ref[at, :] = value.astype(BF16)
        vt_ref[:, at] = value.T.astype(BF16)

    for i in range(length // block):

        @pl.when(step == len(sources) + i)
        def _(i=i):
            low, high = i * block, (i + 1) * block
            raw = dot_nt(k_ref[:high, :], q_ref[low:high, :])
            keys = lax.broadcasted_iota(jnp.int32, raw.shape, 0)
            queries = low + lax.broadcasted_iota(jnp.int32, raw.shape, 1)
            allowed = (keys <= queries) & (keys >= start_ref[:, low:high])
            raw = jnp.where(allowed, raw, NEG)
            top = jnp.max(raw, axis=0, keepdims=True)
            shifted = jnp.exp2((raw - top) * factor)
            total = jnp.sum(shifted, axis=0, keepdims=True)
            probs = (shifted * (1.0 / total)).astype(BF16)
            mixed = dot(vt_ref[:, :high], probs)
            o_ref[low:high, :] = mixed.T.astype(BF16)
            lse_ref[:, low:high] = top * factor + jnp.log2(total)


def attend(blocks, order, weight, cos_table, sin_table, first_place):
    pieces, sources = flatten(blocks)
    length = cos_table.shape[0]
    rows = length // len(sources)
    width = weight.shape[0]
    block = min(256, length)
    last = len(sources) - 1
    whole = lambda shape: pl.BlockSpec(shape, lambda i, order: (0, 0))
    head = jax.ShapeDtypeStruct((length, HEAD_DIM), BF16)
    return pl.pallas_call(
        functools.partial(attend_kernel, sources, block),
        out_shape=[head] * 4
        + [jax.ShapeDtypeStruct((1, length), F32), jax.ShapeDtypeStruct((length, width), BF16)],
        grid_spec=pltpu.PrefetchScalarGridSpec(
            num_scalar_prefetch=1,
            grid=(len(sources) + length // block,),
            in_specs=[whole(piece.shape) for piece in pieces]
            + [
                whole(weight.shape),
                whole((length, HEAD_DIM)),
                whole((length, HEAD_DIM)),
                whole((1, length)),
            ],
            out_specs=[whole((length, HEAD_DIM))] * 4
            + [
                whole((1, length)),
                pl.BlockSpec((rows, width), lambda i, order: (jnp.minimum(i, last), 0)),
            ],
            scratch_shapes=[pltpu.VMEM((HEAD_DIM, length), BF16)],
        ),
        compiler_params=pltpu.CompilerParams(vmem_limit_bytes=52 * 2**20),
        name="attend",
    )(order, *pieces, weight, cos_table, sin_table, first_place)


def attend_back_kernel(
    block, rows, order_ref, q_ref, k_ref, v_ref, do_ref, lse_ref, start_ref, cos_ref, sin_ref, out_ref, kt_ref, dq_ref, dk_ref, dv_ref
):
    length = q_ref.shape[0]
    step = pl.program_id(0)
    scale = HEAD_DIM ** (-0.5)
    factor = scale * LOG2E
    count = length // block

    @pl.when(step == 0)
    def _():
        kt_ref[...] = k_ref[...].astype(F32).T.astype(BF16)
        dk_ref[...] = jnp.zeros_like(dk_ref)
        dv_ref[...] = jnp.zeros_like(dv_ref)

    for i in range(count):

        @pl.when(step == i)
        def _(i=i):
            low, high = i * block, (i + 1) * block
            query, grad = q_ref[low:high, :], do_ref[low:high, :]
            raw = dot_nt(k_ref[:high, :], query)
            keys = lax.broadcasted_iota(jnp.int32, raw.shape, 0)
            queries = low + lax.broadcasted_iota(jnp.int32, raw.shape, 1)
            allowed = (keys <= queries) & (keys >= start_ref[:, low:high])
            raw = jnp.where(allowed, raw * factor - lse_ref[:, low:high], NEG)
            probs = jnp.exp2(raw)
            probs_grad = dot_nt(v_ref[:high, :], grad)
            inner = jnp.sum(probs_grad * probs, axis=0, keepdims=True)
            score_grad = (probs * (probs_grad - inner)).astype(BF16)
            dv_ref[:high, :] += dot(probs.astype(BF16), grad)
            dk_ref[:high, :] += dot(score_grad, query)
            dq_ref[low:high, :] = dot(kt_ref[:, :high], score_grad).T

    @pl.when(step == count - 1)
    def _():
        for n in range(length // rows):
            at = pl.ds(pl.multiple_of(order_ref[n] * rows, rows), rows)
            to = slice(n * rows, (n + 1) * rows)
            cos_table, sin_table = cos_ref[at, :], -sin_ref[at, :]
            out_ref[to, :HEAD_DIM] = turn(dq_ref[at, :] * scale, cos_table, sin_table).astype(BF16)
            out_ref[to, HEAD_DIM : 2 * HEAD_DIM] = turn(
                dk_ref[at, :] * scale, cos_table, sin_table
            ).astype(BF16)
            out_ref[to, 2 * HEAD_DIM :] = dv_ref[at, :].astype(BF16)


def attend_back(query, key, value, grad, lse, first_place, cos_table, sin_table, order):
    length = query.shape[0]
    block = min(256, length)
    whole = lambda shape: pl.BlockSpec(shape, lambda i, order: (0, 0))
    head = whole((length, HEAD_DIM))
    return pl.pallas_call(
        functools.partial(attend_back_kernel, block, length // order.shape[0]),
        out_shape=jax.ShapeDtypeStruct((length, 3 * HEAD_DIM), BF16),
        grid_spec=pltpu.PrefetchScalarGridSpec(
            num_scalar_prefetch=1,
            grid=(length // block,),
            in_specs=[head] * 4 + [whole((1, length))] * 2 + [head] * 2,
            out_specs=whole((length, 3 * HEAD_DIM)),
            scratch_shapes=[pltpu.VMEM((HEAD_DIM, length), BF16)]
            + [pltpu.VMEM((length, HEAD_DIM), F32)] * 3,
        ),
        compiler_params=pltpu.CompilerParams(vmem_limit_bytes=48 * 2**20),
        name="attend_back",
    )(order, query, key, value, grad, lse, first_place, cos_table, sin_table)


def dp_gather(value):
    count = lax.axis_size("dp")
    if count == 1:
        return value[None]
    here = lax.axis_index("dp")
    parts = [value] + [
        lax.ppermute(value, "dp", [(i, (i - step) % count) for i in range(count)])
        for step in range(1, count)
    ]
    if count == 2:
        first = here == 0
        return jnp.stack(
            [jnp.where(first, parts[0], parts[1]), jnp.where(first, parts[1], parts[0])]
        )
    whole = jnp.zeros((count,) + value.shape, value.dtype)
    for step, part in enumerate(parts):
        whole = lax.dynamic_update_index_in_dim(whole, part, (here + step) % count, 0)
    return whole


def dp_scatter(value):
    count = lax.axis_size("dp")
    here = lax.axis_index("dp")
    total = lax.dynamic_index_in_dim(value, here, 0, keepdims=False)
    for step in range(1, count):
        block = lax.dynamic_index_in_dim(value, (here + step) % count, 0, keepdims=False)
        got = lax.ppermute(
            block.astype(BF16), "dp", [(i, (i + step) % count) for i in range(count)]
        )
        total = total + got.astype(F32)
    return total


def ring_order():
    pairs = lax.axis_size("expert") // 2
    return list(range(0, pairs, 2)) + list(range(pairs - 1, 0, -2))


def ring_shift(value, step):
    order = ring_order()
    pairs = len(order)
    perm = [
        (order[q] * 2 + c, order[(q + step) % pairs] * 2 + c) for q in range(pairs) for c in range(2)
    ]
    return lax.ppermute(value, "expert", perm)


def core_swap(value):
    count = lax.axis_size("expert")
    return lax.ppermute(value, "expert", [(i, i ^ 1) for i in range(count)])


def ring_offsets():
    half = lax.axis_size("expert") // 4
    return [0] + [o for step in range(1, half) for o in (step, -step)] + [half]


def ring_blocks():
    order = ring_order()
    pairs = len(order)
    table = [[0] * (2 * pairs) for _ in range(2 * pairs)]
    for q in range(pairs):
        for c in range(2):
            for j, offset in enumerate(ring_offsets()):
                for other in range(2):
                    table[order[q] * 2 + c][2 * j + other] = (
                        order[(q - offset) % pairs] * 2 + (c ^ other)
                    )
    return lax.dynamic_index_in_dim(
        jnp.asarray(table, jnp.int32), lax.axis_index("expert"), 0, keepdims=False
    )


def tied(value, *tokens):
    token = sum(t.astype(F32).reshape(-1)[0] for t in tokens) * 0.0
    return (value.astype(F32) * (1.0 + token)).astype(value.dtype)


def ring_gather(value, gates=None):
    gates = gates or {}
    half_rows = value.shape[0] // 2
    half = lax.axis_size("expert") // 4
    blocks = {}

    def keep(parts, offset):
        blocks[offset] = (parts, [core_swap(part) for part in parts])

    keep([value], 0)
    ahead = back = value
    for step in range(1, half):
        if step in gates:
            token = gates[step](blocks)
            ahead, back = tied(ahead, token), tied(back, token)
        ahead, back = ring_shift(ahead, 1), ring_shift(back, -1)
        keep([ahead], step)
        keep([back], -step)
    if half in gates:
        token = gates[half](blocks)
        ahead, back = tied(ahead, token), tied(back, token)
    last = [ring_shift(ahead[:half_rows], 1), ring_shift(back[half_rows:], -1)]
    keep(last, half)
    return [parts for offset in ring_offsets() for parts in blocks[offset]]


def flatten(blocks):
    pieces = [piece for parts in blocks for piece in parts]
    sources, n = [], 0
    for parts in blocks:
        sources.append(tuple(range(n, n + len(parts))))
        n += len(parts)
    return pieces, tuple(sources)


def place_kernel(sources, widths, order_ref, *refs):
    pieces, outs = refs[: -len(widths)], refs[-len(widths) :]
    step = pl.program_id(0)
    for n, parts in enumerate(sources):

        @pl.when(step == n)
        def _(parts=parts):
            low = 0
            for part in parts:
                size = pieces[part].shape[0]
                left = 0
                for out, wide in zip(outs, widths):
                    block = pieces[part][:, left : left + wide]
                    if len(out.shape) == 3:
                        groups, rows, _ = out.shape
                        rows = min(rows, size)
                        per = size // rows
                        for g in range(per):
                            at = low + g * rows
                            out[at // out.shape[1], at % out.shape[1] : at % out.shape[1] + rows, :] = block[
                                g * rows : (g + 1) * rows
                            ]
                    else:
                        out[low : low + size, :] = block
                    left += wide
                low += size


def place(blocks, order, widths, groups=1):
    pieces, sources = flatten(blocks)
    rows = sum(pieces[part].shape[0] for part in sources[0])
    length = rows * len(blocks)
    shapes = [jax.ShapeDtypeStruct((length, wide), pieces[0].dtype) for wide in widths]
    specs = [pl.BlockSpec((rows, wide), lambda i, order: (order[i], 0)) for wide in widths]
    if groups > 1:
        shapes[0] = jax.ShapeDtypeStruct((groups, length // groups, widths[0]), pieces[0].dtype)
        specs[0] = pl.BlockSpec((groups, rows // groups, widths[0]), lambda i, order: (0, order[i], 0))
    return pl.pallas_call(
        functools.partial(place_kernel, sources, tuple(widths)),
        out_shape=shapes,
        grid_spec=pltpu.PrefetchScalarGridSpec(
            num_scalar_prefetch=1,
            grid=(len(blocks),),
            in_specs=[pl.BlockSpec(piece.shape, lambda i, order: (0, 0)) for piece in pieces],
            out_specs=specs,
        ),
        compiler_params=pltpu.CompilerParams(vmem_limit_bytes=48 * 2**20),
        name="place",
    )(order, *pieces)


def ring_scatter(block, *after):
    half = lax.axis_size("expert") // 4
    offsets = ring_offsets()
    spare = {}

    def mine(offset):
        if offset not in spare:
            j = offsets.index(offset)
            spare[offset] = block(2 * j).astype(F32) + core_swap(block(2 * j + 1)).astype(F32)
        return spare[offset]

    far = (tied(mine(half), *after) if after else mine(half)).astype(BF16)
    half_rows = far.shape[0] // 2
    ahead = ring_shift(far[:half_rows], 1)
    back = ring_shift(far[half_rows:], -1)
    for step in range(half - 1, 0, -1):
        onward, homeward = mine(-step), mine(step)
        if step == half - 1:
            onward = jnp.concatenate(
                [onward[:half_rows] + ahead.astype(F32), onward[half_rows:]], axis=0
            )
            homeward = jnp.concatenate(
                [homeward[:half_rows], homeward[half_rows:] + back.astype(F32)], axis=0
            )
        else:
            onward = onward + ahead.astype(F32)
            homeward = homeward + back.astype(F32)
        ahead = ring_shift(onward.astype(BF16), 1)
        back = ring_shift(homeward.astype(BF16), -1)
    return mine(0) + ahead.astype(F32) + back.astype(F32)


def combine_kernel(turned, select_ref, rows_ref, act_ref, weight_ref, out_ref):
    mul = dot_nt if turned else dot
    out_ref[...] = (
        dot_tn(select_ref[0], rows_ref[0]) + mul(act_ref[...], weight_ref[...])
    ).astype(BF16)


def combine(select, rows, act, weight, turned):
    blocks, capacity, count = select.shape
    width = rows.shape[-1]
    return pl.pallas_call(
        functools.partial(combine_kernel, turned),
        grid=(blocks,),
        out_shape=jax.ShapeDtypeStruct((blocks * count, width), BF16),
        in_specs=[
            pl.BlockSpec((1, capacity, count), lambda i: (i, 0, 0)),
            pl.BlockSpec((1, capacity, width), lambda i: (i, 0, 0)),
            pl.BlockSpec((count, act.shape[1]), lambda i: (i, 0)),
            pl.BlockSpec(weight.shape, lambda i: (0, 0)),
        ],
        out_specs=pl.BlockSpec((count, width), lambda i: (i, 0)),
        compiler_params=pltpu.CompilerParams(vmem_limit_bytes=32 * 2**20),
        name="combine",
    )(select, rows, act, weight)


def swap(value):
    return lax.all_to_all(value, "expert", split_axis=0, concat_axis=0, tiled=True)


def per_device(
    tokens,
    cotangent,
    segment_ids,
    routes,
    attn_in,
    attn_out,
    gain_attn,
    shared_in,
    shared_out,
    router,
    gain_ffn,
    expert_in,
    expert_out,
):
    n_dp, n_e = lax.axis_size("dp"), lax.axis_size("expert")
    me = lax.axis_index("expert")
    count, width = tokens.shape
    segments = segment_ids[0]
    length = segments.shape[0]
    rows = attn_in.shape[0]
    capacity = min(count, 3 * TOP * count // (2 * n_e))
    shared_rows = shared_out.shape[0]
    shared_width = shared_rows * n_dp
    expert_width = expert_out.shape[1] * n_dp

    order = ring_blocks()
    steady = jnp.arange(n_e, dtype=jnp.int32)
    hidden_in = tokens.astype(F32)
    inverse_one = lax.rsqrt(jnp.mean(hidden_in * hidden_in, axis=-1, keepdims=True) + EPS)
    normed_one = hidden_in * inverse_one
    gain_rows = gain_attn.astype(F32)[:, None]
    head_w = []

    def head_sent(blocks):
        own = (attn_in.astype(F32) * tied(gain_rows, blocks[1][0][0])).astype(BF16)
        own = own.reshape(rows, 3, n_e, HEAD_DIM).transpose(2, 0, 1, 3)
        head_w.append(swap(own.reshape(n_e, rows, 3 * HEAD_DIM)))
        return head_w[0]

    def head_whole(blocks):
        head_w.append(dp_gather(head_w[0]).reshape(width, 3 * HEAD_DIM))
        return head_w[1]

    half = n_e // 4
    norm_blocks = ring_gather(normed_one.astype(BF16), {half - 1: head_sent, half: head_whole})
    head_w = head_w[1]

    cos_table, sin_table, first_place = rope_tables(segments)
    mixed, query, key, value, lse, norm_all = attend(
        norm_blocks, order, head_w, cos_table, sin_table, first_place
    )
    mixed = swap(mixed.reshape(n_e, count, HEAD_DIM))
    mixed = mixed.transpose(1, 0, 2).reshape(count, width)

    small = jnp.concatenate([router, gain_ffn[:, None]], axis=1)
    small = dp_gather(small).reshape(-1, router.shape[1] + 1)
    small_rows = small.shape[0]
    extra = jnp.zeros((count, 128), BF16)
    extra = extra.at[:small_rows, : small.shape[1]].set(small)
    extra = extra.at[:, 64 : 64 + TOP].set(routes.astype(BF16))
    proj_all = jnp.concatenate([dp_gather(attn_out).reshape(n_dp * rows, width), extra], axis=1)
    proj_all = ring_gather(
        tied(proj_all, norm_blocks[-1][0], norm_blocks[-1][-1]),
        {half - 2: lambda blocks: lse, half - 1: lambda blocks: mixed},
    )
    proj_all, extra_all = place(proj_all, order, [width, 128], n_dp)
    proj_all = proj_all.reshape(width, width)
    small = extra_all.reshape(n_e, count, 128)[:, :small_rows, : router.shape[1] + 1]
    small = small.reshape(n_e, n_dp, rows, -1).transpose(1, 0, 2, 3).reshape(width, -1)
    router_full = small[:, : router.shape[1]]
    gain_second = small[:, router.shape[1]].astype(F32)
    routes_all = extra_all[:, 64 : 64 + TOP].astype(F32)

    expert_up = lax.all_gather(expert_in, "dp", axis=1, tiled=True)[0]
    down_parts = jnp.split(expert_out[0], 2, axis=0)
    down_parts = [dp_gather(part) for part in down_parts]
    expert_down = jnp.concatenate(down_parts, axis=1).reshape(expert_width, width)
    share_w = shared_in.reshape(rows, 2, n_dp, n_e, shared_rows).transpose(3, 0, 1, 2, 4)
    share_w = share_w.reshape(n_e, rows, 2 * shared_width)
    share_w = swap(tied(share_w, norm_blocks[-1][0], norm_blocks[-1][-1]))
    share_w = dp_gather(share_w).reshape(width, 2 * shared_width)
    share_out = dp_gather(shared_out).reshape(shared_width, width)
    resid = tied(hidden_in, expert_up) + dot(mixed, proj_all)

    inverse_two = lax.rsqrt(jnp.mean(resid * resid, axis=-1, keepdims=True) + EPS)
    normed_two = resid * inverse_two
    norm_two = (normed_two * gain_second).astype(BF16)
    logits = dot(norm_two, router_full)
    picked = jnp.any(routes[:, :, None] == jnp.arange(n_e)[None, None, :], axis=1)
    chosen = jnp.where(picked, logits, NEG)
    chosen = jnp.where(picked, jnp.exp(chosen - jnp.max(chosen, axis=-1, keepdims=True)), 0.0)
    gates = chosen / jnp.sum(chosen, axis=-1, keepdims=True)
    gate_high = gates.astype(BF16)
    gate_low = (gates - gate_high.astype(F32)).astype(BF16)
    blank = jnp.zeros((count, 128 - 2 * n_e), BF16)
    payload = jnp.concatenate([norm_two, gate_high, gate_low, blank], axis=1)
    payload = ring_gather(payload)
    cot_all = tied(cotangent, payload[-1][0], payload[-1][-1], down_parts[0][0], down_parts[0][-1])
    norm_two_all, payload = place(payload, steady, [width, 128])
    (cot_all,) = place(ring_gather(cot_all), steady, [width])
    mine = jnp.arange(n_e) == me
    gate_all = payload[:, : 2 * n_e].astype(F32).reshape(length, 2, n_e)
    gate_all = jnp.sum(jnp.where(mine, gate_all, 0.0), axis=(1, 2))

    named = jnp.any(routes_all == me.astype(F32), axis=1).reshape(n_e, count)
    named = jnp.take(named, order, axis=0)
    ranking = jnp.cumsum(named.astype(jnp.int32), axis=1) - 1
    select = (
        named[:, None, :]
        & (ranking[:, None, :] == jnp.arange(capacity, dtype=jnp.int32)[None, :, None])
    ).astype(BF16)
    arrived = jnp.einsum(
        "bct,btd->bcd",
        select,
        norm_two_all.reshape(n_e, count, width),
        preferred_element_type=F32,
    ).astype(BF16).reshape(n_e * capacity, width)
    cot_rows = jnp.einsum(
        "bct,btd->bcd", select, cot_all.reshape(n_e, count, width), preferred_element_type=F32
    ).reshape(n_e * capacity, width)
    gate_rows = jnp.sum(
        jnp.where(select != 0, gate_all.reshape(n_e, 1, count), 0.0), axis=-1
    ).reshape(n_e * capacity, 1)

    expert_pre = dot(arrived, expert_up)
    expert_act = (
        jax.nn.silu(expert_pre[:, :expert_width]) * expert_pre[:, expert_width:]
    ).astype(BF16)
    expert_res = dot(expert_act, expert_down).astype(BF16).astype(F32)
    gate_grad = jnp.sum(cot_rows * expert_res, axis=-1).reshape(n_e, capacity, 1)
    gate_grad = jnp.sum(jnp.where(select != 0, gate_grad, 0.0), axis=1)
    gate_grad = jnp.sum(
        jnp.where(order[:, None, None] == steady[None, :, None], gate_grad[:, None, :], 0.0), axis=0
    )
    gate_grad = swap(gate_grad)
    weighted = (gate_rows * expert_res).astype(BF16).reshape(n_e, capacity, width)

    shared_pre = dot(norm_two_all, share_w)
    shared_act = (
        jax.nn.silu(shared_pre[:, :shared_width]) * shared_pre[:, shared_width:]
    ).astype(BF16)
    out_part = combine(select, weighted, shared_act, share_out, False)
    routed_out = ring_scatter(lambda n: out_part[n * count : (n + 1) * count])

    route_grad = (gate_rows * cot_rows).astype(BF16)
    act_grad = dot_nt(route_grad, expert_down)
    pre_grad = silu_back(
        act_grad, expert_pre[:, :expert_width], expert_pre[:, expert_width:]
    ).astype(BF16)
    row_grad = dot_nt(pre_grad, expert_up).astype(BF16).reshape(n_e, capacity, width)
    shared_act_grad = dot_nt(cot_all, share_out)
    shared_pre_grad = silu_back(
        shared_act_grad, shared_pre[:, :shared_width], shared_pre[:, shared_width:]
    ).astype(BF16)
    norm_two_part = combine(select, row_grad, shared_pre_grad, share_w, True)
    norm_two_grad = ring_scatter(
        lambda n: norm_two_part[n * count : (n + 1) * count], routed_out
    )

    down_grad = dot_tn(expert_act, route_grad)
    up_grad = dot_tn(arrived, pre_grad)
    expert_out_grad = lax.psum_scatter(
        down_grad.astype(BF16), "dp", scatter_dimension=0, tiled=True
    ).astype(F32)[None]
    expert_in_grad = lax.psum_scatter(
        up_grad.astype(BF16), "dp", scatter_dimension=0, tiled=True
    ).astype(F32)[None]
    share_out_grad = dp_scatter(dot_tn(shared_act, cot_all).reshape(n_dp, shared_rows, width))
    share_in_grad = dot_tn(norm_two_all, shared_pre_grad)
    share_in_grad = dp_scatter(share_in_grad.reshape(n_dp, n_e, rows, 2 * shared_width))
    share_in_grad = swap(share_in_grad.astype(BF16)).astype(F32)
    share_in_grad = (
        share_in_grad.reshape(n_e, rows, 2, n_dp, shared_rows)
        .transpose(1, 2, 3, 0, 4)
        .reshape(rows, -1)
    )

    gate_grad = gate_grad.T
    logit_grad = gates * (gate_grad - jnp.sum(gates * gate_grad, axis=-1, keepdims=True))
    router_grad = jnp.dot(
        logit_grad.T, norm_two.astype(F32), precision=HIGHEST, preferred_element_type=F32
    )
    norm_two_grad = norm_two_grad + jnp.dot(
        logit_grad, router_full.astype(F32).T, precision=HIGHEST, preferred_element_type=F32
    )
    gain_two_grad = jnp.sum(norm_two_grad * normed_two, axis=0)
    upstream = cotangent.astype(F32)
    scaled_two = norm_two_grad * gain_second
    resid_grad = upstream + inverse_two * (
        scaled_two - normed_two * jnp.mean(scaled_two * normed_two, axis=-1, keepdims=True)
    )
    small_grad = jnp.concatenate([router_grad, gain_two_grad[None]], axis=0)

    branch_cot = resid_grad.astype(BF16)
    mixed_grad = dot_nt(branch_cot, proj_all).astype(BF16)
    mixed_grad = swap(mixed_grad.reshape(count, n_e, HEAD_DIM).transpose(1, 0, 2))
    mixed_grad = mixed_grad.reshape(length, HEAD_DIM)
    proj_grad = dot_tn(mixed, branch_cot).astype(BF16)
    proj_grad = proj_grad.reshape(n_dp, n_e, rows, width)
    proj_grad = ring_scatter(
        lambda n: lax.dynamic_index_in_dim(proj_grad, order[n], 1, False).reshape(-1, width)
    )
    attn_out_grad = dp_scatter(proj_grad.reshape(n_dp, rows, width))
    qkv_grad = attend_back(
        query, key, value, mixed_grad, lse, first_place, cos_table, sin_table, order
    )
    small_grad = tied(small_grad, qkv_grad).reshape(n_e + 1, n_dp * n_e, rows).transpose(1, 0, 2)
    small_grad = lax.all_to_all(
        small_grad, ("dp", "expert"), split_axis=0, concat_axis=0, tiled=True
    )
    small_grad = jnp.sum(small_grad, axis=0)
    norm_one_part = dot_nt(qkv_grad, head_w).astype(BF16)
    scaled_one = ring_scatter(
        lambda n: norm_one_part[n * count : (n + 1) * count], attn_out_grad
    )
    input_grad = resid_grad + inverse_one * (
        scaled_one - normed_one * jnp.mean(scaled_one * normed_one, axis=-1, keepdims=True)
    )
    head_grad = dot_tn(norm_all, qkv_grad).reshape(n_dp, n_e, rows, 3 * HEAD_DIM)
    head_grad = swap(dp_scatter(head_grad).astype(BF16)).astype(F32)
    head_grad = (
        head_grad.reshape(n_e, rows, 3, HEAD_DIM).transpose(1, 2, 0, 3).reshape(rows, 3 * width)
    )
    gain_attn_grad = jnp.sum(head_grad * attn_in.astype(F32), axis=1)
    attn_in_grad = head_grad * gain_rows
    return (
        (resid + routed_out).astype(BF16),
        input_grad.astype(BF16),
        attn_in_grad,
        attn_out_grad,
        gain_attn_grad,
        share_in_grad,
        share_out_grad,
        small_grad[:n_e].T,
        small_grad[n_e],
        expert_in_grad,
        expert_out_grad,
    )


def solution(mesh):
    return jax.shard_map(
        per_device,
        mesh=mesh,
        in_specs=(
            P(("dp", "expert"), None),
            P(("dp", "expert"), None),
            P("dp", None),
            P(("dp", "expert"), None),
            P(("dp", "expert"), None),
            P(("dp", "expert"), None),
            P(("dp", "expert")),
            P(("dp", "expert"), None),
            P(("dp", "expert"), None),
            P(("dp", "expert"), None),
            P(("dp", "expert")),
            P("expert", "dp", None),
            P("expert", "dp", None),
        ),
        out_specs=(
            P(("dp", "expert"), None),
            P(("dp", "expert"), None),
            P(("dp", "expert"), None),
            P(("dp", "expert"), None),
            P(("dp", "expert")),
            P(("dp", "expert"), None),
            P(("dp", "expert"), None),
            P(("dp", "expert"), None),
            P(("dp", "expert")),
            P("expert", "dp", None),
            P("expert", "dp", None),
        ),
        check_vma=False,
    )
```

```python
import functools
import math

import jax
import jax.numpy as jnp
from jax import lax
from jax.experimental import pallas as pl
from jax.experimental.pallas import tpu as pltpu
from jax.sharding import PartitionSpec as P

HEADS = 16
HEAD_DIM = 128
TOP = 6


EPS = 1e-06
THETA = 10000.0
NEG = -1e30
HIGHEST = lax.Precision.HIGHEST
BF16 = jnp.bfloat16
F32 = jnp.float32
LOG2E = math.log2(math.e)


def rope_tables(segments):
    length = segments.shape[0]
    places = jnp.arange(length, dtype=jnp.int32)
    starts = jnp.concatenate([jnp.ones((1,), dtype=jnp.bool_), segments[1:] != segments[:-1]])
    first_place = lax.cummax(jnp.where(starts, places, 0), axis=0)
    offset = (places - first_place).astype(jnp.float32)
    half_dim = HEAD_DIM // 2
    freqs = jnp.exp(jnp.arange(half_dim, dtype=jnp.float32) * (-2.0 * math.log(THETA) / HEAD_DIM))
    angles = offset[:, None] * freqs[None, :]
    cos_table, sin_table = jnp.cos(angles), jnp.sin(angles)
    return (
        jnp.concatenate([cos_table, cos_table], axis=1),
        jnp.concatenate([-sin_table, sin_table], axis=1),
        first_place[None, :],
    )


def silu_back(grad_act, gate_part, up_part):
    sigmoid_gate = jax.nn.sigmoid(gate_part)
    gate_grad = grad_act * up_part * sigmoid_gate * (1.0 + gate_part * (1.0 - sigmoid_gate))
    up_grad = grad_act * gate_part * sigmoid_gate
    return jnp.concatenate([gate_grad, up_grad], axis=-1)


def dot(left, right):
    return jnp.dot(left, right, preferred_element_type=F32)


def dot_tn(left, right):
    return lax.dot_general(left, right, (((0,), (0,)), ((), ())), preferred_element_type=F32)


def dot_nt(left, right):
    return lax.dot_general(left, right, (((1,), (1,)), ((), ())), preferred_element_type=F32)


def turn(values, cos_table, sin_table):
    return values * cos_table + pltpu.roll(values, HEAD_DIM // 2, 1) * sin_table


def attend_kernel(sources, block, order_ref, *refs):
    pieces = refs[: sources[-1][-1] + 1]
    weight_ref, cos_ref, sin_ref, start_ref = refs[len(pieces) : len(pieces) + 4]
    o_ref, q_ref, k_ref, v_ref, lse_ref, rows_ref, vt_ref = refs[len(pieces) + 4 :]
    step = pl.program_id(0)
    length = q_ref.shape[0]
    factor = HEAD_DIM ** (-0.5) * LOG2E
    rows = rows_ref.shape[0]

    for n, parts in enumerate(sources):

        @pl.when(step == n)
        def _(parts=parts):
            low = 0
            for part in parts:
                size = pieces[part].shape[0]
                rows_ref[low : low + size, :] = pieces[part][...]
                low += size

    @pl.when(step < len(sources))
    def _():
        qkv = dot(rows_ref[...], weight_ref[...])
        at = pl.ds(pl.multiple_of(order_ref[step] * rows, rows), rows)
        cos_table, sin_table = cos_ref[at, :], sin_ref[at, :]
        q_ref[at, :] = turn(qkv[:, :HEAD_DIM], cos_table, sin_table).astype(BF16)
        k_ref[at, :] = turn(qkv[:, HEAD_DIM : 2 * HEAD_DIM], cos_table, sin_table).astype(BF16)
        value = qkv[:, 2 * HEAD_DIM :]
        v_ref[at, :] = value.astype(BF16)
        vt_ref[:, at] = value.T.astype(BF16)

    for i in range(length // block):

        @pl.when(step == len(sources) + i)
        def _(i=i):
            low, high = i * block, (i + 1) * block
            raw = dot_nt(k_ref[:high, :], q_ref[low:high, :])
            keys = lax.broadcasted_iota(jnp.int32, raw.shape, 0)
            queries = low + lax.broadcasted_iota(jnp.int32, raw.shape, 1)
            allowed = (keys <= queries) & (keys >= start_ref[:, low:high])
            raw = jnp.where(allowed, raw, NEG)
            top = jnp.max(raw, axis=0, keepdims=True)
            shifted = jnp.exp2((raw - top) * factor)
            total = jnp.sum(shifted, axis=0, keepdims=True)
            probs = (shifted * (1.0 / total)).astype(BF16)
            mixed = dot(vt_ref[:, :high], probs)
            o_ref[low:high, :] = mixed.T.astype(BF16)
            lse_ref[:, low:high] = top * factor + jnp.log2(total)


def attend(blocks, order, weight, cos_table, sin_table, first_place):
    pieces, sources = flatten(blocks)
    length = cos_table.shape[0]
    rows = length // len(sources)
    width = weight.shape[0]
    block = min(256, length)
    last = len(sources) - 1
    whole = lambda shape: pl.BlockSpec(shape, lambda i, order: (0, 0))
    head = jax.ShapeDtypeStruct((length, HEAD_DIM), BF16)
    return pl.pallas_call(
        functools.partial(attend_kernel, sources, block),
        out_shape=[head] * 4
        + [jax.ShapeDtypeStruct((1, length), F32), jax.ShapeDtypeStruct((length, width), BF16)],
        grid_spec=pltpu.PrefetchScalarGridSpec(
            num_scalar_prefetch=1,
            grid=(len(sources) + length // block,),
            in_specs=[whole(piece.shape) for piece in pieces]
            + [
                whole(weight.shape),
                whole((length, HEAD_DIM)),
                whole((length, HEAD_DIM)),
                whole((1, length)),
            ],
            out_specs=[whole((length, HEAD_DIM))] * 4
            + [
                whole((1, length)),
                pl.BlockSpec((rows, width), lambda i, order: (jnp.minimum(i, last), 0)),
            ],
            scratch_shapes=[pltpu.VMEM((HEAD_DIM, length), BF16)],
        ),
        compiler_params=pltpu.CompilerParams(vmem_limit_bytes=52 * 2**20),
        name="attend",
    )(order, *pieces, weight, cos_table, sin_table, first_place)


def attend_back_kernel(
    block, rows, order_ref, q_ref, k_ref, v_ref, do_ref, lse_ref, start_ref, cos_ref, sin_ref, out_ref, kt_ref, dq_ref, dk_ref, dv_ref
):
    length = q_ref.shape[0]
    step = pl.program_id(0)
    scale = HEAD_DIM ** (-0.5)
    factor = scale * LOG2E
    count = length // block

    @pl.when(step == 0)
    def _():
        kt_ref[...] = k_ref[...].astype(F32).T.astype(BF16)
        dk_ref[...] = jnp.zeros_like(dk_ref)
        dv_ref[...] = jnp.zeros_like(dv_ref)

    for i in range(count):

        @pl.when(step == i)
        def _(i=i):
            low, high = i * block, (i + 1) * block
            query, grad = q_ref[low:high, :], do_ref[low:high, :]
            raw = dot_nt(k_ref[:high, :], query)
            keys = lax.broadcasted_iota(jnp.int32, raw.shape, 0)
            queries = low + lax.broadcasted_iota(jnp.int32, raw.shape, 1)
            allowed = (keys <= queries) & (keys >= start_ref[:, low:high])
            raw = jnp.where(allowed, raw * factor - lse_ref[:, low:high], NEG)
            probs = jnp.exp2(raw)
            probs_grad = dot_nt(v_ref[:high, :], grad)
            inner = jnp.sum(probs_grad * probs, axis=0, keepdims=True)
            score_grad = (probs * (probs_grad - inner)).astype(BF16)
            dv_ref[:high, :] += dot(probs.astype(BF16), grad)
            dk_ref[:high, :] += dot(score_grad, query)
            dq_ref[low:high, :] = dot(kt_ref[:, :high], score_grad).T

    @pl.when(step == count - 1)
    def _():
        for n in range(length // rows):
            at = pl.ds(pl.multiple_of(order_ref[n] * rows, rows), rows)
            to = slice(n * rows, (n + 1) * rows)
            cos_table, sin_table = cos_ref[at, :], -sin_ref[at, :]
            out_ref[to, :HEAD_DIM] = turn(dq_ref[at, :] * scale, cos_table, sin_table).astype(BF16)
            out_ref[to, HEAD_DIM : 2 * HEAD_DIM] = turn(
                dk_ref[at, :] * scale, cos_table, sin_table
            ).astype(BF16)
            out_ref[to, 2 * HEAD_DIM :] = dv_ref[at, :].astype(BF16)


def attend_back(query, key, value, grad, lse, first_place, cos_table, sin_table, order):
    length = query.shape[0]
    block = min(256, length)
    whole = lambda shape: pl.BlockSpec(shape, lambda i, order: (0, 0))
    head = whole((length, HEAD_DIM))
    return pl.pallas_call(
        functools.partial(attend_back_kernel, block, length // order.shape[0]),
        out_shape=jax.ShapeDtypeStruct((length, 3 * HEAD_DIM), BF16),
        grid_spec=pltpu.PrefetchScalarGridSpec(
            num_scalar_prefetch=1,
            grid=(length // block,),
            in_specs=[head] * 4 + [whole((1, length))] * 2 + [head] * 2,
            out_specs=whole((length, 3 * HEAD_DIM)),
            scratch_shapes=[pltpu.VMEM((HEAD_DIM, length), BF16)]
            + [pltpu.VMEM((length, HEAD_DIM), F32)] * 3,
        ),
        compiler_params=pltpu.CompilerParams(vmem_limit_bytes=48 * 2**20),
        name="attend_back",
    )(order, query, key, value, grad, lse, first_place, cos_table, sin_table)


def dp_gather(value):
    count = lax.axis_size("dp")
    if count == 1:
        return value[None]
    here = lax.axis_index("dp")
    parts = [value] + [
        lax.ppermute(value, "dp", [(i, (i - step) % count) for i in range(count)])
        for step in range(1, count)
    ]
    if count == 2:
        first = here == 0
        return jnp.stack(
            [jnp.where(first, parts[0], parts[1]), jnp.where(first, parts[1], parts[0])]
        )
    whole = jnp.zeros((count,) + value.shape, value.dtype)
    for step, part in enumerate(parts):
        whole = lax.dynamic_update_index_in_dim(whole, part, (here + step) % count, 0)
    return whole


def dp_scatter(value):
    count = lax.axis_size("dp")
    here = lax.axis_index("dp")
    total = lax.dynamic_index_in_dim(value, here, 0, keepdims=False)
    for step in range(1, count):
        block = lax.dynamic_index_in_dim(value, (here + step) % count, 0, keepdims=False)
        got = lax.ppermute(
            block.astype(BF16), "dp", [(i, (i + step) % count) for i in range(count)]
        )
        total = total + got.astype(F32)
    return total


def ring_order():
    pairs = lax.axis_size("expert") // 2
    return list(range(0, pairs, 2)) + list(range(pairs - 1, 0, -2))


def ring_shift(value, step):
    order = ring_order()
    pairs = len(order)
    perm = [
        (order[q] * 2 + c, order[(q + step) % pairs] * 2 + c) for q in range(pairs) for c in range(2)
    ]
    return lax.ppermute(value, "expert", perm)


def core_swap(value):
    count = lax.axis_size("expert")
    return lax.ppermute(value, "expert", [(i, i ^ 1) for i in range(count)])


def ring_offsets():
    half = lax.axis_size("expert") // 4
    return [0] + [o for step in range(1, half) for o in (step, -step)] + [half]


def ring_blocks():
    order = ring_order()
    pairs = len(order)
    table = [[0] * (2 * pairs) for _ in range(2 * pairs)]
    for q in range(pairs):
        for c in range(2):
            for j, offset in enumerate(ring_offsets()):
                for other in range(2):
                    table[order[q] * 2 + c][2 * j + other] = (
                        order[(q - offset) % pairs] * 2 + (c ^ other)
                    )
    return lax.dynamic_index_in_dim(
        jnp.asarray(table, jnp.int32), lax.axis_index("expert"), 0, keepdims=False
    )


def tied(value, *tokens):
    firsts = [lax.slice(t, (0,) * t.ndim, (1,) * t.ndim).reshape(()) for t in tokens]
    token = sum(t.astype(F32) for t in firsts) * 0.0
    return (value.astype(F32) * (1.0 + token)).astype(value.dtype)


def ring_gather(value, gates=None):
    gates = gates or {}
    half_rows = value.shape[0] // 2
    half = lax.axis_size("expert") // 4
    blocks = {}

    def keep(parts, offset):
        blocks[offset] = (parts, [core_swap(part) for part in parts])

    keep([value], 0)
    ahead = back = value
    for step in range(1, half):
        if step in gates:
            token = gates[step](blocks)
            ahead, back = tied(ahead, token), tied(back, token)
        ahead, back = ring_shift(ahead, 1), ring_shift(back, -1)
        keep([ahead], step)
        keep([back], -step)
    if half in gates:
        token = gates[half](blocks)
        ahead, back = tied(ahead, token), tied(back, token)
    last = [ring_shift(ahead[:half_rows], 1), ring_shift(back[half_rows:], -1)]
    keep(last, half)
    return [parts for offset in ring_offsets() for parts in blocks[offset]]


def flatten(blocks):
    pieces = [piece for parts in blocks for piece in parts]
    sources, n = [], 0
    for parts in blocks:
        sources.append(tuple(range(n, n + len(parts))))
        n += len(parts)
    return pieces, tuple(sources)


def place_kernel(sources, widths, order_ref, *refs):
    pieces, outs = refs[: -len(widths)], refs[-len(widths) :]
    step = pl.program_id(0)
    for n, parts in enumerate(sources):

        @pl.when(step == n)
        def _(parts=parts):
            low = 0
            for part in parts:
                size = pieces[part].shape[0]
                left = 0
                for out, wide in zip(outs, widths):
                    block = pieces[part][:, left : left + wide]
                    if len(out.shape) == 3:
                        groups, rows, _ = out.shape
                        rows = min(rows, size)
                        per = size // rows
                        for g in range(per):
                            at = low + g * rows
                            out[at // out.shape[1], at % out.shape[1] : at % out.shape[1] + rows, :] = block[
                                g * rows : (g + 1) * rows
                            ]
                    else:
                        out[low : low + size, :] = block
                    left += wide
                low += size


def place(blocks, order, widths, groups=1):
    pieces, sources = flatten(blocks)
    rows = sum(pieces[part].shape[0] for part in sources[0])
    length = rows * len(blocks)
    shapes = [jax.ShapeDtypeStruct((length, wide), pieces[0].dtype) for wide in widths]
    specs = [pl.BlockSpec((rows, wide), lambda i, order: (order[i], 0)) for wide in widths]
    if groups > 1:
        shapes[0] = jax.ShapeDtypeStruct((groups, length // groups, widths[0]), pieces[0].dtype)
        specs[0] = pl.BlockSpec((groups, rows // groups, widths[0]), lambda i, order: (0, order[i], 0))
    return pl.pallas_call(
        functools.partial(place_kernel, sources, tuple(widths)),
        out_shape=shapes,
        grid_spec=pltpu.PrefetchScalarGridSpec(
            num_scalar_prefetch=1,
            grid=(len(blocks),),
            in_specs=[pl.BlockSpec(piece.shape, lambda i, order: (0, 0)) for piece in pieces],
            out_specs=specs,
        ),
        compiler_params=pltpu.CompilerParams(vmem_limit_bytes=48 * 2**20),
        name="place",
    )(order, *pieces)


def ring_scatter(block, *after):
    half = lax.axis_size("expert") // 4
    offsets = ring_offsets()
    spare = {}

    def mine(offset):
        if offset not in spare:
            j = offsets.index(offset)
            spare[offset] = block(2 * j).astype(F32) + core_swap(block(2 * j + 1)).astype(F32)
        return spare[offset]

    far = (tied(mine(half), *after) if after else mine(half)).astype(BF16)
    half_rows = far.shape[0] // 2
    ahead = ring_shift(far[:half_rows], 1)
    back = ring_shift(far[half_rows:], -1)
    for step in range(half - 1, 0, -1):
        onward, homeward = mine(-step), mine(step)
        if step == half - 1:
            onward = jnp.concatenate(
                [onward[:half_rows] + ahead.astype(F32), onward[half_rows:]], axis=0
            )
            homeward = jnp.concatenate(
                [homeward[:half_rows], homeward[half_rows:] + back.astype(F32)], axis=0
            )
        else:
            onward = onward + ahead.astype(F32)
            homeward = homeward + back.astype(F32)
        ahead = ring_shift(onward.astype(BF16), 1)
        back = ring_shift(homeward.astype(BF16), -1)
    return mine(0) + ahead.astype(F32) + back.astype(F32)


def chosen(pos_ref, base, window):
    count = pos_ref.shape[-1]
    row = base + lax.broadcasted_iota(jnp.int32, (window, count), 0)
    return row == pos_ref[0]


def dispatch_kernel(sources, widths, window, base_ref, pos_ref, gate_ref, *refs):
    outs = refs[-len(widths) - 2 :]
    pieces, blocks, rows_ref, weights_ref = refs[: -len(outs)], outs[:-2], outs[-2], outs[-1]
    step = pl.program_id(0)

    @pl.when(step == 0)
    def _():
        rows_ref[...] = jnp.zeros_like(rows_ref)
        weights_ref[...] = jnp.zeros_like(weights_ref)

    for n, parts in enumerate(sources):

        @pl.when(step == n)
        def _(parts=parts):
            low = 0
            for part in parts:
                size = pieces[part].shape[0]
                left = 0
                for block, wide in zip(blocks, widths):
                    block[low : low + size, :] = pieces[part][:, left : left + wide]
                    left += wide
                low += size

    base = pl.multiple_of(base_ref[step], 16)
    pick = chosen(pos_ref, base, window)
    at = pl.ds(base, window)
    found = dot(pick.astype(F32).astype(BF16), blocks[0][...])
    rows_ref[at, :] = (rows_ref[at, :].astype(F32) + found).astype(BF16)
    weights_ref[at, :] += jnp.sum(jnp.where(pick, gate_ref[0], 0.0), axis=1, keepdims=True)


def dispatch(blocks, widths, packing, gates):
    base, pos, _, window, packed = packing
    pieces, sources = flatten(blocks)
    rows = sum(pieces[part].shape[0] for part in sources[0])
    length = rows * len(blocks)
    row_spec = pl.BlockSpec((1, 1, rows), lambda i, base: (i, 0, 0))
    return pl.pallas_call(
        functools.partial(dispatch_kernel, sources, tuple(widths), window),
        out_shape=[jax.ShapeDtypeStruct((length, wide), BF16) for wide in widths]
        + [
            jax.ShapeDtypeStruct((packed, widths[0]), BF16),
            jax.ShapeDtypeStruct((packed, 1), F32),
        ],
        grid_spec=pltpu.PrefetchScalarGridSpec(
            num_scalar_prefetch=1,
            grid=(len(blocks),),
            in_specs=[row_spec, row_spec]
            + [pl.BlockSpec(piece.shape, lambda i, base: (0, 0)) for piece in pieces],
            out_specs=[pl.BlockSpec((rows, wide), lambda i, base: (i, 0)) for wide in widths]
            + [
                pl.BlockSpec((packed, widths[0]), lambda i, base: (0, 0)),
                pl.BlockSpec((packed, 1), lambda i, base: (0, 0)),
            ],
        ),
        compiler_params=pltpu.CompilerParams(vmem_limit_bytes=52 * 2**20),
        name="dispatch",
    )(base, pos, gates, *pieces)


def expert_kernel(total_ref, x_ref, g_ref, gate_ref, up_ref, down_ref, wy_ref, dn_ref, ea_ref, dy_ref, db_ref, dg_ref):
    step = pl.program_id(0)
    rows, hidden = ea_ref.shape
    some = step * rows < total_ref[0]

    @pl.when(some)
    def _():
        pre = dot(x_ref[...], up_ref[...])
        gate_part, up_part = pre[:, :hidden], pre[:, hidden:]
        sigmoid_gate = 1.0 / (1.0 + jnp.exp(-gate_part))
        silu = gate_part * sigmoid_gate
        act = (silu * up_part).astype(BF16)
        ea_ref[...] = act
        result = dot(act, down_ref[...]).astype(BF16).astype(F32)
        grad = g_ref[...].astype(F32)
        gate = gate_ref[...]
        dg_ref[...] = jnp.sum(grad * result, axis=1, keepdims=True)
        wy_ref[...] = (gate * result).astype(BF16)
        out_grad = (gate * grad).astype(BF16)
        dy_ref[...] = out_grad
        act_grad = dot_nt(out_grad, down_ref[...])
        db_ref[:, :hidden] = (
            act_grad * up_part * sigmoid_gate * (1.0 + gate_part * (1.0 - sigmoid_gate))
        ).astype(BF16)
        db_ref[:, hidden:] = (act_grad * silu).astype(BF16)
        dn_ref[...] = dot_nt(db_ref[...], up_ref[...]).astype(BF16)

    @pl.when(jnp.logical_not(some))
    def _():
        for ref in (wy_ref, dn_ref, ea_ref, dy_ref, db_ref, dg_ref):
            ref[...] = jnp.zeros_like(ref)


def expert(total, rows, grads, gates, up, down):
    packed, width = rows.shape
    hidden = down.shape[0]
    tile = 256
    spec = lambda wide: pl.BlockSpec((tile, wide), lambda i, total: (i, 0))
    whole = lambda ref: pl.BlockSpec(
        ref.shape, lambda i, total: (0, 0), pipeline_mode=pl.Buffered(1)
    )
    widths = (width, width, hidden, width, 2 * hidden)
    return pl.pallas_call(
        expert_kernel,
        out_shape=[jax.ShapeDtypeStruct((packed, wide), BF16) for wide in widths]
        + [jax.ShapeDtypeStruct((packed, 1), F32)],
        grid_spec=pltpu.PrefetchScalarGridSpec(
            num_scalar_prefetch=1,
            grid=(packed // tile,),
            in_specs=[spec(width), spec(width), spec(1), whole(up), whole(down)],
            out_specs=[spec(wide) for wide in widths] + [spec(1)],
        ),
        compiler_params=pltpu.CompilerParams(vmem_limit_bytes=58 * 2**20),
        name="expert",
    )(total, rows, grads, gates, up, down)


def combine_kernel(turned, window, base_ref, order_ref, pos_ref, rows_ref, dg_ref, act_ref, weight_ref, out_ref, back_ref):
    mul = dot_nt if turned else dot
    base = pl.multiple_of(base_ref[pl.program_id(0)], 16)
    pick = chosen(pos_ref, base, window)
    at = pl.ds(base, window)
    out_ref[...] = (
        dot_tn(pick.astype(F32).astype(BF16), rows_ref[at, :]) + mul(act_ref[...], weight_ref[...])
    ).astype(BF16)
    back_ref[0] = jnp.sum(jnp.where(pick, dg_ref[at, :], 0.0), axis=0, keepdims=True)


def combine(packing, order, rows, dg, act, weight, turned):
    base, pos, _, window, packed = packing
    blocks, _, count = pos.shape
    width = rows.shape[-1]
    whole = lambda ref: pl.BlockSpec(ref.shape, lambda i, base, order: (0, 0))
    return pl.pallas_call(
        functools.partial(combine_kernel, turned, window),
        out_shape=[
            jax.ShapeDtypeStruct((blocks * count, width), BF16),
            jax.ShapeDtypeStruct((blocks, 1, count), F32),
        ],
        grid_spec=pltpu.PrefetchScalarGridSpec(
            num_scalar_prefetch=2,
            grid=(blocks,),
            in_specs=[
                pl.BlockSpec((1, 1, count), lambda i, base, order: (i, 0, 0)),
                whole(rows),
                whole(dg),
                pl.BlockSpec((count, act.shape[1]), lambda i, base, order: (i, 0)),
                whole(weight),
            ],
            out_specs=[
                pl.BlockSpec((count, width), lambda i, base, order: (order[i], 0)),
                pl.BlockSpec((1, 1, count), lambda i, base, order: (order[i], 0, 0)),
            ],
        ),
        compiler_params=pltpu.CompilerParams(vmem_limit_bytes=40 * 2**20),
        name="combine",
    )(base, order, pos, rows, dg, act, weight)


def swap(value):
    return lax.all_to_all(value, "expert", split_axis=0, concat_axis=0, tiled=True)


def per_device(
    tokens,
    cotangent,
    segment_ids,
    routes,
    attn_in,
    attn_out,
    gain_attn,
    shared_in,
    shared_out,
    router,
    gain_ffn,
    expert_in,
    expert_out,
):
    n_dp, n_e = lax.axis_size("dp"), lax.axis_size("expert")
    me = lax.axis_index("expert")
    count, width = tokens.shape
    segments = segment_ids[0]
    length = segments.shape[0]
    rows = attn_in.shape[0]
    capacity = min(count, 3 * TOP * count // (2 * n_e))
    shared_rows = shared_out.shape[0]
    shared_width = shared_rows * n_dp
    expert_width = expert_out.shape[1] * n_dp

    order = ring_blocks()
    steady = jnp.arange(n_e, dtype=jnp.int32)
    hidden_in = tokens.astype(F32)
    inverse_one = lax.rsqrt(jnp.mean(hidden_in * hidden_in, axis=-1, keepdims=True) + EPS)
    normed_one = hidden_in * inverse_one
    gain_rows = gain_attn.astype(F32)[:, None]
    head_w = []

    def head_sent(blocks):
        own = (attn_in.astype(F32) * tied(gain_rows, blocks[0][1][0])).astype(BF16)
        own = own.reshape(rows, 3, n_e, HEAD_DIM).transpose(2, 0, 1, 3)
        head_w.append(swap(own.reshape(n_e, rows, 3 * HEAD_DIM)))
        return head_w[0]

    def head_whole(blocks):
        head_w.append(dp_gather(head_w[0]).reshape(width, 3 * HEAD_DIM))
        return head_w[1]

    small = jnp.concatenate([router, gain_ffn[:, None]], axis=1)
    small = dp_gather(small).reshape(-1, router.shape[1] + 1)
    small_rows = small.shape[0]
    extra = jnp.zeros((count, 128), BF16)
    extra = extra.at[:small_rows, : small.shape[1]].set(small)
    extra = extra.at[:, 64 : 64 + TOP].set(routes.astype(BF16))
    proj_all = jnp.concatenate([dp_gather(attn_out).reshape(n_dp * rows, width), extra], axis=1)
    cos_table, sin_table, first_place = rope_tables(segments)

    half = n_e // 4
    norm_blocks = ring_gather(
        normed_one.astype(BF16),
        {
            half - 2: lambda blocks: proj_all + cos_table[:1, :1].astype(BF16),
            half - 1: head_sent,
            half: head_whole,
        },
    )
    head_w = head_w[1]

    mixed, query, key, value, lse, norm_all = attend(
        norm_blocks, order, head_w, cos_table, sin_table, first_place
    )
    mixed = swap(mixed.reshape(n_e, count, HEAD_DIM))
    mixed = mixed.transpose(1, 0, 2).reshape(count, width)
    proj_all = ring_gather(
        tied(proj_all, norm_blocks[-1][0], norm_blocks[-1][-1]),
        {half - 2: lambda blocks: lse, half - 1: lambda blocks: mixed},
    )
    cot_blocks = ring_gather(tied(cotangent, proj_all[-1][0], proj_all[-1][-1]))
    proj_all, extra_all = place(proj_all, order, [width, 128], n_dp)
    proj_all = proj_all.reshape(width, width)
    small = extra_all.reshape(n_e, count, 128)[:, :small_rows, : router.shape[1] + 1]
    small = small.reshape(n_e, n_dp, rows, -1).transpose(1, 0, 2, 3).reshape(width, -1)
    router_full = small[:, : router.shape[1]]
    gain_second = small[:, router.shape[1]].astype(F32)
    routes_all = extra_all[:, 64 : 64 + TOP].astype(F32)

    expert_up = lax.all_gather(expert_in, "dp", axis=1, tiled=True)[0]
    expert_down = lax.all_gather(expert_out, "dp", axis=1, tiled=True)[0]
    share_w = shared_in.reshape(rows, 2, n_dp, n_e, shared_rows).transpose(3, 0, 1, 2, 4)
    share_w = share_w.reshape(n_e, rows, 2 * shared_width)
    share_w = swap(tied(share_w, norm_blocks[-1][0], norm_blocks[-1][-1]))
    share_w = dp_gather(share_w).reshape(width, 2 * shared_width)
    share_out = dp_gather(shared_out).reshape(shared_width, width)
    resid = hidden_in + dot(mixed, proj_all)

    inverse_two = lax.rsqrt(jnp.mean(resid * resid, axis=-1, keepdims=True) + EPS)
    normed_two = resid * inverse_two
    norm_two = (normed_two * gain_second).astype(BF16)
    logits = dot(norm_two, router_full)
    picked = jnp.any(routes[:, :, None] == jnp.arange(n_e)[None, None, :], axis=1)
    chosen = jnp.where(picked, logits, NEG)
    chosen = jnp.where(picked, jnp.exp(chosen - jnp.max(chosen, axis=-1, keepdims=True)), 0.0)
    gates = chosen / jnp.sum(chosen, axis=-1, keepdims=True)
    gate_high = gates.astype(BF16)
    gate_low = (gates - gate_high.astype(F32)).astype(BF16)
    blank = jnp.zeros((count, 128 - 2 * n_e), BF16)
    payload = jnp.concatenate([norm_two, gate_high, gate_low, blank], axis=1)
    norm_blocks = ring_gather(
        tied(payload, cot_blocks[-1][0], cot_blocks[-1][-1]), {half - 1: lambda blocks: expert_up}
    )

    named = jnp.any(routes_all == me.astype(F32), axis=1).reshape(n_e, count)
    named = jnp.take(named, order, axis=0)
    ranking = jnp.cumsum(named.astype(jnp.int32), axis=1)
    ends = jnp.cumsum(ranking[:, -1])
    begins = ends - ranking[:, -1]
    pos = jnp.where(named, begins[:, None] + ranking - 1, -1)[:, None, :]
    window = -(-(capacity + 15) // 16) * 16
    packed = -(-(n_e * capacity + 32) // 256) * 256
    packing = (begins // 16 * 16, pos, ends[-1:], window, packed)
    norm_two_all, payload, arrived, _ = dispatch(
        norm_blocks, [width, 128], packing, jnp.zeros((n_e, 1, count), F32)
    )
    mine = jnp.arange(n_e) == me
    gate_all = payload[:, : 2 * n_e].astype(F32).reshape(length, 2, n_e)
    gate_all = jnp.sum(jnp.where(mine, gate_all, 0.0), axis=(1, 2)).reshape(n_e, 1, count)
    cot_all, cot_rows, gate_rows = dispatch(cot_blocks, [width], packing, gate_all)
    weighted, row_grad, expert_act, route_grad, pre_grad, gate_grad = expert(
        packing[2], arrived, cot_rows, gate_rows, expert_up, expert_down
    )

    shared_pre = dot(norm_two_all, share_w)
    shared_act = (
        jax.nn.silu(shared_pre[:, :shared_width]) * shared_pre[:, shared_width:]
    ).astype(BF16)
    shared_act_grad = dot_nt(cot_all, share_out)
    shared_pre_grad = silu_back(
        shared_act_grad, shared_pre[:, :shared_width], shared_pre[:, shared_width:]
    ).astype(BF16)
    norm_two_part, gate_grad = combine(
        packing, steady, row_grad, gate_grad, shared_pre_grad, share_w, True
    )
    norm_two_grad = ring_scatter(lambda n: norm_two_part[n * count : (n + 1) * count])
    gate_grad = jnp.sum(
        jnp.where(order[:, None, None] == steady[None, :, None], gate_grad, 0.0), axis=0
    )
    gate_grad = swap(gate_grad)
    out_part, _ = combine(
        packing, order, weighted, gate_rows, shared_act, share_out, False
    )
    routed_out = lax.psum_scatter(out_part, "expert", scatter_dimension=0, tiled=True)

    def shard_grad(left, right):
        size = left.shape[1] // n_dp
        here = lax.axis_index("dp")
        cut = lambda i: lax.dynamic_slice_in_dim(left, i * size, size, 1)
        got = [
            lax.ppermute(
                dot_tn(cut((here + step) % n_dp), right).astype(BF16),
                "dp",
                [(i, (i + step) % n_dp) for i in range(n_dp)],
            )
            for step in range(1, n_dp)
        ]
        return (dot_tn(cut(here), right) + sum(part.astype(F32) for part in got))[None]

    expert_out_grad = shard_grad(expert_act, route_grad)
    expert_in_grad = shard_grad(arrived, pre_grad)
    share_out_grad = dp_scatter(dot_tn(shared_act, cot_all).reshape(n_dp, shared_rows, width))
    share_in_grad = dot_tn(norm_two_all, shared_pre_grad)
    share_in_grad = dp_scatter(share_in_grad.reshape(n_dp, n_e, rows, 2 * shared_width))
    share_in_grad = swap(share_in_grad.astype(BF16)).astype(F32)
    share_in_grad = (
        share_in_grad.reshape(n_e, rows, 2, n_dp, shared_rows)
        .transpose(1, 2, 3, 0, 4)
        .reshape(rows, -1)
    )

    gate_grad = gate_grad.T
    logit_grad = gates * (gate_grad - jnp.sum(gates * gate_grad, axis=-1, keepdims=True))
    router_grad = jnp.dot(
        logit_grad.T, norm_two.astype(F32), precision=HIGHEST, preferred_element_type=F32
    )
    norm_two_grad = norm_two_grad + jnp.dot(
        logit_grad, router_full.astype(F32).T, precision=HIGHEST, preferred_element_type=F32
    )
    gain_two_grad = jnp.sum(norm_two_grad * normed_two, axis=0)
    upstream = cotangent.astype(F32)
    scaled_two = norm_two_grad * gain_second
    resid_grad = upstream + inverse_two * (
        scaled_two - normed_two * jnp.mean(scaled_two * normed_two, axis=-1, keepdims=True)
    )
    small_grad = jnp.concatenate([router_grad, gain_two_grad[None]], axis=0)

    branch_cot = resid_grad.astype(BF16)
    mixed_grad = dot_nt(branch_cot, proj_all).astype(BF16)
    mixed_grad = swap(mixed_grad.reshape(count, n_e, HEAD_DIM).transpose(1, 0, 2))
    mixed_grad = mixed_grad.reshape(length, HEAD_DIM)
    mixed = mixed.reshape(count, n_dp, n_e, rows).transpose(0, 2, 1, 3).reshape(count, width)
    proj_grad = lax.psum_scatter(
        dot_tn(mixed, branch_cot).astype(BF16), "expert", scatter_dimension=0, tiled=True
    )
    attn_out_grad = dp_scatter(proj_grad.astype(F32).reshape(n_dp, rows, width))
    qkv_grad = attend_back(
        query, key, value, mixed_grad, lse, first_place, cos_table, sin_table, order
    )
    small_grad = tied(small_grad, qkv_grad).reshape(n_e + 1, n_dp * n_e, rows).transpose(1, 0, 2)
    small_grad = lax.all_to_all(
        small_grad, ("dp", "expert"), split_axis=0, concat_axis=0, tiled=True
    )
    small_grad = jnp.sum(small_grad, axis=0)
    norm_one_part = dot_nt(qkv_grad, head_w).astype(BF16)
    scaled_one = ring_scatter(lambda n: norm_one_part[n * count : (n + 1) * count])
    input_grad = resid_grad + inverse_one * (
        scaled_one - normed_one * jnp.mean(scaled_one * normed_one, axis=-1, keepdims=True)
    )
    head_grad = dot_tn(norm_all, qkv_grad).reshape(n_dp, n_e, rows, 3 * HEAD_DIM)
    head_grad = swap(dp_scatter(head_grad).astype(BF16)).astype(F32)
    head_grad = (
        head_grad.reshape(n_e, rows, 3, HEAD_DIM).transpose(1, 2, 0, 3).reshape(rows, 3 * width)
    )
    gain_attn_grad = jnp.sum(head_grad * attn_in.astype(F32), axis=1)
    attn_in_grad = head_grad * gain_rows
    return (
        (resid + routed_out.astype(F32)).astype(BF16),
        input_grad.astype(BF16),
        attn_in_grad,
        attn_out_grad,
        gain_attn_grad,
        share_in_grad,
        share_out_grad,
        small_grad[:n_e].T,
        small_grad[n_e],
        expert_in_grad,
        expert_out_grad,
    )


def solution(mesh):
    return jax.shard_map(
        per_device,
        mesh=mesh,
        in_specs=(
            P(("dp", "expert"), None),
            P(("dp", "expert"), None),
            P("dp", None),
            P(("dp", "expert"), None),
            P(("dp", "expert"), None),
            P(("dp", "expert"), None),
            P(("dp", "expert")),
            P(("dp", "expert"), None),
            P(("dp", "expert"), None),
            P(("dp", "expert"), None),
            P(("dp", "expert")),
            P("expert", "dp", None),
            P("expert", "dp", None),
        ),
        out_specs=(
            P(("dp", "expert"), None),
            P(("dp", "expert"), None),
            P(("dp", "expert"), None),
            P(("dp", "expert"), None),
            P(("dp", "expert")),
            P(("dp", "expert"), None),
            P(("dp", "expert"), None),
            P(("dp", "expert"), None),
            P(("dp", "expert")),
            P("expert", "dp", None),
            P("expert", "dp", None),
        ),
        check_vma=False,
    )
```

```python
import functools
import math

import jax
import jax.numpy as jnp
from jax import lax
from jax.experimental import pallas as pl
from jax.experimental.pallas import tpu as pltpu
from jax.sharding import PartitionSpec as P

HEADS = 16
HEAD_DIM = 128
TOP = 6


EPS = 1e-06
THETA = 10000.0
NEG = -1e30
HIGHEST = lax.Precision.HIGHEST
BF16 = jnp.bfloat16
F32 = jnp.float32
LOG2E = math.log2(math.e)


def rope_tables(segments):
    length = segments.shape[0]
    places = jnp.arange(length, dtype=jnp.int32)
    starts = jnp.concatenate([jnp.ones((1,), dtype=jnp.bool_), segments[1:] != segments[:-1]])
    first_place = lax.cummax(jnp.where(starts, places, 0), axis=0)
    offset = (places - first_place).astype(jnp.float32)
    half_dim = HEAD_DIM // 2
    freqs = jnp.exp(jnp.arange(half_dim, dtype=jnp.float32) * (-2.0 * math.log(THETA) / HEAD_DIM))
    angles = offset[:, None] * freqs[None, :]
    cos_table, sin_table = jnp.cos(angles), jnp.sin(angles)
    return (
        jnp.concatenate([cos_table, cos_table], axis=1),
        jnp.concatenate([-sin_table, sin_table], axis=1),
        first_place[None, :],
    )


def silu_back(grad_act, gate_part, up_part):
    sigmoid_gate = jax.nn.sigmoid(gate_part)
    gate_grad = grad_act * up_part * sigmoid_gate * (1.0 + gate_part * (1.0 - sigmoid_gate))
    up_grad = grad_act * gate_part * sigmoid_gate
    return jnp.concatenate([gate_grad, up_grad], axis=-1)


def dot(left, right):
    return jnp.dot(left, right, preferred_element_type=F32)


def dot_tn(left, right):
    return lax.dot_general(left, right, (((0,), (0,)), ((), ())), preferred_element_type=F32)


def dot_nt(left, right):
    return lax.dot_general(left, right, (((1,), (1,)), ((), ())), preferred_element_type=F32)


def turn(values, cos_table, sin_table):
    return values * cos_table + pltpu.roll(values, HEAD_DIM // 2, 1) * sin_table


def attend_kernel(sources, block, order_ref, *refs):
    pieces = refs[: sources[-1][-1] + 1]
    weight_ref, cos_ref, sin_ref, start_ref = refs[len(pieces) : len(pieces) + 4]
    o_ref, q_ref, k_ref, v_ref, lse_ref, rows_ref, vt_ref = refs[len(pieces) + 4 :]
    step = pl.program_id(0)
    length = q_ref.shape[0]
    factor = HEAD_DIM ** (-0.5) * LOG2E
    rows = rows_ref.shape[0]

    for n, parts in enumerate(sources):

        @pl.when(step == n)
        def _(parts=parts):
            low = 0
            for part in parts:
                size = pieces[part].shape[0]
                rows_ref[low : low + size, :] = pieces[part][...]
                low += size

    @pl.when(step < len(sources))
    def _():
        qkv = dot(rows_ref[...], weight_ref[...])
        at = pl.ds(pl.multiple_of(order_ref[step] * rows, rows), rows)
        cos_table, sin_table = cos_ref[at, :], sin_ref[at, :]
        q_ref[at, :] = turn(qkv[:, :HEAD_DIM], cos_table, sin_table).astype(BF16)
        k_ref[at, :] = turn(qkv[:, HEAD_DIM : 2 * HEAD_DIM], cos_table, sin_table).astype(BF16)
        value = qkv[:, 2 * HEAD_DIM :]
        v_ref[at, :] = value.astype(BF16)
        vt_ref[:, at] = value.T.astype(BF16)

    for i in range(length // block):

        @pl.when(step == len(sources) + i)
        def _(i=i):
            low, high = i * block, (i + 1) * block
            raw = dot_nt(k_ref[:high, :], q_ref[low:high, :])
            keys = lax.broadcasted_iota(jnp.int32, raw.shape, 0)
            queries = low + lax.broadcasted_iota(jnp.int32, raw.shape, 1)
            allowed = (keys <= queries) & (keys >= start_ref[:, low:high])
            raw = jnp.where(allowed, raw, NEG)
            top = jnp.max(raw, axis=0, keepdims=True)
            shifted = jnp.exp2((raw - top) * factor)
            total = jnp.sum(shifted, axis=0, keepdims=True)
            probs = (shifted * (1.0 / total)).astype(BF16)
            mixed = dot(vt_ref[:, :high], probs)
            o_ref[low:high, :] = mixed.T.astype(BF16)
            lse_ref[:, low:high] = top * factor + jnp.log2(total)


def attend(blocks, order, weight, cos_table, sin_table, first_place):
    pieces, sources = flatten(blocks)
    length = cos_table.shape[0]
    rows = length // len(sources)
    width = weight.shape[0]
    block = min(256, length)
    last = len(sources) - 1
    whole = lambda shape: pl.BlockSpec(shape, lambda i, order: (0, 0))
    head = jax.ShapeDtypeStruct((length, HEAD_DIM), BF16)
    return pl.pallas_call(
        functools.partial(attend_kernel, sources, block),
        out_shape=[head] * 4
        + [jax.ShapeDtypeStruct((1, length), F32), jax.ShapeDtypeStruct((length, width), BF16)],
        grid_spec=pltpu.PrefetchScalarGridSpec(
            num_scalar_prefetch=1,
            grid=(len(sources) + length // block,),
            in_specs=[whole(piece.shape) for piece in pieces]
            + [
                whole(weight.shape),
                whole((length, HEAD_DIM)),
                whole((length, HEAD_DIM)),
                whole((1, length)),
            ],
            out_specs=[whole((length, HEAD_DIM))] * 4
            + [
                whole((1, length)),
                pl.BlockSpec((rows, width), lambda i, order: (jnp.minimum(i, last), 0)),
            ],
            scratch_shapes=[pltpu.VMEM((HEAD_DIM, length), BF16)],
        ),
        compiler_params=pltpu.CompilerParams(vmem_limit_bytes=52 * 2**20),
        name="attend",
    )(order, *pieces, weight, cos_table, sin_table, first_place)


def attend_back_kernel(
    block, rows, order_ref, q_ref, k_ref, v_ref, do_ref, lse_ref, start_ref, cos_ref, sin_ref, out_ref, kt_ref, dq_ref, dk_ref, dv_ref
):
    length = q_ref.shape[0]
    step = pl.program_id(0)
    scale = HEAD_DIM ** (-0.5)
    factor = scale * LOG2E
    count = length // block

    @pl.when(step == 0)
    def _():
        kt_ref[...] = k_ref[...].astype(F32).T.astype(BF16)
        dk_ref[...] = jnp.zeros_like(dk_ref)
        dv_ref[...] = jnp.zeros_like(dv_ref)

    for i in range(count):

        @pl.when(step == i)
        def _(i=i):
            low, high = i * block, (i + 1) * block
            query, grad = q_ref[low:high, :], do_ref[low:high, :]
            raw = dot_nt(k_ref[:high, :], query)
            keys = lax.broadcasted_iota(jnp.int32, raw.shape, 0)
            queries = low + lax.broadcasted_iota(jnp.int32, raw.shape, 1)
            allowed = (keys <= queries) & (keys >= start_ref[:, low:high])
            raw = jnp.where(allowed, raw * factor - lse_ref[:, low:high], NEG)
            probs = jnp.exp2(raw)
            probs_grad = dot_nt(v_ref[:high, :], grad)
            inner = jnp.sum(probs_grad * probs, axis=0, keepdims=True)
            score_grad = (probs * (probs_grad - inner)).astype(BF16)
            dv_ref[:high, :] += dot(probs.astype(BF16), grad)
            dk_ref[:high, :] += dot(score_grad, query)
            dq_ref[low:high, :] = dot(kt_ref[:, :high], score_grad).T

    @pl.when(step == count - 1)
    def _():
        for n in range(length // rows):
            at = pl.ds(pl.multiple_of(order_ref[n] * rows, rows), rows)
            to = slice(n * rows, (n + 1) * rows)
            cos_table, sin_table = cos_ref[at, :], -sin_ref[at, :]
            out_ref[to, :HEAD_DIM] = turn(dq_ref[at, :] * scale, cos_table, sin_table).astype(BF16)
            out_ref[to, HEAD_DIM : 2 * HEAD_DIM] = turn(
                dk_ref[at, :] * scale, cos_table, sin_table
            ).astype(BF16)
            out_ref[to, 2 * HEAD_DIM :] = dv_ref[at, :].astype(BF16)


def attend_back(query, key, value, grad, lse, first_place, cos_table, sin_table, order):
    length = query.shape[0]
    block = min(256, length)
    whole = lambda shape: pl.BlockSpec(shape, lambda i, order: (0, 0))
    head = whole((length, HEAD_DIM))
    return pl.pallas_call(
        functools.partial(attend_back_kernel, block, length // order.shape[0]),
        out_shape=jax.ShapeDtypeStruct((length, 3 * HEAD_DIM), BF16),
        grid_spec=pltpu.PrefetchScalarGridSpec(
            num_scalar_prefetch=1,
            grid=(length // block,),
            in_specs=[head] * 4 + [whole((1, length))] * 2 + [head] * 2,
            out_specs=whole((length, 3 * HEAD_DIM)),
            scratch_shapes=[pltpu.VMEM((HEAD_DIM, length), BF16)]
            + [pltpu.VMEM((length, HEAD_DIM), F32)] * 3,
        ),
        compiler_params=pltpu.CompilerParams(vmem_limit_bytes=48 * 2**20),
        name="attend_back",
    )(order, query, key, value, grad, lse, first_place, cos_table, sin_table)


def dp_gather(value):
    count = lax.axis_size("dp")
    if count == 1:
        return value[None]
    here = lax.axis_index("dp")
    parts = [value] + [
        lax.ppermute(value, "dp", [(i, (i - step) % count) for i in range(count)])
        for step in range(1, count)
    ]
    if count == 2:
        first = here == 0
        return jnp.stack(
            [jnp.where(first, parts[0], parts[1]), jnp.where(first, parts[1], parts[0])]
        )
    whole = jnp.zeros((count,) + value.shape, value.dtype)
    for step, part in enumerate(parts):
        whole = lax.dynamic_update_index_in_dim(whole, part, (here + step) % count, 0)
    return whole


def dp_scatter(value):
    count = lax.axis_size("dp")
    here = lax.axis_index("dp")
    total = lax.dynamic_index_in_dim(value, here, 0, keepdims=False)
    for step in range(1, count):
        block = lax.dynamic_index_in_dim(value, (here + step) % count, 0, keepdims=False)
        got = lax.ppermute(
            block.astype(BF16), "dp", [(i, (i + step) % count) for i in range(count)]
        )
        total = total + got.astype(F32)
    return total


def ring_order():
    pairs = lax.axis_size("expert") // 2
    return list(range(0, pairs, 2)) + list(range(pairs - 1, 0, -2))


def ring_shift(value, step):
    order = ring_order()
    pairs = len(order)
    perm = [
        (order[q] * 2 + c, order[(q + step) % pairs] * 2 + c) for q in range(pairs) for c in range(2)
    ]
    return lax.ppermute(value, "expert", perm)


def core_swap(value):
    count = lax.axis_size("expert")
    return lax.ppermute(value, "expert", [(i, i ^ 1) for i in range(count)])


def ring_offsets():
    half = lax.axis_size("expert") // 4
    return [0] + [o for step in range(1, half) for o in (step, -step)] + [half]


def ring_blocks():
    order = ring_order()
    pairs = len(order)
    table = [[0] * (2 * pairs) for _ in range(2 * pairs)]
    for q in range(pairs):
        for c in range(2):
            for j, offset in enumerate(ring_offsets()):
                for other in range(2):
                    table[order[q] * 2 + c][2 * j + other] = (
                        order[(q - offset) % pairs] * 2 + (c ^ other)
                    )
    return lax.dynamic_index_in_dim(
        jnp.asarray(table, jnp.int32), lax.axis_index("expert"), 0, keepdims=False
    )


def tied(value, *tokens):
    firsts = [lax.slice(t, (0,) * t.ndim, (1,) * t.ndim).reshape(()) for t in tokens]
    token = sum(t.astype(F32) for t in firsts) * 0.0
    return (value.astype(F32) * (1.0 + token)).astype(value.dtype)


def ring_gather(value, gates=None):
    gates = gates or {}
    half_rows = value.shape[0] // 2
    half = lax.axis_size("expert") // 4
    blocks = {}

    def keep(parts, offset):
        blocks[offset] = (parts, [core_swap(part) for part in parts])

    keep([value], 0)
    ahead = back = value
    for step in range(1, half):
        if step in gates:
            token = gates[step](blocks)
            ahead, back = tied(ahead, *token), tied(back, *token)
        ahead, back = ring_shift(ahead, 1), ring_shift(back, -1)
        keep([ahead], step)
        keep([back], -step)
    if half in gates:
        token = gates[half](blocks)
        ahead, back = tied(ahead, *token), tied(back, *token)
    last = [ring_shift(ahead[:half_rows], 1), ring_shift(back[half_rows:], -1)]
    keep(last, half)
    return [parts for offset in ring_offsets() for parts in blocks[offset]]


def flatten(blocks):
    pieces = [piece for parts in blocks for piece in parts]
    sources, n = [], 0
    for parts in blocks:
        sources.append(tuple(range(n, n + len(parts))))
        n += len(parts)
    return pieces, tuple(sources)


def ring_scatter(block, gates=None):
    gates = gates or {}
    half = lax.axis_size("expert") // 4
    offsets = ring_offsets()
    spare = {}

    def mine(offset):
        if offset not in spare:
            j = offsets.index(offset)
            spare[offset] = block(2 * j).astype(F32) + core_swap(block(2 * j + 1)).astype(F32)
        return spare[offset]

    far = mine(half).astype(BF16)
    half_rows = far.shape[0] // 2
    ahead = ring_shift(far[:half_rows], 1)
    back = ring_shift(far[half_rows:], -1)
    for step in range(half - 1, 0, -1):
        onward, homeward = mine(-step), mine(step)
        if step == half - 1:
            onward = jnp.concatenate(
                [onward[:half_rows] + ahead.astype(F32), onward[half_rows:]], axis=0
            )
            homeward = jnp.concatenate(
                [homeward[:half_rows], homeward[half_rows:] + back.astype(F32)], axis=0
            )
        else:
            onward = onward + ahead.astype(F32)
            homeward = homeward + back.astype(F32)
        if half - step in gates:
            onward, homeward = tied(onward, *gates[half - step]), tied(homeward, *gates[half - step])
        ahead = ring_shift(onward.astype(BF16), 1)
        back = ring_shift(homeward.astype(BF16), -1)
    return mine(0) + ahead.astype(F32) + back.astype(F32)


def chosen(pos_ref, base, window):
    count = pos_ref.shape[-1]
    row = base + lax.broadcasted_iota(jnp.int32, (window, count), 0)
    return row == pos_ref[0]


def dispatch_kernel(sources, widths, window, base_ref, order_ref, pos_ref, gate_ref, *refs):
    outs = refs[-len(widths) - 2 :]
    pieces, blocks, rows_ref, weights_ref = refs[: -len(outs)], outs[:-2], outs[-2], outs[-1]
    step = pl.program_id(0)

    @pl.when(step == 0)
    def _():
        rows_ref[...] = jnp.zeros_like(rows_ref)
        weights_ref[...] = jnp.zeros_like(weights_ref)

    if sources is None:
        blocks[0][...] = pieces[0][...]
    else:
        for n, parts in enumerate(sources):

            @pl.when(step == n)
            def _(parts=parts):
                low = 0
                for part in parts:
                    size = pieces[part].shape[0]
                    left = 0
                    for block, wide in zip(blocks, widths):
                        block[low : low + size, :] = pieces[part][:, left : left + wide]
                        left += wide
                    low += size

    base = pl.multiple_of(base_ref[step], 16)
    pick = chosen(pos_ref, base, window)
    at = pl.ds(base, window)
    found = dot(pick.astype(F32).astype(BF16), blocks[0][...])
    rows_ref[at, :] = (rows_ref[at, :].astype(F32) + found).astype(BF16)
    weights_ref[at, :] += jnp.sum(jnp.where(pick, gate_ref[0], 0.0), axis=1, keepdims=True)


def dispatch(blocks, widths, packing, order, gates):
    base, pos, _, window, packed = packing
    count = pos.shape[0]
    if isinstance(blocks, list):
        pieces, sources = flatten(blocks)
        rows = sum(pieces[part].shape[0] for part in sources[0])
        piece_specs = [pl.BlockSpec(piece.shape, lambda i, base, order: (0, 0)) for piece in pieces]
    else:
        pieces, sources = [blocks], None
        rows = blocks.shape[0] // count
        piece_specs = [pl.BlockSpec((rows, widths[0]), lambda i, base, order: (order[i], 0))]
    row_spec = pl.BlockSpec((1, 1, rows), lambda i, base, order: (i, 0, 0))
    return pl.pallas_call(
        functools.partial(dispatch_kernel, sources, tuple(widths), window),
        out_shape=[jax.ShapeDtypeStruct((rows * count, wide), BF16) for wide in widths]
        + [
            jax.ShapeDtypeStruct((packed, widths[0]), BF16),
            jax.ShapeDtypeStruct((packed, 1), F32),
        ],
        grid_spec=pltpu.PrefetchScalarGridSpec(
            num_scalar_prefetch=2,
            grid=(count,),
            in_specs=[row_spec, row_spec] + piece_specs,
            out_specs=[pl.BlockSpec((rows, wide), lambda i, base, order: (i, 0)) for wide in widths]
            + [
                pl.BlockSpec((packed, widths[0]), lambda i, base, order: (0, 0)),
                pl.BlockSpec((packed, 1), lambda i, base, order: (0, 0)),
            ],
        ),
        compiler_params=pltpu.CompilerParams(vmem_limit_bytes=52 * 2**20),
        name="dispatch",
    )(base, order, pos, gates, *pieces)


def expert_kernel(ups, total_ref, starts_ref, x_ref, g_ref, gate_ref, *refs):
    parts, refs = refs[:-9], refs[-9:]
    wy_ref, dn_ref, ea_ref, dy_ref, db_ref, dg_ref, up_ref, down_ref, sems = refs
    step = pl.program_id(0)
    rows, hidden = ea_ref.shape
    some = step * rows < total_ref[0]

    @pl.when(step == 0)
    def _():
        copies = []
        for n, part in enumerate(parts):
            at = pl.ds(pl.multiple_of(starts_ref[n], 16), part.shape[0])
            whole = up_ref if n < ups else down_ref
            copies.append(pltpu.make_async_copy(part, whole.at[at, :], sems.at[n]))
        for copy in copies:
            copy.start()
        for copy in copies:
            copy.wait()

    @pl.when(some)
    def _():
        pre = dot(x_ref[...], up_ref[...])
        gate_part, up_part = pre[:, :hidden], pre[:, hidden:]
        sigmoid_gate = 1.0 / (1.0 + jnp.exp(-gate_part))
        silu = gate_part * sigmoid_gate
        act = (silu * up_part).astype(BF16)
        ea_ref[...] = act
        result = dot(act, down_ref[...]).astype(BF16).astype(F32)
        grad = g_ref[...].astype(F32)
        gate = gate_ref[...]
        dg_ref[...] = jnp.sum(grad * result, axis=1, keepdims=True)
        wy_ref[...] = (gate * result).astype(BF16)
        out_grad = (gate * grad).astype(BF16)
        dy_ref[...] = out_grad
        act_grad = dot_nt(out_grad, down_ref[...])
        db_ref[:, :hidden] = (
            act_grad * up_part * sigmoid_gate * (1.0 + gate_part * (1.0 - sigmoid_gate))
        ).astype(BF16)
        db_ref[:, hidden:] = (act_grad * silu).astype(BF16)
        dn_ref[...] = dot_nt(db_ref[...], up_ref[...]).astype(BF16)

    @pl.when(jnp.logical_not(some))
    def _():
        for ref in (wy_ref, dn_ref, ea_ref, dy_ref, db_ref, dg_ref):
            ref[...] = jnp.zeros_like(ref)


def expert(total, rows, grads, gates, ups, downs):
    packed, width = rows.shape
    hidden = sum(part.shape[0] for part, _ in downs)
    tile = 256
    parts = [part for part, _ in ups + downs]
    starts = jnp.stack([start for _, start in ups + downs]).astype(jnp.int32)
    spec = lambda wide: pl.BlockSpec((tile, wide), lambda i, total, starts: (i, 0))
    widths = (width, width, hidden, width, 2 * hidden)
    return pl.pallas_call(
        functools.partial(expert_kernel, len(ups)),
        out_shape=[jax.ShapeDtypeStruct((packed, wide), BF16) for wide in widths]
        + [jax.ShapeDtypeStruct((packed, 1), F32)],
        grid_spec=pltpu.PrefetchScalarGridSpec(
            num_scalar_prefetch=2,
            grid=(packed // tile,),
            in_specs=[spec(width), spec(width), spec(1)]
            + [pl.BlockSpec(memory_space=pl.ANY)] * len(parts),
            out_specs=[spec(wide) for wide in widths] + [spec(1)],
            scratch_shapes=[
                pltpu.VMEM((width, 2 * hidden), BF16),
                pltpu.VMEM((hidden, width), BF16),
                pltpu.SemaphoreType.DMA((len(parts),)),
            ],
        ),
        compiler_params=pltpu.CompilerParams(vmem_limit_bytes=58 * 2**20),
        name="expert",
    )(total, starts, rows, grads, gates, *parts)


def combine_kernel(turned, window, base_ref, order_ref, pos_ref, rows_ref, dg_ref, act_ref, weight_ref, out_ref, back_ref):
    mul = dot_nt if turned else dot
    base = pl.multiple_of(base_ref[pl.program_id(0)], 16)
    pick = chosen(pos_ref, base, window)
    at = pl.ds(base, window)
    out_ref[...] = (
        dot_tn(pick.astype(F32).astype(BF16), rows_ref[at, :]) + mul(act_ref[...], weight_ref[...])
    ).astype(BF16)
    back_ref[0] = jnp.sum(jnp.where(pick, dg_ref[at, :], 0.0), axis=0, keepdims=True)


def combine(packing, order, rows, dg, act, weight, turned):
    base, pos, _, window, packed = packing
    blocks, _, count = pos.shape
    width = rows.shape[-1]
    whole = lambda ref: pl.BlockSpec(ref.shape, lambda i, base, order: (0, 0))
    return pl.pallas_call(
        functools.partial(combine_kernel, turned, window),
        out_shape=[
            jax.ShapeDtypeStruct((blocks * count, width), BF16),
            jax.ShapeDtypeStruct((blocks, 1, count), F32),
        ],
        grid_spec=pltpu.PrefetchScalarGridSpec(
            num_scalar_prefetch=2,
            grid=(blocks,),
            in_specs=[
                pl.BlockSpec((1, 1, count), lambda i, base, order: (i, 0, 0)),
                whole(rows),
                whole(dg),
                pl.BlockSpec((count, act.shape[1]), lambda i, base, order: (i, 0)),
                whole(weight),
            ],
            out_specs=[
                pl.BlockSpec((count, width), lambda i, base, order: (order[i], 0)),
                pl.BlockSpec((1, 1, count), lambda i, base, order: (order[i], 0, 0)),
            ],
        ),
        compiler_params=pltpu.CompilerParams(vmem_limit_bytes=40 * 2**20),
        name="combine",
    )(base, order, pos, rows, dg, act, weight)


def gather_all(value):
    return lax.all_gather(value, "expert", axis=0, tiled=True)


def swap(value):
    return lax.all_to_all(value, "expert", split_axis=0, concat_axis=0, tiled=True)


def per_device(
    tokens,
    cotangent,
    segment_ids,
    routes,
    attn_in,
    attn_out,
    gain_attn,
    shared_in,
    shared_out,
    router,
    gain_ffn,
    expert_in,
    expert_out,
):
    n_dp, n_e = lax.axis_size("dp"), lax.axis_size("expert")
    me = lax.axis_index("expert")
    count, width = tokens.shape
    segments = segment_ids[0]
    length = segments.shape[0]
    rows = attn_in.shape[0]
    capacity = min(count, 3 * TOP * count // (2 * n_e))
    shared_rows = shared_out.shape[0]
    shared_width = shared_rows * n_dp
    expert_width = expert_out.shape[1] * n_dp

    order = ring_blocks()
    steady = jnp.arange(n_e, dtype=jnp.int32)
    hidden_in = tokens.astype(F32)
    inverse_one = lax.rsqrt(jnp.mean(hidden_in * hidden_in, axis=-1, keepdims=True) + EPS)
    normed_one = hidden_in * inverse_one
    gain_rows = gain_attn.astype(F32)[:, None]
    head_w = []

    def head_sent(blocks):
        own = (attn_in.astype(F32) * tied(gain_rows, blocks[0][1][0])).astype(BF16)
        own = own.reshape(rows, 3, n_e, HEAD_DIM).transpose(2, 0, 1, 3)
        head_w.append(swap(own.reshape(n_e, rows, 3 * HEAD_DIM)))
        return head_w[0]

    def head_whole(blocks):
        head_w.append(dp_gather(head_w[0]).reshape(width, 3 * HEAD_DIM))
        return head_w[1]

    here = lax.axis_index("dp")

    def spread(shard, chunks):
        while shard.shape[0] % (16 * chunks):
            chunks -= 1
        size = shard.shape[0] // chunks
        parts = [[(shard, here * shard.shape[0])]]
        for j in range(chunks):
            parts.append([])
            for step in range(1, n_dp):
                got = lax.ppermute(
                    shard[j * size : (j + 1) * size],
                    "dp",
                    [(i, (i - step) % n_dp) for i in range(n_dp)],
                )
                parts[-1].append((got, (here + step) % n_dp * shard.shape[0] + j * size))
        return parts

    up_parts = spread(expert_in[0], max(1, min(4, expert_in.shape[1] // 256)))
    down_parts = spread(expert_out[0], 2)
    first = lambda parts: [part for part, _ in parts]
    up_tokens = [first(parts) for parts in up_parts[1:]] + [[]] * 4

    small = jnp.concatenate([router, gain_ffn[:, None]], axis=1)
    small = dp_gather(small).reshape(-1, n_e + 1)
    extra_rows = 32
    extra = jnp.concatenate([small.T, routes.T.astype(BF16)], axis=0)
    extra = jnp.pad(extra, ((0, extra_rows - extra.shape[0]), (0, 0)))
    extra = jnp.broadcast_to(extra, (n_e,) + extra.shape)
    cos_table, sin_table, first_place = rope_tables(segments)
    share_w = shared_in.reshape(rows, 2, n_dp, n_e, shared_rows).transpose(3, 0, 1, 2, 4)
    share_w = share_w.reshape(n_e, rows, 2 * shared_width)

    half = n_e // 4
    norm_blocks = ring_gather(
        normed_one.astype(BF16),
        {
            half - 1: lambda blocks: [head_sent(blocks)] + up_tokens[0],
            half: lambda blocks: [head_whole(blocks), cos_table, sin_table, extra, share_w],
        },
    )
    head_w = head_w[1]

    mixed, query, key, value, lse, norm_all = attend(
        norm_blocks, order, head_w, cos_table, sin_table, first_place
    )
    mixed = jnp.concatenate([mixed.reshape(n_e, count, HEAD_DIM), extra], axis=1)
    mixed = swap(tied(mixed, *up_tokens[1]) if up_tokens[1] else mixed)
    small = mixed[:, count:]
    mixed = mixed[:, :count].transpose(1, 0, 2).reshape(count, n_dp, n_e, rows)
    mixed = mixed.transpose(0, 2, 1, 3).reshape(count, width)
    share_w = swap(tied(share_w, lse))
    proj_all = gather_all(dp_gather(attn_out).reshape(n_dp * rows, width))
    routes_all = small[:, n_e + 1 : n_e + 1 + TOP].astype(F32)
    small = small[:, : n_e + 1].reshape(n_e, n_e + 1, n_dp, rows).transpose(1, 2, 0, 3)
    small = small.reshape(n_e + 1, width)
    router_full = small[:n_e]
    gain_second = small[n_e].astype(F32)
    cot_all = gather_all(cotangent)

    share_sent = share_w
    share_w = dp_gather(share_w).reshape(width, 2 * shared_width)
    share_out = dp_gather(shared_out).reshape(shared_width, width)
    resid = hidden_in + dot(mixed, proj_all)
    if up_tokens[2]:
        resid = tied(resid, *up_tokens[2])

    inverse_two = lax.rsqrt(jnp.mean(resid * resid, axis=-1, keepdims=True) + EPS)
    normed_two = resid * inverse_two
    norm_two = (normed_two * gain_second).astype(BF16)
    logits = dot_nt(norm_two, router_full)
    picked = jnp.any(routes[:, :, None] == jnp.arange(n_e)[None, None, :], axis=1)
    chosen = jnp.where(picked, logits, NEG)
    chosen = jnp.where(picked, jnp.exp(chosen - jnp.max(chosen, axis=-1, keepdims=True)), 0.0)
    gates = chosen / jnp.sum(chosen, axis=-1, keepdims=True)
    gate_high = gates.astype(BF16)
    gate_low = (gates - gate_high.astype(F32)).astype(BF16)
    blank = jnp.zeros((count, 128 - 2 * n_e), BF16)
    payload = jnp.concatenate([norm_two, gate_high, gate_low, blank], axis=1)
    norm_blocks = ring_gather(
        payload,
        {
            half - 2: lambda blocks: [share_sent] + up_tokens[3],
            half: lambda blocks: first(down_parts[1]),
        },
    )

    named = jnp.any(routes_all == me.astype(F32), axis=1)
    named = jnp.take(named, order, axis=0)
    ranking = jnp.cumsum(named.astype(jnp.int32), axis=1)
    ends = jnp.cumsum(ranking[:, -1])
    begins = ends - ranking[:, -1]
    pos = jnp.where(named, begins[:, None] + ranking - 1, -1)[:, None, :]
    window = -(-(capacity + 15) // 16) * 16
    packed = -(-(n_e * capacity + 32) // 256) * 256
    packing = (begins // 16 * 16, pos, ends[-1:], window, packed)
    norm_two_all, payload, arrived, _ = dispatch(
        norm_blocks, [width, 128], packing, order, jnp.zeros((n_e, 1, count), F32)
    )
    mine = jnp.arange(n_e) == me
    gate_all = payload[:, : 2 * n_e].astype(F32).reshape(length, 2, n_e)
    gate_all = jnp.sum(jnp.where(mine, gate_all, 0.0), axis=(1, 2)).reshape(n_e, 1, count)
    cot_all, cot_rows, gate_rows = dispatch(cot_all, [width], packing, order, gate_all)
    weighted, row_grad, expert_act, route_grad, pre_grad, gate_grad = expert(
        packing[2],
        arrived,
        cot_rows,
        gate_rows,
        [part for parts in up_parts for part in parts],
        [part for parts in down_parts for part in parts],
    )

    def shard_grads(left, right, chunks):
        size = left.shape[1] // n_dp
        part = size // chunks
        cut = lambda start, wide: lax.dynamic_slice_in_dim(left, start, wide, 1)
        got = [
            [
                lax.ppermute(
                    dot_tn(cut((here + step) % n_dp * size + j * part, part), right).astype(BF16),
                    "dp",
                    [(i, (i + step) % n_dp) for i in range(n_dp)],
                )
                for step in range(1, n_dp)
            ]
            for j in range(chunks)
        ]
        return dot_tn(cut(here * size, size), right), got

    def shard_sum(own, got, tokens):
        part = own.shape[0] // len(got)
        for j, (parts, token) in enumerate(zip(got, tokens)):
            block = own[j * part : (j + 1) * part] + sum(tied(p.astype(F32), token) for p in parts)
            own = lax.dynamic_update_slice_in_dim(own, block, j * part, 0)
        return own[None]

    down_own, down_got = shard_grads(expert_act, route_grad, 2)
    up_own, up_got = shard_grads(arrived, pre_grad, len(up_parts) - 1)

    shared_pre = dot(norm_two_all, share_w)
    shared_act = (
        jax.nn.silu(shared_pre[:, :shared_width]) * shared_pre[:, shared_width:]
    ).astype(BF16)
    shared_act_grad = dot_nt(cot_all, share_out)
    shared_pre_grad = silu_back(
        shared_act_grad, shared_pre[:, :shared_width], shared_pre[:, shared_width:]
    ).astype(BF16)
    norm_two_part, gate_grad = combine(
        packing, steady, row_grad, gate_grad, shared_pre_grad, share_w, True
    )
    norm_two_grad = ring_scatter(lambda n: norm_two_part[n * count : (n + 1) * count])
    gate_grad = jnp.sum(
        jnp.where(order[:, None, None] == steady[None, :, None], gate_grad, 0.0), axis=0
    )
    gate_grad = swap(gate_grad)
    out_part, _ = combine(
        packing, order, weighted, gate_rows, shared_act, share_out, False
    )
    routed_out = lax.psum_scatter(out_part, "expert", scatter_dimension=0, tiled=True)

    share_out_grad = dp_scatter(dot_tn(shared_act, cot_all).reshape(n_dp, shared_rows, width))
    share_in_grad = dot_tn(norm_two_all, shared_pre_grad)
    share_in_grad = dp_scatter(share_in_grad.reshape(n_dp, n_e, rows, 2 * shared_width))
    share_in_grad = swap(share_in_grad.astype(BF16)).astype(F32)
    share_in_grad = (
        share_in_grad.reshape(n_e, rows, 2, n_dp, shared_rows)
        .transpose(1, 2, 3, 0, 4)
        .reshape(rows, -1)
    )

    gate_grad = gate_grad.T
    logit_grad = gates * (gate_grad - jnp.sum(gates * gate_grad, axis=-1, keepdims=True))
    router_grad = jnp.dot(
        logit_grad.T, norm_two.astype(F32), precision=HIGHEST, preferred_element_type=F32
    )
    norm_two_grad = norm_two_grad + jnp.dot(
        logit_grad, router_full.astype(F32), precision=HIGHEST, preferred_element_type=F32
    )
    gain_two_grad = jnp.sum(norm_two_grad * normed_two, axis=0)
    upstream = tied(cotangent.astype(F32), *down_got[0])
    scaled_two = norm_two_grad * gain_second
    resid_grad = upstream + inverse_two * (
        scaled_two - normed_two * jnp.mean(scaled_two * normed_two, axis=-1, keepdims=True)
    )
    small_grad = jnp.concatenate([router_grad, gain_two_grad[None]], axis=0)

    branch_cot = resid_grad.astype(BF16)
    mixed_grad = tied(dot_nt(branch_cot, proj_all), *down_got[1]).astype(BF16)
    mixed_grad = mixed_grad.reshape(count, n_e, n_dp, rows).transpose(0, 2, 1, 3)
    mixed_grad = swap(mixed_grad.reshape(count, n_e, HEAD_DIM).transpose(1, 0, 2))
    mixed_grad = mixed_grad.reshape(length, HEAD_DIM)
    proj_grad = lax.psum_scatter(
        dot_tn(mixed, branch_cot).astype(BF16), "expert", scatter_dimension=0, tiled=True
    )
    attn_out_grad = dp_scatter(proj_grad.astype(F32).reshape(n_dp, rows, width))
    qkv_grad = attend_back(
        query, key, value, mixed_grad, lse, first_place, cos_table, sin_table, order
    )
    small_grad = tied(small_grad, qkv_grad).reshape(n_e + 1, n_dp * n_e, rows).transpose(1, 0, 2)
    small_grad = lax.all_to_all(
        small_grad, ("dp", "expert"), split_axis=0, concat_axis=0, tiled=True
    )
    small_grad = jnp.sum(small_grad, axis=0)
    norm_one_part = dot_nt(qkv_grad, head_w).astype(BF16)
    scaled_one = ring_scatter(
        lambda n: norm_one_part[n * count : (n + 1) * count],
        {1: up_got[0], half - 1: up_got[min(1, len(up_got) - 1)]},
    )
    expert_out_grad = shard_sum(down_own, down_got, [norm_two_grad, mixed_grad])
    expert_in_grad = shard_sum(up_own, up_got, ([qkv_grad] + [scaled_one] * 3)[: len(up_got)])
    input_grad = resid_grad + inverse_one * (
        scaled_one - normed_one * jnp.mean(scaled_one * normed_one, axis=-1, keepdims=True)
    )
    head_grad = dot_tn(norm_all, qkv_grad).reshape(n_dp, n_e, rows, 3 * HEAD_DIM)
    head_grad = swap(dp_scatter(head_grad).astype(BF16)).astype(F32)
    head_grad = (
        head_grad.reshape(n_e, rows, 3, HEAD_DIM).transpose(1, 2, 0, 3).reshape(rows, 3 * width)
    )
    gain_attn_grad = jnp.sum(head_grad * attn_in.astype(F32), axis=1)
    attn_in_grad = head_grad * gain_rows
    return (
        (resid + routed_out.astype(F32)).astype(BF16),
        input_grad.astype(BF16),
        attn_in_grad,
        attn_out_grad,
        gain_attn_grad,
        share_in_grad,
        share_out_grad,
        small_grad[:n_e].T,
        small_grad[n_e],
        expert_in_grad,
        expert_out_grad,
    )


def solution(mesh):
    return jax.shard_map(
        per_device,
        mesh=mesh,
        in_specs=(
            P(("dp", "expert"), None),
            P(("dp", "expert"), None),
            P("dp", None),
            P(("dp", "expert"), None),
            P(("dp", "expert"), None),
            P(("dp", "expert"), None),
            P(("dp", "expert")),
            P(("dp", "expert"), None),
            P(("dp", "expert"), None),
            P(("dp", "expert"), None),
            P(("dp", "expert")),
            P("expert", "dp", None),
            P("expert", "dp", None),
        ),
        out_specs=(
            P(("dp", "expert"), None),
            P(("dp", "expert"), None),
            P(("dp", "expert"), None),
            P(("dp", "expert"), None),
            P(("dp", "expert")),
            P(("dp", "expert"), None),
            P(("dp", "expert"), None),
            P(("dp", "expert"), None),
            P(("dp", "expert")),
            P("expert", "dp", None),
            P("expert", "dp", None),
        ),
        check_vma=False,
    )
```

```python
import functools
import math

import jax
import jax.numpy as jnp
from jax import lax
from jax.experimental import pallas as pl
from jax.experimental.pallas import tpu as pltpu
from jax.sharding import PartitionSpec as P

HEADS = 16
HEAD_DIM = 128
TOP = 6


EPS = 1e-06
THETA = 10000.0
NEG = -1e30
HIGHEST = lax.Precision.HIGHEST
BF16 = jnp.bfloat16
F32 = jnp.float32
LOG2E = math.log2(math.e)


def rope_tables(segments):
    length = segments.shape[0]
    places = jnp.arange(length, dtype=jnp.int32)
    starts = jnp.concatenate([jnp.ones((1,), dtype=jnp.bool_), segments[1:] != segments[:-1]])
    first_place = lax.cummax(jnp.where(starts, places, 0), axis=0)
    offset = (places - first_place).astype(jnp.float32)
    half_dim = HEAD_DIM // 2
    freqs = jnp.exp(jnp.arange(half_dim, dtype=jnp.float32) * (-2.0 * math.log(THETA) / HEAD_DIM))
    angles = offset[:, None] * freqs[None, :]
    cos_table, sin_table = jnp.cos(angles), jnp.sin(angles)
    return (
        jnp.concatenate([cos_table, cos_table], axis=1),
        jnp.concatenate([-sin_table, sin_table], axis=1),
        first_place[None, :],
    )


def silu_back(grad_act, gate_part, up_part):
    sigmoid_gate = jax.nn.sigmoid(gate_part)
    gate_grad = grad_act * up_part * sigmoid_gate * (1.0 + gate_part * (1.0 - sigmoid_gate))
    up_grad = grad_act * gate_part * sigmoid_gate
    return jnp.concatenate([gate_grad, up_grad], axis=-1)


def dot(left, right):
    return jnp.dot(left, right, preferred_element_type=F32)


def dot_tn(left, right):
    return lax.dot_general(left, right, (((0,), (0,)), ((), ())), preferred_element_type=F32)


def dot_nt(left, right):
    return lax.dot_general(left, right, (((1,), (1,)), ((), ())), preferred_element_type=F32)


def turn(values, cos_table, sin_table):
    return values * cos_table + pltpu.roll(values, HEAD_DIM // 2, 1) * sin_table


def attend_kernel(sources, block, order_ref, *refs):
    pieces = refs[: sources[-1][-1] + 1]
    weight_ref, cos_ref, sin_ref, start_ref = refs[len(pieces) : len(pieces) + 4]
    o_ref, q_ref, k_ref, v_ref, lse_ref, rows_ref, vt_ref = refs[len(pieces) + 4 :]
    step = pl.program_id(0)
    length = q_ref.shape[0]
    factor = HEAD_DIM ** (-0.5) * LOG2E
    rows = rows_ref.shape[0]

    for n, parts in enumerate(sources):

        @pl.when(step == n)
        def _(parts=parts):
            low = 0
            for part in parts:
                size = pieces[part].shape[0]
                rows_ref[low : low + size, :] = pieces[part][...]
                low += size

    @pl.when(step < len(sources))
    def _():
        qkv = dot(rows_ref[...], weight_ref[...])
        at = pl.ds(pl.multiple_of(order_ref[step] * rows, rows), rows)
        cos_table, sin_table = cos_ref[at, :], sin_ref[at, :]
        q_ref[at, :] = turn(qkv[:, :HEAD_DIM], cos_table, sin_table).astype(BF16)
        k_ref[at, :] = turn(qkv[:, HEAD_DIM : 2 * HEAD_DIM], cos_table, sin_table).astype(BF16)
        value = qkv[:, 2 * HEAD_DIM :]
        v_ref[at, :] = value.astype(BF16)
        vt_ref[:, at] = value.T.astype(BF16)

    for i in range(length // block):

        @pl.when(step == len(sources) + i)
        def _(i=i):
            low, high = i * block, (i + 1) * block
            raw = dot_nt(k_ref[:high, :], q_ref[low:high, :])
            keys = lax.broadcasted_iota(jnp.int32, raw.shape, 0)
            queries = low + lax.broadcasted_iota(jnp.int32, raw.shape, 1)
            allowed = (keys <= queries) & (keys >= start_ref[:, low:high])
            raw = jnp.where(allowed, raw, NEG)
            top = jnp.max(raw, axis=0, keepdims=True)
            shifted = jnp.exp2((raw - top) * factor)
            total = jnp.sum(shifted, axis=0, keepdims=True)
            probs = (shifted * (1.0 / total)).astype(BF16)
            mixed = dot(vt_ref[:, :high], probs)
            o_ref[low:high, :] = mixed.T.astype(BF16)
            lse_ref[:, low:high] = top * factor + jnp.log2(total)


def attend(blocks, order, weight, cos_table, sin_table, first_place):
    pieces, sources = flatten(blocks)
    length = cos_table.shape[0]
    rows = length // len(sources)
    width = weight.shape[0]
    block = min(256, length)
    last = len(sources) - 1
    whole = lambda shape: pl.BlockSpec(shape, lambda i, order: (0, 0))
    head = jax.ShapeDtypeStruct((length, HEAD_DIM), BF16)
    return pl.pallas_call(
        functools.partial(attend_kernel, sources, block),
        out_shape=[head] * 4
        + [jax.ShapeDtypeStruct((1, length), F32), jax.ShapeDtypeStruct((length, width), BF16)],
        grid_spec=pltpu.PrefetchScalarGridSpec(
            num_scalar_prefetch=1,
            grid=(len(sources) + length // block,),
            in_specs=[whole(piece.shape) for piece in pieces]
            + [
                whole(weight.shape),
                whole((length, HEAD_DIM)),
                whole((length, HEAD_DIM)),
                whole((1, length)),
            ],
            out_specs=[whole((length, HEAD_DIM))] * 4
            + [
                whole((1, length)),
                pl.BlockSpec((rows, width), lambda i, order: (jnp.minimum(i, last), 0)),
            ],
            scratch_shapes=[pltpu.VMEM((HEAD_DIM, length), BF16)],
        ),
        compiler_params=pltpu.CompilerParams(vmem_limit_bytes=52 * 2**20),
        name="attend",
    )(order, *pieces, weight, cos_table, sin_table, first_place)


def attend_back_kernel(sources, block, order_ref, *refs):
    pieces = refs[: sources[-1][-1] + 1]
    (
        weight_ref, q_ref, k_ref, v_ref, o_ref, lse_ref, start_ref, cos_ref, sin_ref,
        out_ref, weight_grad_ref,
        rows_ref, kt_ref, do_ref, dq_ref, dk_ref, dv_ref,
    ) = refs[len(pieces) :]
    length = q_ref.shape[0]
    rows = rows_ref.shape[0]
    step = pl.program_id(0)
    scale = HEAD_DIM ** (-0.5)
    factor = scale * LOG2E
    blocks = len(sources)
    count = length // block

    @pl.when(step == 0)
    def _():
        kt_ref[...] = k_ref[...].astype(F32).T.astype(BF16)
        dk_ref[...] = jnp.zeros_like(dk_ref)
        dv_ref[...] = jnp.zeros_like(dv_ref)
        weight_grad_ref[...] = jnp.zeros_like(weight_grad_ref)

    for n, parts in enumerate(sources):

        @pl.when(step == n)
        def _(parts=parts):
            low = 0
            for part in parts:
                size = pieces[part].shape[0]
                rows_ref[low : low + size, :] = pieces[part][...]
                low += size

    @pl.when(step < blocks)
    def _():
        at = pl.ds(pl.multiple_of(order_ref[step] * rows, rows), rows)
        do_ref[at, :] = dot_nt(rows_ref[...], weight_ref[...]).astype(BF16)
        weight_grad_ref[...] += dot_tn(o_ref[at, :], rows_ref[...])

    for i in range(count):

        @pl.when(step == blocks + i)
        def _(i=i):
            low, high = i * block, (i + 1) * block
            query, grad = q_ref[low:high, :], do_ref[low:high, :]
            raw = dot_nt(k_ref[:high, :], query)
            keys = lax.broadcasted_iota(jnp.int32, raw.shape, 0)
            queries = low + lax.broadcasted_iota(jnp.int32, raw.shape, 1)
            allowed = (keys <= queries) & (keys >= start_ref[:, low:high])
            raw = jnp.where(allowed, raw * factor - lse_ref[:, low:high], NEG)
            probs = jnp.exp2(raw)
            probs_grad = dot_nt(v_ref[:high, :], grad)
            inner = jnp.sum(probs_grad * probs, axis=0, keepdims=True)
            score_grad = (probs * (probs_grad - inner)).astype(BF16)
            dv_ref[:high, :] += dot(probs.astype(BF16), grad)
            dk_ref[:high, :] += dot(score_grad, query)
            dq_ref[low:high, :] = dot(kt_ref[:, :high], score_grad).T

    @pl.when(step == blocks + count - 1)
    def _():
        for n in range(blocks):
            at = pl.ds(pl.multiple_of(order_ref[n] * rows, rows), rows)
            to = slice(n * rows, (n + 1) * rows)
            cos_table, sin_table = cos_ref[at, :], -sin_ref[at, :]
            out_ref[to, :HEAD_DIM] = turn(dq_ref[at, :] * scale, cos_table, sin_table).astype(BF16)
            out_ref[to, HEAD_DIM : 2 * HEAD_DIM] = turn(
                dk_ref[at, :] * scale, cos_table, sin_table
            ).astype(BF16)
            out_ref[to, 2 * HEAD_DIM :] = dv_ref[at, :].astype(BF16)


def attend_back(grads, order, weight, query, key, value, mixed, lse, first_place, cos_table, sin_table):
    pieces, sources = flatten(grads)
    length = query.shape[0]
    block = min(256, length)
    rows = length // len(sources)
    whole = lambda shape: pl.BlockSpec(shape, lambda i, order: (0, 0))
    head = whole((length, HEAD_DIM))
    return pl.pallas_call(
        functools.partial(attend_back_kernel, sources, block),
        out_shape=[
            jax.ShapeDtypeStruct((length, 3 * HEAD_DIM), BF16),
            jax.ShapeDtypeStruct(weight.shape, F32),
        ],
        grid_spec=pltpu.PrefetchScalarGridSpec(
            num_scalar_prefetch=1,
            grid=(len(sources) + length // block,),
            in_specs=[whole(piece.shape) for piece in pieces]
            + [whole(weight.shape)]
            + [head] * 4
            + [whole((1, length))] * 2
            + [head] * 2,
            out_specs=[whole((length, 3 * HEAD_DIM)), whole(weight.shape)],
            scratch_shapes=[
                pltpu.VMEM((rows, weight.shape[1]), BF16),
                pltpu.VMEM((HEAD_DIM, length), BF16),
                pltpu.VMEM((length, HEAD_DIM), BF16),
            ]
            + [pltpu.VMEM((length, HEAD_DIM), F32)] * 3,
        ),
        compiler_params=pltpu.CompilerParams(vmem_limit_bytes=56 * 2**20),
        name="attend_back",
    )(order, *pieces, weight, query, key, value, mixed, lse, first_place, cos_table, sin_table)


def dp_gather(value):
    count = lax.axis_size("dp")
    if count == 1:
        return value[None]
    here = lax.axis_index("dp")
    parts = [value] + [
        lax.ppermute(value, "dp", [(i, (i - step) % count) for i in range(count)])
        for step in range(1, count)
    ]
    if count == 2:
        first = here == 0
        return jnp.stack(
            [jnp.where(first, parts[0], parts[1]), jnp.where(first, parts[1], parts[0])]
        )
    whole = jnp.zeros((count,) + value.shape, value.dtype)
    for step, part in enumerate(parts):
        whole = lax.dynamic_update_index_in_dim(whole, part, (here + step) % count, 0)
    return whole


def dp_scatter(value):
    count = lax.axis_size("dp")
    here = lax.axis_index("dp")
    total = lax.dynamic_index_in_dim(value, here, 0, keepdims=False)
    for step in range(1, count):
        block = lax.dynamic_index_in_dim(value, (here + step) % count, 0, keepdims=False)
        got = lax.ppermute(
            block.astype(BF16), "dp", [(i, (i + step) % count) for i in range(count)]
        )
        total = total + got.astype(F32)
    return total


def ring_order():
    pairs = lax.axis_size("expert") // 2
    return list(range(0, pairs, 2)) + list(range(pairs - 1, 0, -2))


def ring_shift(value, step):
    order = ring_order()
    pairs = len(order)
    perm = [
        (order[q] * 2 + c, order[(q + step) % pairs] * 2 + c) for q in range(pairs) for c in range(2)
    ]
    return lax.ppermute(value, "expert", perm)


def core_swap(value):
    count = lax.axis_size("expert")
    return lax.ppermute(value, "expert", [(i, i ^ 1) for i in range(count)])


def ring_offsets():
    half = lax.axis_size("expert") // 4
    return [0] + [o for step in range(1, half) for o in (step, -step)] + [half]


def ring_blocks():
    order = ring_order()
    pairs = len(order)
    table = [[0] * (2 * pairs) for _ in range(2 * pairs)]
    for q in range(pairs):
        for c in range(2):
            for j, offset in enumerate(ring_offsets()):
                for other in range(2):
                    table[order[q] * 2 + c][2 * j + other] = (
                        order[(q - offset) % pairs] * 2 + (c ^ other)
                    )
    return lax.dynamic_index_in_dim(
        jnp.asarray(table, jnp.int32), lax.axis_index("expert"), 0, keepdims=False
    )


def tied(value, *tokens):
    firsts = [lax.slice(t, (0,) * t.ndim, (1,) * t.ndim).reshape(()) for t in tokens]
    token = sum(t.astype(F32) for t in firsts) * 0.0
    return (value.astype(F32) * (1.0 + token)).astype(value.dtype)


def ring_gather(value, gates=None):
    gates = gates or {}
    half_rows = value.shape[0] // 2
    half = lax.axis_size("expert") // 4
    blocks = {}

    def keep(parts, offset):
        blocks[offset] = (parts, [core_swap(part) for part in parts])

    keep([value], 0)
    ahead = back = value
    for step in range(1, half):
        if step in gates:
            token = gates[step](blocks)
            ahead, back = tied(ahead, *token), tied(back, *token)
        ahead, back = ring_shift(ahead, 1), ring_shift(back, -1)
        keep([ahead], step)
        keep([back], -step)
    if half in gates:
        token = gates[half](blocks)
        ahead, back = tied(ahead, *token), tied(back, *token)
    last = [ring_shift(ahead[:half_rows], 1), ring_shift(back[half_rows:], -1)]
    keep(last, half)
    return [parts for offset in ring_offsets() for parts in blocks[offset]]


def flatten(blocks):
    pieces = [piece for parts in blocks for piece in parts]
    sources, n = [], 0
    for parts in blocks:
        sources.append(tuple(range(n, n + len(parts))))
        n += len(parts)
    return pieces, tuple(sources)


def ring_scatter(block, gates=None, marks=None):
    gates = gates or {}
    half = lax.axis_size("expert") // 4
    offsets = ring_offsets()
    spare = {}

    def mine(offset):
        if offset not in spare:
            j = offsets.index(offset)
            spare[offset] = block(2 * j).astype(F32) + core_swap(block(2 * j + 1)).astype(F32)
        return spare[offset]

    far = mine(half).astype(BF16)
    half_rows = far.shape[0] // 2
    ahead = ring_shift(far[:half_rows], 1)
    back = ring_shift(far[half_rows:], -1)
    if marks is not None:
        marks.extend([ahead, back])
    for step in range(half - 1, 0, -1):
        onward, homeward = mine(-step), mine(step)
        if step == half - 1:
            onward = jnp.concatenate(
                [onward[:half_rows] + ahead.astype(F32), onward[half_rows:]], axis=0
            )
            homeward = jnp.concatenate(
                [homeward[:half_rows], homeward[half_rows:] + back.astype(F32)], axis=0
            )
        else:
            onward = onward + ahead.astype(F32)
            homeward = homeward + back.astype(F32)
        if half - step in gates:
            onward, homeward = tied(onward, *gates[half - step]), tied(homeward, *gates[half - step])
        ahead = ring_shift(onward.astype(BF16), 1)
        back = ring_shift(homeward.astype(BF16), -1)
    return mine(0) + ahead.astype(F32) + back.astype(F32)


def chosen(pos_ref, base, window):
    count = pos_ref.shape[-1]
    row = base + lax.broadcasted_iota(jnp.int32, (window, count), 0)
    return row == pos_ref[0]


def dispatch_kernel(sources, widths, window, base_ref, order_ref, pos_ref, gate_ref, *refs):
    outs = refs[-len(widths) - 2 :]
    pieces, blocks, rows_ref, weights_ref = refs[: -len(outs)], outs[:-2], outs[-2], outs[-1]
    step = pl.program_id(0)

    @pl.when(step == 0)
    def _():
        rows_ref[...] = jnp.zeros_like(rows_ref)
        weights_ref[...] = jnp.zeros_like(weights_ref)

    for n, parts in enumerate(sources):

        @pl.when(step == n)
        def _(parts=parts):
            low = 0
            for part in parts:
                size = pieces[part].shape[0]
                left = 0
                for block, wide in zip(blocks, widths):
                    block[low : low + size, :] = pieces[part][:, left : left + wide]
                    left += wide
                low += size

    base = pl.multiple_of(base_ref[step], 16)
    pick = chosen(pos_ref, base, window)
    at = pl.ds(base, window)
    found = dot(pick.astype(F32).astype(BF16), (blocks or pieces)[0][...])
    rows_ref[at, :] = (rows_ref[at, :].astype(F32) + found).astype(BF16)
    weights_ref[at, :] += jnp.sum(jnp.where(pick, gate_ref[0], 0.0), axis=1, keepdims=True)


def dispatch(blocks, widths, packing, order, gates):
    base, pos, _, window, packed = packing
    count, _, rows = pos.shape
    if isinstance(blocks, list):
        pieces, sources = flatten(blocks)
        piece_specs = [pl.BlockSpec(piece.shape, lambda i, base, order: (0, 0)) for piece in pieces]
    else:
        pieces, sources, widths = [blocks], (), []
        piece_specs = [pl.BlockSpec((rows, blocks.shape[1]), lambda i, base, order: (order[i], 0))]
    width = (widths or [pieces[0].shape[1]])[0]
    return pl.pallas_call(
        functools.partial(dispatch_kernel, sources, tuple(widths), window),
        out_shape=[jax.ShapeDtypeStruct((rows * count, wide), BF16) for wide in widths]
        + [
            jax.ShapeDtypeStruct((packed, width), BF16),
            jax.ShapeDtypeStruct((packed, 1), F32),
        ],
        grid_spec=pltpu.PrefetchScalarGridSpec(
            num_scalar_prefetch=2,
            grid=(count,),
            in_specs=[
                pl.BlockSpec((1, 1, rows), lambda i, base, order: (i, 0, 0)),
                pl.BlockSpec((1, 1, rows), lambda i, base, order: (order[i], 0, 0)),
            ]
            + piece_specs,
            out_specs=[
                pl.BlockSpec((rows, wide), lambda i, base, order: (order[i], 0)) for wide in widths
            ]
            + [
                pl.BlockSpec((packed, width), lambda i, base, order: (0, 0)),
                pl.BlockSpec((packed, 1), lambda i, base, order: (0, 0)),
            ],
        ),
        compiler_params=pltpu.CompilerParams(vmem_limit_bytes=52 * 2**20),
        name="dispatch",
    )(base, order, pos, gates, *pieces)


def expert_kernel(ups, total_ref, starts_ref, x_ref, g_ref, gate_ref, *refs):
    parts, refs = refs[:-9], refs[-9:]
    wy_ref, dn_ref, ea_ref, dy_ref, db_ref, dg_ref, up_ref, down_ref, sems = refs
    step = pl.program_id(0)
    rows, hidden = ea_ref.shape
    some = step * rows < total_ref[0]

    @pl.when(step == 0)
    def _():
        copies = []
        for n, part in enumerate(parts):
            at = pl.ds(pl.multiple_of(starts_ref[n], 16), part.shape[0])
            whole = up_ref if n < ups else down_ref
            copies.append(pltpu.make_async_copy(part, whole.at[at, :], sems.at[n]))
        for copy in copies:
            copy.start()
        for copy in copies:
            copy.wait()

    @pl.when(some)
    def _():
        pre = dot(x_ref[...], up_ref[...])
        gate_part, up_part = pre[:, :hidden], pre[:, hidden:]
        sigmoid_gate = 1.0 / (1.0 + jnp.exp(-gate_part))
        silu = gate_part * sigmoid_gate
        act = (silu * up_part).astype(BF16)
        ea_ref[...] = act
        result = dot(act, down_ref[...]).astype(BF16).astype(F32)
        grad = g_ref[...].astype(F32)
        gate = gate_ref[...]
        dg_ref[...] = jnp.sum(grad * result, axis=1, keepdims=True)
        wy_ref[...] = (gate * result).astype(BF16)
        out_grad = (gate * grad).astype(BF16)
        dy_ref[...] = out_grad
        act_grad = dot_nt(out_grad, down_ref[...])
        db_ref[:, :hidden] = (
            act_grad * up_part * sigmoid_gate * (1.0 + gate_part * (1.0 - sigmoid_gate))
        ).astype(BF16)
        db_ref[:, hidden:] = (act_grad * silu).astype(BF16)
        dn_ref[...] = dot_nt(db_ref[...], up_ref[...]).astype(BF16)

    @pl.when(jnp.logical_not(some))
    def _():
        for ref in (wy_ref, dn_ref, ea_ref, dy_ref, db_ref, dg_ref):
            ref[...] = jnp.zeros_like(ref)


def expert(total, rows, grads, gates, ups, downs):
    packed, width = rows.shape
    hidden = sum(part.shape[0] for part, _ in downs)
    tile = 256
    parts = [part for part, _ in ups + downs]
    starts = jnp.stack([start for _, start in ups + downs]).astype(jnp.int32)
    spec = lambda wide: pl.BlockSpec((tile, wide), lambda i, total, starts: (i, 0))
    widths = (width, width, hidden, width, 2 * hidden)
    return pl.pallas_call(
        functools.partial(expert_kernel, len(ups)),
        out_shape=[jax.ShapeDtypeStruct((packed, wide), BF16) for wide in widths]
        + [jax.ShapeDtypeStruct((packed, 1), F32)],
        grid_spec=pltpu.PrefetchScalarGridSpec(
            num_scalar_prefetch=2,
            grid=(packed // tile,),
            in_specs=[spec(width), spec(width), spec(1)]
            + [pl.BlockSpec(memory_space=pl.ANY)] * len(parts),
            out_specs=[spec(wide) for wide in widths] + [spec(1)],
            scratch_shapes=[
                pltpu.VMEM((width, 2 * hidden), BF16),
                pltpu.VMEM((hidden, width), BF16),
                pltpu.SemaphoreType.DMA((len(parts),)),
            ],
        ),
        compiler_params=pltpu.CompilerParams(vmem_limit_bytes=58 * 2**20),
        name="expert",
    )(total, starts, rows, grads, gates, *parts)


def combine_kernel(turned, window, extra, base_ref, order_ref, to_ref, me_ref, pos_ref, rows_ref, dg_ref, act_ref, weight_ref, out_ref):
    mul = dot_nt if turned else dot
    base = pl.multiple_of(base_ref[pl.program_id(0)], 16)
    pick = chosen(pos_ref, base, window)
    at = pl.ds(base, window)
    width = rows_ref.shape[1]
    out_ref[:, :width] = (
        dot_tn(pick.astype(F32).astype(BF16), rows_ref[at, :]) + mul(act_ref[...], weight_ref[...])
    ).astype(BF16)
    if extra:
        count = pick.shape[1]
        line = jnp.sum(jnp.where(pick, dg_ref[at, :], 0.0), axis=0, keepdims=True)
        row = lax.broadcasted_iota(jnp.int32, (count, count), 0)
        lane = lax.broadcasted_iota(jnp.int32, (count, count), 1)
        column = jnp.sum(jnp.where(row == lane, line, 0.0), axis=1, keepdims=True)
        high = column.astype(BF16).astype(F32)
        lane = lax.broadcasted_iota(jnp.int32, (count, extra), 1)
        out_ref[:, width:] = jnp.where(
            lane == me_ref[0], high, jnp.where(lane == me_ref[0] + extra // 2, column - high, 0.0)
        ).astype(BF16)


def combine(packing, order, to, me, rows, dg, act, weight, turned, extra):
    base, pos, _, window, packed = packing
    blocks, _, count = pos.shape
    width = rows.shape[-1]
    whole = lambda ref: pl.BlockSpec(ref.shape, lambda i, *_: (0, 0))
    return pl.pallas_call(
        functools.partial(combine_kernel, turned, window, extra),
        out_shape=jax.ShapeDtypeStruct((blocks * count, width + extra), BF16),
        grid_spec=pltpu.PrefetchScalarGridSpec(
            num_scalar_prefetch=4,
            grid=(blocks,),
            in_specs=[
                pl.BlockSpec((1, 1, count), lambda i, *_: (i, 0, 0)),
                whole(rows),
                whole(dg),
                pl.BlockSpec((count, act.shape[1]), lambda i, base, order, to, me: (order[i], 0)),
                whole(weight),
            ],
            out_specs=pl.BlockSpec(
                (count, width + extra), lambda i, base, order, to, me: (to[i], 0)
            ),
        ),
        compiler_params=pltpu.CompilerParams(vmem_limit_bytes=40 * 2**20),
        name="combine",
    )(base, order, to, me.reshape(1), pos, rows, dg, act, weight)


def gather_all(value):
    return lax.all_gather(value, "expert", axis=0, tiled=True)


def swap(value):
    return lax.all_to_all(value, "expert", split_axis=0, concat_axis=0, tiled=True)


def per_device(
    tokens,
    cotangent,
    segment_ids,
    routes,
    attn_in,
    attn_out,
    gain_attn,
    shared_in,
    shared_out,
    router,
    gain_ffn,
    expert_in,
    expert_out,
):
    n_dp, n_e = lax.axis_size("dp"), lax.axis_size("expert")
    me = lax.axis_index("expert")
    count, width = tokens.shape
    segments = segment_ids[0]
    length = segments.shape[0]
    rows = attn_in.shape[0]
    capacity = min(count, 3 * TOP * count // (2 * n_e))
    shared_rows = shared_out.shape[0]
    shared_width = shared_rows * n_dp
    expert_width = expert_out.shape[1] * n_dp

    order = ring_blocks()
    steady = jnp.arange(n_e, dtype=jnp.int32)
    hidden_in = tokens.astype(F32)
    inverse_one = lax.rsqrt(jnp.mean(hidden_in * hidden_in, axis=-1, keepdims=True) + EPS)
    normed_one = hidden_in * inverse_one
    gain_rows = gain_attn.astype(F32)[:, None]
    head_w = []

    def head_sent(blocks):
        own = (attn_in.astype(F32) * tied(gain_rows, blocks[0][1][0])).astype(BF16)
        own = own.reshape(rows, 3, n_e, HEAD_DIM).transpose(2, 0, 1, 3)
        head_w.append(swap(own.reshape(n_e, rows, 3 * HEAD_DIM)))
        return head_w[0]

    def head_whole(blocks):
        head_w.append(dp_gather(head_w[0]).reshape(width, 3 * HEAD_DIM))
        return head_w[1]

    here = lax.axis_index("dp")

    def spread(shard, chunks):
        while shard.shape[0] % (16 * chunks):
            chunks -= 1
        size = shard.shape[0] // chunks
        parts = [[(shard, here * shard.shape[0])]]
        for j in range(chunks):
            parts.append([])
            for step in range(1, n_dp):
                got = lax.ppermute(
                    shard[j * size : (j + 1) * size],
                    "dp",
                    [(i, (i - step) % n_dp) for i in range(n_dp)],
                )
                parts[-1].append((got, (here + step) % n_dp * shard.shape[0] + j * size))
        return parts

    up_parts = spread(expert_in[0], max(1, min(4, expert_in.shape[1] // 256)))
    down_parts = spread(expert_out[0], 2)
    first = lambda parts: [part for part, _ in parts]
    up_tokens = [first(parts) for parts in up_parts[1:]] + [[]] * 4

    small = jnp.concatenate([router, gain_ffn[:, None]], axis=1)
    small = dp_gather(small).reshape(-1, n_e + 1)
    extra_rows = 32
    extra = jnp.concatenate([small.T, routes.T.astype(BF16)], axis=0)
    extra = jnp.pad(extra, ((0, extra_rows - extra.shape[0]), (0, 0)))
    extra = jnp.broadcast_to(extra, (n_e,) + extra.shape)
    cos_table, sin_table, first_place = rope_tables(segments)
    share_w = shared_in.reshape(rows, 2, n_dp, n_e, shared_rows).transpose(3, 0, 1, 2, 4)
    share_w = share_w.reshape(n_e, rows, 2 * shared_width)

    half = n_e // 4
    norm_blocks = ring_gather(
        normed_one.astype(BF16),
        {
            half - 1: lambda blocks: [head_sent(blocks)] + up_tokens[0],
            half: lambda blocks: [head_whole(blocks), cos_table, sin_table, extra, share_w],
        },
    )
    head_w = head_w[1]

    head_out, query, key, value, lse, norm_all = attend(
        norm_blocks, order, head_w, cos_table, sin_table, first_place
    )
    mixed = jnp.concatenate([head_out.reshape(n_e, count, HEAD_DIM), extra], axis=1)
    mixed = swap(tied(mixed, *up_tokens[1]) if up_tokens[1] else mixed)
    small = mixed[:, count:]
    mixed = mixed[:, :count].transpose(1, 0, 2).reshape(count, n_dp, n_e, rows)
    mixed = mixed.transpose(0, 2, 1, 3).reshape(count, width)
    share_w = swap(tied(share_w, lse))
    proj_all = dp_gather(attn_out).reshape(n_dp * rows, width)
    proj_all = gather_all(tied(proj_all, norm_blocks[-3][0], norm_blocks[-5][0]))
    routes_all = small[:, n_e + 1 : n_e + 1 + TOP].astype(F32)
    small = small[:, : n_e + 1].reshape(n_e, n_e + 1, n_dp, rows).transpose(1, 2, 0, 3)
    small = small.reshape(n_e + 1, width)
    router_full = small[:n_e]
    gain_second = small[n_e].astype(F32)
    cot_all = gather_all(tied(cotangent, proj_all))

    share_sent = share_w
    share_w = dp_gather(share_w).reshape(width, 2 * shared_width)
    share_out = dp_gather(shared_out).reshape(shared_width, width)
    resid = hidden_in + dot(mixed, proj_all)

    inverse_two = lax.rsqrt(jnp.mean(resid * resid, axis=-1, keepdims=True) + EPS)
    normed_two = resid * inverse_two
    norm_two = (normed_two * gain_second).astype(BF16)
    logits = dot_nt(norm_two, router_full)
    picked = jnp.any(routes[:, :, None] == jnp.arange(n_e)[None, None, :], axis=1)
    chosen = jnp.where(picked, logits, NEG)
    chosen = jnp.where(picked, jnp.exp(chosen - jnp.max(chosen, axis=-1, keepdims=True)), 0.0)
    gates = chosen / jnp.sum(chosen, axis=-1, keepdims=True)
    gate_high = gates.astype(BF16)
    gate_low = (gates - gate_high.astype(F32)).astype(BF16)
    blank = jnp.zeros((count, 128 - 2 * n_e), BF16)
    payload = jnp.concatenate([norm_two, gate_high, gate_low, blank], axis=1)
    norm_blocks = ring_gather(
        payload,
        {
            half - 1: lambda blocks: [share_sent] + up_tokens[2],
            half: lambda blocks: [share_sent] + up_tokens[3],
        },
    )

    named = jnp.any(routes_all == me.astype(F32), axis=1)
    named = jnp.take(named, order, axis=0)
    ranking = jnp.cumsum(named.astype(jnp.int32), axis=1)
    ends = jnp.cumsum(ranking[:, -1])
    begins = ends - ranking[:, -1]
    pos = jnp.where(named, begins[:, None] + ranking - 1, -1)[:, None, :]
    window = -(-(capacity + 15) // 16) * 16
    packed = -(-(n_e * capacity + 32) // 256) * 256
    packing = (begins // 16 * 16, pos, ends[-1:], window, packed)
    norm_two_all, payload, arrived, _ = dispatch(
        norm_blocks, [width, 128], packing, order, jnp.zeros((n_e, 1, count), F32)
    )
    mine = jnp.arange(n_e) == me
    gate_all = payload[:, : 2 * n_e].astype(F32).reshape(length, 2, n_e)
    gate_all = jnp.sum(jnp.where(mine, gate_all, 0.0), axis=(1, 2)).reshape(n_e, 1, count)
    gate_all = tied(gate_all, *first(down_parts[1]))
    cot_rows, gate_rows = dispatch(cot_all, None, packing, order, gate_all)
    weighted, row_grad, expert_act, route_grad, pre_grad, gate_grad = expert(
        packing[2],
        arrived,
        cot_rows,
        gate_rows,
        [part for parts in up_parts for part in parts],
        [part for parts in down_parts for part in parts],
    )

    shared_pre = dot(norm_two_all, share_w)
    shared_act = (
        jax.nn.silu(shared_pre[:, :shared_width]) * shared_pre[:, shared_width:]
    ).astype(BF16)
    shared_act_grad = dot_nt(cot_all, share_out)
    shared_pre_grad = silu_back(
        shared_act_grad, shared_pre[:, :shared_width], shared_pre[:, shared_width:]
    ).astype(BF16)
    norm_two_part = combine(
        packing, order, steady, me, row_grad, gate_grad, shared_pre_grad, share_w, True, 128
    )
    marks = []
    norm_two_grad = ring_scatter(
        lambda n: norm_two_part[n * count : (n + 1) * count], None, marks
    )
    gate_grad = norm_two_grad[:, width : width + n_e] + norm_two_grad[:, width + 64 : width + 64 + n_e]
    norm_two_grad = norm_two_grad[:, :width]
    out_part = combine(
        packing, order, order, me, weighted, gate_rows, shared_act, share_out, False, 0
    )
    routed_out = lax.psum_scatter(out_part, "expert", scatter_dimension=0, tiled=True)

    def shard_grads(left, right, chunks):
        size = left.shape[1] // n_dp
        part = size // chunks
        cut = lambda start, wide: tied(lax.dynamic_slice_in_dim(left, start, wide, 1), *marks)
        got = [
            [
                lax.ppermute(
                    dot_tn(cut((here + step) % n_dp * size + j * part, part), right).astype(BF16),
                    "dp",
                    [(i, (i + step) % n_dp) for i in range(n_dp)],
                )
                for step in range(1, n_dp)
            ]
            for j in range(chunks)
        ]
        return dot_tn(cut(here * size, size), right), got

    def shard_sum(own, got, tokens):
        part = own.shape[0] // len(got)
        own = own[None]
        for j, (parts, token) in enumerate(zip(got, tokens)):
            block = sum(tied(p.astype(F32), token) for p in parts)[None]
            block = own[:, j * part : (j + 1) * part] + block
            own = lax.dynamic_update_slice_in_dim(own, block, j * part, 1)
        return own

    down_own, down_got = shard_grads(expert_act, route_grad, 2)
    up_own, up_got = shard_grads(arrived, pre_grad, len(up_parts) - 1)

    share_out_grad = dp_scatter(dot_tn(shared_act, cot_all).reshape(n_dp, shared_rows, width))
    share_in_grad = dot_tn(norm_two_all, shared_pre_grad)
    share_in_grad = dp_scatter(share_in_grad.reshape(n_dp, n_e, rows, 2 * shared_width))
    share_in_grad = swap(share_in_grad.astype(BF16)).astype(F32)
    share_in_grad = (
        share_in_grad.reshape(n_e, rows, 2, n_dp, shared_rows)
        .transpose(1, 2, 3, 0, 4)
        .reshape(rows, -1)
    )

    logit_grad = gates * (gate_grad - jnp.sum(gates * gate_grad, axis=-1, keepdims=True))
    router_grad = jnp.dot(
        logit_grad.T, norm_two.astype(F32), precision=HIGHEST, preferred_element_type=F32
    )
    norm_two_grad = norm_two_grad + jnp.dot(
        logit_grad, router_full.astype(F32), precision=HIGHEST, preferred_element_type=F32
    )
    gain_two_grad = jnp.sum(norm_two_grad * normed_two, axis=0)
    upstream = cotangent.astype(F32)
    scaled_two = norm_two_grad * gain_second
    resid_grad = upstream + inverse_two * (
        scaled_two - normed_two * jnp.mean(scaled_two * normed_two, axis=-1, keepdims=True)
    )
    small_grad = jnp.concatenate([router_grad, gain_two_grad[None]], axis=0)

    branch_cot = resid_grad.astype(BF16)
    split = HEAD_DIM // rows
    proj_all = proj_all.reshape(n_e, n_dp, rows, width)
    owners = [(me * split + r) % n_e for r in range(split)], [(me * split + r) // n_e for r in range(split)]
    head_out_w = jnp.concatenate(
        [lax.dynamic_slice(proj_all, (e, d, 0, 0), (1, 1, rows, width))[0, 0] for e, d in zip(*owners)]
    )
    branch_blocks = ring_gather(
        branch_cot,
        {half - 1: lambda blocks: down_got[0], half: lambda blocks: down_got[1]},
    )
    qkv_grad, proj_grad = attend_back(
        branch_blocks, order, head_out_w, query, key, value, head_out, lse, first_place, cos_table, sin_table
    )
    proj_grad = proj_grad.astype(BF16)
    attn_out_grad = 0.0
    for r in range(split):
        for shift in range(n_dp):
            perm = [
                (((h * split + r) // n_e + shift) % n_dp * n_e + h, h * split + r)
                for h in range(n_e)
            ]
            part = lax.ppermute(proj_grad[r * rows : (r + 1) * rows], ("dp", "expert"), perm)
            attn_out_grad = attn_out_grad + part.astype(F32)
    small_grad = tied(small_grad, qkv_grad).reshape(n_e + 1, n_dp * n_e, rows).transpose(1, 0, 2)
    small_grad = lax.all_to_all(
        small_grad, ("dp", "expert"), split_axis=0, concat_axis=0, tiled=True
    )
    small_grad = jnp.sum(small_grad, axis=0)
    norm_one_part = dot_nt(qkv_grad, head_w).astype(BF16)
    scaled_one = ring_scatter(
        lambda n: norm_one_part[n * count : (n + 1) * count],
        {1: up_got[0], half - 1: up_got[min(1, len(up_got) - 1)]},
    )
    expert_out_grad = shard_sum(down_own, down_got, [branch_cot, qkv_grad])
    expert_in_grad = shard_sum(up_own, up_got, ([qkv_grad] + [scaled_one] * 3)[: len(up_got)])
    input_grad = resid_grad + inverse_one * (
        scaled_one - normed_one * jnp.mean(scaled_one * normed_one, axis=-1, keepdims=True)
    )
    head_grad = dot_tn(norm_all, qkv_grad).reshape(n_dp, n_e, rows, 3 * HEAD_DIM)
    head_grad = swap(dp_scatter(head_grad).astype(BF16)).astype(F32)
    head_grad = (
        head_grad.reshape(n_e, rows, 3, HEAD_DIM).transpose(1, 2, 0, 3).reshape(rows, 3 * width)
    )
    gain_attn_grad = jnp.sum(head_grad * attn_in.astype(F32), axis=1)
    attn_in_grad = head_grad * gain_rows
    return (
        (resid + routed_out.astype(F32)).astype(BF16),
        input_grad.astype(BF16),
        attn_in_grad,
        attn_out_grad,
        gain_attn_grad,
        share_in_grad,
        share_out_grad,
        small_grad[:n_e].T,
        small_grad[n_e],
        expert_in_grad,
        expert_out_grad,
    )


def solution(mesh):
    return jax.shard_map(
        per_device,
        mesh=mesh,
        in_specs=(
            P(("dp", "expert"), None),
            P(("dp", "expert"), None),
            P("dp", None),
            P(("dp", "expert"), None),
            P(("dp", "expert"), None),
            P(("dp", "expert"), None),
            P(("dp", "expert")),
            P(("dp", "expert"), None),
            P(("dp", "expert"), None),
            P(("dp", "expert"), None),
            P(("dp", "expert")),
            P("expert", "dp", None),
            P("expert", "dp", None),
        ),
        out_specs=(
            P(("dp", "expert"), None),
            P(("dp", "expert"), None),
            P(("dp", "expert"), None),
            P(("dp", "expert"), None),
            P(("dp", "expert")),
            P(("dp", "expert"), None),
            P(("dp", "expert"), None),
            P(("dp", "expert"), None),
            P(("dp", "expert")),
            P("expert", "dp", None),
            P("expert", "dp", None),
        ),
        check_vma=False,
    )
```

```python
import functools
import math

import jax
import jax.numpy as jnp
from jax import lax
from jax.experimental import pallas as pl
from jax.experimental.pallas import tpu as pltpu
from jax.sharding import PartitionSpec as P

HEADS = 16
HEAD_DIM = 128
TOP = 6


EPS = 1e-06
THETA = 10000.0
NEG = -1e30
HIGHEST = lax.Precision.HIGHEST
BF16 = jnp.bfloat16
F32 = jnp.float32
LOG2E = math.log2(math.e)


def rope_tables(segments):
    length = segments.shape[0]
    places = jnp.arange(length, dtype=jnp.int32)
    starts = jnp.concatenate([jnp.ones((1,), dtype=jnp.bool_), segments[1:] != segments[:-1]])
    first_place = lax.cummax(jnp.where(starts, places, 0), axis=0)
    offset = (places - first_place).astype(jnp.float32)
    half_dim = HEAD_DIM // 2
    freqs = jnp.exp(jnp.arange(half_dim, dtype=jnp.float32) * (-2.0 * math.log(THETA) / HEAD_DIM))
    angles = offset[:, None] * freqs[None, :]
    cos_table, sin_table = jnp.cos(angles), jnp.sin(angles)
    return (
        jnp.concatenate([cos_table, cos_table], axis=1),
        jnp.concatenate([-sin_table, sin_table], axis=1),
        first_place[None, :],
    )


def silu_back(grad_act, gate_part, up_part):
    sigmoid_gate = jax.nn.sigmoid(gate_part)
    gate_grad = grad_act * up_part * sigmoid_gate * (1.0 + gate_part * (1.0 - sigmoid_gate))
    up_grad = grad_act * gate_part * sigmoid_gate
    return jnp.concatenate([gate_grad, up_grad], axis=-1)


def dot(left, right):
    return jnp.dot(left, right, preferred_element_type=F32)


def dot_tn(left, right):
    return lax.dot_general(left, right, (((0,), (0,)), ((), ())), preferred_element_type=F32)


def dot_nt(left, right):
    return lax.dot_general(left, right, (((1,), (1,)), ((), ())), preferred_element_type=F32)


def cost(micros):
    return pl.CostEstimate(flops=int(micros * 1.1e9), bytes_accessed=0, transcendentals=0)


def turn(values, cos_table, sin_table):
    return values * cos_table + pltpu.roll(values, HEAD_DIM // 2, 1) * sin_table


def attend_kernel(sources, block, order_ref, *refs):
    pieces = refs[: sources[-1][-1] + 1]
    weight_ref, cos_ref, sin_ref, start_ref = refs[len(pieces) : len(pieces) + 4]
    o_ref, q_ref, k_ref, v_ref, lse_ref, rows_ref, vt_ref = refs[len(pieces) + 4 :]
    step = pl.program_id(0)
    length = q_ref.shape[0]
    factor = HEAD_DIM ** (-0.5) * LOG2E
    rows = rows_ref.shape[0]

    for n, parts in enumerate(sources):

        @pl.when(step == n)
        def _(parts=parts):
            low = 0
            for part in parts:
                size = pieces[part].shape[0]
                rows_ref[low : low + size, :] = pieces[part][...]
                low += size

    @pl.when(step < len(sources))
    def _():
        qkv = dot(rows_ref[...], weight_ref[...])
        at = pl.ds(pl.multiple_of(order_ref[step] * rows, rows), rows)
        cos_table, sin_table = cos_ref[at, :], sin_ref[at, :]
        q_ref[at, :] = turn(qkv[:, :HEAD_DIM], cos_table, sin_table).astype(BF16)
        k_ref[at, :] = turn(qkv[:, HEAD_DIM : 2 * HEAD_DIM], cos_table, sin_table).astype(BF16)
        value = qkv[:, 2 * HEAD_DIM :]
        v_ref[at, :] = value.astype(BF16)
        vt_ref[:, at] = value.T.astype(BF16)

    for i in range(length // block):

        @pl.when(step == len(sources) + i)
        def _(i=i):
            low, high = i * block, (i + 1) * block
            raw = dot_nt(k_ref[:high, :], q_ref[low:high, :])
            keys = lax.broadcasted_iota(jnp.int32, raw.shape, 0)
            queries = low + lax.broadcasted_iota(jnp.int32, raw.shape, 1)
            allowed = (keys <= queries) & (keys >= start_ref[:, low:high])
            raw = jnp.where(allowed, raw, NEG)
            top = jnp.max(raw, axis=0, keepdims=True)
            shifted = jnp.exp2((raw - top) * factor)
            total = jnp.sum(shifted, axis=0, keepdims=True)
            probs = (shifted * (1.0 / total)).astype(BF16)
            mixed = dot(vt_ref[:, :high], probs)
            o_ref[low:high, :] = mixed.T.astype(BF16)
            lse_ref[:, low:high] = top * factor + jnp.log2(total)


def attend(blocks, order, weight, cos_table, sin_table, first_place):
    pieces, sources = flatten(blocks)
    length = cos_table.shape[0]
    rows = length // len(sources)
    width = weight.shape[0]
    block = min(256, length)
    last = len(sources) - 1
    whole = lambda shape: pl.BlockSpec(shape, lambda i, order: (0, 0))
    head = jax.ShapeDtypeStruct((length, HEAD_DIM), BF16)
    return pl.pallas_call(
        functools.partial(attend_kernel, sources, block),
        out_shape=[head] * 4
        + [jax.ShapeDtypeStruct((1, length), F32), jax.ShapeDtypeStruct((length, width), BF16)],
        grid_spec=pltpu.PrefetchScalarGridSpec(
            num_scalar_prefetch=1,
            grid=(len(sources) + length // block,),
            in_specs=[whole(piece.shape) for piece in pieces]
            + [
                whole(weight.shape),
                whole((length, HEAD_DIM)),
                whole((length, HEAD_DIM)),
                whole((1, length)),
            ],
            out_specs=[whole((length, HEAD_DIM))] * 4
            + [
                whole((1, length)),
                pl.BlockSpec((rows, width), lambda i, order: (jnp.minimum(i, last), 0)),
            ],
            scratch_shapes=[pltpu.VMEM((HEAD_DIM, length), BF16)],
        ),
        compiler_params=pltpu.CompilerParams(vmem_limit_bytes=52 * 2**20),
        cost_estimate=cost(28),
        name="attend",
    )(order, *pieces, weight, cos_table, sin_table, first_place)


def attend_back_kernel(sources, block, order_ref, *refs):
    pieces = refs[: sources[-1][-1] + 1]
    (
        weight_ref, q_ref, k_ref, v_ref, o_ref, lse_ref, start_ref, cos_ref, sin_ref,
        out_ref, weight_grad_ref,
        rows_ref, kt_ref, do_ref, dq_ref, dk_ref, dv_ref,
    ) = refs[len(pieces) :]
    length = q_ref.shape[0]
    rows = rows_ref.shape[0]
    step = pl.program_id(0)
    scale = HEAD_DIM ** (-0.5)
    factor = scale * LOG2E
    blocks = len(sources)
    count = length // block

    @pl.when(step == 0)
    def _():
        kt_ref[...] = k_ref[...].astype(F32).T.astype(BF16)
        dk_ref[...] = jnp.zeros_like(dk_ref)
        dv_ref[...] = jnp.zeros_like(dv_ref)
        weight_grad_ref[...] = jnp.zeros_like(weight_grad_ref)

    for n, parts in enumerate(sources):

        @pl.when(step == n)
        def _(parts=parts):
            low = 0
            for part in parts:
                size = pieces[part].shape[0]
                rows_ref[low : low + size, :] = pieces[part][...]
                low += size

    @pl.when(step < blocks)
    def _():
        at = pl.ds(pl.multiple_of(order_ref[step] * rows, rows), rows)
        do_ref[at, :] = dot_nt(rows_ref[...], weight_ref[...]).astype(BF16)
        weight_grad_ref[...] += dot_tn(o_ref[at, :], rows_ref[...])

    for i in range(count):

        @pl.when(step == blocks + i)
        def _(i=i):
            low, high = i * block, (i + 1) * block
            query, grad = q_ref[low:high, :], do_ref[low:high, :]
            raw = dot_nt(k_ref[:high, :], query)
            keys = lax.broadcasted_iota(jnp.int32, raw.shape, 0)
            queries = low + lax.broadcasted_iota(jnp.int32, raw.shape, 1)
            allowed = (keys <= queries) & (keys >= start_ref[:, low:high])
            raw = jnp.where(allowed, raw * factor - lse_ref[:, low:high], NEG)
            probs = jnp.exp2(raw)
            probs_grad = dot_nt(v_ref[:high, :], grad)
            inner = jnp.sum(probs_grad * probs, axis=0, keepdims=True)
            score_grad = (probs * (probs_grad - inner)).astype(BF16)
            dv_ref[:high, :] += dot(probs.astype(BF16), grad)
            dk_ref[:high, :] += dot(score_grad, query)
            dq_ref[low:high, :] = dot(kt_ref[:, :high], score_grad).T

    @pl.when(step == blocks + count - 1)
    def _():
        for n in range(blocks):
            at = pl.ds(pl.multiple_of(order_ref[n] * rows, rows), rows)
            to = slice(n * rows, (n + 1) * rows)
            cos_table, sin_table = cos_ref[at, :], -sin_ref[at, :]
            out_ref[to, :HEAD_DIM] = turn(dq_ref[at, :] * scale, cos_table, sin_table).astype(BF16)
            out_ref[to, HEAD_DIM : 2 * HEAD_DIM] = turn(
                dk_ref[at, :] * scale, cos_table, sin_table
            ).astype(BF16)
            out_ref[to, 2 * HEAD_DIM :] = dv_ref[at, :].astype(BF16)


def attend_back(grads, order, weight, query, key, value, mixed, lse, first_place, cos_table, sin_table):
    pieces, sources = flatten(grads)
    length = query.shape[0]
    block = min(256, length)
    rows = length // len(sources)
    whole = lambda shape: pl.BlockSpec(shape, lambda i, order: (0, 0))
    head = whole((length, HEAD_DIM))
    return pl.pallas_call(
        functools.partial(attend_back_kernel, sources, block),
        out_shape=[
            jax.ShapeDtypeStruct((length, 3 * HEAD_DIM), BF16),
            jax.ShapeDtypeStruct(weight.shape, F32),
        ],
        grid_spec=pltpu.PrefetchScalarGridSpec(
            num_scalar_prefetch=1,
            grid=(len(sources) + length // block,),
            in_specs=[whole(piece.shape) for piece in pieces]
            + [whole(weight.shape)]
            + [head] * 4
            + [whole((1, length))] * 2
            + [head] * 2,
            out_specs=[whole((length, 3 * HEAD_DIM)), whole(weight.shape)],
            scratch_shapes=[
                pltpu.VMEM((rows, weight.shape[1]), BF16),
                pltpu.VMEM((HEAD_DIM, length), BF16),
                pltpu.VMEM((length, HEAD_DIM), BF16),
            ]
            + [pltpu.VMEM((length, HEAD_DIM), F32)] * 3,
        ),
        compiler_params=pltpu.CompilerParams(vmem_limit_bytes=56 * 2**20),
        cost_estimate=cost(30),
        name="attend_back",
    )(order, *pieces, weight, query, key, value, mixed, lse, first_place, cos_table, sin_table)


def dp_gather(value):
    count = lax.axis_size("dp")
    if count == 1:
        return value[None]
    here = lax.axis_index("dp")
    parts = [value] + [
        lax.ppermute(value, "dp", [(i, (i - step) % count) for i in range(count)])
        for step in range(1, count)
    ]
    if count == 2:
        first = here == 0
        return jnp.stack(
            [jnp.where(first, parts[0], parts[1]), jnp.where(first, parts[1], parts[0])]
        )
    whole = jnp.zeros((count,) + value.shape, value.dtype)
    for step, part in enumerate(parts):
        whole = lax.dynamic_update_index_in_dim(whole, part, (here + step) % count, 0)
    return whole


def dp_scatter(value):
    count = lax.axis_size("dp")
    here = lax.axis_index("dp")
    total = lax.dynamic_index_in_dim(value, here, 0, keepdims=False)
    for step in range(1, count):
        block = lax.dynamic_index_in_dim(value, (here + step) % count, 0, keepdims=False)
        got = lax.ppermute(
            block.astype(BF16), "dp", [(i, (i + step) % count) for i in range(count)]
        )
        total = total + got.astype(F32)
    return total


def ring_order():
    pairs = lax.axis_size("expert") // 2
    return list(range(0, pairs, 2)) + list(range(pairs - 1, 0, -2))


def ring_shift(value, step):
    order = ring_order()
    pairs = len(order)
    perm = [
        (order[q] * 2 + c, order[(q + step) % pairs] * 2 + c) for q in range(pairs) for c in range(2)
    ]
    return lax.ppermute(value, "expert", perm)


def core_swap(value):
    count = lax.axis_size("expert")
    return lax.ppermute(value, "expert", [(i, i ^ 1) for i in range(count)])


def ring_offsets():
    half = lax.axis_size("expert") // 4
    return [0] + [o for step in range(1, half) for o in (step, -step)] + [half]


def ring_blocks():
    order = ring_order()
    pairs = len(order)
    table = [[0] * (2 * pairs) for _ in range(2 * pairs)]
    for q in range(pairs):
        for c in range(2):
            for j, offset in enumerate(ring_offsets()):
                for other in range(2):
                    table[order[q] * 2 + c][2 * j + other] = (
                        order[(q - offset) % pairs] * 2 + (c ^ other)
                    )
    return lax.dynamic_index_in_dim(
        jnp.asarray(table, jnp.int32), lax.axis_index("expert"), 0, keepdims=False
    )


def tied(value, *tokens):
    firsts = [lax.slice(t, (0,) * t.ndim, (1,) * t.ndim).reshape(()) for t in tokens]
    token = sum(t.astype(F32) for t in firsts) * 0.0
    return (value.astype(F32) * (1.0 + token)).astype(value.dtype)


def ring_gather(value, gates=None):
    gates = gates or {}
    half_rows = value.shape[0] // 2
    half = lax.axis_size("expert") // 4
    blocks = {}

    def keep(parts, offset):
        blocks[offset] = (parts, [core_swap(part) for part in parts])

    keep([value], 0)
    ahead = back = value
    for step in range(1, half):
        if step in gates:
            token = gates[step](blocks)
            ahead, back = tied(ahead, *token), tied(back, *token)
        ahead, back = ring_shift(ahead, 1), ring_shift(back, -1)
        keep([ahead], step)
        keep([back], -step)
    if half in gates:
        token = gates[half](blocks)
        ahead, back = tied(ahead, *token), tied(back, *token)
    last = [ring_shift(ahead[:half_rows], 1), ring_shift(back[half_rows:], -1)]
    keep(last, half)
    return [parts for offset in ring_offsets() for parts in blocks[offset]]


def flatten(blocks):
    pieces = [piece for parts in blocks for piece in parts]
    sources, n = [], 0
    for parts in blocks:
        sources.append(tuple(range(n, n + len(parts))))
        n += len(parts)
    return pieces, tuple(sources)


def ring_scatter(block, gates=None, marks=None):
    gates = gates or {}
    half = lax.axis_size("expert") // 4
    offsets = ring_offsets()
    spare = {}

    def mine(offset):
        if offset not in spare:
            j = offsets.index(offset)
            spare[offset] = block(2 * j).astype(F32) + core_swap(block(2 * j + 1)).astype(F32)
        return spare[offset]

    far = mine(half).astype(BF16)
    half_rows = far.shape[0] // 2
    ahead = ring_shift(far[:half_rows], 1)
    back = ring_shift(far[half_rows:], -1)
    if marks is not None:
        marks.extend([ahead, back])
    for step in range(half - 1, 0, -1):
        onward, homeward = mine(-step), mine(step)
        if step == half - 1:
            onward = jnp.concatenate(
                [onward[:half_rows] + ahead.astype(F32), onward[half_rows:]], axis=0
            )
            homeward = jnp.concatenate(
                [homeward[:half_rows], homeward[half_rows:] + back.astype(F32)], axis=0
            )
        else:
            onward = onward + ahead.astype(F32)
            homeward = homeward + back.astype(F32)
        if half - step in gates:
            onward, homeward = tied(onward, *gates[half - step]), tied(homeward, *gates[half - step])
        ahead = ring_shift(onward.astype(BF16), 1)
        back = ring_shift(homeward.astype(BF16), -1)
    return mine(0) + ahead.astype(F32) + back.astype(F32)


def chosen(pos_ref, base, window):
    count = pos_ref.shape[-1]
    row = base + lax.broadcasted_iota(jnp.int32, (window, count), 0)
    return row == pos_ref[0]


def dispatch_kernel(sources, widths, window, base_ref, order_ref, pos_ref, gate_ref, *refs):
    outs = refs[-len(widths) - 2 :]
    pieces, blocks, rows_ref, weights_ref = refs[: -len(outs)], outs[:-2], outs[-2], outs[-1]
    step = pl.program_id(0)

    @pl.when(step == 0)
    def _():
        rows_ref[...] = jnp.zeros_like(rows_ref)
        weights_ref[...] = jnp.zeros_like(weights_ref)

    for n, parts in enumerate(sources):

        @pl.when(step == n)
        def _(parts=parts):
            low = 0
            for part in parts:
                size = pieces[part].shape[0]
                left = 0
                for block, wide in zip(blocks, widths):
                    block[low : low + size, :] = pieces[part][:, left : left + wide]
                    left += wide
                low += size

    base = pl.multiple_of(base_ref[step], 16)
    pick = chosen(pos_ref, base, window)
    at = pl.ds(base, window)
    found = dot(pick.astype(F32).astype(BF16), (blocks or pieces)[0][...])
    rows_ref[at, :] = (rows_ref[at, :].astype(F32) + found).astype(BF16)
    weights_ref[at, :] += jnp.sum(jnp.where(pick, gate_ref[0], 0.0), axis=1, keepdims=True)


def dispatch(blocks, widths, packing, order, gates):
    base, pos, _, window, packed = packing
    count, _, rows = pos.shape
    if isinstance(blocks, list):
        pieces, sources = flatten(blocks)
        piece_specs = [pl.BlockSpec(piece.shape, lambda i, base, order: (0, 0)) for piece in pieces]
    else:
        pieces, sources, widths = [blocks], (), []
        piece_specs = [pl.BlockSpec((rows, blocks.shape[1]), lambda i, base, order: (order[i], 0))]
    width = (widths or [pieces[0].shape[1]])[0]
    return pl.pallas_call(
        functools.partial(dispatch_kernel, sources, tuple(widths), window),
        out_shape=[jax.ShapeDtypeStruct((rows * count, wide), BF16) for wide in widths]
        + [
            jax.ShapeDtypeStruct((packed, width), BF16),
            jax.ShapeDtypeStruct((packed, 1), F32),
        ],
        grid_spec=pltpu.PrefetchScalarGridSpec(
            num_scalar_prefetch=2,
            grid=(count,),
            in_specs=[
                pl.BlockSpec((1, 1, rows), lambda i, base, order: (i, 0, 0)),
                pl.BlockSpec((1, 1, rows), lambda i, base, order: (order[i], 0, 0)),
            ]
            + piece_specs,
            out_specs=[
                pl.BlockSpec((rows, wide), lambda i, base, order: (order[i], 0)) for wide in widths
            ]
            + [
                pl.BlockSpec((packed, width), lambda i, base, order: (0, 0)),
                pl.BlockSpec((packed, 1), lambda i, base, order: (0, 0)),
            ],
        ),
        compiler_params=pltpu.CompilerParams(vmem_limit_bytes=52 * 2**20),
        cost_estimate=cost(13),
        name="dispatch",
    )(base, order, pos, gates, *pieces)


def fetch(parts, starts_ref, wholes, counts, sems):
    copies, n = [], 0
    for whole, count in zip(wholes, counts):
        copies.append([])
        for _ in range(count):
            at = pl.ds(pl.multiple_of(starts_ref[n], 16), parts[n].shape[0])
            copies[-1].append(pltpu.make_async_copy(parts[n], whole.at[at, :], sems.at[n]))
            n += 1
    return copies


def expert_kernel(counts, total_ref, starts_ref, x_ref, *refs):
    parts, refs = refs[: sum(counts)], refs[sum(counts) :]
    pre_ref, ea_ref, y_ref, up_ref, down_ref, sems = refs
    step = pl.program_id(0)
    rows, hidden = ea_ref.shape
    ups, downs = fetch(parts, starts_ref, (up_ref, down_ref), counts, sems)
    some = (step == 0) | (step * rows < total_ref[0])

    @pl.when(step == 0)
    def _():
        for copy in ups + downs:
            copy.start()
        for copy in ups:
            copy.wait()

    @pl.when(some)
    def _():
        pre = dot(x_ref[...], up_ref[...])
        pre_ref[...] = pre
        gate_part = pre[:, :hidden]
        act = (gate_part / (1.0 + jnp.exp(-gate_part)) * pre[:, hidden:]).astype(BF16)
        ea_ref[...] = act

        @pl.when(step == 0)
        def _():
            for copy in downs:
                copy.wait()

        y_ref[...] = dot(act, down_ref[...]).astype(BF16)

    @pl.when(jnp.logical_not(some))
    def _():
        for ref in (ea_ref, y_ref):
            ref[...] = jnp.zeros_like(ref)


def expert_back_kernel(counts, total_ref, starts_ref, g_ref, gate_ref, pre_ref, y_ref, *refs):
    parts, refs = refs[: sum(counts)], refs[sum(counts) :]
    dn_ref, dy_ref, db_ref, dg_ref, down_ref, up_ref, sems = refs
    step = pl.program_id(0)
    rows = g_ref.shape[0]
    hidden = down_ref.shape[0]
    downs, ups = fetch(parts, starts_ref, (down_ref, up_ref), counts, sems)
    some = (step == 0) | (step * rows < total_ref[0])

    @pl.when(step == 0)
    def _():
        for copy in downs + ups:
            copy.start()
        for copy in downs:
            copy.wait()

    @pl.when(some)
    def _():
        grad = g_ref[...].astype(F32)
        dg_ref[...] = jnp.sum(grad * y_ref[...].astype(F32), axis=1, keepdims=True)
        out_grad = (gate_ref[...] * grad).astype(BF16)
        dy_ref[...] = out_grad
        act_grad = dot_nt(out_grad, down_ref[...])
        gate_part, up_part = pre_ref[:, :hidden], pre_ref[:, hidden:]
        sigmoid_gate = 1.0 / (1.0 + jnp.exp(-gate_part))
        db_ref[:, :hidden] = (
            act_grad * up_part * sigmoid_gate * (1.0 + gate_part * (1.0 - sigmoid_gate))
        ).astype(BF16)
        db_ref[:, hidden:] = (act_grad * gate_part * sigmoid_gate).astype(BF16)

        @pl.when(step == 0)
        def _():
            for copy in ups:
                copy.wait()

        dn_ref[...] = dot_nt(db_ref[...], up_ref[...]).astype(BF16)

    @pl.when(jnp.logical_not(some))
    def _():
        for ref in (dn_ref, dy_ref, db_ref, dg_ref):
            ref[...] = jnp.zeros_like(ref)


def expert_call(kernel, name, total, tiled, weights, outs):
    packed = tiled[0].shape[0]
    tile = 256
    parts = [part for group in weights for part, _ in group]
    starts = jnp.stack([start for group in weights for _, start in group]).astype(jnp.int32)
    spec = lambda wide: pl.BlockSpec((tile, wide), lambda i, total, starts: (i, 0))
    return pl.pallas_call(
        functools.partial(kernel, tuple(len(group) for group in weights)),
        out_shape=[jax.ShapeDtypeStruct((packed, wide), kind) for wide, kind in outs],
        grid_spec=pltpu.PrefetchScalarGridSpec(
            num_scalar_prefetch=2,
            grid=(packed // tile,),
            in_specs=[spec(array.shape[1]) for array in tiled]
            + [pl.BlockSpec(memory_space=pl.ANY)] * len(parts),
            out_specs=[spec(wide) for wide, _ in outs],
            scratch_shapes=[
                pltpu.VMEM((sum(p.shape[0] for p, _ in group), group[0][0].shape[1]), BF16)
                for group in weights
            ]
            + [pltpu.SemaphoreType.DMA((len(parts),))],
        ),
        compiler_params=pltpu.CompilerParams(vmem_limit_bytes=58 * 2**20),
        cost_estimate=cost(27),
        name=name,
    )(total, starts, *tiled, *parts)


def upright(line):
    count = line.shape[1]
    row = lax.broadcasted_iota(jnp.int32, (count, count), 0)
    lane = lax.broadcasted_iota(jnp.int32, (count, count), 1)
    return jnp.sum(jnp.where(row == lane, line, 0.0), axis=1, keepdims=True)


def combine_kernel(turned, window, extra, base_ref, order_ref, to_ref, me_ref, pos_ref, rows_ref, side_ref, act_ref, weight_ref, out_ref):
    base = pl.multiple_of(base_ref[pl.program_id(0)], 16)
    pick = chosen(pos_ref, base, window)
    at = pl.ds(base, window)
    width = rows_ref.shape[1]
    found = dot_tn(pick.astype(F32).astype(BF16), rows_ref[at, :])
    if not turned:
        found = found * upright(side_ref[0])
    found = found + (dot_nt if turned else dot)(act_ref[...], weight_ref[...])
    out_ref[:, :width] = found.astype(BF16)
    if turned:
        line = jnp.sum(jnp.where(pick, side_ref[at, :], 0.0), axis=0, keepdims=True)
        column = upright(line)
        high = column.astype(BF16).astype(F32)
        lane = lax.broadcasted_iota(jnp.int32, (pick.shape[1], extra), 1)
        out_ref[:, width:] = jnp.where(
            lane == me_ref[0], high, jnp.where(lane == me_ref[0] + extra // 2, column - high, 0.0)
        ).astype(BF16)


def combine(packing, order, to, me, rows, side, act, weight, turned, extra):
    base, pos, _, window, packed = packing
    blocks, _, count = pos.shape
    width = rows.shape[-1]
    whole = lambda ref: pl.BlockSpec(ref.shape, lambda i, *_: (0, 0))
    return pl.pallas_call(
        functools.partial(combine_kernel, turned, window, extra),
        out_shape=jax.ShapeDtypeStruct((blocks * count, width + extra), BF16),
        grid_spec=pltpu.PrefetchScalarGridSpec(
            num_scalar_prefetch=4,
            grid=(blocks,),
            in_specs=[
                pl.BlockSpec((1, 1, count), lambda i, *_: (i, 0, 0)),
                whole(rows),
                whole(side)
                if turned
                else pl.BlockSpec((1, 1, count), lambda i, base, order, to, me: (order[i], 0, 0)),
                pl.BlockSpec((count, act.shape[1]), lambda i, base, order, to, me: (order[i], 0)),
                whole(weight),
            ],
            out_specs=pl.BlockSpec(
                (count, width + extra), lambda i, base, order, to, me: (to[i], 0)
            ),
        ),
        compiler_params=pltpu.CompilerParams(vmem_limit_bytes=40 * 2**20),
        cost_estimate=cost(10),
        name="combine",
    )(base, order, to, me.reshape(1), pos, rows, side, act, weight)


def gather_all(value):
    return lax.all_gather(value, "expert", axis=0, tiled=True)


def swap(value):
    return lax.all_to_all(value, "expert", split_axis=0, concat_axis=0, tiled=True)


def per_device(
    tokens,
    cotangent,
    segment_ids,
    routes,
    attn_in,
    attn_out,
    gain_attn,
    shared_in,
    shared_out,
    router,
    gain_ffn,
    expert_in,
    expert_out,
):
    n_dp, n_e = lax.axis_size("dp"), lax.axis_size("expert")
    me = lax.axis_index("expert")
    count, width = tokens.shape
    segments = segment_ids[0]
    length = segments.shape[0]
    rows = attn_in.shape[0]
    capacity = min(count, 3 * TOP * count // (2 * n_e))
    shared_rows = shared_out.shape[0]
    shared_width = shared_rows * n_dp
    expert_width = expert_out.shape[1] * n_dp

    order = ring_blocks()
    steady = jnp.arange(n_e, dtype=jnp.int32)
    hidden_in = tokens.astype(F32)
    inverse_one = lax.rsqrt(jnp.mean(hidden_in * hidden_in, axis=-1, keepdims=True) + EPS)
    normed_one = hidden_in * inverse_one
    gain_rows = gain_attn.astype(F32)[:, None]
    head_w = []

    def head_sent(blocks):
        own = (attn_in.astype(F32) * tied(gain_rows, blocks[0][1][0])).astype(BF16)
        own = own.reshape(rows, 3, n_e, HEAD_DIM).transpose(2, 0, 1, 3)
        head_w.append(swap(own.reshape(n_e, rows, 3 * HEAD_DIM)))
        return head_w[0]

    def head_whole(blocks):
        head_w.append(dp_gather(head_w[0]).reshape(width, 3 * HEAD_DIM))
        return head_w[1]

    here = lax.axis_index("dp")

    def spread(shard, chunks):
        while shard.shape[0] % (16 * chunks):
            chunks -= 1
        size = shard.shape[0] // chunks
        parts = [[(shard, here * shard.shape[0])]]
        for j in range(chunks):
            parts.append([])
            for step in range(1, n_dp):
                got = lax.ppermute(
                    shard[j * size : (j + 1) * size],
                    "dp",
                    [(i, (i - step) % n_dp) for i in range(n_dp)],
                )
                parts[-1].append((got, (here + step) % n_dp * shard.shape[0] + j * size))
        return parts

    up_parts = spread(expert_in[0], max(1, min(4, expert_in.shape[1] // 256)))
    down_parts = spread(expert_out[0], 2)
    first = lambda parts: [part for part, _ in parts]
    up_tokens = [first(parts) for parts in up_parts[1:]] + [[]] * 4

    small = jnp.concatenate([router, gain_ffn[:, None]], axis=1)
    small = dp_gather(small).reshape(-1, n_e + 1)
    extra_rows = 32
    extra = jnp.concatenate([small.T, routes.T.astype(BF16)], axis=0)
    extra = jnp.pad(extra, ((0, extra_rows - extra.shape[0]), (0, 0)))
    extra = jnp.broadcast_to(extra, (n_e,) + extra.shape)
    cos_table, sin_table, first_place = rope_tables(segments)
    share_w = shared_in.reshape(rows, 2, n_dp, n_e, shared_rows).transpose(3, 0, 1, 2, 4)
    share_w = share_w.reshape(n_e, rows, 2 * shared_width)

    half = n_e // 4
    norm_blocks = ring_gather(
        normed_one.astype(BF16),
        {
            half - 1: lambda blocks: [head_sent(blocks)] + up_tokens[0],
            half: lambda blocks: [head_whole(blocks), cos_table, sin_table, extra, share_w],
        },
    )
    head_sent_w, head_w = head_w

    head_out, query, key, value, lse, norm_all = attend(
        norm_blocks, order, head_w, cos_table, sin_table, first_place
    )
    mixed = jnp.concatenate([head_out.reshape(n_e, count, HEAD_DIM), extra], axis=1)
    share_w = swap(tied(share_w, head_sent_w))
    mixed = swap(tied(mixed, share_w, *up_tokens[1]))
    small = mixed[:, count:]
    mixed = mixed[:, :count].transpose(1, 0, 2).reshape(count, n_dp, n_e, rows)
    mixed = mixed.transpose(0, 2, 1, 3).reshape(count, width)
    proj_all = dp_gather(attn_out).reshape(n_dp * rows, width)
    proj_all = gather_all(tied(proj_all, norm_blocks[-3][0], norm_blocks[-5][0]))
    routes_all = small[:, n_e + 1 : n_e + 1 + TOP].astype(F32)
    small = small[:, : n_e + 1].reshape(n_e, n_e + 1, n_dp, rows).transpose(1, 2, 0, 3)
    small = small.reshape(n_e + 1, width)
    router_full = small[:n_e]
    gain_second = small[n_e].astype(F32)

    share_sent = share_w
    share_w = dp_gather(share_w).reshape(width, 2 * shared_width)
    share_out = dp_gather(shared_out).reshape(shared_width, width)
    resid = hidden_in + dot(mixed, proj_all)

    inverse_two = lax.rsqrt(jnp.mean(resid * resid, axis=-1, keepdims=True) + EPS)
    normed_two = resid * inverse_two
    norm_two = (normed_two * gain_second).astype(BF16)
    logits = dot_nt(norm_two, router_full)
    picked = jnp.any(routes[:, :, None] == jnp.arange(n_e)[None, None, :], axis=1)
    chosen = jnp.where(picked, logits, NEG)
    chosen = jnp.where(picked, jnp.exp(chosen - jnp.max(chosen, axis=-1, keepdims=True)), 0.0)
    gates = chosen / jnp.sum(chosen, axis=-1, keepdims=True)
    gate_high = gates.astype(BF16)
    gate_low = (gates - gate_high.astype(F32)).astype(BF16)
    blank = jnp.zeros((count, 128 - 2 * n_e), BF16)
    payload = jnp.concatenate([norm_two, gate_high, gate_low, blank], axis=1)
    norm_blocks = ring_gather(
        payload,
        {
            half - 1: lambda blocks: [share_sent] + up_tokens[2],
            half: lambda blocks: [share_sent] + up_tokens[3],
        },
    )

    cot_all = gather_all(tied(cotangent, norm_blocks[-1][0], norm_blocks[-1][1]))

    named = jnp.any(routes_all == me.astype(F32), axis=1)
    named = jnp.take(named, order, axis=0)
    ranking = jnp.cumsum(named.astype(jnp.int32), axis=1)
    ends = jnp.cumsum(ranking[:, -1])
    begins = ends - ranking[:, -1]
    pos = jnp.where(named, begins[:, None] + ranking - 1, -1)[:, None, :]
    window = -(-(capacity + 15) // 16) * 16
    packed = -(-(n_e * capacity + 32) // 256) * 256
    packing = (begins // 16 * 16, pos, ends[-1:], window, packed)
    norm_two_all, payload, arrived, _ = dispatch(
        norm_blocks, [width, 128], packing, order, jnp.zeros((n_e, 1, count), F32)
    )
    mine = jnp.arange(n_e) == me
    gate_all = payload[:, : 2 * n_e].astype(F32).reshape(length, 2, n_e)
    gate_all = jnp.sum(jnp.where(mine, gate_all, 0.0), axis=(1, 2)).reshape(n_e, 1, count)
    ups = [part for parts in up_parts for part in parts]
    downs = [part for parts in down_parts for part in parts]
    expert_width = expert_out.shape[1] * n_dp
    expert_pre, expert_act, expert_res = expert_call(
        expert_kernel,
        "expert",
        packing[2],
        [arrived],
        [ups, downs],
        [(2 * expert_width, F32), (expert_width, BF16), (width, BF16)],
    )

    shared_pre = dot(norm_two_all, share_w)
    shared_act = (
        jax.nn.silu(shared_pre[:, :shared_width]) * shared_pre[:, shared_width:]
    ).astype(BF16)
    out_part = combine(
        packing, order, order, me, expert_res, gate_all, shared_act, share_out, False, 0
    )
    routed_out = lax.psum_scatter(out_part, "expert", scatter_dimension=0, tiled=True)

    cot_rows, gate_rows = dispatch(cot_all, None, packing, order, gate_all)
    row_grad, route_grad, pre_grad, gate_grad = expert_call(
        expert_back_kernel,
        "expert_back",
        packing[2],
        [cot_rows, gate_rows, expert_pre, expert_res],
        [downs, ups],
        [(width, BF16), (width, BF16), (2 * expert_width, BF16), (1, F32)],
    )
    shared_act_grad = dot_nt(cot_all, share_out)
    shared_pre_grad = silu_back(
        shared_act_grad, shared_pre[:, :shared_width], shared_pre[:, shared_width:]
    ).astype(BF16)
    norm_two_part = combine(
        packing, order, steady, me, row_grad, gate_grad, shared_pre_grad, share_w, True, 128
    )
    marks = []
    norm_two_grad = ring_scatter(
        lambda n: norm_two_part[n * count : (n + 1) * count], None, marks
    )
    gate_grad = norm_two_grad[:, width : width + n_e] + norm_two_grad[:, width + 64 : width + 64 + n_e]
    norm_two_grad = norm_two_grad[:, :width]

    up_grad = dot_tn(tied(arrived, *marks), pre_grad).astype(BF16)
    expert_in_grad = lax.psum_scatter(up_grad, "dp", scatter_dimension=0, tiled=True)
    size = expert_out.shape[1]
    cut = lambda i: tied(lax.dynamic_slice_in_dim(expert_act, i % n_dp * size, size, 1), *marks)
    down_grad = dot_tn(cut(here), route_grad)
    down_got = [
        lax.ppermute(
            dot_tn(cut(here + step), route_grad).astype(BF16),
            "dp",
            [(i, (i + step) % n_dp) for i in range(n_dp)],
        )
        for step in range(1, n_dp)
    ]
    share_out_grad = dp_scatter(dot_tn(shared_act, cot_all).reshape(n_dp, shared_rows, width))
    share_in_grad = dot_tn(norm_two_all, shared_pre_grad)
    share_in_grad = dp_scatter(share_in_grad.reshape(n_dp, n_e, rows, 2 * shared_width))
    share_in_grad = swap(share_in_grad.astype(BF16)).astype(F32)
    share_in_grad = (
        share_in_grad.reshape(n_e, rows, 2, n_dp, shared_rows)
        .transpose(1, 2, 3, 0, 4)
        .reshape(rows, -1)
    )

    logit_grad = gates * (gate_grad - jnp.sum(gates * gate_grad, axis=-1, keepdims=True))
    router_grad = jnp.dot(
        logit_grad.T, norm_two.astype(F32), precision=HIGHEST, preferred_element_type=F32
    )
    norm_two_grad = norm_two_grad + jnp.dot(
        logit_grad, router_full.astype(F32), precision=HIGHEST, preferred_element_type=F32
    )
    gain_two_grad = jnp.sum(norm_two_grad * normed_two, axis=0)
    upstream = cotangent.astype(F32)
    scaled_two = norm_two_grad * gain_second
    resid_grad = upstream + inverse_two * (
        scaled_two - normed_two * jnp.mean(scaled_two * normed_two, axis=-1, keepdims=True)
    )
    small_grad = jnp.concatenate([router_grad, gain_two_grad[None]], axis=0)

    branch_cot = resid_grad.astype(BF16)
    split = HEAD_DIM // rows
    proj_all = proj_all.reshape(n_e, n_dp, rows, width)
    owners = [(me * split + r) % n_e for r in range(split)], [(me * split + r) // n_e for r in range(split)]
    head_out_w = jnp.concatenate(
        [lax.dynamic_slice(proj_all, (e, d, 0, 0), (1, 1, rows, width))[0, 0] for e, d in zip(*owners)]
    )
    branch_blocks = ring_gather(branch_cot)
    qkv_grad, proj_grad = attend_back(
        branch_blocks, order, head_out_w, query, key, value, head_out, lse, first_place, cos_table, sin_table
    )
    proj_grad = proj_grad.astype(BF16)
    attn_out_grad = 0.0
    for r in range(split):
        for shift in range(n_dp):
            perm = [
                (((h * split + r) // n_e + shift) % n_dp * n_e + h, h * split + r)
                for h in range(n_e)
            ]
            part = lax.ppermute(proj_grad[r * rows : (r + 1) * rows], ("dp", "expert"), perm)
            attn_out_grad = attn_out_grad + part.astype(F32)
    small_grad = tied(small_grad, qkv_grad).reshape(n_e + 1, n_dp * n_e, rows).transpose(1, 0, 2)
    small_grad = lax.all_to_all(
        small_grad, ("dp", "expert"), split_axis=0, concat_axis=0, tiled=True
    )
    small_grad = jnp.sum(small_grad, axis=0)
    norm_one_part = dot_nt(qkv_grad, head_w).astype(BF16)
    scaled_one = ring_scatter(
        lambda n: norm_one_part[n * count : (n + 1) * count], {1: down_got}
    )
    expert_in_grad = expert_in_grad.astype(F32)[None]
    expert_out_grad = (down_grad + sum(part.astype(F32) for part in down_got))[None]
    input_grad = resid_grad + inverse_one * (
        scaled_one - normed_one * jnp.mean(scaled_one * normed_one, axis=-1, keepdims=True)
    )
    head_grad = dot_tn(norm_all, qkv_grad).reshape(n_dp, n_e, rows, 3 * HEAD_DIM)
    head_grad = swap(dp_scatter(head_grad).astype(BF16)).astype(F32)
    head_grad = (
        head_grad.reshape(n_e, rows, 3, HEAD_DIM).transpose(1, 2, 0, 3).reshape(rows, 3 * width)
    )
    gain_attn_grad = jnp.sum(head_grad * attn_in.astype(F32), axis=1)
    attn_in_grad = head_grad * gain_rows
    return (
        (resid + routed_out.astype(F32)).astype(BF16),
        input_grad.astype(BF16),
        attn_in_grad,
        attn_out_grad,
        gain_attn_grad,
        share_in_grad,
        share_out_grad,
        small_grad[:n_e].T,
        small_grad[n_e],
        expert_in_grad,
        expert_out_grad,
    )


def solution(mesh):
    return jax.shard_map(
        per_device,
        mesh=mesh,
        in_specs=(
            P(("dp", "expert"), None),
            P(("dp", "expert"), None),
            P("dp", None),
            P(("dp", "expert"), None),
            P(("dp", "expert"), None),
            P(("dp", "expert"), None),
            P(("dp", "expert")),
            P(("dp", "expert"), None),
            P(("dp", "expert"), None),
            P(("dp", "expert"), None),
            P(("dp", "expert")),
            P("expert", "dp", None),
            P("expert", "dp", None),
        ),
        out_specs=(
            P(("dp", "expert"), None),
            P(("dp", "expert"), None),
            P(("dp", "expert"), None),
            P(("dp", "expert"), None),
            P(("dp", "expert")),
            P(("dp", "expert"), None),
            P(("dp", "expert"), None),
            P(("dp", "expert"), None),
            P(("dp", "expert")),
            P("expert", "dp", None),
            P("expert", "dp", None),
        ),
        check_vma=False,
    )
```

```python
import functools
import math

import jax
import jax.numpy as jnp
from jax import lax
from jax.experimental import pallas as pl
from jax.experimental.pallas import tpu as pltpu
from jax.sharding import PartitionSpec as P

HEADS = 16
HEAD_DIM = 128
TOP = 6


EPS = 1e-06
THETA = 10000.0
NEG = -1e30
HIGHEST = lax.Precision.HIGHEST
BF16 = jnp.bfloat16
F32 = jnp.float32
LOG2E = math.log2(math.e)


def rope_tables(segments):
    length = segments.shape[0]
    places = jnp.arange(length, dtype=jnp.int32)
    starts = jnp.concatenate([jnp.ones((1,), dtype=jnp.bool_), segments[1:] != segments[:-1]])
    first_place = lax.cummax(jnp.where(starts, places, 0), axis=0)
    offset = (places - first_place).astype(jnp.float32)
    half_dim = HEAD_DIM // 2
    freqs = jnp.exp(jnp.arange(half_dim, dtype=jnp.float32) * (-2.0 * math.log(THETA) / HEAD_DIM))
    angles = offset[:, None] * freqs[None, :]
    cos_table, sin_table = jnp.cos(angles), jnp.sin(angles)
    return (
        jnp.concatenate([cos_table, cos_table], axis=1),
        jnp.concatenate([-sin_table, sin_table], axis=1),
        first_place[None, :],
    )


def silu_back(grad_act, gate_part, up_part):
    sigmoid_gate = jax.nn.sigmoid(gate_part)
    gate_grad = grad_act * up_part * sigmoid_gate * (1.0 + gate_part * (1.0 - sigmoid_gate))
    up_grad = grad_act * gate_part * sigmoid_gate
    return jnp.concatenate([gate_grad, up_grad], axis=-1)


def dot(left, right):
    return jnp.dot(left, right, preferred_element_type=F32)


def dot_tn(left, right):
    return lax.dot_general(left, right, (((0,), (0,)), ((), ())), preferred_element_type=F32)


def dot_nt(left, right):
    return lax.dot_general(left, right, (((1,), (1,)), ((), ())), preferred_element_type=F32)


def cost(micros):
    return pl.CostEstimate(flops=int(micros * 1.1e9), bytes_accessed=0, transcendentals=0)


def turn(values, cos_table, sin_table):
    return values * cos_table + pltpu.roll(values, HEAD_DIM // 2, 1) * sin_table


def attend_kernel(sources, block, order_ref, *refs):
    pieces = refs[: sources[-1][-1] + 1]
    weight_ref, cos_ref, sin_ref, start_ref = refs[len(pieces) : len(pieces) + 4]
    o_ref, q_ref, k_ref, v_ref, lse_ref, rows_ref, vt_ref = refs[len(pieces) + 4 :]
    step = pl.program_id(0)
    length = q_ref.shape[0]
    factor = HEAD_DIM ** (-0.5) * LOG2E
    rows = rows_ref.shape[0]

    for n, parts in enumerate(sources):

        @pl.when(step == n)
        def _(parts=parts):
            low = 0
            for part in parts:
                size = pieces[part].shape[0]
                rows_ref[low : low + size, :] = pieces[part][...]
                low += size

    @pl.when(step < len(sources))
    def _():
        qkv = dot(rows_ref[...], weight_ref[...])
        at = pl.ds(pl.multiple_of(order_ref[step] * rows, rows), rows)
        cos_table, sin_table = cos_ref[at, :], sin_ref[at, :]
        q_ref[at, :] = turn(qkv[:, :HEAD_DIM], cos_table, sin_table).astype(BF16)
        k_ref[at, :] = turn(qkv[:, HEAD_DIM : 2 * HEAD_DIM], cos_table, sin_table).astype(BF16)
        value = qkv[:, 2 * HEAD_DIM :]
        v_ref[at, :] = value.astype(BF16)
        vt_ref[:, at] = value.T.astype(BF16)

    for i in range(length // block):

        @pl.when(step == len(sources) + i)
        def _(i=i):
            low, high = i * block, (i + 1) * block
            raw = dot_nt(k_ref[:high, :], q_ref[low:high, :])
            keys = lax.broadcasted_iota(jnp.int32, raw.shape, 0)
            queries = low + lax.broadcasted_iota(jnp.int32, raw.shape, 1)
            allowed = (keys <= queries) & (keys >= start_ref[:, low:high])
            raw = jnp.where(allowed, raw, NEG)
            top = jnp.max(raw, axis=0, keepdims=True)
            shifted = jnp.exp2((raw - top) * factor)
            total = jnp.sum(shifted, axis=0, keepdims=True)
            probs = (shifted * (1.0 / total)).astype(BF16)
            mixed = dot(vt_ref[:, :high], probs)
            o_ref[low:high, :] = mixed.T.astype(BF16)
            lse_ref[:, low:high] = top * factor + jnp.log2(total)


def attend(blocks, order, weight, cos_table, sin_table, first_place):
    pieces, sources = flatten(blocks)
    length = cos_table.shape[0]
    rows = length // len(sources)
    width = weight.shape[0]
    block = min(256, length)
    last = len(sources) - 1
    whole = lambda shape: pl.BlockSpec(shape, lambda i, order: (0, 0))
    head = jax.ShapeDtypeStruct((length, HEAD_DIM), BF16)
    return pl.pallas_call(
        functools.partial(attend_kernel, sources, block),
        out_shape=[head] * 4
        + [jax.ShapeDtypeStruct((1, length), F32), jax.ShapeDtypeStruct((length, width), BF16)],
        grid_spec=pltpu.PrefetchScalarGridSpec(
            num_scalar_prefetch=1,
            grid=(len(sources) + length // block,),
            in_specs=[whole(piece.shape) for piece in pieces]
            + [
                whole(weight.shape),
                whole((length, HEAD_DIM)),
                whole((length, HEAD_DIM)),
                whole((1, length)),
            ],
            out_specs=[whole((length, HEAD_DIM))] * 4
            + [
                whole((1, length)),
                pl.BlockSpec((rows, width), lambda i, order: (jnp.minimum(i, last), 0)),
            ],
            scratch_shapes=[pltpu.VMEM((HEAD_DIM, length), BF16)],
        ),
        compiler_params=pltpu.CompilerParams(vmem_limit_bytes=52 * 2**20),
        cost_estimate=cost(28),
        name="attend",
    )(order, *pieces, weight, cos_table, sin_table, first_place)


def attend_back_kernel(sources, block, order_ref, *refs):
    pieces = refs[: sources[-1][-1] + 1]
    (
        weight_ref, q_ref, k_ref, v_ref, o_ref, lse_ref, start_ref, cos_ref, sin_ref,
        out_ref, weight_grad_ref,
        rows_ref, kt_ref, do_ref, dq_ref, dk_ref, dv_ref,
    ) = refs[len(pieces) :]
    length = q_ref.shape[0]
    rows = rows_ref.shape[0]
    step = pl.program_id(0)
    scale = HEAD_DIM ** (-0.5)
    factor = scale * LOG2E
    blocks = len(sources)
    count = length // block

    @pl.when(step == 0)
    def _():
        kt_ref[...] = k_ref[...].astype(F32).T.astype(BF16)
        dk_ref[...] = jnp.zeros_like(dk_ref)
        dv_ref[...] = jnp.zeros_like(dv_ref)
        weight_grad_ref[...] = jnp.zeros_like(weight_grad_ref)

    for n, parts in enumerate(sources):

        @pl.when(step == n)
        def _(parts=parts):
            low = 0
            for part in parts:
                size = pieces[part].shape[0]
                rows_ref[low : low + size, :] = pieces[part][...]
                low += size

    @pl.when(step < blocks)
    def _():
        at = pl.ds(pl.multiple_of(order_ref[step] * rows, rows), rows)
        do_ref[at, :] = dot_nt(rows_ref[...], weight_ref[...]).astype(BF16)
        weight_grad_ref[...] += dot_tn(o_ref[at, :], rows_ref[...])

    for i in range(count):

        @pl.when(step == blocks + i)
        def _(i=i):
            low, high = i * block, (i + 1) * block
            query, grad = q_ref[low:high, :], do_ref[low:high, :]
            raw = dot_nt(k_ref[:high, :], query)
            keys = lax.broadcasted_iota(jnp.int32, raw.shape, 0)
            queries = low + lax.broadcasted_iota(jnp.int32, raw.shape, 1)
            allowed = (keys <= queries) & (keys >= start_ref[:, low:high])
            raw = jnp.where(allowed, raw * factor - lse_ref[:, low:high], NEG)
            probs = jnp.exp2(raw)
            probs_grad = dot_nt(v_ref[:high, :], grad)
            inner = jnp.sum(probs_grad * probs, axis=0, keepdims=True)
            score_grad = (probs * (probs_grad - inner)).astype(BF16)
            dv_ref[:high, :] += dot(probs.astype(BF16), grad)
            dk_ref[:high, :] += dot(score_grad, query)
            dq_ref[low:high, :] = dot(kt_ref[:, :high], score_grad).T

    @pl.when(step == blocks + count - 1)
    def _():
        for n in range(blocks):
            at = pl.ds(pl.multiple_of(order_ref[n] * rows, rows), rows)
            to = slice(n * rows, (n + 1) * rows)
            cos_table, sin_table = cos_ref[at, :], -sin_ref[at, :]
            out_ref[to, :HEAD_DIM] = turn(dq_ref[at, :] * scale, cos_table, sin_table).astype(BF16)
            out_ref[to, HEAD_DIM : 2 * HEAD_DIM] = turn(
                dk_ref[at, :] * scale, cos_table, sin_table
            ).astype(BF16)
            out_ref[to, 2 * HEAD_DIM :] = dv_ref[at, :].astype(BF16)


def attend_back(grads, order, weight, query, key, value, mixed, lse, first_place, cos_table, sin_table):
    pieces, sources = flatten(grads)
    length = query.shape[0]
    block = min(256, length)
    rows = length // len(sources)
    whole = lambda shape: pl.BlockSpec(shape, lambda i, order: (0, 0))
    head = whole((length, HEAD_DIM))
    return pl.pallas_call(
        functools.partial(attend_back_kernel, sources, block),
        out_shape=[
            jax.ShapeDtypeStruct((length, 3 * HEAD_DIM), BF16),
            jax.ShapeDtypeStruct(weight.shape, F32),
        ],
        grid_spec=pltpu.PrefetchScalarGridSpec(
            num_scalar_prefetch=1,
            grid=(len(sources) + length // block,),
            in_specs=[whole(piece.shape) for piece in pieces]
            + [whole(weight.shape)]
            + [head] * 4
            + [whole((1, length))] * 2
            + [head] * 2,
            out_specs=[whole((length, 3 * HEAD_DIM)), whole(weight.shape)],
            scratch_shapes=[
                pltpu.VMEM((rows, weight.shape[1]), BF16),
                pltpu.VMEM((HEAD_DIM, length), BF16),
                pltpu.VMEM((length, HEAD_DIM), BF16),
            ]
            + [pltpu.VMEM((length, HEAD_DIM), F32)] * 3,
        ),
        compiler_params=pltpu.CompilerParams(vmem_limit_bytes=56 * 2**20),
        cost_estimate=cost(30),
        name="attend_back",
    )(order, *pieces, weight, query, key, value, mixed, lse, first_place, cos_table, sin_table)


def dp_gather(value):
    count = lax.axis_size("dp")
    if count == 1:
        return value[None]
    here = lax.axis_index("dp")
    parts = [value] + [
        lax.ppermute(value, "dp", [(i, (i - step) % count) for i in range(count)])
        for step in range(1, count)
    ]
    if count == 2:
        first = here == 0
        return jnp.stack(
            [jnp.where(first, parts[0], parts[1]), jnp.where(first, parts[1], parts[0])]
        )
    whole = jnp.zeros((count,) + value.shape, value.dtype)
    for step, part in enumerate(parts):
        whole = lax.dynamic_update_index_in_dim(whole, part, (here + step) % count, 0)
    return whole


def dp_scatter(value):
    count = lax.axis_size("dp")
    here = lax.axis_index("dp")
    total = lax.dynamic_index_in_dim(value, here, 0, keepdims=False)
    for step in range(1, count):
        block = lax.dynamic_index_in_dim(value, (here + step) % count, 0, keepdims=False)
        got = lax.ppermute(
            block.astype(BF16), "dp", [(i, (i + step) % count) for i in range(count)]
        )
        total = total + got.astype(F32)
    return total


def ring_order():
    pairs = lax.axis_size("expert") // 2
    return list(range(0, pairs, 2)) + list(range(pairs - 1, 0, -2))


def ring_shift(value, step):
    order = ring_order()
    pairs = len(order)
    perm = [
        (order[q] * 2 + c, order[(q + step) % pairs] * 2 + c) for q in range(pairs) for c in range(2)
    ]
    return lax.ppermute(value, "expert", perm)


def core_swap(value):
    count = lax.axis_size("expert")
    return lax.ppermute(value, "expert", [(i, i ^ 1) for i in range(count)])


def ring_offsets():
    half = lax.axis_size("expert") // 4
    return [0] + [o for step in range(1, half) for o in (step, -step)] + [half]


def ring_blocks():
    order = ring_order()
    pairs = len(order)
    table = [[0] * (2 * pairs) for _ in range(2 * pairs)]
    for q in range(pairs):
        for c in range(2):
            for j, offset in enumerate(ring_offsets()):
                for other in range(2):
                    table[order[q] * 2 + c][2 * j + other] = (
                        order[(q - offset) % pairs] * 2 + (c ^ other)
                    )
    return lax.dynamic_index_in_dim(
        jnp.asarray(table, jnp.int32), lax.axis_index("expert"), 0, keepdims=False
    )


def tied(value, *tokens):
    firsts = [lax.slice(t, (0,) * t.ndim, (1,) * t.ndim).reshape(()) for t in tokens]
    token = sum(t.astype(F32) for t in firsts) * 0.0
    return (value.astype(F32) * (1.0 + token)).astype(value.dtype)


def ring_gather(value, gates=None):
    gates = gates or {}
    half_rows = value.shape[0] // 2
    half = lax.axis_size("expert") // 4
    blocks = {}

    def keep(parts, offset):
        blocks[offset] = (parts, [core_swap(part) for part in parts])

    keep([value], 0)
    ahead = back = value
    for step in range(1, half):
        if step in gates:
            token = gates[step](blocks)
            ahead, back = tied(ahead, *token), tied(back, *token)
        ahead, back = ring_shift(ahead, 1), ring_shift(back, -1)
        keep([ahead], step)
        keep([back], -step)
    if half in gates:
        token = gates[half](blocks)
        ahead, back = tied(ahead, *token), tied(back, *token)
    last = [ring_shift(ahead[:half_rows], 1), ring_shift(back[half_rows:], -1)]
    keep(last, half)
    return [parts for offset in ring_offsets() for parts in blocks[offset]]


def flatten(blocks):
    pieces = [piece for parts in blocks for piece in parts]
    sources, n = [], 0
    for parts in blocks:
        sources.append(tuple(range(n, n + len(parts))))
        n += len(parts)
    return pieces, tuple(sources)


def project_kernel(sources, rows_each, order_ref, want_ref, base_ref, mixed_ref, *refs):
    pieces, (out_ref, mine_ref, rows_ref) = refs[:-3], refs[-3:]
    step = pl.program_id(0)
    rows = rows_ref.shape[0]

    @pl.when(step == 0)
    def _():
        out_ref[...] = base_ref[...].astype(F32)

    for n, parts in enumerate(sources):

        @pl.when(step == n)
        def _(parts=parts):
            low = 0
            for part in parts:
                size = pieces[part].shape[0]
                rows_ref[low : low + size, :] = pieces[part][...]
                low += size

    block = order_ref[step]
    lanes = pl.ds(pl.multiple_of(block * rows, rows), rows)
    out_ref[...] += dot(mixed_ref[:, lanes], rows_ref[...])
    groups = rows // rows_each
    for r in range(mine_ref.shape[0] // rows_each):
        for d in range(groups):

            @pl.when((block == want_ref[2 * r]) & (want_ref[2 * r + 1] == d))
            def _(r=r, d=d):
                mine_ref[r * rows_each : (r + 1) * rows_each, :] = rows_ref[
                    d * rows_each : (d + 1) * rows_each, :
                ]


def project(blocks, order, want, base, mixed, rows_each):
    pieces, sources = flatten(blocks)
    rows = sum(pieces[part].shape[0] for part in sources[0])
    count, width = base.shape
    whole = lambda shape: pl.BlockSpec(shape, lambda i, *_: (0, 0))
    mine = (want.shape[0] // 2 * rows_each, width)
    return pl.pallas_call(
        functools.partial(project_kernel, sources, rows_each),
        out_shape=[jax.ShapeDtypeStruct((count, width), F32), jax.ShapeDtypeStruct(mine, BF16)],
        grid_spec=pltpu.PrefetchScalarGridSpec(
            num_scalar_prefetch=2,
            grid=(len(blocks),),
            in_specs=[whole(base.shape), whole(mixed.shape)]
            + [whole(piece.shape) for piece in pieces],
            out_specs=[whole((count, width)), whole(mine)],
            scratch_shapes=[pltpu.VMEM((rows, width), BF16)],
        ),
        compiler_params=pltpu.CompilerParams(vmem_limit_bytes=48 * 2**20),
        cost_estimate=cost(8),
        name="project",
    )(order, want, base, mixed, *pieces)


def ring_scatter(block, gates=None, marks=None):
    gates = gates or {}
    half = lax.axis_size("expert") // 4
    offsets = ring_offsets()
    spare = {}

    def mine(offset):
        if offset not in spare:
            j = offsets.index(offset)
            spare[offset] = block(2 * j).astype(F32) + core_swap(block(2 * j + 1)).astype(F32)
        return spare[offset]

    far = mine(half).astype(BF16)
    half_rows = far.shape[0] // 2
    ahead = ring_shift(far[:half_rows], 1)
    back = ring_shift(far[half_rows:], -1)
    if marks is not None:
        marks.extend([ahead, back])
    for step in range(half - 1, 0, -1):
        onward, homeward = mine(-step), mine(step)
        if step == half - 1:
            onward = jnp.concatenate(
                [onward[:half_rows] + ahead.astype(F32), onward[half_rows:]], axis=0
            )
            homeward = jnp.concatenate(
                [homeward[:half_rows], homeward[half_rows:] + back.astype(F32)], axis=0
            )
        else:
            onward = onward + ahead.astype(F32)
            homeward = homeward + back.astype(F32)
        if half - step in gates:
            onward, homeward = tied(onward, *gates[half - step]), tied(homeward, *gates[half - step])
        ahead = ring_shift(onward.astype(BF16), 1)
        back = ring_shift(homeward.astype(BF16), -1)
    return mine(0) + ahead.astype(F32) + back.astype(F32)


def chosen(pos_ref, base, window):
    count = pos_ref.shape[-1]
    row = base + lax.broadcasted_iota(jnp.int32, (window, count), 0)
    return row == pos_ref[0]


def dispatch_kernel(sources, widths, window, base_ref, order_ref, pos_ref, gate_ref, *refs):
    outs = refs[-len(widths) - 2 :]
    pieces, blocks, rows_ref, weights_ref = refs[: -len(outs)], outs[:-2], outs[-2], outs[-1]
    step = pl.program_id(0)

    @pl.when(step == 0)
    def _():
        rows_ref[...] = jnp.zeros_like(rows_ref)
        weights_ref[...] = jnp.zeros_like(weights_ref)

    for n, parts in enumerate(sources):

        @pl.when(step == n)
        def _(parts=parts):
            low = 0
            for part in parts:
                size = pieces[part].shape[0]
                left = 0
                for block, wide in zip(blocks, widths):
                    block[low : low + size, :] = pieces[part][:, left : left + wide]
                    left += wide
                low += size

    base = pl.multiple_of(base_ref[step], 16)
    pick = chosen(pos_ref, base, window)
    at = pl.ds(base, window)
    found = dot(pick.astype(F32).astype(BF16), (blocks or pieces)[0][...])
    rows_ref[at, :] = (rows_ref[at, :].astype(F32) + found).astype(BF16)
    weights_ref[at, :] += jnp.sum(jnp.where(pick, gate_ref[0], 0.0), axis=1, keepdims=True)


def dispatch(blocks, widths, packing, order, gates):
    base, pos, _, window, packed = packing
    count, _, rows = pos.shape
    if isinstance(blocks, list):
        pieces, sources = flatten(blocks)
        piece_specs = [pl.BlockSpec(piece.shape, lambda i, base, order: (0, 0)) for piece in pieces]
    else:
        pieces, sources, widths = [blocks], (), []
        piece_specs = [pl.BlockSpec((rows, blocks.shape[1]), lambda i, base, order: (order[i], 0))]
    width = (widths or [pieces[0].shape[1]])[0]
    return pl.pallas_call(
        functools.partial(dispatch_kernel, sources, tuple(widths), window),
        out_shape=[jax.ShapeDtypeStruct((rows * count, wide), BF16) for wide in widths]
        + [
            jax.ShapeDtypeStruct((packed, width), BF16),
            jax.ShapeDtypeStruct((packed, 1), F32),
        ],
        grid_spec=pltpu.PrefetchScalarGridSpec(
            num_scalar_prefetch=2,
            grid=(count,),
            in_specs=[
                pl.BlockSpec((1, 1, rows), lambda i, base, order: (i, 0, 0)),
                pl.BlockSpec((1, 1, rows), lambda i, base, order: (order[i], 0, 0)),
            ]
            + piece_specs,
            out_specs=[
                pl.BlockSpec((rows, wide), lambda i, base, order: (order[i], 0)) for wide in widths
            ]
            + [
                pl.BlockSpec((packed, width), lambda i, base, order: (0, 0)),
                pl.BlockSpec((packed, 1), lambda i, base, order: (0, 0)),
            ],
        ),
        compiler_params=pltpu.CompilerParams(vmem_limit_bytes=52 * 2**20),
        cost_estimate=cost(13),
        name="dispatch",
    )(base, order, pos, gates, *pieces)


def fetch(parts, starts_ref, wholes, counts, sems):
    copies, n = [], 0
    for whole, count in zip(wholes, counts):
        copies.append([])
        for _ in range(count):
            at = pl.ds(pl.multiple_of(starts_ref[n], 16), parts[n].shape[0])
            copies[-1].append(pltpu.make_async_copy(parts[n], whole.at[at, :], sems.at[n]))
            n += 1
    return copies


def expert_kernel(counts, total_ref, starts_ref, x_ref, *refs):
    parts, refs = refs[: sum(counts)], refs[sum(counts) :]
    pre_ref, ea_ref, y_ref, up_ref, down_ref, sems = refs
    step = pl.program_id(0)
    rows, hidden = ea_ref.shape
    ups, downs = fetch(parts, starts_ref, (up_ref, down_ref), counts, sems)
    some = (step == 0) | (step * rows < total_ref[0])

    @pl.when(step == 0)
    def _():
        for copy in ups + downs:
            copy.start()
        for copy in ups:
            copy.wait()

    @pl.when(some)
    def _():
        pre = dot(x_ref[...], up_ref[...])
        pre_ref[...] = pre
        gate_part = pre[:, :hidden]
        act = (gate_part / (1.0 + jnp.exp(-gate_part)) * pre[:, hidden:]).astype(BF16)
        ea_ref[...] = act

        @pl.when(step == 0)
        def _():
            for copy in downs:
                copy.wait()

        y_ref[...] = dot(act, down_ref[...]).astype(BF16)

    @pl.when(jnp.logical_not(some))
    def _():
        for ref in (ea_ref, y_ref):
            ref[...] = jnp.zeros_like(ref)


def expert_back_kernel(counts, total_ref, starts_ref, g_ref, gate_ref, pre_ref, y_ref, *refs):
    parts, refs = refs[: sum(counts)], refs[sum(counts) :]
    dn_ref, dy_ref, db_ref, dg_ref, down_ref, up_ref, sems = refs
    step = pl.program_id(0)
    rows = g_ref.shape[0]
    hidden = down_ref.shape[0]
    downs, ups = fetch(parts, starts_ref, (down_ref, up_ref), counts, sems)
    some = (step == 0) | (step * rows < total_ref[0])

    @pl.when(step == 0)
    def _():
        for copy in downs + ups:
            copy.start()
        for copy in downs:
            copy.wait()

    @pl.when(some)
    def _():
        grad = g_ref[...].astype(F32)
        dg_ref[...] = jnp.sum(grad * y_ref[...].astype(F32), axis=1, keepdims=True)
        out_grad = (gate_ref[...] * grad).astype(BF16)
        dy_ref[...] = out_grad
        act_grad = dot_nt(out_grad, down_ref[...])
        gate_part, up_part = pre_ref[:, :hidden], pre_ref[:, hidden:]
        sigmoid_gate = 1.0 / (1.0 + jnp.exp(-gate_part))
        db_ref[:, :hidden] = (
            act_grad * up_part * sigmoid_gate * (1.0 + gate_part * (1.0 - sigmoid_gate))
        ).astype(BF16)
        db_ref[:, hidden:] = (act_grad * gate_part * sigmoid_gate).astype(BF16)

        @pl.when(step == 0)
        def _():
            for copy in ups:
                copy.wait()

        dn_ref[...] = dot_nt(db_ref[...], up_ref[...]).astype(BF16)

    @pl.when(jnp.logical_not(some))
    def _():
        for ref in (dn_ref, dy_ref, db_ref, dg_ref):
            ref[...] = jnp.zeros_like(ref)


def expert_call(kernel, name, total, tiled, weights, outs):
    packed = tiled[0].shape[0]
    tile = 256
    parts = [part for group in weights for part, _ in group]
    starts = jnp.stack([start for group in weights for _, start in group]).astype(jnp.int32)
    spec = lambda wide: pl.BlockSpec((tile, wide), lambda i, total, starts: (i, 0))
    return pl.pallas_call(
        functools.partial(kernel, tuple(len(group) for group in weights)),
        out_shape=[jax.ShapeDtypeStruct((packed, wide), kind) for wide, kind in outs],
        grid_spec=pltpu.PrefetchScalarGridSpec(
            num_scalar_prefetch=2,
            grid=(packed // tile,),
            in_specs=[spec(array.shape[1]) for array in tiled]
            + [pl.BlockSpec(memory_space=pl.ANY)] * len(parts),
            out_specs=[spec(wide) for wide, _ in outs],
            scratch_shapes=[
                pltpu.VMEM((sum(p.shape[0] for p, _ in group), group[0][0].shape[1]), BF16)
                for group in weights
            ]
            + [pltpu.SemaphoreType.DMA((len(parts),))],
        ),
        compiler_params=pltpu.CompilerParams(vmem_limit_bytes=58 * 2**20),
        cost_estimate=cost(27),
        name=name,
    )(total, starts, *tiled, *parts)


def upright(line):
    count = line.shape[1]
    row = lax.broadcasted_iota(jnp.int32, (count, count), 0)
    lane = lax.broadcasted_iota(jnp.int32, (count, count), 1)
    return jnp.sum(jnp.where(row == lane, line, 0.0), axis=1, keepdims=True)


def combine_kernel(turned, window, extra, base_ref, order_ref, to_ref, me_ref, pos_ref, rows_ref, side_ref, act_ref, weight_ref, out_ref):
    base = pl.multiple_of(base_ref[pl.program_id(0)], 16)
    pick = chosen(pos_ref, base, window)
    at = pl.ds(base, window)
    width = rows_ref.shape[1]
    found = dot_tn(pick.astype(F32).astype(BF16), rows_ref[at, :])
    if not turned:
        found = found * upright(side_ref[0])
    found = found + (dot_nt if turned else dot)(act_ref[...], weight_ref[...])
    out_ref[:, :width] = found.astype(BF16)
    if turned:
        line = jnp.sum(jnp.where(pick, side_ref[at, :], 0.0), axis=0, keepdims=True)
        column = upright(line)
        high = column.astype(BF16).astype(F32)
        lane = lax.broadcasted_iota(jnp.int32, (pick.shape[1], extra), 1)
        out_ref[:, width:] = jnp.where(
            lane == me_ref[0], high, jnp.where(lane == me_ref[0] + extra // 2, column - high, 0.0)
        ).astype(BF16)


def combine(packing, order, to, me, rows, side, act, weight, turned, extra):
    base, pos, _, window, packed = packing
    blocks, _, count = pos.shape
    width = rows.shape[-1]
    whole = lambda ref: pl.BlockSpec(ref.shape, lambda i, *_: (0, 0))
    return pl.pallas_call(
        functools.partial(combine_kernel, turned, window, extra),
        out_shape=jax.ShapeDtypeStruct((blocks * count, width + extra), BF16),
        grid_spec=pltpu.PrefetchScalarGridSpec(
            num_scalar_prefetch=4,
            grid=(blocks,),
            in_specs=[
                pl.BlockSpec((1, 1, count), lambda i, *_: (i, 0, 0)),
                whole(rows),
                whole(side)
                if turned
                else pl.BlockSpec((1, 1, count), lambda i, base, order, to, me: (order[i], 0, 0)),
                pl.BlockSpec((count, act.shape[1]), lambda i, base, order, to, me: (order[i], 0)),
                whole(weight),
            ],
            out_specs=pl.BlockSpec(
                (count, width + extra), lambda i, base, order, to, me: (to[i], 0)
            ),
        ),
        compiler_params=pltpu.CompilerParams(vmem_limit_bytes=40 * 2**20),
        cost_estimate=cost(10),
        name="combine",
    )(base, order, to, me.reshape(1), pos, rows, side, act, weight)


def gather_all(value):
    return lax.all_gather(value, "expert", axis=0, tiled=True)


def swap(value):
    return lax.all_to_all(value, "expert", split_axis=0, concat_axis=0, tiled=True)


def per_device(
    tokens,
    cotangent,
    segment_ids,
    routes,
    attn_in,
    attn_out,
    gain_attn,
    shared_in,
    shared_out,
    router,
    gain_ffn,
    expert_in,
    expert_out,
):
    n_dp, n_e = lax.axis_size("dp"), lax.axis_size("expert")
    me = lax.axis_index("expert")
    count, width = tokens.shape
    segments = segment_ids[0]
    length = segments.shape[0]
    rows = attn_in.shape[0]
    capacity = min(count, 3 * TOP * count // (2 * n_e))
    shared_rows = shared_out.shape[0]
    shared_width = shared_rows * n_dp
    expert_width = expert_out.shape[1] * n_dp

    order = ring_blocks()
    steady = jnp.arange(n_e, dtype=jnp.int32)
    hidden_in = tokens.astype(F32)
    inverse_one = lax.rsqrt(jnp.mean(hidden_in * hidden_in, axis=-1, keepdims=True) + EPS)
    normed_one = hidden_in * inverse_one
    gain_rows = gain_attn.astype(F32)[:, None]
    head_w = []

    def head_sent(blocks):
        own = (attn_in.astype(F32) * tied(gain_rows, blocks[0][1][0])).astype(BF16)
        own = own.reshape(rows, 3, n_e, HEAD_DIM).transpose(2, 0, 1, 3)
        head_w.append(swap(own.reshape(n_e, rows, 3 * HEAD_DIM)))
        return head_w[0]

    def head_whole(blocks):
        head_w.append(dp_gather(head_w[0]).reshape(width, 3 * HEAD_DIM))
        return head_w[1]

    here = lax.axis_index("dp")

    def spread(shard, chunks):
        while shard.shape[0] % (16 * chunks):
            chunks -= 1
        size = shard.shape[0] // chunks
        parts = [[(shard, here * shard.shape[0])]]
        for j in range(chunks):
            parts.append([])
            for step in range(1, n_dp):
                got = lax.ppermute(
                    shard[j * size : (j + 1) * size],
                    "dp",
                    [(i, (i - step) % n_dp) for i in range(n_dp)],
                )
                parts[-1].append((got, (here + step) % n_dp * shard.shape[0] + j * size))
        return parts

    expert_up = lax.all_gather(expert_in, "dp", axis=1, tiled=True)[0]
    down_parts = spread(expert_out[0], 2)
    first = lambda parts: [part for part, _ in parts]
    down_tokens = [first(parts) for parts in down_parts[1:]] + [[]]

    small = jnp.concatenate([router, gain_ffn[:, None]], axis=1)
    small = dp_gather(small).reshape(-1, n_e + 1)
    extra_rows = 32
    extra = jnp.concatenate([small.T, routes.T.astype(BF16)], axis=0)
    extra = jnp.pad(extra, ((0, extra_rows - extra.shape[0]), (0, 0)))
    extra = jnp.broadcast_to(extra, (n_e,) + extra.shape)
    cos_table, sin_table, first_place = rope_tables(segments)
    share_w = shared_in.reshape(rows, 2, n_dp, n_e, shared_rows).transpose(3, 0, 1, 2, 4)
    share_w = share_w.reshape(n_e, rows, 2 * shared_width)

    half = n_e // 4
    norm_blocks = ring_gather(
        normed_one.astype(BF16),
        {
            half - 1: lambda blocks: [head_sent(blocks), head_whole(blocks)],
            half: lambda blocks: [cos_table, sin_table, extra, share_w],
        },
    )
    head_sent_w, head_w = head_w

    head_out, query, key, value, lse, norm_all = attend(
        norm_blocks, order, head_w, cos_table, sin_table, first_place
    )
    mixed = jnp.concatenate([head_out.reshape(n_e, count, HEAD_DIM), extra], axis=1)
    share_w = swap(tied(share_w, head_sent_w))
    mixed = swap(tied(mixed, share_w))
    small = mixed[:, count:]
    mixed = mixed[:, :count].transpose(1, 0, 2).reshape(count, n_dp, n_e, rows)
    mixed = mixed.transpose(0, 2, 1, 3).reshape(count, width)
    proj_blocks = dp_gather(attn_out).reshape(n_dp * rows, width)
    proj_blocks = ring_gather(
        tied(proj_blocks, norm_blocks[-1][0], norm_blocks[-1][-1]),
        {half - 2: lambda blocks: [lse], half - 1: lambda blocks: [mixed]},
    )
    split = HEAD_DIM // rows
    want = [(me * split + r) // k % m for r in range(split) for k, m in ((1, n_e), (n_e, n_dp))]
    resid, head_out_w = project(
        proj_blocks, order, jnp.stack(want).astype(jnp.int32), tokens, mixed, rows
    )
    routes_all = small[:, n_e + 1 : n_e + 1 + TOP].astype(F32)
    small = small[:, : n_e + 1].reshape(n_e, n_e + 1, n_dp, rows).transpose(1, 2, 0, 3)
    small = small.reshape(n_e + 1, width)
    router_full = small[:n_e]
    gain_second = small[n_e].astype(F32)

    share_sent = share_w
    share_w = dp_gather(share_w).reshape(width, 2 * shared_width)
    share_out = dp_gather(shared_out).reshape(shared_width, width)

    inverse_two = lax.rsqrt(jnp.mean(resid * resid, axis=-1, keepdims=True) + EPS)
    normed_two = resid * inverse_two
    norm_two = (normed_two * gain_second).astype(BF16)
    logits = dot_nt(norm_two, router_full)
    picked = jnp.any(routes[:, :, None] == jnp.arange(n_e)[None, None, :], axis=1)
    chosen = jnp.where(picked, logits, NEG)
    chosen = jnp.where(picked, jnp.exp(chosen - jnp.max(chosen, axis=-1, keepdims=True)), 0.0)
    gates = chosen / jnp.sum(chosen, axis=-1, keepdims=True)
    gate_high = gates.astype(BF16)
    gate_low = (gates - gate_high.astype(F32)).astype(BF16)
    blank = jnp.zeros((count, 128 - 2 * n_e), BF16)
    payload = jnp.concatenate([norm_two, gate_high, gate_low, blank], axis=1)
    norm_blocks = ring_gather(
        payload,
        {
            half - 1: lambda blocks: [share_sent] + down_tokens[0],
            half: lambda blocks: [share_sent] + down_tokens[1],
        },
    )

    cot_all = gather_all(tied(cotangent, norm_blocks[-1][0], norm_blocks[-1][1]))

    named = jnp.any(routes_all == me.astype(F32), axis=1)
    named = jnp.take(named, order, axis=0)
    ranking = jnp.cumsum(named.astype(jnp.int32), axis=1)
    ends = jnp.cumsum(ranking[:, -1])
    begins = ends - ranking[:, -1]
    pos = jnp.where(named, begins[:, None] + ranking - 1, -1)[:, None, :]
    window = -(-(capacity + 15) // 16) * 16
    packed = -(-(n_e * capacity + 32) // 256) * 256
    packing = (begins // 16 * 16, pos, ends[-1:], window, packed)
    norm_two_all, payload, arrived, _ = dispatch(
        norm_blocks, [width, 128], packing, order, jnp.zeros((n_e, 1, count), F32)
    )
    mine = jnp.arange(n_e) == me
    gate_all = payload[:, : 2 * n_e].astype(F32).reshape(length, 2, n_e)
    gate_all = jnp.sum(jnp.where(mine, gate_all, 0.0), axis=(1, 2)).reshape(n_e, 1, count)
    ups = [(expert_up, jnp.int32(0))]
    downs = [part for parts in down_parts for part in parts]
    expert_width = expert_out.shape[1] * n_dp
    expert_pre, expert_act, expert_res = expert_call(
        expert_kernel,
        "expert",
        packing[2],
        [arrived],
        [ups, downs],
        [(2 * expert_width, F32), (expert_width, BF16), (width, BF16)],
    )

    shared_pre = dot(norm_two_all, share_w)
    shared_act = (
        jax.nn.silu(shared_pre[:, :shared_width]) * shared_pre[:, shared_width:]
    ).astype(BF16)
    out_part = combine(
        packing, order, order, me, expert_res, gate_all, shared_act, share_out, False, 0
    )
    routed_out = lax.psum_scatter(out_part, "expert", scatter_dimension=0, tiled=True)

    cot_rows, gate_rows = dispatch(cot_all, None, packing, order, gate_all)
    row_grad, route_grad, pre_grad, gate_grad = expert_call(
        expert_back_kernel,
        "expert_back",
        packing[2],
        [cot_rows, gate_rows, expert_pre, expert_res],
        [downs, ups],
        [(width, BF16), (width, BF16), (2 * expert_width, BF16), (1, F32)],
    )
    shared_act_grad = dot_nt(cot_all, share_out)
    shared_pre_grad = silu_back(
        shared_act_grad, shared_pre[:, :shared_width], shared_pre[:, shared_width:]
    ).astype(BF16)
    norm_two_part = combine(
        packing, order, steady, me, row_grad, gate_grad, shared_pre_grad, share_w, True, 128
    )
    share_out_grad = dp_scatter(dot_tn(shared_act, cot_all).reshape(n_dp, shared_rows, width))
    share_in_grad = dot_tn(norm_two_all, shared_pre_grad)
    share_in_grad = dp_scatter(share_in_grad.reshape(n_dp, n_e, rows, 2 * shared_width)).astype(BF16)
    marks = []
    norm_two_grad = ring_scatter(
        lambda n: norm_two_part[n * count : (n + 1) * count],
        {1: [share_out_grad, share_in_grad]},
        marks,
    )
    share_in_sent = swap(share_in_grad)
    share_in_grad = share_in_sent.astype(F32)
    gate_grad = norm_two_grad[:, width : width + n_e] + norm_two_grad[:, width + 64 : width + 64 + n_e]
    norm_two_grad = norm_two_grad[:, :width]

    up_grad = dot_tn(tied(arrived, *marks), pre_grad).astype(BF16)
    expert_in_grad = lax.psum_scatter(up_grad, "dp", scatter_dimension=0, tiled=True)
    size = expert_out.shape[1]
    cut = lambda i: tied(lax.dynamic_slice_in_dim(expert_act, i % n_dp * size, size, 1), *marks)
    down_grad = dot_tn(cut(here), route_grad)
    down_got = [
        lax.ppermute(
            dot_tn(cut(here + step), route_grad).astype(BF16),
            "dp",
            [(i, (i + step) % n_dp) for i in range(n_dp)],
        )
        for step in range(1, n_dp)
    ]
    share_in_grad = (
        share_in_grad.reshape(n_e, rows, 2, n_dp, shared_rows)
        .transpose(1, 2, 3, 0, 4)
        .reshape(rows, -1)
    )

    logit_grad = gates * (gate_grad - jnp.sum(gates * gate_grad, axis=-1, keepdims=True))
    router_grad = jnp.dot(
        logit_grad.T, norm_two.astype(F32), precision=HIGHEST, preferred_element_type=F32
    )
    norm_two_grad = norm_two_grad + jnp.dot(
        logit_grad, router_full.astype(F32), precision=HIGHEST, preferred_element_type=F32
    )
    gain_two_grad = jnp.sum(norm_two_grad * normed_two, axis=0)
    upstream = cotangent.astype(F32)
    scaled_two = norm_two_grad * gain_second
    resid_grad = upstream + inverse_two * (
        scaled_two - normed_two * jnp.mean(scaled_two * normed_two, axis=-1, keepdims=True)
    )
    small_grad = jnp.concatenate([router_grad, gain_two_grad[None]], axis=0)

    branch_cot = resid_grad.astype(BF16)
    branch_blocks = ring_gather(branch_cot, {half - 2: lambda blocks: [share_in_sent]})
    qkv_grad, proj_grad = attend_back(
        branch_blocks, order, head_out_w, query, key, value, head_out, lse, first_place, cos_table, sin_table
    )
    proj_grad = proj_grad.astype(BF16)
    attn_out_grad = 0.0
    for r in range(split):
        for shift in range(n_dp):
            perm = [
                (((h * split + r) // n_e + shift) % n_dp * n_e + h, h * split + r)
                for h in range(n_e)
            ]
            part = lax.ppermute(proj_grad[r * rows : (r + 1) * rows], ("dp", "expert"), perm)
            attn_out_grad = attn_out_grad + part.astype(F32)
    small_grad = tied(small_grad, qkv_grad).reshape(n_e + 1, n_dp * n_e, rows).transpose(1, 0, 2)
    small_grad = lax.all_to_all(
        small_grad, ("dp", "expert"), split_axis=0, concat_axis=0, tiled=True
    )
    small_grad = jnp.sum(small_grad, axis=0)
    norm_one_part = dot_nt(qkv_grad, head_w).astype(BF16)
    scaled_one = ring_scatter(
        lambda n: norm_one_part[n * count : (n + 1) * count], {half - 1: down_got}
    )
    expert_in_grad = expert_in_grad.astype(F32)[None]
    expert_out_grad = (down_grad + sum(part.astype(F32) for part in down_got))[None]
    input_grad = resid_grad + inverse_one * (
        scaled_one - normed_one * jnp.mean(scaled_one * normed_one, axis=-1, keepdims=True)
    )
    head_grad = dot_tn(norm_all, qkv_grad).reshape(n_dp, n_e, rows, 3 * HEAD_DIM)
    head_grad = swap(dp_scatter(head_grad).astype(BF16)).astype(F32)
    head_grad = (
        head_grad.reshape(n_e, rows, 3, HEAD_DIM).transpose(1, 2, 0, 3).reshape(rows, 3 * width)
    )
    gain_attn_grad = jnp.sum(head_grad * attn_in.astype(F32), axis=1)
    attn_in_grad = head_grad * gain_rows
    return (
        (resid + routed_out.astype(F32)).astype(BF16),
        input_grad.astype(BF16),
        attn_in_grad,
        attn_out_grad,
        gain_attn_grad,
        share_in_grad,
        share_out_grad,
        small_grad[:n_e].T,
        small_grad[n_e],
        expert_in_grad,
        expert_out_grad,
    )


def solution(mesh):
    return jax.shard_map(
        per_device,
        mesh=mesh,
        in_specs=(
            P(("dp", "expert"), None),
            P(("dp", "expert"), None),
            P("dp", None),
            P(("dp", "expert"), None),
            P(("dp", "expert"), None),
            P(("dp", "expert"), None),
            P(("dp", "expert")),
            P(("dp", "expert"), None),
            P(("dp", "expert"), None),
            P(("dp", "expert"), None),
            P(("dp", "expert")),
            P("expert", "dp", None),
            P("expert", "dp", None),
        ),
        out_specs=(
            P(("dp", "expert"), None),
            P(("dp", "expert"), None),
            P(("dp", "expert"), None),
            P(("dp", "expert"), None),
            P(("dp", "expert")),
            P(("dp", "expert"), None),
            P(("dp", "expert"), None),
            P(("dp", "expert"), None),
            P(("dp", "expert")),
            P("expert", "dp", None),
            P("expert", "dp", None),
        ),
        check_vma=False,
    )
```

```python
import functools
import math

import jax
import jax.numpy as jnp
from jax import lax
from jax.experimental import pallas as pl
from jax.experimental.pallas import tpu as pltpu
from jax.sharding import PartitionSpec as P

HEADS = 16
HEAD_DIM = 128
TOP = 6


EPS = 1e-06
THETA = 10000.0
NEG = -1e30
HIGHEST = lax.Precision.HIGHEST
BF16 = jnp.bfloat16
F32 = jnp.float32
LOG2E = math.log2(math.e)


def rope_tables(segments):
    length = segments.shape[0]
    places = jnp.arange(length, dtype=jnp.int32)
    starts = jnp.concatenate([jnp.ones((1,), dtype=jnp.bool_), segments[1:] != segments[:-1]])
    first_place = lax.cummax(jnp.where(starts, places, 0), axis=0)
    offset = (places - first_place).astype(jnp.float32)
    half_dim = HEAD_DIM // 2
    freqs = jnp.exp(jnp.arange(half_dim, dtype=jnp.float32) * (-2.0 * math.log(THETA) / HEAD_DIM))
    angles = offset[:, None] * freqs[None, :]
    cos_table, sin_table = jnp.cos(angles), jnp.sin(angles)
    return (
        jnp.concatenate([cos_table, cos_table], axis=1),
        jnp.concatenate([-sin_table, sin_table], axis=1),
        first_place[None, :],
    )


def silu_back(grad_act, gate_part, up_part):
    sigmoid_gate = jax.nn.sigmoid(gate_part)
    gate_grad = grad_act * up_part * sigmoid_gate * (1.0 + gate_part * (1.0 - sigmoid_gate))
    up_grad = grad_act * gate_part * sigmoid_gate
    return jnp.concatenate([gate_grad, up_grad], axis=-1)


def dot(left, right):
    return jnp.dot(left, right, preferred_element_type=F32)


def dot_tn(left, right):
    return lax.dot_general(left, right, (((0,), (0,)), ((), ())), preferred_element_type=F32)


def dot_nt(left, right):
    return lax.dot_general(left, right, (((1,), (1,)), ((), ())), preferred_element_type=F32)


def cost(micros):
    return pl.CostEstimate(flops=int(micros * 1.1e9), bytes_accessed=0, transcendentals=0)


def turn(values, cos_table, sin_table):
    return values * cos_table + pltpu.roll(values, HEAD_DIM // 2, 1) * sin_table


def attend_kernel(sources, block, order_ref, *refs):
    pieces = refs[: sources[-1][-1] + 1]
    weight_ref, cos_ref, sin_ref, start_ref = refs[len(pieces) : len(pieces) + 4]
    o_ref, q_ref, k_ref, v_ref, lse_ref, rows_ref, vt_ref = refs[len(pieces) + 4 :]
    step = pl.program_id(0)
    length = q_ref.shape[0]
    factor = HEAD_DIM ** (-0.5) * LOG2E
    rows = rows_ref.shape[0]

    for n, parts in enumerate(sources):

        @pl.when(step == n)
        def _(parts=parts):
            low = 0
            for part in parts:
                size = pieces[part].shape[0]
                rows_ref[low : low + size, :] = pieces[part][...]
                low += size

    @pl.when(step < len(sources))
    def _():
        qkv = dot(rows_ref[...], weight_ref[...])
        at = pl.ds(pl.multiple_of(order_ref[step] * rows, rows), rows)
        cos_table, sin_table = cos_ref[at, :], sin_ref[at, :]
        q_ref[at, :] = turn(qkv[:, :HEAD_DIM], cos_table, sin_table).astype(BF16)
        k_ref[at, :] = turn(qkv[:, HEAD_DIM : 2 * HEAD_DIM], cos_table, sin_table).astype(BF16)
        value = qkv[:, 2 * HEAD_DIM :]
        v_ref[at, :] = value.astype(BF16)
        vt_ref[:, at] = value.T.astype(BF16)

    for i in range(length // block):

        @pl.when(step == len(sources) + i)
        def _(i=i):
            low, high = i * block, (i + 1) * block
            raw = dot_nt(k_ref[:high, :], q_ref[low:high, :])
            keys = lax.broadcasted_iota(jnp.int32, raw.shape, 0)
            queries = low + lax.broadcasted_iota(jnp.int32, raw.shape, 1)
            allowed = (keys <= queries) & (keys >= start_ref[:, low:high])
            raw = jnp.where(allowed, raw, NEG)
            top = jnp.max(raw, axis=0, keepdims=True)
            shifted = jnp.exp2((raw - top) * factor)
            total = jnp.sum(shifted, axis=0, keepdims=True)
            probs = (shifted * (1.0 / total)).astype(BF16)
            mixed = dot(vt_ref[:, :high], probs)
            o_ref[low:high, :] = mixed.T.astype(BF16)
            lse_ref[:, low:high] = top * factor + jnp.log2(total)


def attend(blocks, order, weight, cos_table, sin_table, first_place):
    pieces, sources = flatten(blocks)
    length = cos_table.shape[0]
    rows = length // len(sources)
    width = weight.shape[0]
    block = min(256, length)
    last = len(sources) - 1
    whole = lambda shape: pl.BlockSpec(shape, lambda i, order: (0, 0))
    head = jax.ShapeDtypeStruct((length, HEAD_DIM), BF16)
    return pl.pallas_call(
        functools.partial(attend_kernel, sources, block),
        out_shape=[head] * 4
        + [jax.ShapeDtypeStruct((1, length), F32), jax.ShapeDtypeStruct((length, width), BF16)],
        grid_spec=pltpu.PrefetchScalarGridSpec(
            num_scalar_prefetch=1,
            grid=(len(sources) + length // block,),
            in_specs=[whole(piece.shape) for piece in pieces]
            + [
                whole(weight.shape),
                whole((length, HEAD_DIM)),
                whole((length, HEAD_DIM)),
                whole((1, length)),
            ],
            out_specs=[whole((length, HEAD_DIM))] * 4
            + [
                whole((1, length)),
                pl.BlockSpec((rows, width), lambda i, order: (jnp.minimum(i, last), 0)),
            ],
            scratch_shapes=[pltpu.VMEM((HEAD_DIM, length), BF16)],
        ),
        compiler_params=pltpu.CompilerParams(vmem_limit_bytes=52 * 2**20),
        cost_estimate=cost(28),
        name="attend",
    )(order, *pieces, weight, cos_table, sin_table, first_place)


def attend_back_kernel(sources, block, order_ref, *refs):
    pieces = refs[: sources[-1][-1] + 1]
    (
        weight_ref, q_ref, k_ref, v_ref, o_ref, lse_ref, start_ref, cos_ref, sin_ref,
        out_ref, weight_grad_ref,
        rows_ref, kt_ref, do_ref, dq_ref, dk_ref, dv_ref,
    ) = refs[len(pieces) :]
    length = q_ref.shape[0]
    rows = rows_ref.shape[0]
    step = pl.program_id(0)
    scale = HEAD_DIM ** (-0.5)
    factor = scale * LOG2E
    blocks = len(sources)
    count = length // block

    @pl.when(step == 0)
    def _():
        kt_ref[...] = k_ref[...].astype(F32).T.astype(BF16)
        dk_ref[...] = jnp.zeros_like(dk_ref)
        dv_ref[...] = jnp.zeros_like(dv_ref)
        weight_grad_ref[...] = jnp.zeros_like(weight_grad_ref)

    for n, parts in enumerate(sources):

        @pl.when(step == n)
        def _(parts=parts):
            low = 0
            for part in parts:
                size = pieces[part].shape[0]
                rows_ref[low : low + size, :] = pieces[part][...]
                low += size

    @pl.when(step < blocks)
    def _():
        at = pl.ds(pl.multiple_of(order_ref[step] * rows, rows), rows)
        do_ref[at, :] = dot_nt(rows_ref[...], weight_ref[...]).astype(BF16)
        weight_grad_ref[...] += dot_tn(o_ref[at, :], rows_ref[...])

    for i in range(count):

        @pl.when(step == blocks + i)
        def _(i=i):
            low, high = i * block, (i + 1) * block
            query, grad = q_ref[low:high, :], do_ref[low:high, :]
            raw = dot_nt(k_ref[:high, :], query)
            keys = lax.broadcasted_iota(jnp.int32, raw.shape, 0)
            queries = low + lax.broadcasted_iota(jnp.int32, raw.shape, 1)
            allowed = (keys <= queries) & (keys >= start_ref[:, low:high])
            raw = jnp.where(allowed, raw * factor - lse_ref[:, low:high], NEG)
            probs = jnp.exp2(raw)
            probs_grad = dot_nt(v_ref[:high, :], grad)
            inner = jnp.sum(probs_grad * probs, axis=0, keepdims=True)
            score_grad = (probs * (probs_grad - inner)).astype(BF16)
            dv_ref[:high, :] += dot(probs.astype(BF16), grad)
            dk_ref[:high, :] += dot(score_grad, query)
            dq_ref[low:high, :] = dot(kt_ref[:, :high], score_grad).T

    @pl.when(step == blocks + count - 1)
    def _():
        for n in range(blocks):
            at = pl.ds(pl.multiple_of(order_ref[n] * rows, rows), rows)
            to = slice(n * rows, (n + 1) * rows)
            cos_table, sin_table = cos_ref[at, :], -sin_ref[at, :]
            out_ref[to, :HEAD_DIM] = turn(dq_ref[at, :] * scale, cos_table, sin_table).astype(BF16)
            out_ref[to, HEAD_DIM : 2 * HEAD_DIM] = turn(
                dk_ref[at, :] * scale, cos_table, sin_table
            ).astype(BF16)
            out_ref[to, 2 * HEAD_DIM :] = dv_ref[at, :].astype(BF16)


def attend_back(grads, order, weight, query, key, value, mixed, lse, first_place, cos_table, sin_table):
    pieces, sources = flatten(grads)
    length = query.shape[0]
    block = min(256, length)
    rows = length // len(sources)
    whole = lambda shape: pl.BlockSpec(shape, lambda i, order: (0, 0))
    head = whole((length, HEAD_DIM))
    return pl.pallas_call(
        functools.partial(attend_back_kernel, sources, block),
        out_shape=[
            jax.ShapeDtypeStruct((length, 3 * HEAD_DIM), BF16),
            jax.ShapeDtypeStruct(weight.shape, F32),
        ],
        grid_spec=pltpu.PrefetchScalarGridSpec(
            num_scalar_prefetch=1,
            grid=(len(sources) + length // block,),
            in_specs=[whole(piece.shape) for piece in pieces]
            + [whole(weight.shape)]
            + [head] * 4
            + [whole((1, length))] * 2
            + [head] * 2,
            out_specs=[whole((length, 3 * HEAD_DIM)), whole(weight.shape)],
            scratch_shapes=[
                pltpu.VMEM((rows, weight.shape[1]), BF16),
                pltpu.VMEM((HEAD_DIM, length), BF16),
                pltpu.VMEM((length, HEAD_DIM), BF16),
            ]
            + [pltpu.VMEM((length, HEAD_DIM), F32)] * 3,
        ),
        compiler_params=pltpu.CompilerParams(vmem_limit_bytes=56 * 2**20),
        cost_estimate=cost(30),
        name="attend_back",
    )(order, *pieces, weight, query, key, value, mixed, lse, first_place, cos_table, sin_table)


def dp_order(parts):
    count = len(parts)
    here = lax.axis_index("dp")
    if count == 1:
        return parts[0][None]
    if count == 2:
        first = here == 0
        return jnp.stack(
            [jnp.where(first, parts[0], parts[1]), jnp.where(first, parts[1], parts[0])]
        )
    whole = jnp.zeros((count,) + parts[0].shape, parts[0].dtype)
    for step, part in enumerate(parts):
        whole = lax.dynamic_update_index_in_dim(whole, part, (here + step) % count, 0)
    return whole


def dp_parts(value):
    count = lax.axis_size("dp")
    return [value] + [
        lax.ppermute(value, "dp", [(i, (i - step) % count) for i in range(count)])
        for step in range(1, count)
    ]


def dp_gather(value):
    return dp_order(dp_parts(value))


def dp_scatter(value):
    count = lax.axis_size("dp")
    here = lax.axis_index("dp")
    total = lax.dynamic_index_in_dim(value, here, 0, keepdims=False)
    for step in range(1, count):
        block = lax.dynamic_index_in_dim(value, (here + step) % count, 0, keepdims=False)
        got = lax.ppermute(
            block.astype(BF16), "dp", [(i, (i + step) % count) for i in range(count)]
        )
        total = total + got.astype(F32)
    return total


def ring_order():
    pairs = lax.axis_size("expert") // 2
    return list(range(0, pairs, 2)) + list(range(pairs - 1, 0, -2))


def ring_shift(value, step):
    order = ring_order()
    pairs = len(order)
    perm = [
        (order[q] * 2 + c, order[(q + step) % pairs] * 2 + c) for q in range(pairs) for c in range(2)
    ]
    return lax.ppermute(value, "expert", perm)


def core_swap(value):
    count = lax.axis_size("expert")
    return lax.ppermute(value, "expert", [(i, i ^ 1) for i in range(count)])


def ring_offsets():
    half = lax.axis_size("expert") // 4
    return [0] + [o for step in range(1, half) for o in (step, -step)] + [half]


def ring_blocks():
    order = ring_order()
    pairs = len(order)
    table = [[0] * (2 * pairs) for _ in range(2 * pairs)]
    for q in range(pairs):
        for c in range(2):
            for j, offset in enumerate(ring_offsets()):
                for other in range(2):
                    table[order[q] * 2 + c][2 * j + other] = (
                        order[(q - offset) % pairs] * 2 + (c ^ other)
                    )
    return lax.dynamic_index_in_dim(
        jnp.asarray(table, jnp.int32), lax.axis_index("expert"), 0, keepdims=False
    )


def tied(value, *tokens):
    firsts = [lax.slice(t, (0,) * t.ndim, (1,) * t.ndim).reshape(()) for t in tokens]
    token = sum(t.astype(F32) for t in firsts) * 0.0
    return (value.astype(F32) * (1.0 + token)).astype(value.dtype)


def ring_gather(value, gates=None):
    gates = gates or {}
    half_rows = value.shape[0] // 2
    half = lax.axis_size("expert") // 4
    blocks = {}

    def keep(parts, offset):
        blocks[offset] = (parts, [core_swap(part) for part in parts])

    keep([value], 0)
    ahead = back = value
    for step in range(1, half):
        if step in gates:
            token = gates[step](blocks)
            ahead, back = tied(ahead, *token), tied(back, *token)
        ahead, back = ring_shift(ahead, 1), ring_shift(back, -1)
        keep([ahead], step)
        keep([back], -step)
    if half in gates:
        token = gates[half](blocks)
        ahead, back = tied(ahead, *token), tied(back, *token)
    last = [ring_shift(ahead[:half_rows], 1), ring_shift(back[half_rows:], -1)]
    keep(last, half)
    return [parts for offset in ring_offsets() for parts in blocks[offset]]


def flatten(blocks):
    pieces = [piece for parts in blocks for piece in parts]
    sources, n = [], 0
    for parts in blocks:
        sources.append(tuple(range(n, n + len(parts))))
        n += len(parts)
    return pieces, tuple(sources)


def ring_scatter(block, gates=None, marks=None):
    gates = gates or {}
    half = lax.axis_size("expert") // 4
    offsets = ring_offsets()
    spare = {}

    def mine(offset):
        if offset not in spare:
            j = offsets.index(offset)
            spare[offset] = block(2 * j).astype(F32) + core_swap(block(2 * j + 1)).astype(F32)
        return spare[offset]

    far = mine(half).astype(BF16)
    half_rows = far.shape[0] // 2
    ahead = ring_shift(far[:half_rows], 1)
    back = ring_shift(far[half_rows:], -1)
    if marks is not None:
        marks.extend([ahead, back])
    for step in range(half - 1, 0, -1):
        onward, homeward = mine(-step), mine(step)
        if step == half - 1:
            onward = jnp.concatenate(
                [onward[:half_rows] + ahead.astype(F32), onward[half_rows:]], axis=0
            )
            homeward = jnp.concatenate(
                [homeward[:half_rows], homeward[half_rows:] + back.astype(F32)], axis=0
            )
        else:
            onward = onward + ahead.astype(F32)
            homeward = homeward + back.astype(F32)
        if half - step in gates:
            onward, homeward = tied(onward, *gates[half - step]), tied(homeward, *gates[half - step])
        ahead = ring_shift(onward.astype(BF16), 1)
        back = ring_shift(homeward.astype(BF16), -1)
    return mine(0) + ahead.astype(F32) + back.astype(F32)


def chosen(pos_ref, base, window):
    count = pos_ref.shape[-1]
    row = base + lax.broadcasted_iota(jnp.int32, (window, count), 0)
    return row == pos_ref[0]


def dispatch_kernel(sources, widths, window, base_ref, order_ref, pos_ref, gate_ref, *refs):
    outs = refs[-len(widths) - 2 :]
    pieces, blocks, rows_ref, weights_ref = refs[: -len(outs)], outs[:-2], outs[-2], outs[-1]
    step = pl.program_id(0)

    @pl.when(step == 0)
    def _():
        rows_ref[...] = jnp.zeros_like(rows_ref)
        weights_ref[...] = jnp.zeros_like(weights_ref)

    for n, parts in enumerate(sources):

        @pl.when(step == n)
        def _(parts=parts):
            low = 0
            for part in parts:
                size = pieces[part].shape[0]
                left = 0
                for block, wide in zip(blocks, widths):
                    block[low : low + size, :] = pieces[part][:, left : left + wide]
                    left += wide
                low += size

    base = pl.multiple_of(base_ref[step], 16)
    pick = chosen(pos_ref, base, window)
    at = pl.ds(base, window)
    found = dot(pick.astype(F32).astype(BF16), (blocks or pieces)[0][...])
    rows_ref[at, :] = (rows_ref[at, :].astype(F32) + found).astype(BF16)
    weights_ref[at, :] += jnp.sum(jnp.where(pick, gate_ref[0], 0.0), axis=1, keepdims=True)


def dispatch(blocks, widths, packing, order, gates):
    base, pos, _, window, packed = packing
    count, _, rows = pos.shape
    if isinstance(blocks, list):
        pieces, sources = flatten(blocks)
        piece_specs = [pl.BlockSpec(piece.shape, lambda i, base, order: (0, 0)) for piece in pieces]
    else:
        pieces, sources, widths = [blocks], (), []
        piece_specs = [pl.BlockSpec((rows, blocks.shape[1]), lambda i, base, order: (order[i], 0))]
    width = (widths or [pieces[0].shape[1]])[0]
    return pl.pallas_call(
        functools.partial(dispatch_kernel, sources, tuple(widths), window),
        out_shape=[jax.ShapeDtypeStruct((rows * count, wide), BF16) for wide in widths]
        + [
            jax.ShapeDtypeStruct((packed, width), BF16),
            jax.ShapeDtypeStruct((packed, 1), F32),
        ],
        grid_spec=pltpu.PrefetchScalarGridSpec(
            num_scalar_prefetch=2,
            grid=(count,),
            in_specs=[
                pl.BlockSpec((1, 1, rows), lambda i, base, order: (i, 0, 0)),
                pl.BlockSpec((1, 1, rows), lambda i, base, order: (order[i], 0, 0)),
            ]
            + piece_specs,
            out_specs=[
                pl.BlockSpec((rows, wide), lambda i, base, order: (order[i], 0)) for wide in widths
            ]
            + [
                pl.BlockSpec((packed, width), lambda i, base, order: (0, 0)),
                pl.BlockSpec((packed, 1), lambda i, base, order: (0, 0)),
            ],
        ),
        compiler_params=pltpu.CompilerParams(vmem_limit_bytes=52 * 2**20),
        cost_estimate=cost(13),
        name="dispatch",
    )(base, order, pos, gates, *pieces)


def fetch(parts, starts_ref, wholes, counts, sems):
    copies, n = [], 0
    for whole, count in zip(wholes, counts):
        copies.append([])
        for _ in range(count):
            at = pl.ds(pl.multiple_of(starts_ref[n], 16), parts[n].shape[0])
            copies[-1].append(pltpu.make_async_copy(parts[n], whole.at[at, :], sems.at[n]))
            n += 1
    return copies


def expert_kernel(counts, total_ref, starts_ref, x_ref, *refs):
    parts, refs = refs[: sum(counts)], refs[sum(counts) :]
    pre_ref, ea_ref, y_ref, up_ref, down_ref, sems = refs
    step = pl.program_id(0)
    rows, hidden = ea_ref.shape
    ups, downs = fetch(parts, starts_ref, (up_ref, down_ref), counts, sems)
    some = (step == 0) | (step * rows < total_ref[0])

    @pl.when(step == 0)
    def _():
        for copy in ups + downs:
            copy.start()
        for copy in ups:
            copy.wait()

    @pl.when(some)
    def _():
        pre = dot(x_ref[...], up_ref[...])
        pre_ref[...] = pre
        gate_part = pre[:, :hidden]
        act = (gate_part / (1.0 + jnp.exp(-gate_part)) * pre[:, hidden:]).astype(BF16)
        ea_ref[...] = act

        @pl.when(step == 0)
        def _():
            for copy in downs:
                copy.wait()

        y_ref[...] = dot(act, down_ref[...]).astype(BF16)

    @pl.when(jnp.logical_not(some))
    def _():
        for ref in (ea_ref, y_ref):
            ref[...] = jnp.zeros_like(ref)


def expert_back_kernel(counts, total_ref, starts_ref, g_ref, gate_ref, pre_ref, y_ref, *refs):
    parts, refs = refs[: sum(counts)], refs[sum(counts) :]
    dn_ref, dy_ref, db_ref, dg_ref, down_ref, up_ref, sems = refs
    step = pl.program_id(0)
    rows = g_ref.shape[0]
    hidden = down_ref.shape[0]
    downs, ups = fetch(parts, starts_ref, (down_ref, up_ref), counts, sems)
    some = (step == 0) | (step * rows < total_ref[0])

    @pl.when(step == 0)
    def _():
        for copy in downs + ups:
            copy.start()
        for copy in downs:
            copy.wait()

    @pl.when(some)
    def _():
        grad = g_ref[...].astype(F32)
        dg_ref[...] = jnp.sum(grad * y_ref[...].astype(F32), axis=1, keepdims=True)
        out_grad = (gate_ref[...] * grad).astype(BF16)
        dy_ref[...] = out_grad
        act_grad = dot_nt(out_grad, down_ref[...])
        gate_part, up_part = pre_ref[:, :hidden], pre_ref[:, hidden:]
        sigmoid_gate = 1.0 / (1.0 + jnp.exp(-gate_part))
        db_ref[:, :hidden] = (
            act_grad * up_part * sigmoid_gate * (1.0 + gate_part * (1.0 - sigmoid_gate))
        ).astype(BF16)
        db_ref[:, hidden:] = (act_grad * gate_part * sigmoid_gate).astype(BF16)

        @pl.when(step == 0)
        def _():
            for copy in ups:
                copy.wait()

        dn_ref[...] = dot_nt(db_ref[...], up_ref[...]).astype(BF16)

    @pl.when(jnp.logical_not(some))
    def _():
        for ref in (dn_ref, dy_ref, db_ref, dg_ref):
            ref[...] = jnp.zeros_like(ref)


def expert_call(kernel, name, total, tiled, weights, outs):
    packed = tiled[0].shape[0]
    tile = 256
    parts = [part for group in weights for part, _ in group]
    starts = jnp.stack([start for group in weights for _, start in group]).astype(jnp.int32)
    spec = lambda wide: pl.BlockSpec((tile, wide), lambda i, total, starts: (i, 0))
    return pl.pallas_call(
        functools.partial(kernel, tuple(len(group) for group in weights)),
        out_shape=[jax.ShapeDtypeStruct((packed, wide), kind) for wide, kind in outs],
        grid_spec=pltpu.PrefetchScalarGridSpec(
            num_scalar_prefetch=2,
            grid=(packed // tile,),
            in_specs=[spec(array.shape[1]) for array in tiled]
            + [pl.BlockSpec(memory_space=pl.ANY)] * len(parts),
            out_specs=[spec(wide) for wide, _ in outs],
            scratch_shapes=[
                pltpu.VMEM((sum(p.shape[0] for p, _ in group), group[0][0].shape[1]), BF16)
                for group in weights
            ]
            + [pltpu.SemaphoreType.DMA((len(parts),))],
        ),
        compiler_params=pltpu.CompilerParams(vmem_limit_bytes=58 * 2**20),
        cost_estimate=cost(27),
        name=name,
    )(total, starts, *tiled, *parts)


def upright(line):
    count = line.shape[1]
    row = lax.broadcasted_iota(jnp.int32, (count, count), 0)
    lane = lax.broadcasted_iota(jnp.int32, (count, count), 1)
    return jnp.sum(jnp.where(row == lane, line, 0.0), axis=1, keepdims=True)


def combine_kernel(turned, window, extra, base_ref, order_ref, to_ref, me_ref, pos_ref, rows_ref, side_ref, act_ref, weight_ref, out_ref):
    base = pl.multiple_of(base_ref[pl.program_id(0)], 16)
    pick = chosen(pos_ref, base, window)
    at = pl.ds(base, window)
    width = rows_ref.shape[1]
    found = dot_tn(pick.astype(F32).astype(BF16), rows_ref[at, :])
    if not turned:
        found = found * upright(side_ref[0])
    found = found + (dot_nt if turned else dot)(act_ref[...], weight_ref[...])
    out_ref[:, :width] = found.astype(BF16)
    if turned:
        line = jnp.sum(jnp.where(pick, side_ref[at, :], 0.0), axis=0, keepdims=True)
        column = upright(line)
        high = column.astype(BF16).astype(F32)
        lane = lax.broadcasted_iota(jnp.int32, (pick.shape[1], extra), 1)
        out_ref[:, width:] = jnp.where(
            lane == me_ref[0], high, jnp.where(lane == me_ref[0] + extra // 2, column - high, 0.0)
        ).astype(BF16)


def combine(packing, order, to, me, rows, side, act, weight, turned, extra):
    base, pos, _, window, packed = packing
    blocks, _, count = pos.shape
    width = rows.shape[-1]
    whole = lambda ref: pl.BlockSpec(ref.shape, lambda i, *_: (0, 0))
    return pl.pallas_call(
        functools.partial(combine_kernel, turned, window, extra),
        out_shape=jax.ShapeDtypeStruct((blocks * count, width + extra), BF16),
        grid_spec=pltpu.PrefetchScalarGridSpec(
            num_scalar_prefetch=4,
            grid=(blocks,),
            in_specs=[
                pl.BlockSpec((1, 1, count), lambda i, *_: (i, 0, 0)),
                whole(rows),
                whole(side)
                if turned
                else pl.BlockSpec((1, 1, count), lambda i, base, order, to, me: (order[i], 0, 0)),
                pl.BlockSpec((count, act.shape[1]), lambda i, base, order, to, me: (order[i], 0)),
                whole(weight),
            ],
            out_specs=pl.BlockSpec(
                (count, width + extra), lambda i, base, order, to, me: (to[i], 0)
            ),
        ),
        compiler_params=pltpu.CompilerParams(vmem_limit_bytes=40 * 2**20),
        cost_estimate=cost(10),
        name="combine",
    )(base, order, to, me.reshape(1), pos, rows, side, act, weight)


def gather_all(value):
    return lax.all_gather(value, "expert", axis=0, tiled=True)


def swap(value):
    return lax.all_to_all(value, "expert", split_axis=0, concat_axis=0, tiled=True)


def per_device(
    tokens,
    cotangent,
    segment_ids,
    routes,
    attn_in,
    attn_out,
    gain_attn,
    shared_in,
    shared_out,
    router,
    gain_ffn,
    expert_in,
    expert_out,
):
    n_dp, n_e = lax.axis_size("dp"), lax.axis_size("expert")
    me = lax.axis_index("expert")
    count, width = tokens.shape
    segments = segment_ids[0]
    length = segments.shape[0]
    rows = attn_in.shape[0]
    capacity = min(count, 3 * TOP * count // (2 * n_e))
    shared_rows = shared_out.shape[0]
    shared_width = shared_rows * n_dp
    expert_width = expert_out.shape[1] * n_dp

    order = ring_blocks()
    steady = jnp.arange(n_e, dtype=jnp.int32)
    hidden_in = tokens.astype(F32)
    inverse_one = lax.rsqrt(jnp.mean(hidden_in * hidden_in, axis=-1, keepdims=True) + EPS)
    normed_one = hidden_in * inverse_one
    gain_rows = gain_attn.astype(F32)[:, None]
    head_w = []

    def relay(weight):
        weight = weight.reshape(rows, 3, n_e, HEAD_DIM).transpose(2, 0, 1, 3)
        return weight.reshape(n_e, rows, 3 * HEAD_DIM)

    scaled_w = dp_parts((attn_in.astype(F32) * gain_rows).astype(BF16))

    def head_own(blocks):
        head_w.append(swap(relay(tied(scaled_w[0], blocks[0][1][0]))))
        return head_w[0]

    def head_rest(blocks):
        for part in scaled_w[1:]:
            head_w.append(swap(relay(part)))
        return head_w[-1]

    here = lax.axis_index("dp")

    def spread(shard, chunks):
        while shard.shape[0] % (16 * chunks):
            chunks -= 1
        size = shard.shape[0] // chunks
        parts = [[(shard, here * shard.shape[0])]]
        for j in range(chunks):
            parts.append([])
            for step in range(1, n_dp):
                got = lax.ppermute(
                    shard[j * size : (j + 1) * size],
                    "dp",
                    [(i, (i - step) % n_dp) for i in range(n_dp)],
                )
                parts[-1].append((got, (here + step) % n_dp * shard.shape[0] + j * size))
        return parts

    up_parts = spread(expert_in[0], max(1, min(4, expert_in.shape[1] // 256)))
    down_parts = spread(expert_out[0], 2)
    first = lambda parts: [part for part, _ in parts]
    up_tokens = [first(parts) for parts in up_parts[1:]] + [[]] * 4
    down_tokens = [first(parts) for parts in down_parts[1:]] + [[]]

    small = jnp.concatenate([router, gain_ffn[:, None]], axis=1)
    small = dp_gather(small).reshape(-1, n_e + 1)
    extra_rows = 32
    extra = jnp.concatenate([small.T, routes.T.astype(BF16)], axis=0)
    extra = jnp.pad(extra, ((0, extra_rows - extra.shape[0]), (0, 0)))
    extra = jnp.broadcast_to(extra, (n_e,) + extra.shape)
    cos_table, sin_table, first_place = rope_tables(segments)
    share_w = shared_in.reshape(rows, 2, n_dp, n_e, shared_rows).transpose(3, 0, 1, 2, 4)
    share_w = share_w.reshape(n_e, rows, 2 * shared_width)

    half = n_e // 4
    norm_blocks = ring_gather(
        normed_one.astype(BF16),
        {
            half - 1: lambda blocks: [head_own(blocks), share_w],
            half: lambda blocks: [head_rest(blocks), cos_table, sin_table, extra] + up_tokens[0],
        },
    )
    head_w = dp_order(head_w).reshape(width, 3 * HEAD_DIM)

    head_out, query, key, value, lse, norm_all = attend(
        norm_blocks, order, head_w, cos_table, sin_table, first_place
    )
    mixed = jnp.concatenate([head_out.reshape(n_e, count, HEAD_DIM), extra], axis=1)
    share_w = swap(tied(share_w, head_w))
    mixed = swap(tied(mixed, share_w, *up_tokens[1]))
    small = mixed[:, count:]
    mixed = mixed[:, :count].transpose(1, 0, 2).reshape(count, n_dp, n_e, rows)
    mixed = mixed.transpose(0, 2, 1, 3).reshape(count, width)
    proj_all = dp_gather(attn_out).reshape(n_dp * rows, width)
    proj_all = gather_all(tied(proj_all, norm_blocks[6][0]))
    routes_all = small[:, n_e + 1 : n_e + 1 + TOP].astype(F32)
    small = small[:, : n_e + 1].reshape(n_e, n_e + 1, n_dp, rows).transpose(1, 2, 0, 3)
    small = small.reshape(n_e + 1, width)
    router_full = small[:n_e]
    gain_second = small[n_e].astype(F32)

    resid = (tied(hidden_in, *up_tokens[2]) if up_tokens[2] else hidden_in) + dot(mixed, proj_all)

    share_w = dp_gather(share_w).reshape(width, 2 * shared_width)
    share_out = dp_gather(shared_out).reshape(shared_width, width)

    inverse_two = lax.rsqrt(jnp.mean(resid * resid, axis=-1, keepdims=True) + EPS)
    normed_two = resid * inverse_two
    norm_two = (normed_two * gain_second).astype(BF16)
    logits = dot_nt(norm_two, router_full)
    picked = jnp.any(routes[:, :, None] == jnp.arange(n_e)[None, None, :], axis=1)
    chosen = jnp.where(picked, logits, NEG)
    chosen = jnp.where(picked, jnp.exp(chosen - jnp.max(chosen, axis=-1, keepdims=True)), 0.0)
    gates = chosen / jnp.sum(chosen, axis=-1, keepdims=True)
    gate_high = gates.astype(BF16)
    gate_low = (gates - gate_high.astype(F32)).astype(BF16)
    blank = jnp.zeros((count, 128 - 2 * n_e), BF16)
    payload = jnp.concatenate([norm_two, gate_high, gate_low, blank], axis=1)
    norm_blocks = ring_gather(
        payload,
        {
            half - 1: lambda blocks: [mixed] + up_tokens[3],
            half: lambda blocks: [mixed] + down_tokens[0],
        },
    )

    cot_all = gather_all(tied(cotangent, norm_blocks[-1][0], norm_blocks[-1][1]))

    named = jnp.any(routes_all == me.astype(F32), axis=1)
    named = jnp.take(named, order, axis=0)
    ranking = jnp.cumsum(named.astype(jnp.int32), axis=1)
    ends = jnp.cumsum(ranking[:, -1])
    begins = ends - ranking[:, -1]
    pos = jnp.where(named, begins[:, None] + ranking - 1, -1)[:, None, :]
    window = -(-(capacity + 15) // 16) * 16
    packed = -(-(n_e * capacity + 32) // 256) * 256
    packing = (begins // 16 * 16, pos, ends[-1:], window, packed)
    norm_two_all, payload, arrived, _ = dispatch(
        norm_blocks, [width, 128], packing, order, jnp.zeros((n_e, 1, count), F32)
    )
    mine = jnp.arange(n_e) == me
    gate_all = payload[:, : 2 * n_e].astype(F32).reshape(length, 2, n_e)
    gate_all = jnp.sum(jnp.where(mine, gate_all, 0.0), axis=(1, 2)).reshape(n_e, 1, count)
    ups = [part for parts in up_parts for part in parts]
    downs = [part for parts in down_parts for part in parts]
    expert_width = expert_out.shape[1] * n_dp
    expert_pre, expert_act, expert_res = expert_call(
        expert_kernel,
        "expert",
        packing[2],
        [arrived],
        [ups, downs],
        [(2 * expert_width, F32), (expert_width, BF16), (width, BF16)],
    )

    shared_pre = dot(norm_two_all, share_w)
    shared_act = (
        jax.nn.silu(shared_pre[:, :shared_width]) * shared_pre[:, shared_width:]
    ).astype(BF16)
    out_part = combine(
        packing, order, order, me, expert_res, gate_all, shared_act, share_out, False, 0
    )
    routed_out = lax.psum_scatter(out_part, "expert", scatter_dimension=0, tiled=True)

    cot_rows, gate_rows = dispatch(cot_all, None, packing, order, gate_all)
    row_grad, route_grad, pre_grad, gate_grad = expert_call(
        expert_back_kernel,
        "expert_back",
        packing[2],
        [cot_rows, gate_rows, expert_pre, expert_res],
        [downs, ups],
        [(width, BF16), (width, BF16), (2 * expert_width, BF16), (1, F32)],
    )
    shared_act_grad = dot_nt(cot_all, share_out)
    shared_pre_grad = silu_back(
        shared_act_grad, shared_pre[:, :shared_width], shared_pre[:, shared_width:]
    ).astype(BF16)
    norm_two_part = combine(
        packing, order, steady, me, row_grad, gate_grad, shared_pre_grad, share_w, True, 128
    )
    share_out_grad = dp_scatter(dot_tn(shared_act, cot_all).reshape(n_dp, shared_rows, width))
    share_in_grad = dot_tn(norm_two_all, shared_pre_grad)
    share_in_grad = dp_scatter(share_in_grad.reshape(n_dp, n_e, rows, 2 * shared_width)).astype(BF16)
    marks = []
    norm_two_grad = ring_scatter(
        lambda n: norm_two_part[n * count : (n + 1) * count],
        {half - 2: [share_out_grad, share_in_grad]},
        marks,
    )
    share_in_sent = swap(share_in_grad)
    share_in_grad = share_in_sent.astype(F32)
    gate_grad = norm_two_grad[:, width : width + n_e] + norm_two_grad[:, width + 64 : width + 64 + n_e]
    norm_two_grad = norm_two_grad[:, :width]

    up_grad = dot_tn(tied(arrived, *marks), pre_grad).astype(BF16)
    expert_in_grad = lax.psum_scatter(up_grad, "dp", scatter_dimension=0, tiled=True)
    size = expert_out.shape[1]
    cut = lambda i: tied(lax.dynamic_slice_in_dim(expert_act, i % n_dp * size, size, 1), *marks)
    down_grad = dot_tn(cut(here), route_grad)
    down_got = [
        lax.ppermute(
            dot_tn(cut(here + step), route_grad).astype(BF16),
            "dp",
            [(i, (i + step) % n_dp) for i in range(n_dp)],
        )
        for step in range(1, n_dp)
    ]
    share_in_grad = (
        share_in_grad.reshape(n_e, rows, 2, n_dp, shared_rows)
        .transpose(1, 2, 3, 0, 4)
        .reshape(rows, -1)
    )

    logit_grad = gates * (gate_grad - jnp.sum(gates * gate_grad, axis=-1, keepdims=True))
    router_grad = jnp.dot(
        logit_grad.T, norm_two.astype(F32), precision=HIGHEST, preferred_element_type=F32
    )
    norm_two_grad = norm_two_grad + jnp.dot(
        logit_grad, router_full.astype(F32), precision=HIGHEST, preferred_element_type=F32
    )
    gain_two_grad = jnp.sum(norm_two_grad * normed_two, axis=0)
    upstream = cotangent.astype(F32)
    scaled_two = norm_two_grad * gain_second
    resid_grad = upstream + inverse_two * (
        scaled_two - normed_two * jnp.mean(scaled_two * normed_two, axis=-1, keepdims=True)
    )
    small_grad = jnp.concatenate([router_grad, gain_two_grad[None]], axis=0)

    branch_cot = resid_grad.astype(BF16)
    small_grad = small_grad.reshape(n_e + 1, n_dp * n_e, rows).transpose(1, 0, 2)
    small_grad = lax.all_to_all(
        small_grad, ("dp", "expert"), split_axis=0, concat_axis=0, tiled=True
    )
    branch_blocks = ring_gather(
        branch_cot,
        {half - 1: lambda blocks: [share_in_sent, small_grad], half: lambda blocks: down_got},
    )
    split = HEAD_DIM // rows
    proj_all = proj_all.reshape(n_e, n_dp, rows, width)
    owners = [((me * split + r) % n_e, (me * split + r) // n_e) for r in range(split)]
    head_out_w = jnp.concatenate(
        [lax.dynamic_slice(proj_all, (e, d, 0, 0), (1, 1, rows, width))[0, 0] for e, d in owners]
    )
    qkv_grad, proj_grad = attend_back(
        branch_blocks, order, head_out_w, query, key, value, head_out, lse, first_place, cos_table, sin_table
    )
    proj_grad = proj_grad.astype(BF16)
    routed = []
    for r in range(split):
        for shift in range(n_dp):
            perm = [
                (((h * split + r) // n_e + shift) % n_dp * n_e + h, h * split + r)
                for h in range(n_e)
            ]
            part = lax.ppermute(proj_grad[r * rows : (r + 1) * rows], ("dp", "expert"), perm)
            routed.append(part)
    attn_out_grad = sum(part.astype(F32) for part in routed)
    small_grad = jnp.sum(small_grad, axis=0)
    norm_one_part = dot_nt(qkv_grad, head_w).astype(BF16)
    scaled_one = ring_scatter(
        lambda n: norm_one_part[n * count : (n + 1) * count], {half - 2: routed}
    )
    expert_in_grad = expert_in_grad.astype(F32)[None]
    expert_out_grad = (down_grad + sum(part.astype(F32) for part in down_got))[None]
    input_grad = resid_grad + inverse_one * (
        scaled_one - normed_one * jnp.mean(scaled_one * normed_one, axis=-1, keepdims=True)
    )
    head_grad = dot_tn(norm_all, qkv_grad).reshape(n_dp, n_e, rows, 3 * HEAD_DIM)
    head_grad = swap(dp_scatter(head_grad).astype(BF16)).astype(F32)
    head_grad = (
        head_grad.reshape(n_e, rows, 3, HEAD_DIM).transpose(1, 2, 0, 3).reshape(rows, 3 * width)
    )
    gain_attn_grad = jnp.sum(head_grad * attn_in.astype(F32), axis=1)
    attn_in_grad = head_grad * gain_rows
    return (
        (resid + routed_out.astype(F32)).astype(BF16),
        input_grad.astype(BF16),
        attn_in_grad,
        attn_out_grad,
        gain_attn_grad,
        share_in_grad,
        share_out_grad,
        small_grad[:n_e].T,
        small_grad[n_e],
        expert_in_grad,
        expert_out_grad,
    )


def solution(mesh):
    return jax.shard_map(
        per_device,
        mesh=mesh,
        in_specs=(
            P(("dp", "expert"), None),
            P(("dp", "expert"), None),
            P("dp", None),
            P(("dp", "expert"), None),
            P(("dp", "expert"), None),
            P(("dp", "expert"), None),
            P(("dp", "expert")),
            P(("dp", "expert"), None),
            P(("dp", "expert"), None),
            P(("dp", "expert"), None),
            P(("dp", "expert")),
            P("expert", "dp", None),
            P("expert", "dp", None),
        ),
        out_specs=(
            P(("dp", "expert"), None),
            P(("dp", "expert"), None),
            P(("dp", "expert"), None),
            P(("dp", "expert"), None),
            P(("dp", "expert")),
            P(("dp", "expert"), None),
            P(("dp", "expert"), None),
            P(("dp", "expert"), None),
            P(("dp", "expert")),
            P("expert", "dp", None),
            P("expert", "dp", None),
        ),
        check_vma=False,
    )
```

```python
import functools
import math

import jax
import jax.numpy as jnp
from jax import lax
from jax.experimental import pallas as pl
from jax.experimental.pallas import tpu as pltpu
from jax.sharding import PartitionSpec as P

HEADS = 16
HEAD_DIM = 128
TOP = 6


EPS = 1e-06
THETA = 10000.0
NEG = -1e30
HIGHEST = lax.Precision.HIGHEST
BF16 = jnp.bfloat16
F32 = jnp.float32
LOG2E = math.log2(math.e)


def rope_tables(segments):
    length = segments.shape[0]
    places = jnp.arange(length, dtype=jnp.int32)
    starts = jnp.concatenate([jnp.ones((1,), dtype=jnp.bool_), segments[1:] != segments[:-1]])
    first_place = lax.cummax(jnp.where(starts, places, 0), axis=0)
    offset = (places - first_place).astype(jnp.float32)
    half_dim = HEAD_DIM // 2
    freqs = jnp.exp(jnp.arange(half_dim, dtype=jnp.float32) * (-2.0 * math.log(THETA) / HEAD_DIM))
    angles = offset[:, None] * freqs[None, :]
    cos_table, sin_table = jnp.cos(angles), jnp.sin(angles)
    return (
        jnp.concatenate([cos_table, cos_table], axis=1),
        jnp.concatenate([-sin_table, sin_table], axis=1),
        first_place[None, :],
    )


def silu_back(grad_act, gate_part, up_part):
    sigmoid_gate = jax.nn.sigmoid(gate_part)
    gate_grad = grad_act * up_part * sigmoid_gate * (1.0 + gate_part * (1.0 - sigmoid_gate))
    up_grad = grad_act * gate_part * sigmoid_gate
    return jnp.concatenate([gate_grad, up_grad], axis=-1)


def dot(left, right):
    return jnp.dot(left, right, preferred_element_type=F32)


def dot_tn(left, right):
    return lax.dot_general(left, right, (((0,), (0,)), ((), ())), preferred_element_type=F32)


def dot_nt(left, right):
    return lax.dot_general(left, right, (((1,), (1,)), ((), ())), preferred_element_type=F32)


def cost(micros):
    return pl.CostEstimate(flops=int(micros * 1.1e9), bytes_accessed=0, transcendentals=0)


def turn(values, cos_table, sin_table):
    return values * cos_table + pltpu.roll(values, HEAD_DIM // 2, 1) * sin_table


def attend_kernel(sources, block, order_ref, *refs):
    pieces = refs[: sources[-1][-1] + 1]
    weight_ref, cos_ref, sin_ref, start_ref = refs[len(pieces) : len(pieces) + 4]
    o_ref, q_ref, k_ref, v_ref, lse_ref, rows_ref, vt_ref, mixed_ref = refs[len(pieces) + 4 :]
    step = pl.program_id(0)
    length = q_ref.shape[0]
    factor = HEAD_DIM ** (-0.5) * LOG2E
    rows = rows_ref.shape[0]

    for n, parts in enumerate(sources):

        @pl.when(step == n)
        def _(parts=parts):
            low = 0
            for part in parts:
                size = pieces[part].shape[0]
                rows_ref[low : low + size, :] = pieces[part][...]
                low += size

    @pl.when(step < len(sources))
    def _():
        qkv = dot(rows_ref[...], weight_ref[...])
        at = pl.ds(pl.multiple_of(order_ref[step] * rows, rows), rows)
        cos_table, sin_table = cos_ref[at, :], sin_ref[at, :]
        q_ref[at, :] = turn(qkv[:, :HEAD_DIM], cos_table, sin_table).astype(BF16)
        k_ref[at, :] = turn(qkv[:, HEAD_DIM : 2 * HEAD_DIM], cos_table, sin_table).astype(BF16)
        value = qkv[:, 2 * HEAD_DIM :]
        v_ref[at, :] = value.astype(BF16)
        vt_ref[:, at] = value.T.astype(BF16)

    for i in range(length // block):

        @pl.when(step == len(sources) + i)
        def _(i=i):
            low, high = i * block, (i + 1) * block
            raw = dot_nt(k_ref[:high, :], q_ref[low:high, :])
            keys = lax.broadcasted_iota(jnp.int32, raw.shape, 0)
            queries = low + lax.broadcasted_iota(jnp.int32, raw.shape, 1)
            allowed = (keys <= queries) & (keys >= start_ref[:, low:high])
            raw = jnp.where(allowed, raw, NEG)
            top = jnp.max(raw, axis=0, keepdims=True)
            shifted = jnp.exp2((raw - top) * factor)
            total = jnp.sum(shifted, axis=0, keepdims=True)
            probs = (shifted * (1.0 / total)).astype(BF16)
            mixed = dot(vt_ref[:, :high], probs)
            mixed_ref[low:high, :] = mixed.T.astype(BF16)
            lse_ref[:, low:high] = top * factor + jnp.log2(total)

    @pl.when(step == len(sources) + length // block - 1)
    def _():
        for n in range(len(sources)):
            at = pl.ds(pl.multiple_of(order_ref[n] * rows, rows), rows)
            o_ref[n * rows : (n + 1) * rows, :] = mixed_ref[at, :]


def attend(blocks, order, weight, cos_table, sin_table, first_place):
    pieces, sources = flatten(blocks)
    length = cos_table.shape[0]
    rows = length // len(sources)
    width = weight.shape[0]
    block = min(256, length)
    last = len(sources) - 1
    whole = lambda shape: pl.BlockSpec(shape, lambda i, order: (0, 0))
    head = jax.ShapeDtypeStruct((length, HEAD_DIM), BF16)
    return pl.pallas_call(
        functools.partial(attend_kernel, sources, block),
        out_shape=[head] * 4
        + [jax.ShapeDtypeStruct((1, length), F32), jax.ShapeDtypeStruct((length, width), BF16)],
        grid_spec=pltpu.PrefetchScalarGridSpec(
            num_scalar_prefetch=1,
            grid=(len(sources) + length // block,),
            in_specs=[whole(piece.shape) for piece in pieces]
            + [
                whole(weight.shape),
                whole((length, HEAD_DIM)),
                whole((length, HEAD_DIM)),
                whole((1, length)),
            ],
            out_specs=[whole((length, HEAD_DIM))] * 4
            + [
                whole((1, length)),
                pl.BlockSpec((rows, width), lambda i, order: (jnp.minimum(i, last), 0)),
            ],
            scratch_shapes=[
                pltpu.VMEM((HEAD_DIM, length), BF16),
                pltpu.VMEM((length, HEAD_DIM), BF16),
            ],
        ),
        compiler_params=pltpu.CompilerParams(vmem_limit_bytes=52 * 2**20),
        cost_estimate=cost(28),
        name="attend",
    )(order, *pieces, weight, cos_table, sin_table, first_place)


def attend_back_kernel(sources, block, order_ref, *refs):
    pieces = refs[: sources[-1][-1] + 1]
    (
        weight_ref, q_ref, k_ref, v_ref, o_ref, lse_ref, start_ref, cos_ref, sin_ref,
        out_ref, weight_grad_ref,
        rows_ref, kt_ref, do_ref, dq_ref, dk_ref, dv_ref,
    ) = refs[len(pieces) :]
    length = q_ref.shape[0]
    rows = rows_ref.shape[0]
    step = pl.program_id(0)
    scale = HEAD_DIM ** (-0.5)
    factor = scale * LOG2E
    blocks = len(sources)
    count = length // block

    @pl.when(step == 0)
    def _():
        kt_ref[...] = k_ref[...].astype(F32).T.astype(BF16)
        dk_ref[...] = jnp.zeros_like(dk_ref)
        dv_ref[...] = jnp.zeros_like(dv_ref)
        weight_grad_ref[...] = jnp.zeros_like(weight_grad_ref)

    for n, parts in enumerate(sources):

        @pl.when(step == n)
        def _(parts=parts):
            low = 0
            for part in parts:
                size = pieces[part].shape[0]
                rows_ref[low : low + size, :] = pieces[part][...]
                low += size

    @pl.when(step < blocks)
    def _():
        at = pl.ds(pl.multiple_of(order_ref[step] * rows, rows), rows)
        do_ref[at, :] = dot_nt(rows_ref[...], weight_ref[...]).astype(BF16)
        mine = pl.ds(pl.multiple_of(step * rows, rows), rows)
        weight_grad_ref[...] += dot_tn(o_ref[mine, :], rows_ref[...])

    for i in range(count):

        @pl.when(step == blocks + i)
        def _(i=i):
            low, high = i * block, (i + 1) * block
            query, grad = q_ref[low:high, :], do_ref[low:high, :]
            raw = dot_nt(k_ref[:high, :], query)
            keys = lax.broadcasted_iota(jnp.int32, raw.shape, 0)
            queries = low + lax.broadcasted_iota(jnp.int32, raw.shape, 1)
            allowed = (keys <= queries) & (keys >= start_ref[:, low:high])
            raw = jnp.where(allowed, raw * factor - lse_ref[:, low:high], NEG)
            probs = jnp.exp2(raw)
            probs_grad = dot_nt(v_ref[:high, :], grad)
            inner = jnp.sum(probs_grad * probs, axis=0, keepdims=True)
            score_grad = (probs * (probs_grad - inner)).astype(BF16)
            dv_ref[:high, :] += dot(probs.astype(BF16), grad)
            dk_ref[:high, :] += dot(score_grad, query)
            dq_ref[low:high, :] = dot(kt_ref[:, :high], score_grad).T

    @pl.when(step == blocks + count - 1)
    def _():
        for n in range(blocks):
            at = pl.ds(pl.multiple_of(order_ref[n] * rows, rows), rows)
            to = slice(n * rows, (n + 1) * rows)
            cos_table, sin_table = cos_ref[at, :], -sin_ref[at, :]
            out_ref[to, :HEAD_DIM] = turn(dq_ref[at, :] * scale, cos_table, sin_table).astype(BF16)
            out_ref[to, HEAD_DIM : 2 * HEAD_DIM] = turn(
                dk_ref[at, :] * scale, cos_table, sin_table
            ).astype(BF16)
            out_ref[to, 2 * HEAD_DIM :] = dv_ref[at, :].astype(BF16)


def attend_back(grads, order, weight, query, key, value, mixed, lse, first_place, cos_table, sin_table):
    pieces, sources = flatten(grads)
    length = query.shape[0]
    block = min(256, length)
    rows = length // len(sources)
    whole = lambda shape: pl.BlockSpec(shape, lambda i, order: (0, 0))
    head = whole((length, HEAD_DIM))
    return pl.pallas_call(
        functools.partial(attend_back_kernel, sources, block),
        out_shape=[
            jax.ShapeDtypeStruct((length, 3 * HEAD_DIM), BF16),
            jax.ShapeDtypeStruct(weight.shape, F32),
        ],
        grid_spec=pltpu.PrefetchScalarGridSpec(
            num_scalar_prefetch=1,
            grid=(len(sources) + length // block,),
            in_specs=[whole(piece.shape) for piece in pieces]
            + [whole(weight.shape)]
            + [head] * 4
            + [whole((1, length))] * 2
            + [head] * 2,
            out_specs=[whole((length, 3 * HEAD_DIM)), whole(weight.shape)],
            scratch_shapes=[
                pltpu.VMEM((rows, weight.shape[1]), BF16),
                pltpu.VMEM((HEAD_DIM, length), BF16),
                pltpu.VMEM((length, HEAD_DIM), BF16),
            ]
            + [pltpu.VMEM((length, HEAD_DIM), F32)] * 3,
        ),
        compiler_params=pltpu.CompilerParams(vmem_limit_bytes=56 * 2**20),
        cost_estimate=cost(30),
        name="attend_back",
    )(order, *pieces, weight, query, key, value, mixed, lse, first_place, cos_table, sin_table)


def dp_order(parts):
    count = len(parts)
    here = lax.axis_index("dp")
    if count == 1:
        return parts[0][None]
    if count == 2:
        first = here == 0
        return jnp.stack(
            [jnp.where(first, parts[0], parts[1]), jnp.where(first, parts[1], parts[0])]
        )
    whole = jnp.zeros((count,) + parts[0].shape, parts[0].dtype)
    for step, part in enumerate(parts):
        whole = lax.dynamic_update_index_in_dim(whole, part, (here + step) % count, 0)
    return whole


def dp_parts(value):
    count = lax.axis_size("dp")
    return [value] + [
        lax.ppermute(value, "dp", [(i, (i - step) % count) for i in range(count)])
        for step in range(1, count)
    ]


def dp_gather(value):
    return dp_order(dp_parts(value))


def dp_scatter(value):
    count = lax.axis_size("dp")
    here = lax.axis_index("dp")
    total = lax.dynamic_index_in_dim(value, here, 0, keepdims=False)
    for step in range(1, count):
        block = lax.dynamic_index_in_dim(value, (here + step) % count, 0, keepdims=False)
        got = lax.ppermute(
            block.astype(BF16), "dp", [(i, (i + step) % count) for i in range(count)]
        )
        total = total + got.astype(F32)
    return total


def ring_order():
    pairs = lax.axis_size("expert") // 2
    return list(range(0, pairs, 2)) + list(range(pairs - 1, 0, -2))


def ring_shift(value, step):
    order = ring_order()
    pairs = len(order)
    perm = [
        (order[q] * 2 + c, order[(q + step) % pairs] * 2 + c) for q in range(pairs) for c in range(2)
    ]
    return lax.ppermute(value, "expert", perm)


def core_swap(value):
    count = lax.axis_size("expert")
    return lax.ppermute(value, "expert", [(i, i ^ 1) for i in range(count)])


def ring_offsets():
    half = lax.axis_size("expert") // 4
    return [0] + [o for step in range(1, half) for o in (step, -step)] + [half]


def ring_blocks():
    order = ring_order()
    pairs = len(order)
    table = [[0] * (2 * pairs) for _ in range(2 * pairs)]
    for q in range(pairs):
        for c in range(2):
            for j, offset in enumerate(ring_offsets()):
                for other in range(2):
                    table[order[q] * 2 + c][2 * j + other] = (
                        order[(q - offset) % pairs] * 2 + (c ^ other)
                    )
    return lax.dynamic_index_in_dim(
        jnp.asarray(table, jnp.int32), lax.axis_index("expert"), 0, keepdims=False
    )


def tied(value, *tokens):
    firsts = [lax.slice(t, (0,) * t.ndim, (1,) * t.ndim).reshape(()) for t in tokens]
    token = sum(t.astype(F32) for t in firsts) * 0.0
    return (value.astype(F32) * (1.0 + token)).astype(value.dtype)


def ring_gather(value, gates=None):
    gates = gates or {}
    half_rows = value.shape[0] // 2
    half = lax.axis_size("expert") // 4
    blocks = {}

    def keep(parts, offset):
        blocks[offset] = (parts, [core_swap(part) for part in parts])

    keep([value], 0)
    ahead = back = value
    for step in range(1, half):
        if step in gates:
            token = gates[step](blocks)
            ahead, back = tied(ahead, *token), tied(back, *token)
        ahead, back = ring_shift(ahead, 1), ring_shift(back, -1)
        keep([ahead], step)
        keep([back], -step)
    if half in gates:
        token = gates[half](blocks)
        ahead, back = tied(ahead, *token), tied(back, *token)
    last = [ring_shift(ahead[:half_rows], 1), ring_shift(back[half_rows:], -1)]
    keep(last, half)
    return [parts for offset in ring_offsets() for parts in blocks[offset]]


def flatten(blocks):
    pieces = [piece for parts in blocks for piece in parts]
    sources, n = [], 0
    for parts in blocks:
        sources.append(tuple(range(n, n + len(parts))))
        n += len(parts)
    return pieces, tuple(sources)


def ring_scatter(block, gates=None, marks=None):
    gates = gates or {}
    half = lax.axis_size("expert") // 4
    offsets = ring_offsets()
    spare = {}

    def mine(offset):
        if offset not in spare:
            j = offsets.index(offset)
            spare[offset] = block(2 * j).astype(F32) + core_swap(block(2 * j + 1)).astype(F32)
        return spare[offset]

    far = mine(half).astype(BF16)
    half_rows = far.shape[0] // 2
    ahead = ring_shift(far[:half_rows], 1)
    back = ring_shift(far[half_rows:], -1)
    if marks is not None:
        marks.extend([ahead, back])
    for step in range(half - 1, 0, -1):
        onward, homeward = mine(-step), mine(step)
        if step == half - 1:
            onward = jnp.concatenate(
                [onward[:half_rows] + ahead.astype(F32), onward[half_rows:]], axis=0
            )
            homeward = jnp.concatenate(
                [homeward[:half_rows], homeward[half_rows:] + back.astype(F32)], axis=0
            )
        else:
            onward = onward + ahead.astype(F32)
            homeward = homeward + back.astype(F32)
        if half - step in gates:
            onward, homeward = tied(onward, *gates[half - step]), tied(homeward, *gates[half - step])
        ahead = ring_shift(onward.astype(BF16), 1)
        back = ring_shift(homeward.astype(BF16), -1)
    return mine(0) + ahead.astype(F32) + back.astype(F32)


def chosen(pos_ref, base, window):
    count = pos_ref.shape[-1]
    row = base + lax.broadcasted_iota(jnp.int32, (window, count), 0)
    return row == pos_ref[0]


def dispatch_kernel(sources, widths, window, base_ref, order_ref, pos_ref, gate_ref, *refs):
    outs = refs[-len(widths) - 2 :]
    pieces, blocks, rows_ref, weights_ref = refs[: -len(outs)], outs[:-2], outs[-2], outs[-1]
    step = pl.program_id(0)

    @pl.when(step == 0)
    def _():
        rows_ref[...] = jnp.zeros_like(rows_ref)
        weights_ref[...] = jnp.zeros_like(weights_ref)

    for n, parts in enumerate(sources):

        @pl.when(step == n)
        def _(parts=parts):
            low = 0
            for part in parts:
                size = pieces[part].shape[0]
                left = 0
                for block, wide in zip(blocks, widths):
                    block[low : low + size, :] = pieces[part][:, left : left + wide]
                    left += wide
                low += size

    base = pl.multiple_of(base_ref[step], 16)
    pick = chosen(pos_ref, base, window)
    at = pl.ds(base, window)
    found = dot(pick.astype(F32).astype(BF16), (blocks or pieces)[0][...])
    rows_ref[at, :] = (rows_ref[at, :].astype(F32) + found).astype(BF16)
    weights_ref[at, :] += jnp.sum(jnp.where(pick, gate_ref[0], 0.0), axis=1, keepdims=True)


def dispatch(blocks, widths, packing, order, gates):
    base, pos, _, window, packed = packing
    count, _, rows = pos.shape
    if isinstance(blocks, list):
        pieces, sources = flatten(blocks)
        piece_specs = [pl.BlockSpec(piece.shape, lambda i, base, order: (0, 0)) for piece in pieces]
    else:
        pieces, sources, widths = [blocks], (), []
        piece_specs = [pl.BlockSpec((rows, blocks.shape[1]), lambda i, base, order: (order[i], 0))]
    width = (widths or [pieces[0].shape[1]])[0]
    return pl.pallas_call(
        functools.partial(dispatch_kernel, sources, tuple(widths), window),
        out_shape=[jax.ShapeDtypeStruct((rows * count, wide), BF16) for wide in widths]
        + [
            jax.ShapeDtypeStruct((packed, width), BF16),
            jax.ShapeDtypeStruct((packed, 1), F32),
        ],
        grid_spec=pltpu.PrefetchScalarGridSpec(
            num_scalar_prefetch=2,
            grid=(count,),
            in_specs=[
                pl.BlockSpec((1, 1, rows), lambda i, base, order: (i, 0, 0)),
                pl.BlockSpec((1, 1, rows), lambda i, base, order: (order[i], 0, 0)),
            ]
            + piece_specs,
            out_specs=[
                pl.BlockSpec((rows, wide), lambda i, base, order: (order[i], 0)) for wide in widths
            ]
            + [
                pl.BlockSpec((packed, width), lambda i, base, order: (0, 0)),
                pl.BlockSpec((packed, 1), lambda i, base, order: (0, 0)),
            ],
        ),
        compiler_params=pltpu.CompilerParams(vmem_limit_bytes=52 * 2**20),
        cost_estimate=cost(13),
        name="dispatch",
    )(base, order, pos, gates, *pieces)


def fetch(parts, starts_ref, wholes, counts, sems):
    copies, n = [], 0
    for whole, count in zip(wholes, counts):
        copies.append([])
        for _ in range(count):
            at = pl.ds(pl.multiple_of(starts_ref[n], 16), parts[n].shape[0])
            copies[-1].append(pltpu.make_async_copy(parts[n], whole.at[at, :], sems.at[n]))
            n += 1
    return copies


def expert_kernel(counts, total_ref, starts_ref, x_ref, *refs):
    parts, refs = refs[: sum(counts)], refs[sum(counts) :]
    pre_ref, ea_ref, y_ref, up_ref, down_ref, sems = refs
    step = pl.program_id(0)
    rows, hidden = ea_ref.shape
    ups, downs = fetch(parts, starts_ref, (up_ref, down_ref), counts, sems)
    some = (step == 0) | (step * rows < total_ref[0])

    @pl.when(step == 0)
    def _():
        for copy in ups + downs:
            copy.start()
        for copy in ups:
            copy.wait()

    @pl.when(some)
    def _():
        pre = dot(x_ref[...], up_ref[...])
        pre_ref[...] = pre
        gate_part = pre[:, :hidden]
        act = (gate_part / (1.0 + jnp.exp(-gate_part)) * pre[:, hidden:]).astype(BF16)
        ea_ref[...] = act

        @pl.when(step == 0)
        def _():
            for copy in downs:
                copy.wait()

        y_ref[...] = dot(act, down_ref[...]).astype(BF16)

    @pl.when(jnp.logical_not(some))
    def _():
        for ref in (ea_ref, y_ref):
            ref[...] = jnp.zeros_like(ref)


def expert_back_kernel(counts, total_ref, starts_ref, g_ref, gate_ref, pre_ref, y_ref, *refs):
    parts, refs = refs[: sum(counts)], refs[sum(counts) :]
    dn_ref, dy_ref, db_ref, dg_ref, down_ref, up_ref, sems = refs
    step = pl.program_id(0)
    rows = g_ref.shape[0]
    hidden = down_ref.shape[0]
    downs, ups = fetch(parts, starts_ref, (down_ref, up_ref), counts, sems)
    some = (step == 0) | (step * rows < total_ref[0])

    @pl.when(step == 0)
    def _():
        for copy in downs + ups:
            copy.start()
        for copy in downs:
            copy.wait()

    @pl.when(some)
    def _():
        grad = g_ref[...].astype(F32)
        dg_ref[...] = jnp.sum(grad * y_ref[...].astype(F32), axis=1, keepdims=True)
        out_grad = (gate_ref[...] * grad).astype(BF16)
        dy_ref[...] = out_grad
        act_grad = dot_nt(out_grad, down_ref[...])
        gate_part, up_part = pre_ref[:, :hidden], pre_ref[:, hidden:]
        sigmoid_gate = 1.0 / (1.0 + jnp.exp(-gate_part))
        db_ref[:, :hidden] = (
            act_grad * up_part * sigmoid_gate * (1.0 + gate_part * (1.0 - sigmoid_gate))
        ).astype(BF16)
        db_ref[:, hidden:] = (act_grad * gate_part * sigmoid_gate).astype(BF16)

        @pl.when(step == 0)
        def _():
            for copy in ups:
                copy.wait()

        dn_ref[...] = dot_nt(db_ref[...], up_ref[...]).astype(BF16)

    @pl.when(jnp.logical_not(some))
    def _():
        for ref in (dn_ref, dy_ref, db_ref, dg_ref):
            ref[...] = jnp.zeros_like(ref)


def expert_call(kernel, name, total, tiled, weights, outs):
    packed = tiled[0].shape[0]
    tile = 256
    parts = [part for group in weights for part, _ in group]
    starts = jnp.stack([start for group in weights for _, start in group]).astype(jnp.int32)
    spec = lambda wide: pl.BlockSpec((tile, wide), lambda i, total, starts: (i, 0))
    return pl.pallas_call(
        functools.partial(kernel, tuple(len(group) for group in weights)),
        out_shape=[jax.ShapeDtypeStruct((packed, wide), kind) for wide, kind in outs],
        grid_spec=pltpu.PrefetchScalarGridSpec(
            num_scalar_prefetch=2,
            grid=(packed // tile,),
            in_specs=[spec(array.shape[1]) for array in tiled]
            + [pl.BlockSpec(memory_space=pl.ANY)] * len(parts),
            out_specs=[spec(wide) for wide, _ in outs],
            scratch_shapes=[
                pltpu.VMEM((sum(p.shape[0] for p, _ in group), group[0][0].shape[1]), BF16)
                for group in weights
            ]
            + [pltpu.SemaphoreType.DMA((len(parts),))],
        ),
        compiler_params=pltpu.CompilerParams(vmem_limit_bytes=58 * 2**20),
        cost_estimate=cost(27),
        name=name,
    )(total, starts, *tiled, *parts)


def upright(line):
    count = line.shape[1]
    row = lax.broadcasted_iota(jnp.int32, (count, count), 0)
    lane = lax.broadcasted_iota(jnp.int32, (count, count), 1)
    return jnp.sum(jnp.where(row == lane, line, 0.0), axis=1, keepdims=True)


def combine_kernel(turned, window, extra, base_ref, order_ref, to_ref, me_ref, pos_ref, rows_ref, side_ref, act_ref, weight_ref, out_ref):
    base = pl.multiple_of(base_ref[pl.program_id(0)], 16)
    pick = chosen(pos_ref, base, window)
    at = pl.ds(base, window)
    width = rows_ref.shape[1]
    found = dot_tn(pick.astype(F32).astype(BF16), rows_ref[at, :])
    if not turned:
        found = found * upright(side_ref[0])
    found = found + (dot_nt if turned else dot)(act_ref[...], weight_ref[...])
    out_ref[:, :width] = found.astype(BF16)
    if turned:
        line = jnp.sum(jnp.where(pick, side_ref[at, :], 0.0), axis=0, keepdims=True)
        column = upright(line)
        high = column.astype(BF16).astype(F32)
        lane = lax.broadcasted_iota(jnp.int32, (pick.shape[1], extra), 1)
        out_ref[:, width:] = jnp.where(
            lane == me_ref[0], high, jnp.where(lane == me_ref[0] + extra // 2, column - high, 0.0)
        ).astype(BF16)


def combine(packing, order, to, me, rows, side, act, weight, turned, extra):
    base, pos, _, window, packed = packing
    blocks, _, count = pos.shape
    width = rows.shape[-1]
    whole = lambda ref: pl.BlockSpec(ref.shape, lambda i, *_: (0, 0))
    return pl.pallas_call(
        functools.partial(combine_kernel, turned, window, extra),
        out_shape=jax.ShapeDtypeStruct((blocks * count, width + extra), BF16),
        grid_spec=pltpu.PrefetchScalarGridSpec(
            num_scalar_prefetch=4,
            grid=(blocks,),
            in_specs=[
                pl.BlockSpec((1, 1, count), lambda i, *_: (i, 0, 0)),
                whole(rows),
                whole(side)
                if turned
                else pl.BlockSpec((1, 1, count), lambda i, base, order, to, me: (order[i], 0, 0)),
                pl.BlockSpec((count, act.shape[1]), lambda i, base, order, to, me: (order[i], 0)),
                whole(weight),
            ],
            out_specs=pl.BlockSpec(
                (count, width + extra), lambda i, base, order, to, me: (to[i], 0)
            ),
        ),
        compiler_params=pltpu.CompilerParams(vmem_limit_bytes=40 * 2**20),
        cost_estimate=cost(10),
        name="combine",
    )(base, order, to, me.reshape(1), pos, rows, side, act, weight)


def gather_all(value):
    return lax.all_gather(value, "expert", axis=0, tiled=True)


def swap(value):
    return lax.all_to_all(value, "expert", split_axis=0, concat_axis=0, tiled=True)


def per_device(
    tokens,
    cotangent,
    segment_ids,
    routes,
    attn_in,
    attn_out,
    gain_attn,
    shared_in,
    shared_out,
    router,
    gain_ffn,
    expert_in,
    expert_out,
):
    n_dp, n_e = lax.axis_size("dp"), lax.axis_size("expert")
    me = lax.axis_index("expert")
    count, width = tokens.shape
    segments = segment_ids[0]
    length = segments.shape[0]
    rows = attn_in.shape[0]
    capacity = min(count, 3 * TOP * count // (2 * n_e))
    shared_rows = shared_out.shape[0]
    shared_width = shared_rows * n_dp
    expert_width = expert_out.shape[1] * n_dp

    order = ring_blocks()
    steady = jnp.arange(n_e, dtype=jnp.int32)
    hidden_in = tokens.astype(F32)
    inverse_one = lax.rsqrt(jnp.mean(hidden_in * hidden_in, axis=-1, keepdims=True) + EPS)
    normed_one = hidden_in * inverse_one
    gain_rows = gain_attn.astype(F32)[:, None]
    scaled_w = (attn_in.astype(F32) * gain_rows).astype(BF16)
    each = count // rows
    side = jnp.concatenate([router, gain_ffn[:, None]], axis=1)
    side = jnp.pad(side, ((0, 0), (0, 32 - side.shape[1])))
    side = jnp.concatenate([side, routes.reshape(rows, each * TOP).astype(BF16)], axis=1)
    side = jnp.pad(side, ((0, 0), (0, HEAD_DIM - side.shape[1])))
    packs = dp_parts(jnp.concatenate([scaled_w, side], axis=1))
    head_w = []

    def relay(pack):
        weight = pack[:, : 3 * width].reshape(rows, 3, n_e, HEAD_DIM).transpose(2, 0, 1, 3)
        weight = weight.reshape(n_e, rows, 3 * HEAD_DIM)
        own = jnp.broadcast_to(pack[None, :, 3 * width :], (n_e, rows, HEAD_DIM))
        return jnp.concatenate([weight, own], axis=2)

    def head_own(blocks):
        head_w.append(swap(relay(tied(packs[0], blocks[0][1][0]))))
        return head_w[0]

    def head_rest(blocks):
        for pack in packs[1:]:
            head_w.append(swap(relay(pack)))
        return head_w[-1]

    here = lax.axis_index("dp")

    def spread(shard, chunks):
        while shard.shape[0] % (16 * chunks):
            chunks -= 1
        size = shard.shape[0] // chunks
        parts = [[(shard, here * shard.shape[0])]]
        for j in range(chunks):
            parts.append([])
            for step in range(1, n_dp):
                got = lax.ppermute(
                    shard[j * size : (j + 1) * size],
                    "dp",
                    [(i, (i - step) % n_dp) for i in range(n_dp)],
                )
                parts[-1].append((got, (here + step) % n_dp * shard.shape[0] + j * size))
        return parts

    expert_up = lax.all_gather(expert_in, "dp", axis=1, tiled=True)[0]
    down_parts = spread(expert_out[0], 2)
    first = lambda parts: [part for part, _ in parts]
    down_tokens = [first(parts) for parts in down_parts[1:]] + [[]]

    cos_table, sin_table, first_place = rope_tables(segments)
    share_w = shared_in.reshape(rows, 2, n_dp, n_e, shared_rows).transpose(3, 0, 1, 2, 4)
    share_w = share_w.reshape(n_e, rows, 2 * shared_width)

    split = HEAD_DIM // rows
    head_out_w = []
    for r in range(split):
        parts = [
            lax.ppermute(
                attn_out, ("dp", "expert"), [(h * split + r, d * n_e + h) for h in range(n_e)]
            )
            for d in range(n_dp)
        ]
        head_out_w.append(sum(part.astype(F32) for part in parts).astype(BF16))
    head_out_w = jnp.concatenate(head_out_w)

    half = n_e // 4
    norm_blocks = ring_gather(
        normed_one.astype(BF16),
        {
            half - 2: lambda blocks: packs[1:],
            half - 1: lambda blocks: [head_own(blocks), share_w],
            half: lambda blocks: [head_rest(blocks), cos_table, sin_table, head_out_w],
        },
    )
    routes_all = head_w[0][:, :, 3 * HEAD_DIM + 32 : 3 * HEAD_DIM + 32 + each * TOP]
    routes_all = routes_all.reshape(length, TOP).astype(F32)
    head_w = dp_order(head_w).reshape(width, 4 * HEAD_DIM)
    router_full = head_w[:, 3 * HEAD_DIM : 3 * HEAD_DIM + n_e]
    gain_second = head_w[:, 3 * HEAD_DIM + n_e].astype(F32)
    head_w = head_w[:, : 3 * HEAD_DIM]

    head_out, query, key, value, lse, norm_all = attend(
        norm_blocks, order, head_w, cos_table, sin_table, first_place
    )
    share_w = swap(tied(share_w, head_w))
    mixed_part = dot(head_out, head_out_w).astype(BF16)
    resid = hidden_in + ring_scatter(
        lambda n: mixed_part[n * count : (n + 1) * count],
        {half - 2: [share_w], half - 1: down_tokens[0] or [lse]},
    )

    share_w = dp_gather(share_w).reshape(width, 2 * shared_width)
    share_out = dp_gather(shared_out).reshape(shared_width, width)

    inverse_two = lax.rsqrt(jnp.mean(resid * resid, axis=-1, keepdims=True) + EPS)
    normed_two = resid * inverse_two
    norm_two = (normed_two * gain_second).astype(BF16)
    logits = dot(norm_two, router_full)
    picked = jnp.any(routes[:, :, None] == jnp.arange(n_e)[None, None, :], axis=1)
    chosen = jnp.where(picked, logits, NEG)
    chosen = jnp.where(picked, jnp.exp(chosen - jnp.max(chosen, axis=-1, keepdims=True)), 0.0)
    gates = chosen / jnp.sum(chosen, axis=-1, keepdims=True)
    gate_high = gates.astype(BF16)
    gate_low = (gates - gate_high.astype(F32)).astype(BF16)
    blank = jnp.zeros((count, 128 - 2 * n_e), BF16)
    payload = jnp.concatenate([norm_two, gate_high, gate_low, blank], axis=1)
    norm_blocks = ring_gather(
        payload,
        {
            half: lambda blocks: down_tokens[1] or [lse],
        },
    )

    cot_all = gather_all(tied(cotangent, norm_blocks[-1][0], norm_blocks[-1][1]))

    named = jnp.any(routes_all == me.astype(F32), axis=1).reshape(n_e, count)
    named = jnp.take(named, order, axis=0)
    ranking = jnp.cumsum(named.astype(jnp.int32), axis=1)
    ends = jnp.cumsum(ranking[:, -1])
    begins = ends - ranking[:, -1]
    pos = jnp.where(named, begins[:, None] + ranking - 1, -1)[:, None, :]
    window = -(-(capacity + 15) // 16) * 16
    packed = -(-(n_e * capacity + 32) // 256) * 256
    packing = (begins // 16 * 16, pos, ends[-1:], window, packed)
    norm_two_all, payload, arrived, _ = dispatch(
        norm_blocks, [width, 128], packing, order, jnp.zeros((n_e, 1, count), F32)
    )
    mine = jnp.arange(n_e) == me
    gate_all = payload[:, : 2 * n_e].astype(F32).reshape(length, 2, n_e)
    gate_all = jnp.sum(jnp.where(mine, gate_all, 0.0), axis=(1, 2)).reshape(n_e, 1, count)
    ups = [(expert_up, jnp.int32(0))]
    downs = [part for parts in down_parts for part in parts]
    expert_width = expert_out.shape[1] * n_dp
    expert_pre, expert_act, expert_res = expert_call(
        expert_kernel,
        "expert",
        packing[2],
        [arrived],
        [ups, downs],
        [(2 * expert_width, F32), (expert_width, BF16), (width, BF16)],
    )

    shared_pre = dot(norm_two_all, share_w)
    shared_act = (
        jax.nn.silu(shared_pre[:, :shared_width]) * shared_pre[:, shared_width:]
    ).astype(BF16)
    out_part = combine(
        packing, order, order, me, expert_res, gate_all, shared_act, share_out, False, 0
    )
    routed_out = lax.psum_scatter(out_part, "expert", scatter_dimension=0, tiled=True)

    cot_rows, gate_rows = dispatch(cot_all, None, packing, order, gate_all)
    row_grad, route_grad, pre_grad, gate_grad = expert_call(
        expert_back_kernel,
        "expert_back",
        packing[2],
        [cot_rows, gate_rows, expert_pre, expert_res],
        [downs, ups],
        [(width, BF16), (width, BF16), (2 * expert_width, BF16), (1, F32)],
    )
    shared_act_grad = dot_nt(cot_all, share_out)
    shared_pre_grad = silu_back(
        shared_act_grad, shared_pre[:, :shared_width], shared_pre[:, shared_width:]
    ).astype(BF16)
    norm_two_part = combine(
        packing, order, steady, me, row_grad, gate_grad, shared_pre_grad, share_w, True, 128
    )
    share_out_grad = dp_scatter(dot_tn(shared_act, cot_all).reshape(n_dp, shared_rows, width))
    share_in_grad = dot_tn(norm_two_all, shared_pre_grad)
    share_in_grad = dp_scatter(share_in_grad.reshape(n_dp, n_e, rows, 2 * shared_width)).astype(BF16)
    marks = []
    norm_two_grad = ring_scatter(
        lambda n: norm_two_part[n * count : (n + 1) * count],
        {half - 2: [share_out_grad, share_in_grad]},
        marks,
    )
    share_in_sent = swap(share_in_grad)
    share_in_grad = share_in_sent.astype(F32)
    gate_grad = norm_two_grad[:, width : width + n_e] + norm_two_grad[:, width + 64 : width + 64 + n_e]
    norm_two_grad = norm_two_grad[:, :width]

    up_grad = dot_tn(tied(arrived, share_out_grad, share_in_grad), pre_grad).astype(BF16)
    expert_in_grad = lax.psum_scatter(up_grad, "dp", scatter_dimension=0, tiled=True)
    size = expert_out.shape[1]
    cut = lambda i: tied(lax.dynamic_slice_in_dim(expert_act, i % n_dp * size, size, 1), *marks)
    down_grad = dot_tn(cut(here), route_grad)
    down_got = [
        lax.ppermute(
            dot_tn(cut(here + step), route_grad).astype(BF16),
            "dp",
            [(i, (i + step) % n_dp) for i in range(n_dp)],
        )
        for step in range(1, n_dp)
    ]
    share_in_grad = (
        share_in_grad.reshape(n_e, rows, 2, n_dp, shared_rows)
        .transpose(1, 2, 3, 0, 4)
        .reshape(rows, -1)
    )

    logit_grad = gates * (gate_grad - jnp.sum(gates * gate_grad, axis=-1, keepdims=True))
    router_grad = jnp.dot(
        logit_grad.T, norm_two.astype(F32), precision=HIGHEST, preferred_element_type=F32
    )
    norm_two_grad = norm_two_grad + jnp.dot(
        logit_grad, router_full.astype(F32).T, precision=HIGHEST, preferred_element_type=F32
    )
    gain_two_grad = jnp.sum(norm_two_grad * normed_two, axis=0)
    upstream = cotangent.astype(F32)
    scaled_two = norm_two_grad * gain_second
    resid_grad = upstream + inverse_two * (
        scaled_two - normed_two * jnp.mean(scaled_two * normed_two, axis=-1, keepdims=True)
    )
    small_grad = jnp.concatenate([router_grad, gain_two_grad[None]], axis=0)

    branch_cot = resid_grad.astype(BF16)
    branch_blocks = ring_gather(
        branch_cot,
        {half - 1: lambda blocks: [share_in_sent], half: lambda blocks: down_got},
    )
    qkv_grad, proj_grad = attend_back(
        branch_blocks, order, head_out_w, query, key, value, head_out, lse, first_place, cos_table, sin_table
    )
    proj_grad = proj_grad.astype(BF16)
    routed = []
    for r in range(split):
        for shift in range(n_dp):
            perm = [
                (((h * split + r) // n_e + shift) % n_dp * n_e + h, h * split + r)
                for h in range(n_e)
            ]
            part = lax.ppermute(proj_grad[r * rows : (r + 1) * rows], ("dp", "expert"), perm)
            routed.append(part)
    attn_out_grad = sum(part.astype(F32) for part in routed)
    small_grad = tied(small_grad, qkv_grad).reshape(n_e + 1, n_dp * n_e, rows).transpose(1, 0, 2)
    small_grad = lax.all_to_all(
        small_grad, ("dp", "expert"), split_axis=0, concat_axis=0, tiled=True
    )
    small_grad = jnp.sum(small_grad, axis=0)
    norm_one_part = dot_nt(qkv_grad, head_w).astype(BF16)
    scaled_one = ring_scatter(
        lambda n: norm_one_part[n * count : (n + 1) * count], {half - 2: routed}
    )
    expert_in_grad = expert_in_grad.astype(F32)[None]
    expert_out_grad = (down_grad + sum(part.astype(F32) for part in down_got))[None]
    input_grad = resid_grad + inverse_one * (
        scaled_one - normed_one * jnp.mean(scaled_one * normed_one, axis=-1, keepdims=True)
    )
    head_grad = dot_tn(norm_all, qkv_grad).reshape(n_dp, n_e, rows, 3 * HEAD_DIM)
    head_grad = swap(dp_scatter(head_grad).astype(BF16)).astype(F32)
    head_grad = (
        head_grad.reshape(n_e, rows, 3, HEAD_DIM).transpose(1, 2, 0, 3).reshape(rows, 3 * width)
    )
    gain_attn_grad = jnp.sum(head_grad * attn_in.astype(F32), axis=1)
    attn_in_grad = head_grad * gain_rows
    return (
        (resid + routed_out.astype(F32)).astype(BF16),
        input_grad.astype(BF16),
        attn_in_grad,
        attn_out_grad,
        gain_attn_grad,
        share_in_grad,
        share_out_grad,
        small_grad[:n_e].T,
        small_grad[n_e],
        expert_in_grad,
        expert_out_grad,
    )


def solution(mesh):
    return jax.shard_map(
        per_device,
        mesh=mesh,
        in_specs=(
            P(("dp", "expert"), None),
            P(("dp", "expert"), None),
            P("dp", None),
            P(("dp", "expert"), None),
            P(("dp", "expert"), None),
            P(("dp", "expert"), None),
            P(("dp", "expert")),
            P(("dp", "expert"), None),
            P(("dp", "expert"), None),
            P(("dp", "expert"), None),
            P(("dp", "expert")),
            P("expert", "dp", None),
            P("expert", "dp", None),
        ),
        out_specs=(
            P(("dp", "expert"), None),
            P(("dp", "expert"), None),
            P(("dp", "expert"), None),
            P(("dp", "expert"), None),
            P(("dp", "expert")),
            P(("dp", "expert"), None),
            P(("dp", "expert"), None),
            P(("dp", "expert"), None),
            P(("dp", "expert")),
            P("expert", "dp", None),
            P("expert", "dp", None),
        ),
        check_vma=False,
    )
```

```python
import functools
import math

import jax
import jax.numpy as jnp
from jax import lax
from jax.experimental import pallas as pl
from jax.experimental.pallas import tpu as pltpu
from jax.sharding import PartitionSpec as P

HEADS = 16
HEAD_DIM = 128
TOP = 6


EPS = 1e-06
THETA = 10000.0
NEG = -1e30
HIGHEST = lax.Precision.HIGHEST
BF16 = jnp.bfloat16
F32 = jnp.float32
LOG2E = math.log2(math.e)


def rope_tables(segments):
    length = segments.shape[0]
    places = jnp.arange(length, dtype=jnp.int32)
    starts = jnp.concatenate([jnp.ones((1,), dtype=jnp.bool_), segments[1:] != segments[:-1]])
    first_place = lax.cummax(jnp.where(starts, places, 0), axis=0)
    offset = (places - first_place).astype(jnp.float32)
    half_dim = HEAD_DIM // 2
    freqs = jnp.exp(jnp.arange(half_dim, dtype=jnp.float32) * (-2.0 * math.log(THETA) / HEAD_DIM))
    angles = offset[:, None] * freqs[None, :]
    cos_table, sin_table = jnp.cos(angles), jnp.sin(angles)
    return (
        jnp.concatenate([cos_table, cos_table], axis=1),
        jnp.concatenate([-sin_table, sin_table], axis=1),
        first_place[None, :],
    )


def silu_back(grad_act, gate_part, up_part):
    sigmoid_gate = jax.nn.sigmoid(gate_part)
    gate_grad = grad_act * up_part * sigmoid_gate * (1.0 + gate_part * (1.0 - sigmoid_gate))
    up_grad = grad_act * gate_part * sigmoid_gate
    return jnp.concatenate([gate_grad, up_grad], axis=-1)


def dot(left, right):
    return jnp.dot(left, right, preferred_element_type=F32)


def dot_tn(left, right):
    return lax.dot_general(left, right, (((0,), (0,)), ((), ())), preferred_element_type=F32)


def dot_nt(left, right):
    return lax.dot_general(left, right, (((1,), (1,)), ((), ())), preferred_element_type=F32)


def turn(values, cos_table, sin_table):
    return values * cos_table + pltpu.roll(values, HEAD_DIM // 2, 1) * sin_table


def attend_kernel(sources, block, order_ref, *refs):
    pieces = refs[: sources[-1][-1] + 1]
    weight_ref, cos_ref, sin_ref, start_ref = refs[len(pieces) : len(pieces) + 4]
    o_ref, q_ref, k_ref, v_ref, lse_ref, rows_ref, vt_ref = refs[len(pieces) + 4 :]
    step = pl.program_id(0)
    length = q_ref.shape[0]
    factor = HEAD_DIM ** (-0.5) * LOG2E
    rows = rows_ref.shape[0]

    for n, parts in enumerate(sources):

        @pl.when(step == n)
        def _(parts=parts):
            low = 0
            for part in parts:
                size = pieces[part].shape[0]
                rows_ref[low : low + size, :] = pieces[part][...]
                low += size

    @pl.when(step < len(sources))
    def _():
        qkv = dot(rows_ref[...], weight_ref[...])
        at = pl.ds(pl.multiple_of(order_ref[step] * rows, rows), rows)
        cos_table, sin_table = cos_ref[at, :], sin_ref[at, :]
        q_ref[at, :] = turn(qkv[:, :HEAD_DIM], cos_table, sin_table).astype(BF16)
        k_ref[at, :] = turn(qkv[:, HEAD_DIM : 2 * HEAD_DIM], cos_table, sin_table).astype(BF16)
        value = qkv[:, 2 * HEAD_DIM :]
        v_ref[at, :] = value.astype(BF16)
        vt_ref[:, at] = value.T.astype(BF16)

    for i in range(length // block):

        @pl.when(step == len(sources) + i)
        def _(i=i):
            low, high = i * block, (i + 1) * block
            raw = dot_nt(k_ref[:high, :], q_ref[low:high, :])
            keys = lax.broadcasted_iota(jnp.int32, raw.shape, 0)
            queries = low + lax.broadcasted_iota(jnp.int32, raw.shape, 1)
            allowed = (keys <= queries) & (keys >= start_ref[:, low:high])
            raw = jnp.where(allowed, raw, NEG)
            top = jnp.max(raw, axis=0, keepdims=True)
            shifted = jnp.exp2((raw - top) * factor)
            total = jnp.sum(shifted, axis=0, keepdims=True)
            probs = (shifted * (1.0 / total)).astype(BF16)
            mixed = dot(vt_ref[:, :high], probs)
            o_ref[low:high, :] = mixed.T.astype(BF16)
            lse_ref[:, low:high] = top * factor + jnp.log2(total)


def attend(blocks, order, weight, cos_table, sin_table, first_place):
    pieces, sources = flatten(blocks)
    length = cos_table.shape[0]
    rows = length // len(sources)
    width = weight.shape[0]
    block = min(256, length)
    last = len(sources) - 1
    whole = lambda shape: pl.BlockSpec(shape, lambda i, order: (0, 0))
    head = jax.ShapeDtypeStruct((length, HEAD_DIM), BF16)
    return pl.pallas_call(
        functools.partial(attend_kernel, sources, block),
        out_shape=[head] * 4
        + [jax.ShapeDtypeStruct((1, length), F32), jax.ShapeDtypeStruct((length, width), BF16)],
        grid_spec=pltpu.PrefetchScalarGridSpec(
            num_scalar_prefetch=1,
            grid=(len(sources) + length // block,),
            in_specs=[whole(piece.shape) for piece in pieces]
            + [
                whole(weight.shape),
                whole((length, HEAD_DIM)),
                whole((length, HEAD_DIM)),
                whole((1, length)),
            ],
            out_specs=[whole((length, HEAD_DIM))] * 4
            + [
                whole((1, length)),
                pl.BlockSpec((rows, width), lambda i, order: (jnp.minimum(i, last), 0)),
            ],
            scratch_shapes=[pltpu.VMEM((HEAD_DIM, length), BF16)],
        ),
        compiler_params=pltpu.CompilerParams(vmem_limit_bytes=52 * 2**20),
        name="attend",
    )(order, *pieces, weight, cos_table, sin_table, first_place)


def attend_back_kernel(
    block, rows, order_ref, q_ref, k_ref, v_ref, do_ref, lse_ref, start_ref, cos_ref, sin_ref, out_ref, kt_ref, dq_ref, dk_ref, dv_ref
):
    length = q_ref.shape[0]
    step = pl.program_id(0)
    scale = HEAD_DIM ** (-0.5)
    factor = scale * LOG2E
    count = length // block

    @pl.when(step == 0)
    def _():
        kt_ref[...] = k_ref[...].astype(F32).T.astype(BF16)
        dk_ref[...] = jnp.zeros_like(dk_ref)
        dv_ref[...] = jnp.zeros_like(dv_ref)

    for i in range(count):

        @pl.when(step == i)
        def _(i=i):
            low, high = i * block, (i + 1) * block
            query, grad = q_ref[low:high, :], do_ref[low:high, :]
            raw = dot_nt(k_ref[:high, :], query)
            keys = lax.broadcasted_iota(jnp.int32, raw.shape, 0)
            queries = low + lax.broadcasted_iota(jnp.int32, raw.shape, 1)
            allowed = (keys <= queries) & (keys >= start_ref[:, low:high])
            raw = jnp.where(allowed, raw * factor - lse_ref[:, low:high], NEG)
            probs = jnp.exp2(raw)
            probs_grad = dot_nt(v_ref[:high, :], grad)
            inner = jnp.sum(probs_grad * probs, axis=0, keepdims=True)
            score_grad = (probs * (probs_grad - inner)).astype(BF16)
            dv_ref[:high, :] += dot(probs.astype(BF16), grad)
            dk_ref[:high, :] += dot(score_grad, query)
            dq_ref[low:high, :] = dot(kt_ref[:, :high], score_grad).T

    @pl.when(step == count - 1)
    def _():
        for n in range(length // rows):
            at = pl.ds(pl.multiple_of(order_ref[n] * rows, rows), rows)
            to = slice(n * rows, (n + 1) * rows)
            cos_table, sin_table = cos_ref[at, :], -sin_ref[at, :]
            out_ref[to, :HEAD_DIM] = turn(dq_ref[at, :] * scale, cos_table, sin_table).astype(BF16)
            out_ref[to, HEAD_DIM : 2 * HEAD_DIM] = turn(
                dk_ref[at, :] * scale, cos_table, sin_table
            ).astype(BF16)
            out_ref[to, 2 * HEAD_DIM :] = dv_ref[at, :].astype(BF16)


def attend_back(query, key, value, grad, lse, first_place, cos_table, sin_table, order):
    length = query.shape[0]
    block = min(256, length)
    whole = lambda shape: pl.BlockSpec(shape, lambda i, order: (0, 0))
    head = whole((length, HEAD_DIM))
    return pl.pallas_call(
        functools.partial(attend_back_kernel, block, length // order.shape[0]),
        out_shape=jax.ShapeDtypeStruct((length, 3 * HEAD_DIM), BF16),
        grid_spec=pltpu.PrefetchScalarGridSpec(
            num_scalar_prefetch=1,
            grid=(length // block,),
            in_specs=[head] * 4 + [whole((1, length))] * 2 + [head] * 2,
            out_specs=whole((length, 3 * HEAD_DIM)),
            scratch_shapes=[pltpu.VMEM((HEAD_DIM, length), BF16)]
            + [pltpu.VMEM((length, HEAD_DIM), F32)] * 3,
        ),
        compiler_params=pltpu.CompilerParams(vmem_limit_bytes=48 * 2**20),
        name="attend_back",
    )(order, query, key, value, grad, lse, first_place, cos_table, sin_table)


def dp_gather(value):
    count = lax.axis_size("dp")
    if count == 1:
        return value[None]
    here = lax.axis_index("dp")
    parts = [value] + [
        lax.ppermute(value, "dp", [(i, (i - step) % count) for i in range(count)])
        for step in range(1, count)
    ]
    if count == 2:
        first = here == 0
        return jnp.stack(
            [jnp.where(first, parts[0], parts[1]), jnp.where(first, parts[1], parts[0])]
        )
    whole = jnp.zeros((count,) + value.shape, value.dtype)
    for step, part in enumerate(parts):
        whole = lax.dynamic_update_index_in_dim(whole, part, (here + step) % count, 0)
    return whole


def dp_scatter(value):
    count = lax.axis_size("dp")
    here = lax.axis_index("dp")
    total = lax.dynamic_index_in_dim(value, here, 0, keepdims=False)
    for step in range(1, count):
        block = lax.dynamic_index_in_dim(value, (here + step) % count, 0, keepdims=False)
        got = lax.ppermute(
            block.astype(BF16), "dp", [(i, (i + step) % count) for i in range(count)]
        )
        total = total + got.astype(F32)
    return total


def ring_order():
    pairs = lax.axis_size("expert") // 2
    return list(range(0, pairs, 2)) + list(range(pairs - 1, 0, -2))


def ring_shift(value, step):
    order = ring_order()
    pairs = len(order)
    perm = [
        (order[q] * 2 + c, order[(q + step) % pairs] * 2 + c) for q in range(pairs) for c in range(2)
    ]
    return lax.ppermute(value, "expert", perm)


def core_swap(value):
    count = lax.axis_size("expert")
    return lax.ppermute(value, "expert", [(i, i ^ 1) for i in range(count)])


def ring_offsets():
    half = lax.axis_size("expert") // 4
    return [0] + [o for step in range(1, half) for o in (step, -step)] + [half]


def ring_blocks():
    order = ring_order()
    pairs = len(order)
    table = [[0] * (2 * pairs) for _ in range(2 * pairs)]
    for q in range(pairs):
        for c in range(2):
            for j, offset in enumerate(ring_offsets()):
                for other in range(2):
                    table[order[q] * 2 + c][2 * j + other] = (
                        order[(q - offset) % pairs] * 2 + (c ^ other)
                    )
    return lax.dynamic_index_in_dim(
        jnp.asarray(table, jnp.int32), lax.axis_index("expert"), 0, keepdims=False
    )


def tied(value, *tokens):
    firsts = [lax.slice(t, (0,) * t.ndim, (1,) * t.ndim).reshape(()) for t in tokens]
    token = sum(t.astype(F32) for t in firsts) * 0.0
    return (value.astype(F32) * (1.0 + token)).astype(value.dtype)


def ring_gather(value, gates=None):
    gates = gates or {}
    half_rows = value.shape[0] // 2
    half = lax.axis_size("expert") // 4
    blocks = {}

    def keep(parts, offset):
        blocks[offset] = (parts, [core_swap(part) for part in parts])

    keep([value], 0)
    ahead = back = value
    for step in range(1, half):
        if step in gates:
            token = gates[step](blocks)
            ahead, back = tied(ahead, *token), tied(back, *token)
        ahead, back = ring_shift(ahead, 1), ring_shift(back, -1)
        keep([ahead], step)
        keep([back], -step)
    if half in gates:
        token = gates[half](blocks)
        ahead, back = tied(ahead, *token), tied(back, *token)
    last = [ring_shift(ahead[:half_rows], 1), ring_shift(back[half_rows:], -1)]
    keep(last, half)
    return [parts for offset in ring_offsets() for parts in blocks[offset]]


def flatten(blocks):
    pieces = [piece for parts in blocks for piece in parts]
    sources, n = [], 0
    for parts in blocks:
        sources.append(tuple(range(n, n + len(parts))))
        n += len(parts)
    return pieces, tuple(sources)


def ring_scatter(block, gates=None, marks=None):
    gates = gates or {}
    half = lax.axis_size("expert") // 4
    offsets = ring_offsets()
    spare = {}

    def mine(offset):
        if offset not in spare:
            j = offsets.index(offset)
            spare[offset] = block(2 * j).astype(F32) + core_swap(block(2 * j + 1)).astype(F32)
        return spare[offset]

    far = mine(half).astype(BF16)
    half_rows = far.shape[0] // 2
    ahead = ring_shift(far[:half_rows], 1)
    back = ring_shift(far[half_rows:], -1)
    if marks is not None:
        marks.extend([ahead, back])
    for step in range(half - 1, 0, -1):
        onward, homeward = mine(-step), mine(step)
        if step == half - 1:
            onward = jnp.concatenate(
                [onward[:half_rows] + ahead.astype(F32), onward[half_rows:]], axis=0
            )
            homeward = jnp.concatenate(
                [homeward[:half_rows], homeward[half_rows:] + back.astype(F32)], axis=0
            )
        else:
            onward = onward + ahead.astype(F32)
            homeward = homeward + back.astype(F32)
        if half - step in gates:
            onward, homeward = tied(onward, *gates[half - step]), tied(homeward, *gates[half - step])
        ahead = ring_shift(onward.astype(BF16), 1)
        back = ring_shift(homeward.astype(BF16), -1)
    return mine(0) + ahead.astype(F32) + back.astype(F32)


def chosen(pos_ref, base, window):
    count = pos_ref.shape[-1]
    row = base + lax.broadcasted_iota(jnp.int32, (window, count), 0)
    return row == pos_ref[0]


def dispatch_kernel(sources, widths, window, base_ref, order_ref, pos_ref, gate_ref, *refs):
    outs = refs[-len(widths) - 2 :]
    pieces, blocks, rows_ref, weights_ref = refs[: -len(outs)], outs[:-2], outs[-2], outs[-1]
    step = pl.program_id(0)

    @pl.when(step == 0)
    def _():
        rows_ref[...] = jnp.zeros_like(rows_ref)
        weights_ref[...] = jnp.zeros_like(weights_ref)

    for n, parts in enumerate(sources):

        @pl.when(step == n)
        def _(parts=parts):
            low = 0
            for part in parts:
                size = pieces[part].shape[0]
                left = 0
                for block, wide in zip(blocks, widths):
                    block[low : low + size, :] = pieces[part][:, left : left + wide]
                    left += wide
                low += size

    base = pl.multiple_of(base_ref[step], 16)
    pick = chosen(pos_ref, base, window)
    at = pl.ds(base, window)
    found = dot(pick.astype(F32).astype(BF16), (blocks or pieces)[0][...])
    rows_ref[at, :] = (rows_ref[at, :].astype(F32) + found).astype(BF16)
    weights_ref[at, :] += jnp.sum(jnp.where(pick, gate_ref[0], 0.0), axis=1, keepdims=True)


def dispatch(blocks, widths, packing, order, gates):
    base, pos, _, window, packed = packing
    count, _, rows = pos.shape
    if isinstance(blocks, list):
        pieces, sources = flatten(blocks)
        piece_specs = [pl.BlockSpec(piece.shape, lambda i, base, order: (0, 0)) for piece in pieces]
    else:
        pieces, sources, widths = [blocks], (), []
        piece_specs = [pl.BlockSpec((rows, blocks.shape[1]), lambda i, base, order: (order[i], 0))]
    width = (widths or [pieces[0].shape[1]])[0]
    return pl.pallas_call(
        functools.partial(dispatch_kernel, sources, tuple(widths), window),
        out_shape=[jax.ShapeDtypeStruct((rows * count, wide), BF16) for wide in widths]
        + [
            jax.ShapeDtypeStruct((packed, width), BF16),
            jax.ShapeDtypeStruct((packed, 1), F32),
        ],
        grid_spec=pltpu.PrefetchScalarGridSpec(
            num_scalar_prefetch=2,
            grid=(count,),
            in_specs=[
                pl.BlockSpec((1, 1, rows), lambda i, base, order: (i, 0, 0)),
                pl.BlockSpec((1, 1, rows), lambda i, base, order: (order[i], 0, 0)),
            ]
            + piece_specs,
            out_specs=[
                pl.BlockSpec((rows, wide), lambda i, base, order: (order[i], 0)) for wide in widths
            ]
            + [
                pl.BlockSpec((packed, width), lambda i, base, order: (0, 0)),
                pl.BlockSpec((packed, 1), lambda i, base, order: (0, 0)),
            ],
        ),
        compiler_params=pltpu.CompilerParams(vmem_limit_bytes=52 * 2**20),
        name="dispatch",
    )(base, order, pos, gates, *pieces)


def expert_kernel(ups, total_ref, starts_ref, x_ref, g_ref, gate_ref, *refs):
    parts, refs = refs[:-9], refs[-9:]
    wy_ref, dn_ref, ea_ref, dy_ref, db_ref, dg_ref, up_ref, down_ref, sems = refs
    step = pl.program_id(0)
    rows, hidden = ea_ref.shape
    some = step * rows < total_ref[0]

    @pl.when(step == 0)
    def _():
        copies = []
        for n, part in enumerate(parts):
            at = pl.ds(pl.multiple_of(starts_ref[n], 16), part.shape[0])
            whole = up_ref if n < ups else down_ref
            copies.append(pltpu.make_async_copy(part, whole.at[at, :], sems.at[n]))
        for copy in copies:
            copy.start()
        for copy in copies:
            copy.wait()

    @pl.when(some)
    def _():
        pre = dot(x_ref[...], up_ref[...])
        gate_part, up_part = pre[:, :hidden], pre[:, hidden:]
        sigmoid_gate = 1.0 / (1.0 + jnp.exp(-gate_part))
        silu = gate_part * sigmoid_gate
        act = (silu * up_part).astype(BF16)
        ea_ref[...] = act
        result = dot(act, down_ref[...]).astype(BF16).astype(F32)
        grad = g_ref[...].astype(F32)
        gate = gate_ref[...]
        dg_ref[...] = jnp.sum(grad * result, axis=1, keepdims=True)
        wy_ref[...] = (gate * result).astype(BF16)
        out_grad = (gate * grad).astype(BF16)
        dy_ref[...] = out_grad
        act_grad = dot_nt(out_grad, down_ref[...])
        db_ref[:, :hidden] = (
            act_grad * up_part * sigmoid_gate * (1.0 + gate_part * (1.0 - sigmoid_gate))
        ).astype(BF16)
        db_ref[:, hidden:] = (act_grad * silu).astype(BF16)
        dn_ref[...] = dot_nt(db_ref[...], up_ref[...]).astype(BF16)

    @pl.when(jnp.logical_not(some))
    def _():
        for ref in (wy_ref, dn_ref, ea_ref, dy_ref, db_ref, dg_ref):
            ref[...] = jnp.zeros_like(ref)


def expert(total, rows, grads, gates, ups, downs):
    packed, width = rows.shape
    hidden = sum(part.shape[0] for part, _ in downs)
    tile = 256
    parts = [part for part, _ in ups + downs]
    starts = jnp.stack([start for _, start in ups + downs]).astype(jnp.int32)
    spec = lambda wide: pl.BlockSpec((tile, wide), lambda i, total, starts: (i, 0))
    widths = (width, width, hidden, width, 2 * hidden)
    return pl.pallas_call(
        functools.partial(expert_kernel, len(ups)),
        out_shape=[jax.ShapeDtypeStruct((packed, wide), BF16) for wide in widths]
        + [jax.ShapeDtypeStruct((packed, 1), F32)],
        grid_spec=pltpu.PrefetchScalarGridSpec(
            num_scalar_prefetch=2,
            grid=(packed // tile,),
            in_specs=[spec(width), spec(width), spec(1)]
            + [pl.BlockSpec(memory_space=pl.ANY)] * len(parts),
            out_specs=[spec(wide) for wide in widths] + [spec(1)],
            scratch_shapes=[
                pltpu.VMEM((width, 2 * hidden), BF16),
                pltpu.VMEM((hidden, width), BF16),
                pltpu.SemaphoreType.DMA((len(parts),)),
            ],
        ),
        compiler_params=pltpu.CompilerParams(vmem_limit_bytes=58 * 2**20),
        name="expert",
    )(total, starts, rows, grads, gates, *parts)


def combine_kernel(turned, window, extra, base_ref, order_ref, to_ref, me_ref, pos_ref, rows_ref, dg_ref, act_ref, weight_ref, out_ref):
    mul = dot_nt if turned else dot
    base = pl.multiple_of(base_ref[pl.program_id(0)], 16)
    pick = chosen(pos_ref, base, window)
    at = pl.ds(base, window)
    width = rows_ref.shape[1]
    out_ref[:, :width] = (
        dot_tn(pick.astype(F32).astype(BF16), rows_ref[at, :]) + mul(act_ref[...], weight_ref[...])
    ).astype(BF16)
    if extra:
        count = pick.shape[1]
        line = jnp.sum(jnp.where(pick, dg_ref[at, :], 0.0), axis=0, keepdims=True)
        row = lax.broadcasted_iota(jnp.int32, (count, count), 0)
        lane = lax.broadcasted_iota(jnp.int32, (count, count), 1)
        column = jnp.sum(jnp.where(row == lane, line, 0.0), axis=1, keepdims=True)
        high = column.astype(BF16).astype(F32)
        lane = lax.broadcasted_iota(jnp.int32, (count, extra), 1)
        out_ref[:, width:] = jnp.where(
            lane == me_ref[0], high, jnp.where(lane == me_ref[0] + extra // 2, column - high, 0.0)
        ).astype(BF16)


def combine(packing, order, to, me, rows, dg, act, weight, turned, extra):
    base, pos, _, window, packed = packing
    blocks, _, count = pos.shape
    width = rows.shape[-1]
    whole = lambda ref: pl.BlockSpec(ref.shape, lambda i, *_: (0, 0))
    return pl.pallas_call(
        functools.partial(combine_kernel, turned, window, extra),
        out_shape=jax.ShapeDtypeStruct((blocks * count, width + extra), BF16),
        grid_spec=pltpu.PrefetchScalarGridSpec(
            num_scalar_prefetch=4,
            grid=(blocks,),
            in_specs=[
                pl.BlockSpec((1, 1, count), lambda i, *_: (i, 0, 0)),
                whole(rows),
                whole(dg),
                pl.BlockSpec((count, act.shape[1]), lambda i, base, order, to, me: (order[i], 0)),
                whole(weight),
            ],
            out_specs=pl.BlockSpec(
                (count, width + extra), lambda i, base, order, to, me: (to[i], 0)
            ),
        ),
        compiler_params=pltpu.CompilerParams(vmem_limit_bytes=40 * 2**20),
        name="combine",
    )(base, order, to, me.reshape(1), pos, rows, dg, act, weight)


def gather_all(value):
    return lax.all_gather(value, "expert", axis=0, tiled=True)


def swap(value):
    return lax.all_to_all(value, "expert", split_axis=0, concat_axis=0, tiled=True)


def per_device(
    tokens,
    cotangent,
    segment_ids,
    routes,
    attn_in,
    attn_out,
    gain_attn,
    shared_in,
    shared_out,
    router,
    gain_ffn,
    expert_in,
    expert_out,
):
    n_dp, n_e = lax.axis_size("dp"), lax.axis_size("expert")
    me = lax.axis_index("expert")
    count, width = tokens.shape
    segments = segment_ids[0]
    length = segments.shape[0]
    rows = attn_in.shape[0]
    capacity = min(count, 3 * TOP * count // (2 * n_e))
    shared_rows = shared_out.shape[0]
    shared_width = shared_rows * n_dp
    expert_width = expert_out.shape[1] * n_dp

    order = ring_blocks()
    steady = jnp.arange(n_e, dtype=jnp.int32)
    hidden_in = tokens.astype(F32)
    inverse_one = lax.rsqrt(jnp.mean(hidden_in * hidden_in, axis=-1, keepdims=True) + EPS)
    normed_one = hidden_in * inverse_one
    gain_rows = gain_attn.astype(F32)[:, None]
    head_w = []

    def head_sent(blocks):
        own = (attn_in.astype(F32) * tied(gain_rows, blocks[0][1][0])).astype(BF16)
        own = own.reshape(rows, 3, n_e, HEAD_DIM).transpose(2, 0, 1, 3)
        head_w.append(swap(own.reshape(n_e, rows, 3 * HEAD_DIM)))
        return head_w[0]

    def head_whole(blocks):
        head_w.append(dp_gather(head_w[0]).reshape(width, 3 * HEAD_DIM))
        return head_w[1]

    here = lax.axis_index("dp")

    def spread(shard, chunks):
        while shard.shape[0] % (16 * chunks):
            chunks -= 1
        size = shard.shape[0] // chunks
        parts = [[(shard, here * shard.shape[0])]]
        for j in range(chunks):
            parts.append([])
            for step in range(1, n_dp):
                got = lax.ppermute(
                    shard[j * size : (j + 1) * size],
                    "dp",
                    [(i, (i - step) % n_dp) for i in range(n_dp)],
                )
                parts[-1].append((got, (here + step) % n_dp * shard.shape[0] + j * size))
        return parts

    up_parts = spread(expert_in[0], max(1, min(4, expert_in.shape[1] // 256)))
    down_parts = spread(expert_out[0], 2)
    first = lambda parts: [part for part, _ in parts]
    up_tokens = [first(parts) for parts in up_parts[1:]] + [[]] * 4

    small = jnp.concatenate([router, gain_ffn[:, None]], axis=1)
    small = dp_gather(small).reshape(-1, n_e + 1)
    extra_rows = 32
    extra = jnp.concatenate([small.T, routes.T.astype(BF16)], axis=0)
    extra = jnp.pad(extra, ((0, extra_rows - extra.shape[0]), (0, 0)))
    extra = jnp.broadcast_to(extra, (n_e,) + extra.shape)
    cos_table, sin_table, first_place = rope_tables(segments)
    share_w = shared_in.reshape(rows, 2, n_dp, n_e, shared_rows).transpose(3, 0, 1, 2, 4)
    share_w = share_w.reshape(n_e, rows, 2 * shared_width)

    half = n_e // 4
    norm_blocks = ring_gather(
        normed_one.astype(BF16),
        {
            half - 1: lambda blocks: [head_sent(blocks)],
            half: lambda blocks: [head_whole(blocks), cos_table, sin_table, extra, share_w]
            + up_tokens[0],
        },
    )
    head_sent_w, head_w = head_w

    head_out, query, key, value, lse, norm_all = attend(
        norm_blocks, order, head_w, cos_table, sin_table, first_place
    )
    mixed = jnp.concatenate([head_out.reshape(n_e, count, HEAD_DIM), extra], axis=1)
    share_w = swap(tied(share_w, head_sent_w))
    mixed = swap(tied(mixed, share_w, *up_tokens[1]))
    small = mixed[:, count:]
    mixed = mixed[:, :count].transpose(1, 0, 2).reshape(count, n_dp, n_e, rows)
    mixed = mixed.transpose(0, 2, 1, 3).reshape(count, width)
    proj_all = gather_all(dp_gather(attn_out).reshape(n_dp * rows, width))
    routes_all = small[:, n_e + 1 : n_e + 1 + TOP].astype(F32)
    small = small[:, : n_e + 1].reshape(n_e, n_e + 1, n_dp, rows).transpose(1, 2, 0, 3)
    small = small.reshape(n_e + 1, width)
    router_full = small[:n_e]
    gain_second = small[n_e].astype(F32)
    cot_all = gather_all(cotangent)

    share_sent = share_w
    share_w = dp_gather(share_w).reshape(width, 2 * shared_width)
    share_out = dp_gather(shared_out).reshape(shared_width, width)
    resid = hidden_in + dot(mixed, proj_all)
    if up_tokens[2]:
        resid = tied(resid, *up_tokens[2])

    inverse_two = lax.rsqrt(jnp.mean(resid * resid, axis=-1, keepdims=True) + EPS)
    normed_two = resid * inverse_two
    norm_two = (normed_two * gain_second).astype(BF16)
    logits = dot_nt(norm_two, router_full)
    picked = jnp.any(routes[:, :, None] == jnp.arange(n_e)[None, None, :], axis=1)
    chosen = jnp.where(picked, logits, NEG)
    chosen = jnp.where(picked, jnp.exp(chosen - jnp.max(chosen, axis=-1, keepdims=True)), 0.0)
    gates = chosen / jnp.sum(chosen, axis=-1, keepdims=True)
    gate_high = gates.astype(BF16)
    gate_low = (gates - gate_high.astype(F32)).astype(BF16)
    blank = jnp.zeros((count, 128 - 2 * n_e), BF16)
    payload = jnp.concatenate([norm_two, gate_high, gate_low, blank], axis=1)
    norm_blocks = ring_gather(
        payload,
        {
            half - 1: lambda blocks: [share_sent] + up_tokens[3],
            half: lambda blocks: first(down_parts[1]) + [share_sent],
        },
    )

    named = jnp.any(routes_all == me.astype(F32), axis=1)
    named = jnp.take(named, order, axis=0)
    ranking = jnp.cumsum(named.astype(jnp.int32), axis=1)
    ends = jnp.cumsum(ranking[:, -1])
    begins = ends - ranking[:, -1]
    pos = jnp.where(named, begins[:, None] + ranking - 1, -1)[:, None, :]
    window = -(-(capacity + 15) // 16) * 16
    packed = -(-(n_e * capacity + 32) // 256) * 256
    packing = (begins // 16 * 16, pos, ends[-1:], window, packed)
    norm_two_all, payload, arrived, _ = dispatch(
        norm_blocks, [width, 128], packing, order, jnp.zeros((n_e, 1, count), F32)
    )
    mine = jnp.arange(n_e) == me
    gate_all = payload[:, : 2 * n_e].astype(F32).reshape(length, 2, n_e)
    gate_all = jnp.sum(jnp.where(mine, gate_all, 0.0), axis=(1, 2)).reshape(n_e, 1, count)
    cot_rows, gate_rows = dispatch(cot_all, None, packing, order, gate_all)
    weighted, row_grad, expert_act, route_grad, pre_grad, gate_grad = expert(
        packing[2],
        arrived,
        cot_rows,
        gate_rows,
        [part for parts in up_parts for part in parts],
        [part for parts in down_parts for part in parts],
    )

    shared_pre = dot(norm_two_all, share_w)
    shared_act = (
        jax.nn.silu(shared_pre[:, :shared_width]) * shared_pre[:, shared_width:]
    ).astype(BF16)
    shared_act_grad = dot_nt(cot_all, share_out)
    shared_pre_grad = silu_back(
        shared_act_grad, shared_pre[:, :shared_width], shared_pre[:, shared_width:]
    ).astype(BF16)
    norm_two_part = combine(
        packing, order, steady, me, row_grad, gate_grad, shared_pre_grad, share_w, True, 128
    )
    marks = []
    norm_two_grad = ring_scatter(
        lambda n: norm_two_part[n * count : (n + 1) * count], None, marks
    )
    gate_grad = norm_two_grad[:, width : width + n_e] + norm_two_grad[:, width + 64 : width + 64 + n_e]
    norm_two_grad = norm_two_grad[:, :width]
    out_part = combine(
        packing, order, order, me, weighted, gate_rows, shared_act, share_out, False, 0
    )
    routed_out = lax.psum_scatter(out_part, "expert", scatter_dimension=0, tiled=True)

    def shard_grads(left, right, chunks):
        size = left.shape[1] // n_dp
        part = size // chunks
        cut = lambda start, wide: tied(lax.dynamic_slice_in_dim(left, start, wide, 1), *marks)
        got = [
            [
                lax.ppermute(
                    dot_tn(cut((here + step) % n_dp * size + j * part, part), right).astype(BF16),
                    "dp",
                    [(i, (i + step) % n_dp) for i in range(n_dp)],
                )
                for step in range(1, n_dp)
            ]
            for j in range(chunks)
        ]
        return dot_tn(cut(here * size, size), right), got

    def shard_sum(own, got, tokens):
        part = own.shape[0] // len(got)
        own = own[None]
        for j, (parts, token) in enumerate(zip(got, tokens)):
            block = sum(tied(p.astype(F32), token) for p in parts)[None]
            block = own[:, j * part : (j + 1) * part] + block
            own = lax.dynamic_update_slice_in_dim(own, block, j * part, 1)
        return own

    down_own, down_got = shard_grads(expert_act, route_grad, 2)
    up_own, up_got = shard_grads(arrived, pre_grad, len(up_parts) - 1)

    share_out_grad = dp_scatter(dot_tn(shared_act, cot_all).reshape(n_dp, shared_rows, width))
    share_in_grad = dot_tn(norm_two_all, shared_pre_grad)
    share_in_grad = dp_scatter(share_in_grad.reshape(n_dp, n_e, rows, 2 * shared_width))
    share_in_grad = swap(share_in_grad.astype(BF16)).astype(F32)
    share_in_grad = (
        share_in_grad.reshape(n_e, rows, 2, n_dp, shared_rows)
        .transpose(1, 2, 3, 0, 4)
        .reshape(rows, -1)
    )

    logit_grad = gates * (gate_grad - jnp.sum(gates * gate_grad, axis=-1, keepdims=True))
    router_grad = jnp.dot(
        logit_grad.T, norm_two.astype(F32), precision=HIGHEST, preferred_element_type=F32
    )
    norm_two_grad = norm_two_grad + jnp.dot(
        logit_grad, router_full.astype(F32), precision=HIGHEST, preferred_element_type=F32
    )
    gain_two_grad = jnp.sum(norm_two_grad * normed_two, axis=0)
    upstream = cotangent.astype(F32)
    scaled_two = norm_two_grad * gain_second
    resid_grad = upstream + inverse_two * (
        scaled_two - normed_two * jnp.mean(scaled_two * normed_two, axis=-1, keepdims=True)
    )
    small_grad = jnp.concatenate([router_grad, gain_two_grad[None]], axis=0)

    branch_cot = resid_grad.astype(BF16)
    proj_grad = dot_tn(mixed, branch_cot).astype(BF16)
    mixed_grad = tied(dot_nt(branch_cot, proj_all), proj_grad, *down_got[0]).astype(BF16)
    mixed_grad = mixed_grad.reshape(count, n_e, n_dp, rows).transpose(0, 2, 1, 3)
    mixed_grad = swap(mixed_grad.reshape(count, n_e, HEAD_DIM).transpose(1, 0, 2))
    mixed_grad = mixed_grad.reshape(length, HEAD_DIM)
    proj_grad = lax.psum_scatter(proj_grad, "expert", scatter_dimension=0, tiled=True)
    attn_out_grad = dp_scatter(proj_grad.astype(F32).reshape(n_dp, rows, width))
    qkv_grad = attend_back(
        query, key, value, mixed_grad, lse, first_place, cos_table, sin_table, order
    )
    small_grad = tied(small_grad, qkv_grad).reshape(n_e + 1, n_dp * n_e, rows).transpose(1, 0, 2)
    small_grad = lax.all_to_all(
        small_grad, ("dp", "expert"), split_axis=0, concat_axis=0, tiled=True
    )
    small_grad = jnp.sum(small_grad, axis=0)
    norm_one_part = dot_nt(qkv_grad, head_w).astype(BF16)
    scaled_one = ring_scatter(
        lambda n: norm_one_part[n * count : (n + 1) * count],
        {1: down_got[1], half - 1: up_got[0]},
    )
    expert_out_grad = shard_sum(down_own, down_got, [mixed_grad, scaled_one])
    expert_in_grad = shard_sum(up_own, up_got, ([qkv_grad] + [scaled_one] * 3)[: len(up_got)])
    input_grad = resid_grad + inverse_one * (
        scaled_one - normed_one * jnp.mean(scaled_one * normed_one, axis=-1, keepdims=True)
    )
    head_grad = dot_tn(norm_all, qkv_grad).reshape(n_dp, n_e, rows, 3 * HEAD_DIM)
    head_grad = swap(dp_scatter(head_grad).astype(BF16)).astype(F32)
    head_grad = (
        head_grad.reshape(n_e, rows, 3, HEAD_DIM).transpose(1, 2, 0, 3).reshape(rows, 3 * width)
    )
    gain_attn_grad = jnp.sum(head_grad * attn_in.astype(F32), axis=1)
    attn_in_grad = head_grad * gain_rows
    return (
        (resid + routed_out.astype(F32)).astype(BF16),
        input_grad.astype(BF16),
        attn_in_grad,
        attn_out_grad,
        gain_attn_grad,
        share_in_grad,
        share_out_grad,
        small_grad[:n_e].T,
        small_grad[n_e],
        expert_in_grad,
        expert_out_grad,
    )


def solution(mesh):
    return jax.shard_map(
        per_device,
        mesh=mesh,
        in_specs=(
            P(("dp", "expert"), None),
            P(("dp", "expert"), None),
            P("dp", None),
            P(("dp", "expert"), None),
            P(("dp", "expert"), None),
            P(("dp", "expert"), None),
            P(("dp", "expert")),
            P(("dp", "expert"), None),
            P(("dp", "expert"), None),
            P(("dp", "expert"), None),
            P(("dp", "expert")),
            P("expert", "dp", None),
            P("expert", "dp", None),
        ),
        out_specs=(
            P(("dp", "expert"), None),
            P(("dp", "expert"), None),
            P(("dp", "expert"), None),
            P(("dp", "expert"), None),
            P(("dp", "expert")),
            P(("dp", "expert"), None),
            P(("dp", "expert"), None),
            P(("dp", "expert"), None),
            P(("dp", "expert")),
            P("expert", "dp", None),
            P("expert", "dp", None),
        ),
        check_vma=False,
    )
```

```python
import functools
import math

import jax
import jax.numpy as jnp
from jax import lax
from jax.experimental import pallas as pl
from jax.experimental.pallas import tpu as pltpu
from jax.sharding import PartitionSpec as P

HEADS = 16
HEAD_DIM = 128
TOP = 6


EPS = 1e-06
THETA = 10000.0
NEG = -1e30
HIGHEST = lax.Precision.HIGHEST
BF16 = jnp.bfloat16
F32 = jnp.float32
LOG2E = math.log2(math.e)


def rope_tables(segments):
    length = segments.shape[0]
    places = jnp.arange(length, dtype=jnp.int32)
    starts = jnp.concatenate([jnp.ones((1,), dtype=jnp.bool_), segments[1:] != segments[:-1]])
    first_place = lax.cummax(jnp.where(starts, places, 0), axis=0)
    offset = (places - first_place).astype(jnp.float32)
    half_dim = HEAD_DIM // 2
    freqs = jnp.exp(jnp.arange(half_dim, dtype=jnp.float32) * (-2.0 * math.log(THETA) / HEAD_DIM))
    angles = offset[:, None] * freqs[None, :]
    cos_table, sin_table = jnp.cos(angles), jnp.sin(angles)
    return (
        jnp.concatenate([cos_table, cos_table], axis=1),
        jnp.concatenate([-sin_table, sin_table], axis=1),
        first_place[None, :],
    )


def silu_back(grad_act, gate_part, up_part):
    sigmoid_gate = jax.nn.sigmoid(gate_part)
    gate_grad = grad_act * up_part * sigmoid_gate * (1.0 + gate_part * (1.0 - sigmoid_gate))
    up_grad = grad_act * gate_part * sigmoid_gate
    return jnp.concatenate([gate_grad, up_grad], axis=-1)


def dot(left, right):
    return jnp.dot(left, right, preferred_element_type=F32)


def dot_tn(left, right):
    return lax.dot_general(left, right, (((0,), (0,)), ((), ())), preferred_element_type=F32)


def dot_nt(left, right):
    return lax.dot_general(left, right, (((1,), (1,)), ((), ())), preferred_element_type=F32)


def turn(values, cos_table, sin_table):
    return values * cos_table + pltpu.roll(values, HEAD_DIM // 2, 1) * sin_table


def attend_kernel(sources, block, order_ref, *refs):
    pieces = refs[: sources[-1][-1] + 1]
    weight_ref, cos_ref, sin_ref, start_ref = refs[len(pieces) : len(pieces) + 4]
    o_ref, q_ref, k_ref, v_ref, lse_ref, rows_ref, vt_ref = refs[len(pieces) + 4 :]
    step = pl.program_id(0)
    length = q_ref.shape[0]
    factor = HEAD_DIM ** (-0.5) * LOG2E
    rows = rows_ref.shape[0]

    for n, parts in enumerate(sources):

        @pl.when(step == n)
        def _(parts=parts):
            low = 0
            for part in parts:
                size = pieces[part].shape[0]
                rows_ref[low : low + size, :] = pieces[part][...]
                low += size

    @pl.when(step < len(sources))
    def _():
        qkv = dot(rows_ref[...], weight_ref[...])
        at = pl.ds(pl.multiple_of(order_ref[step] * rows, rows), rows)
        cos_table, sin_table = cos_ref[at, :], sin_ref[at, :]
        q_ref[at, :] = turn(qkv[:, :HEAD_DIM], cos_table, sin_table).astype(BF16)
        k_ref[at, :] = turn(qkv[:, HEAD_DIM : 2 * HEAD_DIM], cos_table, sin_table).astype(BF16)
        value = qkv[:, 2 * HEAD_DIM :]
        v_ref[at, :] = value.astype(BF16)
        vt_ref[:, at] = value.T.astype(BF16)

    for i in range(length // block):

        @pl.when(step == len(sources) + i)
        def _(i=i):
            low, high = i * block, (i + 1) * block
            raw = dot_nt(k_ref[:high, :], q_ref[low:high, :])
            keys = lax.broadcasted_iota(jnp.int32, raw.shape, 0)
            queries = low + lax.broadcasted_iota(jnp.int32, raw.shape, 1)
            allowed = (keys <= queries) & (keys >= start_ref[:, low:high])
            raw = jnp.where(allowed, raw, NEG)
            top = jnp.max(raw, axis=0, keepdims=True)
            shifted = jnp.exp2((raw - top) * factor)
            total = jnp.sum(shifted, axis=0, keepdims=True)
            probs = (shifted * (1.0 / total)).astype(BF16)
            mixed = dot(vt_ref[:, :high], probs)
            o_ref[low:high, :] = mixed.T.astype(BF16)
            lse_ref[:, low:high] = top * factor + jnp.log2(total)


def attend(blocks, order, weight, cos_table, sin_table, first_place):
    pieces, sources = flatten(blocks)
    length = cos_table.shape[0]
    rows = length // len(sources)
    width = weight.shape[0]
    block = min(256, length)
    last = len(sources) - 1
    whole = lambda shape: pl.BlockSpec(shape, lambda i, order: (0, 0))
    head = jax.ShapeDtypeStruct((length, HEAD_DIM), BF16)
    return pl.pallas_call(
        functools.partial(attend_kernel, sources, block),
        out_shape=[head] * 4
        + [jax.ShapeDtypeStruct((1, length), F32), jax.ShapeDtypeStruct((length, width), BF16)],
        grid_spec=pltpu.PrefetchScalarGridSpec(
            num_scalar_prefetch=1,
            grid=(len(sources) + length // block,),
            in_specs=[whole(piece.shape) for piece in pieces]
            + [
                whole(weight.shape),
                whole((length, HEAD_DIM)),
                whole((length, HEAD_DIM)),
                whole((1, length)),
            ],
            out_specs=[whole((length, HEAD_DIM))] * 4
            + [
                whole((1, length)),
                pl.BlockSpec((rows, width), lambda i, order: (jnp.minimum(i, last), 0)),
            ],
            scratch_shapes=[pltpu.VMEM((HEAD_DIM, length), BF16)],
        ),
        compiler_params=pltpu.CompilerParams(vmem_limit_bytes=52 * 2**20),
        name="attend",
    )(order, *pieces, weight, cos_table, sin_table, first_place)


def attend_back_kernel(
    block, rows, order_ref, q_ref, k_ref, v_ref, do_ref, lse_ref, start_ref, cos_ref, sin_ref, out_ref, kt_ref, dq_ref, dk_ref, dv_ref
):
    length = q_ref.shape[0]
    step = pl.program_id(0)
    scale = HEAD_DIM ** (-0.5)
    factor = scale * LOG2E
    count = length // block

    @pl.when(step == 0)
    def _():
        kt_ref[...] = k_ref[...].astype(F32).T.astype(BF16)
        dk_ref[...] = jnp.zeros_like(dk_ref)
        dv_ref[...] = jnp.zeros_like(dv_ref)

    for i in range(count):

        @pl.when(step == i)
        def _(i=i):
            low, high = i * block, (i + 1) * block
            query, grad = q_ref[low:high, :], do_ref[low:high, :]
            raw = dot_nt(k_ref[:high, :], query)
            keys = lax.broadcasted_iota(jnp.int32, raw.shape, 0)
            queries = low + lax.broadcasted_iota(jnp.int32, raw.shape, 1)
            allowed = (keys <= queries) & (keys >= start_ref[:, low:high])
            raw = jnp.where(allowed, raw * factor - lse_ref[:, low:high], NEG)
            probs = jnp.exp2(raw)
            probs_grad = dot_nt(v_ref[:high, :], grad)
            inner = jnp.sum(probs_grad * probs, axis=0, keepdims=True)
            score_grad = (probs * (probs_grad - inner)).astype(BF16)
            dv_ref[:high, :] += dot(probs.astype(BF16), grad)
            dk_ref[:high, :] += dot(score_grad, query)
            dq_ref[low:high, :] = dot(kt_ref[:, :high], score_grad).T

    @pl.when(step == count - 1)
    def _():
        for n in range(length // rows):
            at = pl.ds(pl.multiple_of(order_ref[n] * rows, rows), rows)
            to = slice(n * rows, (n + 1) * rows)
            cos_table, sin_table = cos_ref[at, :], -sin_ref[at, :]
            out_ref[to, :HEAD_DIM] = turn(dq_ref[at, :] * scale, cos_table, sin_table).astype(BF16)
            out_ref[to, HEAD_DIM : 2 * HEAD_DIM] = turn(
                dk_ref[at, :] * scale, cos_table, sin_table
            ).astype(BF16)
            out_ref[to, 2 * HEAD_DIM :] = dv_ref[at, :].astype(BF16)


def attend_back(query, key, value, grad, lse, first_place, cos_table, sin_table, order):
    length = query.shape[0]
    block = min(256, length)
    whole = lambda shape: pl.BlockSpec(shape, lambda i, order: (0, 0))
    head = whole((length, HEAD_DIM))
    return pl.pallas_call(
        functools.partial(attend_back_kernel, block, length // order.shape[0]),
        out_shape=jax.ShapeDtypeStruct((length, 3 * HEAD_DIM), BF16),
        grid_spec=pltpu.PrefetchScalarGridSpec(
            num_scalar_prefetch=1,
            grid=(length // block,),
            in_specs=[head] * 4 + [whole((1, length))] * 2 + [head] * 2,
            out_specs=whole((length, 3 * HEAD_DIM)),
            scratch_shapes=[pltpu.VMEM((HEAD_DIM, length), BF16)]
            + [pltpu.VMEM((length, HEAD_DIM), F32)] * 3,
        ),
        compiler_params=pltpu.CompilerParams(vmem_limit_bytes=48 * 2**20),
        name="attend_back",
    )(order, query, key, value, grad, lse, first_place, cos_table, sin_table)


def dp_gather(value):
    count = lax.axis_size("dp")
    if count == 1:
        return value[None]
    here = lax.axis_index("dp")
    parts = [value] + [
        lax.ppermute(value, "dp", [(i, (i - step) % count) for i in range(count)])
        for step in range(1, count)
    ]
    if count == 2:
        first = here == 0
        return jnp.stack(
            [jnp.where(first, parts[0], parts[1]), jnp.where(first, parts[1], parts[0])]
        )
    whole = jnp.zeros((count,) + value.shape, value.dtype)
    for step, part in enumerate(parts):
        whole = lax.dynamic_update_index_in_dim(whole, part, (here + step) % count, 0)
    return whole


def dp_scatter(value):
    count = lax.axis_size("dp")
    here = lax.axis_index("dp")
    total = lax.dynamic_index_in_dim(value, here, 0, keepdims=False)
    for step in range(1, count):
        block = lax.dynamic_index_in_dim(value, (here + step) % count, 0, keepdims=False)
        got = lax.ppermute(
            block.astype(BF16), "dp", [(i, (i + step) % count) for i in range(count)]
        )
        total = total + got.astype(F32)
    return total


def ring_order():
    pairs = lax.axis_size("expert") // 2
    return list(range(0, pairs, 2)) + list(range(pairs - 1, 0, -2))


def ring_shift(value, step):
    order = ring_order()
    pairs = len(order)
    perm = [
        (order[q] * 2 + c, order[(q + step) % pairs] * 2 + c) for q in range(pairs) for c in range(2)
    ]
    return lax.ppermute(value, "expert", perm)


def core_swap(value):
    count = lax.axis_size("expert")
    return lax.ppermute(value, "expert", [(i, i ^ 1) for i in range(count)])


def ring_offsets():
    half = lax.axis_size("expert") // 4
    return [0] + [o for step in range(1, half) for o in (step, -step)] + [half]


def ring_blocks():
    order = ring_order()
    pairs = len(order)
    table = [[0] * (2 * pairs) for _ in range(2 * pairs)]
    for q in range(pairs):
        for c in range(2):
            for j, offset in enumerate(ring_offsets()):
                for other in range(2):
                    table[order[q] * 2 + c][2 * j + other] = (
                        order[(q - offset) % pairs] * 2 + (c ^ other)
                    )
    return lax.dynamic_index_in_dim(
        jnp.asarray(table, jnp.int32), lax.axis_index("expert"), 0, keepdims=False
    )


def tied(value, *tokens):
    firsts = [lax.slice(t, (0,) * t.ndim, (1,) * t.ndim).reshape(()) for t in tokens]
    token = sum(t.astype(F32) for t in firsts) * 0.0
    return (value.astype(F32) * (1.0 + token)).astype(value.dtype)


def ring_gather(value, gates=None):
    gates = gates or {}
    half_rows = value.shape[0] // 2
    half = lax.axis_size("expert") // 4
    blocks = {}

    def keep(parts, offset):
        blocks[offset] = (parts, [core_swap(part) for part in parts])

    keep([value], 0)
    ahead = back = value
    for step in range(1, half):
        if step in gates:
            token = gates[step](blocks)
            ahead, back = tied(ahead, *token), tied(back, *token)
        ahead, back = ring_shift(ahead, 1), ring_shift(back, -1)
        keep([ahead], step)
        keep([back], -step)
    if half in gates:
        token = gates[half](blocks)
        ahead, back = tied(ahead, *token), tied(back, *token)
    last = [ring_shift(ahead[:half_rows], 1), ring_shift(back[half_rows:], -1)]
    keep(last, half)
    return [parts for offset in ring_offsets() for parts in blocks[offset]]


def flatten(blocks):
    pieces = [piece for parts in blocks for piece in parts]
    sources, n = [], 0
    for parts in blocks:
        sources.append(tuple(range(n, n + len(parts))))
        n += len(parts)
    return pieces, tuple(sources)


def ring_scatter(block, gates=None, marks=None):
    gates = gates or {}
    half = lax.axis_size("expert") // 4
    offsets = ring_offsets()
    spare = {}

    def mine(offset):
        if offset not in spare:
            j = offsets.index(offset)
            spare[offset] = block(2 * j).astype(F32) + core_swap(block(2 * j + 1)).astype(F32)
        return spare[offset]

    far = mine(half).astype(BF16)
    half_rows = far.shape[0] // 2
    ahead = ring_shift(far[:half_rows], 1)
    back = ring_shift(far[half_rows:], -1)
    if marks is not None:
        marks.extend([ahead, back])
    for step in range(half - 1, 0, -1):
        onward, homeward = mine(-step), mine(step)
        if step == half - 1:
            onward = jnp.concatenate(
                [onward[:half_rows] + ahead.astype(F32), onward[half_rows:]], axis=0
            )
            homeward = jnp.concatenate(
                [homeward[:half_rows], homeward[half_rows:] + back.astype(F32)], axis=0
            )
        else:
            onward = onward + ahead.astype(F32)
            homeward = homeward + back.astype(F32)
        if half - step in gates:
            onward, homeward = tied(onward, *gates[half - step]), tied(homeward, *gates[half - step])
        ahead = ring_shift(onward.astype(BF16), 1)
        back = ring_shift(homeward.astype(BF16), -1)
    return mine(0) + ahead.astype(F32) + back.astype(F32)


def chosen(pos_ref, base, window):
    count = pos_ref.shape[-1]
    row = base + lax.broadcasted_iota(jnp.int32, (window, count), 0)
    return row == pos_ref[0]


def dispatch_kernel(sources, widths, window, base_ref, order_ref, pos_ref, gate_ref, *refs):
    outs = refs[-len(widths) - 2 :]
    pieces, blocks, rows_ref, weights_ref = refs[: -len(outs)], outs[:-2], outs[-2], outs[-1]
    step = pl.program_id(0)

    @pl.when(step == 0)
    def _():
        rows_ref[...] = jnp.zeros_like(rows_ref)
        weights_ref[...] = jnp.zeros_like(weights_ref)

    for n, parts in enumerate(sources):

        @pl.when(step == n)
        def _(parts=parts):
            low = 0
            for part in parts:
                size = pieces[part].shape[0]
                left = 0
                for block, wide in zip(blocks, widths):
                    block[low : low + size, :] = pieces[part][:, left : left + wide]
                    left += wide
                low += size

    base = pl.multiple_of(base_ref[step], 16)
    pick = chosen(pos_ref, base, window)
    at = pl.ds(base, window)
    found = dot(pick.astype(F32).astype(BF16), (blocks or pieces)[0][...])
    rows_ref[at, :] = (rows_ref[at, :].astype(F32) + found).astype(BF16)
    weights_ref[at, :] += jnp.sum(jnp.where(pick, gate_ref[0], 0.0), axis=1, keepdims=True)


def dispatch(blocks, widths, packing, order, gates):
    base, pos, _, window, packed = packing
    count, _, rows = pos.shape
    if isinstance(blocks, list):
        pieces, sources = flatten(blocks)
        piece_specs = [pl.BlockSpec(piece.shape, lambda i, base, order: (0, 0)) for piece in pieces]
    else:
        pieces, sources, widths = [blocks], (), []
        piece_specs = [pl.BlockSpec((rows, blocks.shape[1]), lambda i, base, order: (order[i], 0))]
    width = (widths or [pieces[0].shape[1]])[0]
    return pl.pallas_call(
        functools.partial(dispatch_kernel, sources, tuple(widths), window),
        out_shape=[jax.ShapeDtypeStruct((rows * count, wide), BF16) for wide in widths]
        + [
            jax.ShapeDtypeStruct((packed, width), BF16),
            jax.ShapeDtypeStruct((packed, 1), F32),
        ],
        grid_spec=pltpu.PrefetchScalarGridSpec(
            num_scalar_prefetch=2,
            grid=(count,),
            in_specs=[
                pl.BlockSpec((1, 1, rows), lambda i, base, order: (i, 0, 0)),
                pl.BlockSpec((1, 1, rows), lambda i, base, order: (order[i], 0, 0)),
            ]
            + piece_specs,
            out_specs=[
                pl.BlockSpec((rows, wide), lambda i, base, order: (order[i], 0)) for wide in widths
            ]
            + [
                pl.BlockSpec((packed, width), lambda i, base, order: (0, 0)),
                pl.BlockSpec((packed, 1), lambda i, base, order: (0, 0)),
            ],
        ),
        compiler_params=pltpu.CompilerParams(vmem_limit_bytes=52 * 2**20),
        name="dispatch",
    )(base, order, pos, gates, *pieces)


def expert_kernel(ups, total_ref, starts_ref, x_ref, g_ref, gate_ref, *refs):
    parts, refs = refs[:-9], refs[-9:]
    wy_ref, dn_ref, ea_ref, dy_ref, db_ref, dg_ref, up_ref, down_ref, sems = refs
    step = pl.program_id(0)
    rows, hidden = ea_ref.shape
    some = step * rows < total_ref[0]

    @pl.when(step == 0)
    def _():
        copies = []
        for n, part in enumerate(parts):
            at = pl.ds(pl.multiple_of(starts_ref[n], 16), part.shape[0])
            whole = up_ref if n < ups else down_ref
            copies.append(pltpu.make_async_copy(part, whole.at[at, :], sems.at[n]))
        for copy in copies:
            copy.start()
        for copy in copies:
            copy.wait()

    @pl.when(some)
    def _():
        pre = dot(x_ref[...], up_ref[...])
        gate_part, up_part = pre[:, :hidden], pre[:, hidden:]
        sigmoid_gate = 1.0 / (1.0 + jnp.exp(-gate_part))
        silu = gate_part * sigmoid_gate
        act = (silu * up_part).astype(BF16)
        ea_ref[...] = act
        result = dot(act, down_ref[...]).astype(BF16).astype(F32)
        grad = g_ref[...].astype(F32)
        gate = gate_ref[...]
        dg_ref[...] = jnp.sum(grad * result, axis=1, keepdims=True)
        wy_ref[...] = (gate * result).astype(BF16)
        out_grad = (gate * grad).astype(BF16)
        dy_ref[...] = out_grad
        act_grad = dot_nt(out_grad, down_ref[...])
        db_ref[:, :hidden] = (
            act_grad * up_part * sigmoid_gate * (1.0 + gate_part * (1.0 - sigmoid_gate))
        ).astype(BF16)
        db_ref[:, hidden:] = (act_grad * silu).astype(BF16)
        dn_ref[...] = dot_nt(db_ref[...], up_ref[...]).astype(BF16)

    @pl.when(jnp.logical_not(some))
    def _():
        for ref in (wy_ref, dn_ref, ea_ref, dy_ref, db_ref, dg_ref):
            ref[...] = jnp.zeros_like(ref)


def expert(total, rows, grads, gates, ups, downs):
    packed, width = rows.shape
    hidden = sum(part.shape[0] for part, _ in downs)
    tile = 256
    parts = [part for part, _ in ups + downs]
    starts = jnp.stack([start for _, start in ups + downs]).astype(jnp.int32)
    spec = lambda wide: pl.BlockSpec((tile, wide), lambda i, total, starts: (i, 0))
    widths = (width, width, hidden, width, 2 * hidden)
    return pl.pallas_call(
        functools.partial(expert_kernel, len(ups)),
        out_shape=[jax.ShapeDtypeStruct((packed, wide), BF16) for wide in widths]
        + [jax.ShapeDtypeStruct((packed, 1), F32)],
        grid_spec=pltpu.PrefetchScalarGridSpec(
            num_scalar_prefetch=2,
            grid=(packed // tile,),
            in_specs=[spec(width), spec(width), spec(1)]
            + [pl.BlockSpec(memory_space=pl.ANY)] * len(parts),
            out_specs=[spec(wide) for wide in widths] + [spec(1)],
            scratch_shapes=[
                pltpu.VMEM((width, 2 * hidden), BF16),
                pltpu.VMEM((hidden, width), BF16),
                pltpu.SemaphoreType.DMA((len(parts),)),
            ],
        ),
        compiler_params=pltpu.CompilerParams(vmem_limit_bytes=58 * 2**20),
        name="expert",
    )(total, starts, rows, grads, gates, *parts)


def combine_kernel(window, extra, base_ref, order_ref, me_ref, pos_ref, dn_ref, dg_ref, da_ref, in_ref, wy_ref, sa_ref, out_w_ref, out_ref):
    base = pl.multiple_of(base_ref[pl.program_id(0)], 16)
    pick = chosen(pos_ref, base, window)
    hot = pick.astype(F32).astype(BF16)
    at = pl.ds(base, window)
    width = dn_ref.shape[1]
    out_ref[:, :width] = (
        dot_tn(hot, dn_ref[at, :]) + dot_nt(da_ref[...], in_ref[...])
    ).astype(BF16)
    count = pick.shape[1]
    line = jnp.sum(jnp.where(pick, dg_ref[at, :], 0.0), axis=0, keepdims=True)
    row = lax.broadcasted_iota(jnp.int32, (count, count), 0)
    lane = lax.broadcasted_iota(jnp.int32, (count, count), 1)
    column = jnp.sum(jnp.where(row == lane, line, 0.0), axis=1, keepdims=True)
    high = column.astype(BF16).astype(F32)
    lane = lax.broadcasted_iota(jnp.int32, (count, extra), 1)
    out_ref[:, width : width + extra] = jnp.where(
        lane == me_ref[0], high, jnp.where(lane == me_ref[0] + extra // 2, column - high, 0.0)
    ).astype(BF16)
    out_ref[:, width + extra :] = (
        dot_tn(hot, wy_ref[at, :]) + dot(sa_ref[...], out_w_ref[...])
    ).astype(BF16)


def combine(packing, order, me, dn, dg, da, in_w, wy, sa, out_w, extra):
    base, pos, _, window, packed = packing
    blocks, _, count = pos.shape
    width = dn.shape[-1]
    whole = lambda ref: pl.BlockSpec(ref.shape, lambda i, *_: (0, 0))
    acts = lambda ref: pl.BlockSpec((count, ref.shape[1]), lambda i, base, order, me: (order[i], 0))
    return pl.pallas_call(
        functools.partial(combine_kernel, window, extra),
        out_shape=jax.ShapeDtypeStruct((blocks * count, 2 * width + extra), BF16),
        grid_spec=pltpu.PrefetchScalarGridSpec(
            num_scalar_prefetch=3,
            grid=(blocks,),
            in_specs=[
                pl.BlockSpec((1, 1, count), lambda i, *_: (i, 0, 0)),
                whole(dn), whole(dg), acts(da), whole(in_w), whole(wy), acts(sa), whole(out_w),
            ],
            out_specs=pl.BlockSpec((count, 2 * width + extra), lambda i, *_: (i, 0)),
        ),
        compiler_params=pltpu.CompilerParams(vmem_limit_bytes=48 * 2**20),
        name="combine",
    )(base, order, me.reshape(1), pos, dn, dg, da, in_w, wy, sa, out_w)


def outer_kernel(order_ref, left_ref, right_ref, out_ref):
    size = out_ref.shape[0]
    lanes = pl.ds(pl.multiple_of(order_ref[pl.program_id(0)] * size, size), size)
    out_ref[...] = dot_tn(left_ref[:, lanes], right_ref[...]).astype(BF16)


def outer(left, right, order):
    blocks = order.shape[0]
    size = left.shape[1] // blocks
    return pl.pallas_call(
        outer_kernel,
        out_shape=jax.ShapeDtypeStruct((left.shape[1], right.shape[1]), BF16),
        grid_spec=pltpu.PrefetchScalarGridSpec(
            num_scalar_prefetch=1,
            grid=(blocks,),
            in_specs=[
                pl.BlockSpec(left.shape, lambda i, order: (0, 0)),
                pl.BlockSpec(right.shape, lambda i, order: (0, 0)),
            ],
            out_specs=pl.BlockSpec((size, right.shape[1]), lambda i, order: (i, 0)),
        ),
        name="outer",
    )(order, left, right)


def gather_all(value):
    return lax.all_gather(value, "expert", axis=0, tiled=True)


def swap(value):
    return lax.all_to_all(value, "expert", split_axis=0, concat_axis=0, tiled=True)


def per_device(
    tokens,
    cotangent,
    segment_ids,
    routes,
    attn_in,
    attn_out,
    gain_attn,
    shared_in,
    shared_out,
    router,
    gain_ffn,
    expert_in,
    expert_out,
):
    n_dp, n_e = lax.axis_size("dp"), lax.axis_size("expert")
    me = lax.axis_index("expert")
    count, width = tokens.shape
    segments = segment_ids[0]
    length = segments.shape[0]
    rows = attn_in.shape[0]
    capacity = min(count, 3 * TOP * count // (2 * n_e))
    shared_rows = shared_out.shape[0]
    shared_width = shared_rows * n_dp
    expert_width = expert_out.shape[1] * n_dp

    order = ring_blocks()
    steady = jnp.arange(n_e, dtype=jnp.int32)
    hidden_in = tokens.astype(F32)
    inverse_one = lax.rsqrt(jnp.mean(hidden_in * hidden_in, axis=-1, keepdims=True) + EPS)
    normed_one = hidden_in * inverse_one
    gain_rows = gain_attn.astype(F32)[:, None]
    head_w = []

    def head_sent(blocks):
        own = (attn_in.astype(F32) * tied(gain_rows, blocks[0][1][0])).astype(BF16)
        own = own.reshape(rows, 3, n_e, HEAD_DIM).transpose(2, 0, 1, 3)
        head_w.append(swap(own.reshape(n_e, rows, 3 * HEAD_DIM)))
        return head_w[0]

    def head_whole(blocks):
        head_w.append(dp_gather(head_w[0]).reshape(width, 3 * HEAD_DIM))
        return head_w[1]

    here = lax.axis_index("dp")

    def spread(shard, chunks):
        while shard.shape[0] % (16 * chunks):
            chunks -= 1
        size = shard.shape[0] // chunks
        parts = [[(shard, here * shard.shape[0])]]
        for j in range(chunks):
            parts.append([])
            for step in range(1, n_dp):
                got = lax.ppermute(
                    shard[j * size : (j + 1) * size],
                    "dp",
                    [(i, (i - step) % n_dp) for i in range(n_dp)],
                )
                parts[-1].append((got, (here + step) % n_dp * shard.shape[0] + j * size))
        return parts

    up_parts = spread(expert_in[0], max(1, min(4, expert_in.shape[1] // 256)))
    down_parts = spread(expert_out[0], 2)
    first = lambda parts: [part for part, _ in parts]
    up_tokens = [first(parts) for parts in up_parts[1:]] + [[]] * 4

    small = jnp.concatenate([router, gain_ffn[:, None]], axis=1)
    small = dp_gather(small).reshape(-1, n_e + 1)
    extra_rows = 32
    extra = jnp.concatenate([small.T, routes.T.astype(BF16)], axis=0)
    extra = jnp.pad(extra, ((0, extra_rows - extra.shape[0]), (0, 0)))
    extra = jnp.broadcast_to(extra, (n_e,) + extra.shape)
    cos_table, sin_table, first_place = rope_tables(segments)
    share_w = shared_in.reshape(rows, 2, n_dp, n_e, shared_rows).transpose(3, 0, 1, 2, 4)
    share_w = share_w.reshape(n_e, rows, 2 * shared_width)

    half = n_e // 4
    norm_blocks = ring_gather(
        normed_one.astype(BF16),
        {
            half - 1: lambda blocks: [head_sent(blocks)],
            half: lambda blocks: [head_whole(blocks), cos_table, sin_table, extra, share_w],
        },
    )
    head_sent_w, head_w = head_w

    head_out, query, key, value, lse, norm_all = attend(
        norm_blocks, order, head_w, cos_table, sin_table, first_place
    )
    mixed = jnp.concatenate([head_out.reshape(n_e, count, HEAD_DIM), extra], axis=1)
    share_w = swap(tied(share_w, head_sent_w))
    mixed = swap(tied(mixed, share_w, *up_tokens[0]))
    small = mixed[:, count:]
    mixed = mixed[:, :count].transpose(1, 0, 2).reshape(count, n_dp, n_e, rows)
    mixed = mixed.transpose(0, 2, 1, 3).reshape(count, width)
    proj_all = dp_gather(attn_out).reshape(n_dp * rows, width)
    proj_all = gather_all(tied(proj_all, norm_blocks[6][0]))
    routes_all = small[:, n_e + 1 : n_e + 1 + TOP].astype(F32)
    small = small[:, : n_e + 1].reshape(n_e, n_e + 1, n_dp, rows).transpose(1, 2, 0, 3)
    small = small.reshape(n_e + 1, width)
    router_full = small[:n_e]
    gain_second = small[n_e].astype(F32)
    cot_all = gather_all(tied(cotangent, lse))

    share_sent = share_w
    share_w = dp_gather(share_w).reshape(width, 2 * shared_width)
    share_out = dp_gather(shared_out).reshape(shared_width, width)
    resid = hidden_in + dot(mixed, proj_all)
    if up_tokens[1]:
        resid = tied(resid, *up_tokens[1])

    inverse_two = lax.rsqrt(jnp.mean(resid * resid, axis=-1, keepdims=True) + EPS)
    normed_two = resid * inverse_two
    norm_two = (normed_two * gain_second).astype(BF16)
    logits = dot_nt(norm_two, router_full)
    picked = jnp.any(routes[:, :, None] == jnp.arange(n_e)[None, None, :], axis=1)
    chosen = jnp.where(picked, logits, NEG)
    chosen = jnp.where(picked, jnp.exp(chosen - jnp.max(chosen, axis=-1, keepdims=True)), 0.0)
    gates = chosen / jnp.sum(chosen, axis=-1, keepdims=True)
    gate_high = gates.astype(BF16)
    gate_low = (gates - gate_high.astype(F32)).astype(BF16)
    blank = jnp.zeros((count, 128 - 2 * n_e), BF16)
    payload = jnp.concatenate([norm_two, gate_high, gate_low, blank], axis=1)
    norm_blocks = ring_gather(
        payload,
        {
            half - 1: lambda blocks: [share_sent] + up_tokens[2],
            half: lambda blocks: [share_sent] + up_tokens[3],
        },
    )

    named = jnp.any(routes_all == me.astype(F32), axis=1)
    named = jnp.take(named, order, axis=0)
    ranking = jnp.cumsum(named.astype(jnp.int32), axis=1)
    ends = jnp.cumsum(ranking[:, -1])
    begins = ends - ranking[:, -1]
    pos = jnp.where(named, begins[:, None] + ranking - 1, -1)[:, None, :]
    window = -(-(capacity + 15) // 16) * 16
    packed = -(-(n_e * capacity + 32) // 256) * 256
    packing = (begins // 16 * 16, pos, ends[-1:], window, packed)
    norm_two_all, payload, arrived, _ = dispatch(
        norm_blocks, [width, 128], packing, order, jnp.zeros((n_e, 1, count), F32)
    )
    mine = jnp.arange(n_e) == me
    gate_all = payload[:, : 2 * n_e].astype(F32).reshape(length, 2, n_e)
    gate_all = jnp.sum(jnp.where(mine, gate_all, 0.0), axis=(1, 2)).reshape(n_e, 1, count)
    cot_rows, gate_rows = dispatch(cot_all, None, packing, order, gate_all)
    weighted, row_grad, expert_act, route_grad, pre_grad, gate_grad = expert(
        packing[2],
        arrived,
        cot_rows,
        gate_rows,
        [part for parts in up_parts for part in parts],
        [part for parts in down_parts for part in parts],
    )

    shared_pre = dot(norm_two_all, share_w)
    shared_act = (
        jax.nn.silu(shared_pre[:, :shared_width]) * shared_pre[:, shared_width:]
    ).astype(BF16)
    shared_act_grad = dot_nt(cot_all, share_out)
    shared_pre_grad = silu_back(
        shared_act_grad, shared_pre[:, :shared_width], shared_pre[:, shared_width:]
    ).astype(BF16)
    routed_part = combine(
        packing, order, me, row_grad, gate_grad, shared_pre_grad, share_w,
        weighted, shared_act, share_out, 128,
    )
    marks = []
    routed_sum = ring_scatter(lambda n: routed_part[n * count : (n + 1) * count], None, marks)
    norm_two_grad = routed_sum[:, :width]
    gate_grad = routed_sum[:, width : width + n_e] + routed_sum[:, width + 64 : width + 64 + n_e]
    routed_out = routed_sum[:, width + 128 :]

    def shard_grads(left, right, chunks):
        size = left.shape[1] // n_dp
        part = size // chunks
        cut = lambda start, wide, after: tied(
            lax.dynamic_slice_in_dim(left, start, wide, 1), *after
        )
        got = []
        for j in range(chunks):
            sent.append([])
            for step in range(1, n_dp):
                after = marks + (sent[-3] if len(sent) > 2 else [])
                block = dot_tn(cut((here + step) % n_dp * size + j * part, part, after), right)
                sent[-1].append(
                    lax.ppermute(
                        block.astype(BF16), "dp", [(i, (i + step) % n_dp) for i in range(n_dp)]
                    )
                )
            got.append(sent[-1])
        return dot_tn(cut(here * size, size, marks), right), got

    def shard_sum(own, got, tokens):
        part = own.shape[0] // len(got)
        own = own[None]
        for j, (parts, token) in enumerate(zip(got, tokens)):
            block = sum(tied(p.astype(F32), token) for p in parts)[None]
            block = own[:, j * part : (j + 1) * part] + block
            own = lax.dynamic_update_slice_in_dim(own, block, j * part, 1)
        return own

    sent = []
    down_own, down_got = shard_grads(expert_act, route_grad, 2)
    up_own, up_got = shard_grads(arrived, pre_grad, len(up_parts) - 1)

    share_out_grad = dp_scatter(dot_tn(shared_act, cot_all).reshape(n_dp, shared_rows, width))
    share_in_grad = dot_tn(norm_two_all, shared_pre_grad)
    share_in_grad = dp_scatter(share_in_grad.reshape(n_dp, n_e, rows, 2 * shared_width))
    share_in_sent = swap(share_in_grad.astype(BF16))
    share_in_grad = share_in_sent.astype(F32)
    share_in_grad = (
        share_in_grad.reshape(n_e, rows, 2, n_dp, shared_rows)
        .transpose(1, 2, 3, 0, 4)
        .reshape(rows, -1)
    )

    logit_grad = gates * (gate_grad - jnp.sum(gates * gate_grad, axis=-1, keepdims=True))
    router_grad = jnp.dot(
        logit_grad.T, norm_two.astype(F32), precision=HIGHEST, preferred_element_type=F32
    )
    norm_two_grad = norm_two_grad + jnp.dot(
        logit_grad, router_full.astype(F32), precision=HIGHEST, preferred_element_type=F32
    )
    gain_two_grad = jnp.sum(norm_two_grad * normed_two, axis=0)
    upstream = cotangent.astype(F32)
    scaled_two = norm_two_grad * gain_second
    resid_grad = upstream + inverse_two * (
        scaled_two - normed_two * jnp.mean(scaled_two * normed_two, axis=-1, keepdims=True)
    )
    small_grad = jnp.concatenate([router_grad, gain_two_grad[None]], axis=0)

    branch_cot = resid_grad.astype(BF16)
    proj_part = outer(mixed, branch_cot, order)
    proj_grad = ring_scatter(lambda n: proj_part[n * count : (n + 1) * count])
    mixed_grad = tied(dot_nt(branch_cot, proj_all), share_in_sent, *down_got[0]).astype(BF16)
    mixed_grad = mixed_grad.reshape(count, n_e, n_dp, rows).transpose(0, 2, 1, 3)
    mixed_grad = swap(mixed_grad.reshape(count, n_e, HEAD_DIM).transpose(1, 0, 2))
    mixed_grad = mixed_grad.reshape(length, HEAD_DIM)
    attn_out_grad = dp_scatter(proj_grad.reshape(n_dp, rows, width))
    qkv_grad = attend_back(
        query, key, value, mixed_grad, lse, first_place, cos_table, sin_table, order
    )
    small_grad = tied(small_grad, qkv_grad).reshape(n_e + 1, n_dp * n_e, rows).transpose(1, 0, 2)
    small_grad = lax.all_to_all(
        small_grad, ("dp", "expert"), split_axis=0, concat_axis=0, tiled=True
    )
    small_grad = jnp.sum(small_grad, axis=0)
    norm_one_part = dot_nt(qkv_grad, head_w).astype(BF16)
    scaled_one = ring_scatter(
        lambda n: norm_one_part[n * count : (n + 1) * count],
        {1: [proj_grad] + down_got[1], half - 1: up_got[0]},
    )
    expert_out_grad = shard_sum(down_own, down_got, [mixed_grad, scaled_one])
    expert_in_grad = shard_sum(up_own, up_got, ([qkv_grad] + [scaled_one] * 3)[: len(up_got)])
    input_grad = resid_grad + inverse_one * (
        scaled_one - normed_one * jnp.mean(scaled_one * normed_one, axis=-1, keepdims=True)
    )
    head_grad = dot_tn(norm_all, qkv_grad).reshape(n_dp, n_e, rows, 3 * HEAD_DIM)
    head_grad = swap(dp_scatter(head_grad).astype(BF16)).astype(F32)
    head_grad = (
        head_grad.reshape(n_e, rows, 3, HEAD_DIM).transpose(1, 2, 0, 3).reshape(rows, 3 * width)
    )
    gain_attn_grad = jnp.sum(head_grad * attn_in.astype(F32), axis=1)
    attn_in_grad = head_grad * gain_rows
    return (
        (resid + routed_out).astype(BF16),
        input_grad.astype(BF16),
        attn_in_grad,
        attn_out_grad,
        gain_attn_grad,
        share_in_grad,
        share_out_grad,
        small_grad[:n_e].T,
        small_grad[n_e],
        expert_in_grad,
        expert_out_grad,
    )


def solution(mesh):
    return jax.shard_map(
        per_device,
        mesh=mesh,
        in_specs=(
            P(("dp", "expert"), None),
            P(("dp", "expert"), None),
            P("dp", None),
            P(("dp", "expert"), None),
            P(("dp", "expert"), None),
            P(("dp", "expert"), None),
            P(("dp", "expert")),
            P(("dp", "expert"), None),
            P(("dp", "expert"), None),
            P(("dp", "expert"), None),
            P(("dp", "expert")),
            P("expert", "dp", None),
            P("expert", "dp", None),
        ),
        out_specs=(
            P(("dp", "expert"), None),
            P(("dp", "expert"), None),
            P(("dp", "expert"), None),
            P(("dp", "expert"), None),
            P(("dp", "expert")),
            P(("dp", "expert"), None),
            P(("dp", "expert"), None),
            P(("dp", "expert"), None),
            P(("dp", "expert")),
            P("expert", "dp", None),
            P("expert", "dp", None),
        ),
        check_vma=False,
    )
```

```python
import functools
import math

import jax
import jax.numpy as jnp
from jax import lax
from jax.experimental import pallas as pl
from jax.experimental.pallas import tpu as pltpu
from jax.sharding import PartitionSpec as P

HEADS = 16
HEAD_DIM = 128
TOP = 6


EPS = 1e-06
THETA = 10000.0
NEG = -1e30
HIGHEST = lax.Precision.HIGHEST
BF16 = jnp.bfloat16
F32 = jnp.float32
LOG2E = math.log2(math.e)


def rope_tables(segments):
    length = segments.shape[0]
    places = jnp.arange(length, dtype=jnp.int32)
    starts = jnp.concatenate([jnp.ones((1,), dtype=jnp.bool_), segments[1:] != segments[:-1]])
    first_place = lax.cummax(jnp.where(starts, places, 0), axis=0)
    offset = (places - first_place).astype(jnp.float32)
    half_dim = HEAD_DIM // 2
    freqs = jnp.exp(jnp.arange(half_dim, dtype=jnp.float32) * (-2.0 * math.log(THETA) / HEAD_DIM))
    angles = offset[:, None] * freqs[None, :]
    cos_table, sin_table = jnp.cos(angles), jnp.sin(angles)
    return (
        jnp.concatenate([cos_table, cos_table], axis=1),
        jnp.concatenate([-sin_table, sin_table], axis=1),
        first_place[None, :],
    )


def silu_back(grad_act, gate_part, up_part):
    sigmoid_gate = jax.nn.sigmoid(gate_part)
    gate_grad = grad_act * up_part * sigmoid_gate * (1.0 + gate_part * (1.0 - sigmoid_gate))
    up_grad = grad_act * gate_part * sigmoid_gate
    return jnp.concatenate([gate_grad, up_grad], axis=-1)


def dot(left, right):
    return jnp.dot(left, right, preferred_element_type=F32)


def dot_tn(left, right):
    return lax.dot_general(left, right, (((0,), (0,)), ((), ())), preferred_element_type=F32)


def dot_nt(left, right):
    return lax.dot_general(left, right, (((1,), (1,)), ((), ())), preferred_element_type=F32)


def turn(values, cos_table, sin_table):
    return values * cos_table + pltpu.roll(values, HEAD_DIM // 2, 1) * sin_table


def attend_kernel(blocks, block, rows_ref, weight_ref, cos_ref, sin_ref, start_ref, o_ref, q_ref, k_ref, v_ref, lse_ref, vt_ref):
    step = pl.program_id(0)
    length = q_ref.shape[0]
    factor = HEAD_DIM ** (-0.5) * LOG2E
    rows = rows_ref.shape[0]

    @pl.when(step < blocks)
    def _():
        qkv = dot(rows_ref[...], weight_ref[...])
        at = pl.ds(pl.multiple_of(step * rows, rows), rows)
        cos_table, sin_table = cos_ref[at, :], sin_ref[at, :]
        q_ref[at, :] = turn(qkv[:, :HEAD_DIM], cos_table, sin_table).astype(BF16)
        k_ref[at, :] = turn(qkv[:, HEAD_DIM : 2 * HEAD_DIM], cos_table, sin_table).astype(BF16)
        value = qkv[:, 2 * HEAD_DIM :]
        v_ref[at, :] = value.astype(BF16)
        vt_ref[:, at] = value.T.astype(BF16)

    for i in range(length // block):

        @pl.when(step == blocks + i)
        def _(i=i):
            low, high = i * block, (i + 1) * block
            raw = dot_nt(k_ref[:high, :], q_ref[low:high, :])
            keys = lax.broadcasted_iota(jnp.int32, raw.shape, 0)
            queries = low + lax.broadcasted_iota(jnp.int32, raw.shape, 1)
            allowed = (keys <= queries) & (keys >= start_ref[:, low:high])
            raw = jnp.where(allowed, raw, NEG)
            top = jnp.max(raw, axis=0, keepdims=True)
            shifted = jnp.exp2((raw - top) * factor)
            total = jnp.sum(shifted, axis=0, keepdims=True)
            probs = (shifted * (1.0 / total)).astype(BF16)
            mixed = dot(vt_ref[:, :high], probs)
            o_ref[low:high, :] = mixed.T.astype(BF16)
            lse_ref[:, low:high] = top * factor + jnp.log2(total)


def attend(normed, weight, cos_table, sin_table, first_place):
    length, width = normed.shape
    rows = block = min(256, length)
    blocks = length // rows
    whole = lambda shape: pl.BlockSpec(shape, lambda i: (0, 0))
    head = jax.ShapeDtypeStruct((length, HEAD_DIM), BF16)
    return pl.pallas_call(
        functools.partial(attend_kernel, blocks, block),
        grid=(blocks + length // block,),
        out_shape=[head] * 4 + [jax.ShapeDtypeStruct((1, length), F32)],
        in_specs=[
            pl.BlockSpec((rows, width), lambda i: (jnp.minimum(i, blocks - 1), 0)),
            whole(weight.shape),
            whole((length, HEAD_DIM)),
            whole((length, HEAD_DIM)),
            whole((1, length)),
        ],
        out_specs=[whole((length, HEAD_DIM))] * 4 + [whole((1, length))],
        scratch_shapes=[pltpu.VMEM((HEAD_DIM, length), BF16)],
        compiler_params=pltpu.CompilerParams(vmem_limit_bytes=40 * 2**20),
        name="attend",
    )(normed, weight, cos_table, sin_table, first_place)


def attend_back_kernel(
    block, rows, order_ref, q_ref, k_ref, v_ref, do_ref, lse_ref, start_ref, cos_ref, sin_ref, out_ref, kt_ref, dq_ref, dk_ref, dv_ref
):
    length = q_ref.shape[0]
    step = pl.program_id(0)
    scale = HEAD_DIM ** (-0.5)
    factor = scale * LOG2E
    count = length // block

    @pl.when(step == 0)
    def _():
        kt_ref[...] = k_ref[...].astype(F32).T.astype(BF16)
        dk_ref[...] = jnp.zeros_like(dk_ref)
        dv_ref[...] = jnp.zeros_like(dv_ref)

    for i in range(count):

        @pl.when(step == i)
        def _(i=i):
            low, high = i * block, (i + 1) * block
            query, grad = q_ref[low:high, :], do_ref[low:high, :]
            raw = dot_nt(k_ref[:high, :], query)
            keys = lax.broadcasted_iota(jnp.int32, raw.shape, 0)
            queries = low + lax.broadcasted_iota(jnp.int32, raw.shape, 1)
            allowed = (keys <= queries) & (keys >= start_ref[:, low:high])
            raw = jnp.where(allowed, raw * factor - lse_ref[:, low:high], NEG)
            probs = jnp.exp2(raw)
            probs_grad = dot_nt(v_ref[:high, :], grad)
            inner = jnp.sum(probs_grad * probs, axis=0, keepdims=True)
            score_grad = (probs * (probs_grad - inner)).astype(BF16)
            dv_ref[:high, :] += dot(probs.astype(BF16), grad)
            dk_ref[:high, :] += dot(score_grad, query)
            dq_ref[low:high, :] = dot(kt_ref[:, :high], score_grad).T

    @pl.when(step == count - 1)
    def _():
        for n in range(length // rows):
            at = pl.ds(pl.multiple_of(order_ref[n] * rows, rows), rows)
            to = slice(n * rows, (n + 1) * rows)
            cos_table, sin_table = cos_ref[at, :], -sin_ref[at, :]
            out_ref[to, :HEAD_DIM] = turn(dq_ref[at, :] * scale, cos_table, sin_table).astype(BF16)
            out_ref[to, HEAD_DIM : 2 * HEAD_DIM] = turn(
                dk_ref[at, :] * scale, cos_table, sin_table
            ).astype(BF16)
            out_ref[to, 2 * HEAD_DIM :] = dv_ref[at, :].astype(BF16)


def attend_back(query, key, value, grad, lse, first_place, cos_table, sin_table, order):
    length = query.shape[0]
    block = min(256, length)
    whole = lambda shape: pl.BlockSpec(shape, lambda i, order: (0, 0))
    head = whole((length, HEAD_DIM))
    return pl.pallas_call(
        functools.partial(attend_back_kernel, block, length // order.shape[0]),
        out_shape=jax.ShapeDtypeStruct((length, 3 * HEAD_DIM), BF16),
        grid_spec=pltpu.PrefetchScalarGridSpec(
            num_scalar_prefetch=1,
            grid=(length // block,),
            in_specs=[head] * 4 + [whole((1, length))] * 2 + [head] * 2,
            out_specs=whole((length, 3 * HEAD_DIM)),
            scratch_shapes=[pltpu.VMEM((HEAD_DIM, length), BF16)]
            + [pltpu.VMEM((length, HEAD_DIM), F32)] * 3,
        ),
        compiler_params=pltpu.CompilerParams(vmem_limit_bytes=48 * 2**20),
        name="attend_back",
    )(order, query, key, value, grad, lse, first_place, cos_table, sin_table)


def dp_gather(value):
    count = lax.axis_size("dp")
    if count == 1:
        return value[None]
    here = lax.axis_index("dp")
    parts = [value] + [
        lax.ppermute(value, "dp", [(i, (i - step) % count) for i in range(count)])
        for step in range(1, count)
    ]
    if count == 2:
        first = here == 0
        return jnp.stack(
            [jnp.where(first, parts[0], parts[1]), jnp.where(first, parts[1], parts[0])]
        )
    whole = jnp.zeros((count,) + value.shape, value.dtype)
    for step, part in enumerate(parts):
        whole = lax.dynamic_update_index_in_dim(whole, part, (here + step) % count, 0)
    return whole


def dp_scatter(value):
    count = lax.axis_size("dp")
    here = lax.axis_index("dp")
    total = lax.dynamic_index_in_dim(value, here, 0, keepdims=False)
    for step in range(1, count):
        block = lax.dynamic_index_in_dim(value, (here + step) % count, 0, keepdims=False)
        got = lax.ppermute(
            block.astype(BF16), "dp", [(i, (i + step) % count) for i in range(count)]
        )
        total = total + got.astype(F32)
    return total


def tied(value, *tokens):
    firsts = [lax.slice(t, (0,) * t.ndim, (1,) * t.ndim).reshape(()) for t in tokens]
    token = sum(t.astype(F32) for t in firsts) * 0.0
    return (value.astype(F32) * (1.0 + token)).astype(value.dtype)


def chosen(pos_ref, base, window):
    count = pos_ref.shape[-1]
    row = base + lax.broadcasted_iota(jnp.int32, (window, count), 0)
    return row == pos_ref[0]


def dispatch_kernel(widths, window, base_ref, pos_ref, gate_ref, block_ref, *outs):
    blocks, rows_ref, weights_ref = outs[:-2], outs[-2], outs[-1]
    step = pl.program_id(0)

    @pl.when(step == 0)
    def _():
        rows_ref[...] = jnp.zeros_like(rows_ref)
        weights_ref[...] = jnp.zeros_like(weights_ref)

    left = 0
    for block, wide in zip(blocks, widths):
        block[...] = block_ref[:, left : left + wide]
        left += wide
    base = pl.multiple_of(base_ref[step], 16)
    pick = chosen(pos_ref, base, window)
    at = pl.ds(base, window)
    found = dot(pick.astype(F32).astype(BF16), block_ref[:, : rows_ref.shape[1]])
    rows_ref[at, :] = (rows_ref[at, :].astype(F32) + found).astype(BF16)
    weights_ref[at, :] += jnp.sum(jnp.where(pick, gate_ref[0], 0.0), axis=1, keepdims=True)


def dispatch(array, width, widths, packing, gates):
    base, pos, _, window, packed = packing
    count, _, rows = pos.shape
    row_spec = pl.BlockSpec((1, 1, rows), lambda i, base: (i, 0, 0))
    return pl.pallas_call(
        functools.partial(dispatch_kernel, tuple(widths), window),
        out_shape=[jax.ShapeDtypeStruct((rows * count, wide), BF16) for wide in widths]
        + [
            jax.ShapeDtypeStruct((packed, width), BF16),
            jax.ShapeDtypeStruct((packed, 1), F32),
        ],
        grid_spec=pltpu.PrefetchScalarGridSpec(
            num_scalar_prefetch=1,
            grid=(count,),
            in_specs=[
                row_spec,
                row_spec,
                pl.BlockSpec((rows, array.shape[1]), lambda i, base: (i, 0)),
            ],
            out_specs=[pl.BlockSpec((rows, wide), lambda i, base: (i, 0)) for wide in widths]
            + [
                pl.BlockSpec((packed, width), lambda i, base: (0, 0)),
                pl.BlockSpec((packed, 1), lambda i, base: (0, 0)),
            ],
        ),
        compiler_params=pltpu.CompilerParams(vmem_limit_bytes=40 * 2**20),
        name="dispatch",
    )(base, pos, gates, array)


def expert_kernel(ups, total_ref, starts_ref, x_ref, g_ref, gate_ref, *refs):
    parts, refs = refs[:-9], refs[-9:]
    wy_ref, dn_ref, ea_ref, dy_ref, db_ref, dg_ref, up_ref, down_ref, sems = refs
    step = pl.program_id(0)
    rows, hidden = ea_ref.shape
    some = step * rows < total_ref[0]

    @pl.when(step == 0)
    def _():
        copies = []
        for n, part in enumerate(parts):
            at = pl.ds(pl.multiple_of(starts_ref[n], 16), part.shape[0])
            whole = up_ref if n < ups else down_ref
            copies.append(pltpu.make_async_copy(part, whole.at[at, :], sems.at[n]))
        for copy in copies:
            copy.start()
        for copy in copies:
            copy.wait()

    @pl.when(some)
    def _():
        pre = dot(x_ref[...], up_ref[...])
        gate_part, up_part = pre[:, :hidden], pre[:, hidden:]
        sigmoid_gate = 1.0 / (1.0 + jnp.exp(-gate_part))
        silu = gate_part * sigmoid_gate
        act = (silu * up_part).astype(BF16)
        ea_ref[...] = act
        result = dot(act, down_ref[...]).astype(BF16).astype(F32)
        grad = g_ref[...].astype(F32)
        gate = gate_ref[...]
        dg_ref[...] = jnp.sum(grad * result, axis=1, keepdims=True)
        wy_ref[...] = (gate * result).astype(BF16)
        out_grad = (gate * grad).astype(BF16)
        dy_ref[...] = out_grad
        act_grad = dot_nt(out_grad, down_ref[...])
        db_ref[:, :hidden] = (
            act_grad * up_part * sigmoid_gate * (1.0 + gate_part * (1.0 - sigmoid_gate))
        ).astype(BF16)
        db_ref[:, hidden:] = (act_grad * silu).astype(BF16)
        dn_ref[...] = dot_nt(db_ref[...], up_ref[...]).astype(BF16)

    @pl.when(jnp.logical_not(some))
    def _():
        for ref in (wy_ref, dn_ref, ea_ref, dy_ref, db_ref, dg_ref):
            ref[...] = jnp.zeros_like(ref)


def expert(total, rows, grads, gates, ups, downs):
    packed, width = rows.shape
    hidden = sum(part.shape[0] for part, _ in downs)
    tile = 256
    parts = [part for part, _ in ups + downs]
    starts = jnp.stack([start for _, start in ups + downs]).astype(jnp.int32)
    spec = lambda wide: pl.BlockSpec((tile, wide), lambda i, total, starts: (i, 0))
    widths = (width, width, hidden, width, 2 * hidden)
    return pl.pallas_call(
        functools.partial(expert_kernel, len(ups)),
        out_shape=[jax.ShapeDtypeStruct((packed, wide), BF16) for wide in widths]
        + [jax.ShapeDtypeStruct((packed, 1), F32)],
        grid_spec=pltpu.PrefetchScalarGridSpec(
            num_scalar_prefetch=2,
            grid=(packed // tile,),
            in_specs=[spec(width), spec(width), spec(1)]
            + [pl.BlockSpec(memory_space=pl.ANY)] * len(parts),
            out_specs=[spec(wide) for wide in widths] + [spec(1)],
            scratch_shapes=[
                pltpu.VMEM((width, 2 * hidden), BF16),
                pltpu.VMEM((hidden, width), BF16),
                pltpu.SemaphoreType.DMA((len(parts),)),
            ],
        ),
        compiler_params=pltpu.CompilerParams(vmem_limit_bytes=58 * 2**20),
        name="expert",
    )(total, starts, rows, grads, gates, *parts)


def combine_kernel(turned, window, extra, base_ref, order_ref, to_ref, me_ref, pos_ref, rows_ref, dg_ref, act_ref, weight_ref, out_ref):
    mul = dot_nt if turned else dot
    base = pl.multiple_of(base_ref[pl.program_id(0)], 16)
    pick = chosen(pos_ref, base, window)
    at = pl.ds(base, window)
    width = rows_ref.shape[1]
    out_ref[:, :width] = (
        dot_tn(pick.astype(F32).astype(BF16), rows_ref[at, :]) + mul(act_ref[...], weight_ref[...])
    ).astype(BF16)
    if extra:
        count = pick.shape[1]
        line = jnp.sum(jnp.where(pick, dg_ref[at, :], 0.0), axis=0, keepdims=True)
        row = lax.broadcasted_iota(jnp.int32, (count, count), 0)
        lane = lax.broadcasted_iota(jnp.int32, (count, count), 1)
        column = jnp.sum(jnp.where(row == lane, line, 0.0), axis=1, keepdims=True)
        high = column.astype(BF16).astype(F32)
        lane = lax.broadcasted_iota(jnp.int32, (count, extra), 1)
        out_ref[:, width:] = jnp.where(
            lane == me_ref[0], high, jnp.where(lane == me_ref[0] + extra // 2, column - high, 0.0)
        ).astype(BF16)


def combine(packing, order, to, me, rows, dg, act, weight, turned, extra):
    base, pos, _, window, packed = packing
    blocks, _, count = pos.shape
    width = rows.shape[-1]
    whole = lambda ref: pl.BlockSpec(ref.shape, lambda i, *_: (0, 0))
    return pl.pallas_call(
        functools.partial(combine_kernel, turned, window, extra),
        out_shape=jax.ShapeDtypeStruct((blocks * count, width + extra), BF16),
        grid_spec=pltpu.PrefetchScalarGridSpec(
            num_scalar_prefetch=4,
            grid=(blocks,),
            in_specs=[
                pl.BlockSpec((1, 1, count), lambda i, *_: (i, 0, 0)),
                whole(rows),
                whole(dg),
                pl.BlockSpec((count, act.shape[1]), lambda i, base, order, to, me: (order[i], 0)),
                whole(weight),
            ],
            out_specs=pl.BlockSpec(
                (count, width + extra), lambda i, base, order, to, me: (to[i], 0)
            ),
        ),
        compiler_params=pltpu.CompilerParams(vmem_limit_bytes=40 * 2**20),
        name="combine",
    )(base, order, to, me.reshape(1), pos, rows, dg, act, weight)


def gather_all(value):
    return lax.all_gather(value, "expert", axis=0, tiled=True)


def scatter_all(value):
    return lax.psum_scatter(value, "expert", scatter_dimension=0, tiled=True).astype(F32)


def swap(value):
    return lax.all_to_all(value, "expert", split_axis=0, concat_axis=0, tiled=True)


def per_device(
    tokens,
    cotangent,
    segment_ids,
    routes,
    attn_in,
    attn_out,
    gain_attn,
    shared_in,
    shared_out,
    router,
    gain_ffn,
    expert_in,
    expert_out,
):
    n_dp, n_e = lax.axis_size("dp"), lax.axis_size("expert")
    me = lax.axis_index("expert")
    count, width = tokens.shape
    segments = segment_ids[0]
    length = segments.shape[0]
    rows = attn_in.shape[0]
    capacity = min(count, 3 * TOP * count // (2 * n_e))
    shared_rows = shared_out.shape[0]
    shared_width = shared_rows * n_dp
    expert_width = expert_out.shape[1] * n_dp

    order = jnp.arange(n_e, dtype=jnp.int32)
    hidden_in = tokens.astype(F32)
    inverse_one = lax.rsqrt(jnp.mean(hidden_in * hidden_in, axis=-1, keepdims=True) + EPS)
    normed_one = hidden_in * inverse_one
    gain_rows = gain_attn.astype(F32)[:, None]
    norm_all = gather_all(normed_one.astype(BF16))
    head_w = (attn_in.astype(F32) * gain_rows).astype(BF16)
    head_w = head_w.reshape(rows, 3, n_e, HEAD_DIM).transpose(2, 0, 1, 3)
    head_sent_w = swap(head_w.reshape(n_e, rows, 3 * HEAD_DIM))
    head_w = dp_gather(head_sent_w).reshape(width, 3 * HEAD_DIM)

    here = lax.axis_index("dp")

    def pieces_of(size, chunks):
        while size % (16 * chunks):
            chunks -= 1
        return chunks

    def part_of(shard, chunks, j, *after):
        size = shard.shape[0] // chunks
        block = shard[j * size : (j + 1) * size]
        block = tied(block, *after) if after else block
        return [
            (
                lax.ppermute(block, "dp", [(i, (i - step) % n_dp) for i in range(n_dp)]),
                (here + step) % n_dp * shard.shape[0] + j * size,
            )
            for step in range(1, n_dp)
        ]

    first = lambda parts: [part for part, _ in parts]
    up_chunks = pieces_of(expert_in.shape[1], max(1, min(4, expert_in.shape[1] // 256)))
    down_chunks = pieces_of(expert_out.shape[1], 2)
    ups = [(expert_in[0], here * expert_in.shape[1])]
    downs = [(expert_out[0], here * expert_out.shape[1])]
    ups += part_of(expert_in[0], up_chunks, 0)
    up_first = first(ups[1:])

    small = jnp.concatenate([router, gain_ffn[:, None]], axis=1)
    small = dp_gather(small).reshape(-1, n_e + 1)
    extra_rows = 32
    extra = jnp.concatenate([small.T, routes.T.astype(BF16)], axis=0)
    extra = jnp.pad(extra, ((0, extra_rows - extra.shape[0]), (0, 0)))
    extra = jnp.broadcast_to(extra, (n_e,) + extra.shape)
    cos_table, sin_table, first_place = rope_tables(segments)
    share_w = shared_in.reshape(rows, 2, n_dp, n_e, shared_rows).transpose(3, 0, 1, 2, 4)
    share_w = share_w.reshape(n_e, rows, 2 * shared_width)

    second = part_of(expert_in[0], up_chunks, 1, head_w) if up_chunks > 1 else []
    ups += second

    head_out, query, key, value, lse = attend(
        norm_all, head_w, cos_table, sin_table, tied(first_place.astype(F32), *up_first).astype(jnp.int32)
    )
    mixed = jnp.concatenate([head_out.reshape(n_e, count, HEAD_DIM), extra], axis=1)
    share_w = swap(tied(share_w, head_sent_w))
    mixed = swap(tied(mixed, share_w, *first(second)))
    third = part_of(expert_in[0], up_chunks, 2, lse) if up_chunks > 2 else []
    fourth = part_of(expert_in[0], up_chunks, 3, lse) if up_chunks > 3 else []
    ups += third + fourth
    down_first = part_of(expert_out[0], down_chunks, 0, mixed)
    downs += down_first
    if down_chunks > 1:
        downs += part_of(expert_out[0], down_chunks, 1, mixed)
    small = mixed[:, count:]
    mixed = mixed[:, :count].transpose(1, 0, 2).reshape(count, n_dp, n_e, rows)
    mixed = mixed.transpose(0, 2, 1, 3).reshape(count, width)
    proj_all = dp_gather(attn_out).reshape(n_dp * rows, width)
    proj_all = gather_all(tied(proj_all, norm_all))
    routes_all = small[:, n_e + 1 : n_e + 1 + TOP].astype(F32)
    small = small[:, : n_e + 1].reshape(n_e, n_e + 1, n_dp, rows).transpose(1, 2, 0, 3)
    small = small.reshape(n_e + 1, width)
    router_full = small[:n_e]
    gain_second = small[n_e].astype(F32)

    share_sent = share_w
    share_w = dp_gather(share_w).reshape(width, 2 * shared_width)
    share_out = dp_gather(shared_out).reshape(shared_width, width)
    resid = hidden_in + dot(mixed, proj_all)
    if third:
        resid = tied(resid, *first(third))

    inverse_two = lax.rsqrt(jnp.mean(resid * resid, axis=-1, keepdims=True) + EPS)
    normed_two = resid * inverse_two
    norm_two = (normed_two * gain_second).astype(BF16)
    logits = dot_nt(norm_two, router_full)
    picked = jnp.any(routes[:, :, None] == jnp.arange(n_e)[None, None, :], axis=1)
    chosen = jnp.where(picked, logits, NEG)
    chosen = jnp.where(picked, jnp.exp(chosen - jnp.max(chosen, axis=-1, keepdims=True)), 0.0)
    gates = chosen / jnp.sum(chosen, axis=-1, keepdims=True)
    gate_high = gates.astype(BF16)
    gate_low = (gates - gate_high.astype(F32)).astype(BF16)
    blank = jnp.zeros((count, 128 - 2 * n_e), BF16)
    payload = jnp.concatenate([norm_two, gate_high, gate_low, blank], axis=1)
    payload = gather_all(payload)
    cot_all = gather_all(tied(cotangent, payload))

    named = jnp.any(routes_all == me.astype(F32), axis=1)
    ranking = jnp.cumsum(named.astype(jnp.int32), axis=1)
    ends = jnp.cumsum(ranking[:, -1])
    begins = ends - ranking[:, -1]
    pos = jnp.where(named, begins[:, None] + ranking - 1, -1)[:, None, :]
    window = -(-(capacity + 15) // 16) * 16
    packed = -(-(n_e * capacity + 32) // 256) * 256
    packing = (begins // 16 * 16, pos, ends[-1:], window, packed)
    norm_two_all, payload, arrived, _ = dispatch(
        payload, width, [width, 128], packing, tied(jnp.zeros((n_e, 1, count), F32), *first(fourth + down_first))
    )
    mine = jnp.arange(n_e) == me
    gate_all = payload[:, : 2 * n_e].astype(F32).reshape(length, 2, n_e)
    gate_all = jnp.sum(jnp.where(mine, gate_all, 0.0), axis=(1, 2)).reshape(n_e, 1, count)
    cot_rows, gate_rows = dispatch(cot_all, width, [], packing, gate_all)
    weighted, row_grad, expert_act, route_grad, pre_grad, gate_grad = expert(
        packing[2],
        arrived,
        cot_rows,
        gate_rows,
        ups,
        downs,
    )

    shared_pre = dot(norm_two_all, share_w)
    shared_act = (
        jax.nn.silu(shared_pre[:, :shared_width]) * shared_pre[:, shared_width:]
    ).astype(BF16)
    shared_act_grad = dot_nt(cot_all, share_out)
    shared_pre_grad = silu_back(
        shared_act_grad, shared_pre[:, :shared_width], shared_pre[:, shared_width:]
    ).astype(BF16)
    norm_two_part = combine(
        packing, order, order, me, row_grad, gate_grad, shared_pre_grad, share_w, True, 128
    )
    marks = [norm_two_part]
    norm_two_grad = scatter_all(norm_two_part)
    gate_grad = norm_two_grad[:, width : width + n_e] + norm_two_grad[:, width + 64 : width + 64 + n_e]
    norm_two_grad = norm_two_grad[:, :width]
    out_part = combine(
        packing, order, order, me, weighted, gate_rows, shared_act, share_out, False, 0
    )
    routed_out = scatter_all(out_part)

    def shard_grads(left, right, chunks):
        size = left.shape[1] // n_dp
        part = size // chunks
        cut = lambda start, wide: tied(lax.dynamic_slice_in_dim(left, start, wide, 1), *marks)
        got = [
            [
                lax.ppermute(
                    dot_tn(cut((here + step) % n_dp * size + j * part, part), right).astype(BF16),
                    "dp",
                    [(i, (i + step) % n_dp) for i in range(n_dp)],
                )
                for step in range(1, n_dp)
            ]
            for j in range(chunks)
        ]
        return dot_tn(cut(here * size, size), right), got

    def shard_sum(own, got, tokens):
        part = own.shape[0] // len(got)
        own = own[None]
        for j, (parts, token) in enumerate(zip(got, tokens)):
            block = sum(tied(p.astype(F32), token) for p in parts)[None]
            block = own[:, j * part : (j + 1) * part] + block
            own = lax.dynamic_update_slice_in_dim(own, block, j * part, 1)
        return own

    down_own, down_got = shard_grads(expert_act, route_grad, 2)
    up_own, up_got = shard_grads(arrived, pre_grad, up_chunks)

    share_out_grad = dp_scatter(dot_tn(shared_act, cot_all).reshape(n_dp, shared_rows, width))
    share_in_grad = dot_tn(norm_two_all, shared_pre_grad)
    share_in_grad = dp_scatter(share_in_grad.reshape(n_dp, n_e, rows, 2 * shared_width))
    share_in_sent = swap(share_in_grad.astype(BF16))
    share_in_grad = share_in_sent.astype(F32)
    share_in_grad = (
        share_in_grad.reshape(n_e, rows, 2, n_dp, shared_rows)
        .transpose(1, 2, 3, 0, 4)
        .reshape(rows, -1)
    )

    logit_grad = gates * (gate_grad - jnp.sum(gates * gate_grad, axis=-1, keepdims=True))
    router_grad = jnp.dot(
        logit_grad.T, norm_two.astype(F32), precision=HIGHEST, preferred_element_type=F32
    )
    norm_two_grad = norm_two_grad + jnp.dot(
        logit_grad, router_full.astype(F32), precision=HIGHEST, preferred_element_type=F32
    )
    gain_two_grad = jnp.sum(norm_two_grad * normed_two, axis=0)
    upstream = tied(cotangent.astype(F32), *down_got[0])
    scaled_two = norm_two_grad * gain_second
    resid_grad = upstream + inverse_two * (
        scaled_two - normed_two * jnp.mean(scaled_two * normed_two, axis=-1, keepdims=True)
    )
    small_grad = jnp.concatenate([router_grad, gain_two_grad[None]], axis=0)

    branch_cot = resid_grad.astype(BF16)
    proj_grad = dot_tn(mixed, branch_cot).astype(BF16)
    mixed_grad = tied(dot_nt(branch_cot, proj_all), proj_grad, share_in_sent, *down_got[1]).astype(BF16)
    mixed_grad = mixed_grad.reshape(count, n_e, n_dp, rows).transpose(0, 2, 1, 3)
    mixed_grad = swap(mixed_grad.reshape(count, n_e, HEAD_DIM).transpose(1, 0, 2))
    mixed_grad = mixed_grad.reshape(length, HEAD_DIM)
    proj_grad = scatter_all(proj_grad)
    attn_out_grad = dp_scatter(proj_grad.reshape(n_dp, rows, width))
    qkv_grad = attend_back(
        query, key, value, mixed_grad, tied(lse, *up_got[0]), first_place, cos_table, sin_table, order
    )
    small_grad = tied(small_grad, qkv_grad).reshape(n_e + 1, n_dp * n_e, rows).transpose(1, 0, 2)
    small_grad = lax.all_to_all(
        small_grad, ("dp", "expert"), split_axis=0, concat_axis=0, tiled=True
    )
    small_grad = jnp.sum(small_grad, axis=0)
    norm_one_part = dot_nt(qkv_grad, tied(head_w, *up_got[min(1, len(up_got) - 1)])).astype(BF16)
    scaled_one = scatter_all(norm_one_part)
    expert_out_grad = shard_sum(down_own, down_got, [qkv_grad, qkv_grad])
    expert_in_grad = shard_sum(up_own, up_got, ([qkv_grad] + [scaled_one] * 3)[: len(up_got)])
    input_grad = resid_grad + inverse_one * (
        scaled_one - normed_one * jnp.mean(scaled_one * normed_one, axis=-1, keepdims=True)
    )
    head_grad = dot_tn(norm_all, qkv_grad).reshape(n_dp, n_e, rows, 3 * HEAD_DIM)
    head_grad = swap(dp_scatter(head_grad).astype(BF16)).astype(F32)
    head_grad = (
        head_grad.reshape(n_e, rows, 3, HEAD_DIM).transpose(1, 2, 0, 3).reshape(rows, 3 * width)
    )
    gain_attn_grad = jnp.sum(head_grad * attn_in.astype(F32), axis=1)
    attn_in_grad = head_grad * gain_rows
    return (
        (resid + routed_out).astype(BF16),
        input_grad.astype(BF16),
        attn_in_grad,
        attn_out_grad,
        gain_attn_grad,
        share_in_grad,
        share_out_grad,
        small_grad[:n_e].T,
        small_grad[n_e],
        expert_in_grad,
        expert_out_grad,
    )


def solution(mesh):
    return jax.shard_map(
        per_device,
        mesh=mesh,
        in_specs=(
            P(("dp", "expert"), None),
            P(("dp", "expert"), None),
            P("dp", None),
            P(("dp", "expert"), None),
            P(("dp", "expert"), None),
            P(("dp", "expert"), None),
            P(("dp", "expert")),
            P(("dp", "expert"), None),
            P(("dp", "expert"), None),
            P(("dp", "expert"), None),
            P(("dp", "expert")),
            P("expert", "dp", None),
            P("expert", "dp", None),
        ),
        out_specs=(
            P(("dp", "expert"), None),
            P(("dp", "expert"), None),
            P(("dp", "expert"), None),
            P(("dp", "expert"), None),
            P(("dp", "expert")),
            P(("dp", "expert"), None),
            P(("dp", "expert"), None),
            P(("dp", "expert"), None),
            P(("dp", "expert")),
            P("expert", "dp", None),
            P("expert", "dp", None),
        ),
        check_vma=False,
    )
```

```python
import functools
import math

import jax
import jax.numpy as jnp
from jax import lax
from jax.experimental import pallas as pl
from jax.experimental.pallas import tpu as pltpu
from jax.sharding import PartitionSpec as P

HEADS = 16
HEAD_DIM = 128
TOP = 6


EPS = 1e-06
THETA = 10000.0
NEG = -1e30
HIGHEST = lax.Precision.HIGHEST
BF16 = jnp.bfloat16
F32 = jnp.float32
LOG2E = math.log2(math.e)


def rope_tables(segments):
    length = segments.shape[0]
    places = jnp.arange(length, dtype=jnp.int32)
    starts = jnp.concatenate([jnp.ones((1,), dtype=jnp.bool_), segments[1:] != segments[:-1]])
    first_place = lax.cummax(jnp.where(starts, places, 0), axis=0)
    offset = (places - first_place).astype(jnp.float32)
    half_dim = HEAD_DIM // 2
    freqs = jnp.exp(jnp.arange(half_dim, dtype=jnp.float32) * (-2.0 * math.log(THETA) / HEAD_DIM))
    angles = offset[:, None] * freqs[None, :]
    cos_table, sin_table = jnp.cos(angles), jnp.sin(angles)
    return (
        jnp.concatenate([cos_table, cos_table], axis=1),
        jnp.concatenate([-sin_table, sin_table], axis=1),
        first_place[None, :],
    )


def silu_back(grad_act, gate_part, up_part):
    sigmoid_gate = jax.nn.sigmoid(gate_part)
    gate_grad = grad_act * up_part * sigmoid_gate * (1.0 + gate_part * (1.0 - sigmoid_gate))
    up_grad = grad_act * gate_part * sigmoid_gate
    return jnp.concatenate([gate_grad, up_grad], axis=-1)


def dot(left, right):
    return jnp.dot(left, right, preferred_element_type=F32)


def dot_tn(left, right):
    return lax.dot_general(left, right, (((0,), (0,)), ((), ())), preferred_element_type=F32)


def dot_nt(left, right):
    return lax.dot_general(left, right, (((1,), (1,)), ((), ())), preferred_element_type=F32)


def turn(values, cos_table, sin_table):
    return values * cos_table + pltpu.roll(values, HEAD_DIM // 2, 1) * sin_table


def attend_kernel(sources, block, order_ref, *refs):
    pieces = refs[: sources[-1][-1] + 1]
    weight_ref, cos_ref, sin_ref, start_ref = refs[len(pieces) : len(pieces) + 4]
    o_ref, q_ref, k_ref, v_ref, lse_ref, rows_ref, vt_ref = refs[len(pieces) + 4 :]
    step = pl.program_id(0)
    length = q_ref.shape[0]
    factor = HEAD_DIM ** (-0.5) * LOG2E
    rows = rows_ref.shape[0]

    for n, parts in enumerate(sources):

        @pl.when(step == n)
        def _(parts=parts):
            low = 0
            for part in parts:
                size = pieces[part].shape[0]
                rows_ref[low : low + size, :] = pieces[part][...]
                low += size

    @pl.when(step < len(sources))
    def _():
        qkv = dot(rows_ref[...], weight_ref[...])
        at = pl.ds(pl.multiple_of(order_ref[step] * rows, rows), rows)
        cos_table, sin_table = cos_ref[at, :], sin_ref[at, :]
        q_ref[at, :] = turn(qkv[:, :HEAD_DIM], cos_table, sin_table).astype(BF16)
        k_ref[at, :] = turn(qkv[:, HEAD_DIM : 2 * HEAD_DIM], cos_table, sin_table).astype(BF16)
        value = qkv[:, 2 * HEAD_DIM :]
        v_ref[at, :] = value.astype(BF16)
        vt_ref[:, at] = value.T.astype(BF16)

    for i in range(length // block):

        @pl.when(step == len(sources) + i)
        def _(i=i):
            low, high = i * block, (i + 1) * block
            raw = dot_nt(k_ref[:high, :], q_ref[low:high, :])
            keys = lax.broadcasted_iota(jnp.int32, raw.shape, 0)
            queries = low + lax.broadcasted_iota(jnp.int32, raw.shape, 1)
            allowed = (keys <= queries) & (keys >= start_ref[:, low:high])
            raw = jnp.where(allowed, raw, NEG)
            top = jnp.max(raw, axis=0, keepdims=True)
            shifted = jnp.exp2((raw - top) * factor)
            total = jnp.sum(shifted, axis=0, keepdims=True)
            probs = (shifted * (1.0 / total)).astype(BF16)
            mixed = dot(vt_ref[:, :high], probs)
            o_ref[low:high, :] = mixed.T.astype(BF16)
            lse_ref[:, low:high] = top * factor + jnp.log2(total)


def attend(blocks, order, weight, cos_table, sin_table, first_place):
    pieces, sources = flatten(blocks)
    length = cos_table.shape[0]
    rows = length // len(sources)
    width = weight.shape[0]
    block = min(256, length)
    last = len(sources) - 1
    whole = lambda shape: pl.BlockSpec(shape, lambda i, order: (0, 0))
    head = jax.ShapeDtypeStruct((length, HEAD_DIM), BF16)
    return pl.pallas_call(
        functools.partial(attend_kernel, sources, block),
        out_shape=[head] * 4
        + [jax.ShapeDtypeStruct((1, length), F32), jax.ShapeDtypeStruct((length, width), BF16)],
        grid_spec=pltpu.PrefetchScalarGridSpec(
            num_scalar_prefetch=1,
            grid=(len(sources) + length // block,),
            in_specs=[whole(piece.shape) for piece in pieces]
            + [
                whole(weight.shape),
                whole((length, HEAD_DIM)),
                whole((length, HEAD_DIM)),
                whole((1, length)),
            ],
            out_specs=[whole((length, HEAD_DIM))] * 4
            + [
                whole((1, length)),
                pl.BlockSpec((rows, width), lambda i, order: (jnp.minimum(i, last), 0)),
            ],
            scratch_shapes=[pltpu.VMEM((HEAD_DIM, length), BF16)],
        ),
        compiler_params=pltpu.CompilerParams(vmem_limit_bytes=52 * 2**20),
        name="attend",
    )(order, *pieces, weight, cos_table, sin_table, first_place)


def attend_back_kernel(
    block, rows, order_ref, q_ref, k_ref, v_ref, do_ref, lse_ref, start_ref, cos_ref, sin_ref, out_ref, kt_ref, dq_ref, dk_ref, dv_ref
):
    length = q_ref.shape[0]
    step = pl.program_id(0)
    scale = HEAD_DIM ** (-0.5)
    factor = scale * LOG2E
    count = length // block

    @pl.when(step == 0)
    def _():
        kt_ref[...] = k_ref[...].astype(F32).T.astype(BF16)
        dk_ref[...] = jnp.zeros_like(dk_ref)
        dv_ref[...] = jnp.zeros_like(dv_ref)

    for i in range(count):

        @pl.when(step == i)
        def _(i=i):
            low, high = i * block, (i + 1) * block
            query, grad = q_ref[low:high, :], do_ref[low:high, :]
            raw = dot_nt(k_ref[:high, :], query)
            keys = lax.broadcasted_iota(jnp.int32, raw.shape, 0)
            queries = low + lax.broadcasted_iota(jnp.int32, raw.shape, 1)
            allowed = (keys <= queries) & (keys >= start_ref[:, low:high])
            raw = jnp.where(allowed, raw * factor - lse_ref[:, low:high], NEG)
            probs = jnp.exp2(raw)
            probs_grad = dot_nt(v_ref[:high, :], grad)
            inner = jnp.sum(probs_grad * probs, axis=0, keepdims=True)
            score_grad = (probs * (probs_grad - inner)).astype(BF16)
            dv_ref[:high, :] += dot(probs.astype(BF16), grad)
            dk_ref[:high, :] += dot(score_grad, query)
            dq_ref[low:high, :] = dot(kt_ref[:, :high], score_grad).T

    @pl.when(step == count - 1)
    def _():
        for n in range(length // rows):
            at = pl.ds(pl.multiple_of(order_ref[n] * rows, rows), rows)
            to = slice(n * rows, (n + 1) * rows)
            cos_table, sin_table = cos_ref[at, :], -sin_ref[at, :]
            out_ref[to, :HEAD_DIM] = turn(dq_ref[at, :] * scale, cos_table, sin_table).astype(BF16)
            out_ref[to, HEAD_DIM : 2 * HEAD_DIM] = turn(
                dk_ref[at, :] * scale, cos_table, sin_table
            ).astype(BF16)
            out_ref[to, 2 * HEAD_DIM :] = dv_ref[at, :].astype(BF16)


def attend_back(query, key, value, grad, lse, first_place, cos_table, sin_table, order):
    length = query.shape[0]
    block = min(256, length)
    whole = lambda shape: pl.BlockSpec(shape, lambda i, order: (0, 0))
    head = whole((length, HEAD_DIM))
    return pl.pallas_call(
        functools.partial(attend_back_kernel, block, length // order.shape[0]),
        out_shape=jax.ShapeDtypeStruct((length, 3 * HEAD_DIM), BF16),
        grid_spec=pltpu.PrefetchScalarGridSpec(
            num_scalar_prefetch=1,
            grid=(length // block,),
            in_specs=[head] * 4 + [whole((1, length))] * 2 + [head] * 2,
            out_specs=whole((length, 3 * HEAD_DIM)),
            scratch_shapes=[pltpu.VMEM((HEAD_DIM, length), BF16)]
            + [pltpu.VMEM((length, HEAD_DIM), F32)] * 3,
        ),
        compiler_params=pltpu.CompilerParams(vmem_limit_bytes=48 * 2**20),
        name="attend_back",
    )(order, query, key, value, grad, lse, first_place, cos_table, sin_table)


def dp_gather(value):
    count = lax.axis_size("dp")
    if count == 1:
        return value[None]
    here = lax.axis_index("dp")
    parts = [value] + [
        lax.ppermute(value, "dp", [(i, (i - step) % count) for i in range(count)])
        for step in range(1, count)
    ]
    if count == 2:
        first = here == 0
        return jnp.stack(
            [jnp.where(first, parts[0], parts[1]), jnp.where(first, parts[1], parts[0])]
        )
    whole = jnp.zeros((count,) + value.shape, value.dtype)
    for step, part in enumerate(parts):
        whole = lax.dynamic_update_index_in_dim(whole, part, (here + step) % count, 0)
    return whole


def dp_scatter(value):
    count = lax.axis_size("dp")
    here = lax.axis_index("dp")
    total = lax.dynamic_index_in_dim(value, here, 0, keepdims=False)
    for step in range(1, count):
        block = lax.dynamic_index_in_dim(value, (here + step) % count, 0, keepdims=False)
        got = lax.ppermute(
            block.astype(BF16), "dp", [(i, (i + step) % count) for i in range(count)]
        )
        total = total + got.astype(F32)
    return total


def ring_order():
    pairs = lax.axis_size("expert") // 2
    return list(range(0, pairs, 2)) + list(range(pairs - 1, 0, -2))


def ring_shift(value, step):
    order = ring_order()
    pairs = len(order)
    perm = [
        (order[q] * 2 + c, order[(q + step) % pairs] * 2 + c) for q in range(pairs) for c in range(2)
    ]
    return lax.ppermute(value, "expert", perm)


def core_swap(value):
    count = lax.axis_size("expert")
    return lax.ppermute(value, "expert", [(i, i ^ 1) for i in range(count)])


def ring_offsets():
    half = lax.axis_size("expert") // 4
    return [0] + [o for step in range(1, half) for o in (step, -step)] + [half]


def ring_blocks():
    order = ring_order()
    pairs = len(order)
    table = [[0] * (2 * pairs) for _ in range(2 * pairs)]
    for q in range(pairs):
        for c in range(2):
            for j, offset in enumerate(ring_offsets()):
                for other in range(2):
                    table[order[q] * 2 + c][2 * j + other] = (
                        order[(q - offset) % pairs] * 2 + (c ^ other)
                    )
    return lax.dynamic_index_in_dim(
        jnp.asarray(table, jnp.int32), lax.axis_index("expert"), 0, keepdims=False
    )


def tied(value, *tokens):
    firsts = [lax.slice(t, (0,) * t.ndim, (1,) * t.ndim).reshape(()) for t in tokens]
    token = sum(t.astype(F32) for t in firsts) * 0.0
    return (value.astype(F32) * (1.0 + token)).astype(value.dtype)


def ring_gather(value, gates=None):
    gates = gates or {}
    half_rows = value.shape[0] // 2
    half = lax.axis_size("expert") // 4
    blocks = {}

    def keep(parts, offset):
        blocks[offset] = (parts, [core_swap(part) for part in parts])

    keep([value], 0)
    ahead = back = value
    for step in range(1, half):
        if step in gates:
            token = gates[step](blocks)
            ahead, back = tied(ahead, *token), tied(back, *token)
        ahead, back = ring_shift(ahead, 1), ring_shift(back, -1)
        keep([ahead], step)
        keep([back], -step)
    if half in gates:
        token = gates[half](blocks)
        ahead, back = tied(ahead, *token), tied(back, *token)
    last = [ring_shift(ahead[:half_rows], 1), ring_shift(back[half_rows:], -1)]
    keep(last, half)
    return [parts for offset in ring_offsets() for parts in blocks[offset]]


def flatten(blocks):
    pieces = [piece for parts in blocks for piece in parts]
    sources, n = [], 0
    for parts in blocks:
        sources.append(tuple(range(n, n + len(parts))))
        n += len(parts)
    return pieces, tuple(sources)


def ring_scatter(block, gates=None, marks=None):
    gates = gates or {}
    half = lax.axis_size("expert") // 4
    offsets = ring_offsets()
    spare = {}

    def mine(offset):
        if offset not in spare:
            j = offsets.index(offset)
            spare[offset] = block(2 * j).astype(F32) + core_swap(block(2 * j + 1)).astype(F32)
        return spare[offset]

    far = mine(half).astype(BF16)
    half_rows = far.shape[0] // 2
    ahead = ring_shift(far[:half_rows], 1)
    back = ring_shift(far[half_rows:], -1)
    if marks is not None:
        marks.extend([ahead, back])
    for step in range(half - 1, 0, -1):
        onward, homeward = mine(-step), mine(step)
        if step == half - 1:
            onward = jnp.concatenate(
                [onward[:half_rows] + ahead.astype(F32), onward[half_rows:]], axis=0
            )
            homeward = jnp.concatenate(
                [homeward[:half_rows], homeward[half_rows:] + back.astype(F32)], axis=0
            )
        else:
            onward = onward + ahead.astype(F32)
            homeward = homeward + back.astype(F32)
        if half - step in gates:
            onward, homeward = tied(onward, *gates[half - step]), tied(homeward, *gates[half - step])
        ahead = ring_shift(onward.astype(BF16), 1)
        back = ring_shift(homeward.astype(BF16), -1)
    return mine(0) + ahead.astype(F32) + back.astype(F32)


def chosen(pos_ref, base, window):
    count = pos_ref.shape[-1]
    row = base + lax.broadcasted_iota(jnp.int32, (window, count), 0)
    return row == pos_ref[0]


def dispatch_kernel(sources, widths, window, base_ref, order_ref, pos_ref, gate_ref, *refs):
    outs = refs[-len(widths) - 2 :]
    pieces, blocks, rows_ref, weights_ref = refs[: -len(outs)], outs[:-2], outs[-2], outs[-1]
    step = pl.program_id(0)

    @pl.when(step == 0)
    def _():
        rows_ref[...] = jnp.zeros_like(rows_ref)
        weights_ref[...] = jnp.zeros_like(weights_ref)

    for n, parts in enumerate(sources):

        @pl.when(step == n)
        def _(parts=parts):
            low = 0
            for part in parts:
                size = pieces[part].shape[0]
                left = 0
                for block, wide in zip(blocks, widths):
                    block[low : low + size, :] = pieces[part][:, left : left + wide]
                    left += wide
                low += size

    base = pl.multiple_of(base_ref[step], 16)
    pick = chosen(pos_ref, base, window)
    at = pl.ds(base, window)
    found = dot(pick.astype(F32).astype(BF16), (blocks or pieces)[0][...])
    rows_ref[at, :] = (rows_ref[at, :].astype(F32) + found).astype(BF16)
    weights_ref[at, :] += jnp.sum(jnp.where(pick, gate_ref[0], 0.0), axis=1, keepdims=True)


def dispatch(blocks, widths, packing, order, gates):
    base, pos, _, window, packed = packing
    count, _, rows = pos.shape
    if isinstance(blocks, list):
        pieces, sources = flatten(blocks)
        piece_specs = [pl.BlockSpec(piece.shape, lambda i, base, order: (0, 0)) for piece in pieces]
    else:
        pieces, sources, widths = [blocks], (), []
        piece_specs = [pl.BlockSpec((rows, blocks.shape[1]), lambda i, base, order: (order[i], 0))]
    width = (widths or [pieces[0].shape[1]])[0]
    return pl.pallas_call(
        functools.partial(dispatch_kernel, sources, tuple(widths), window),
        out_shape=[jax.ShapeDtypeStruct((rows * count, wide), BF16) for wide in widths]
        + [
            jax.ShapeDtypeStruct((packed, width), BF16),
            jax.ShapeDtypeStruct((packed, 1), F32),
        ],
        grid_spec=pltpu.PrefetchScalarGridSpec(
            num_scalar_prefetch=2,
            grid=(count,),
            in_specs=[
                pl.BlockSpec((1, 1, rows), lambda i, base, order: (i, 0, 0)),
                pl.BlockSpec((1, 1, rows), lambda i, base, order: (order[i], 0, 0)),
            ]
            + piece_specs,
            out_specs=[
                pl.BlockSpec((rows, wide), lambda i, base, order: (order[i], 0)) for wide in widths
            ]
            + [
                pl.BlockSpec((packed, width), lambda i, base, order: (0, 0)),
                pl.BlockSpec((packed, 1), lambda i, base, order: (0, 0)),
            ],
        ),
        compiler_params=pltpu.CompilerParams(vmem_limit_bytes=52 * 2**20),
        name="dispatch",
    )(base, order, pos, gates, *pieces)


def expert_kernel(ups, total_ref, starts_ref, x_ref, g_ref, gate_ref, *refs):
    parts, refs = refs[:-9], refs[-9:]
    wy_ref, dn_ref, ea_ref, dy_ref, db_ref, dg_ref, up_ref, down_ref, sems = refs
    step = pl.program_id(0)
    rows, hidden = ea_ref.shape
    some = step * rows < total_ref[0]

    @pl.when(step == 0)
    def _():
        copies = []
        for n, part in enumerate(parts):
            at = pl.ds(pl.multiple_of(starts_ref[n], 16), part.shape[0])
            whole = up_ref if n < ups else down_ref
            copies.append(pltpu.make_async_copy(part, whole.at[at, :], sems.at[n]))
        for copy in copies:
            copy.start()
        for copy in copies:
            copy.wait()

    @pl.when(some)
    def _():
        pre = dot(x_ref[...], up_ref[...])
        gate_part, up_part = pre[:, :hidden], pre[:, hidden:]
        sigmoid_gate = 1.0 / (1.0 + jnp.exp(-gate_part))
        silu = gate_part * sigmoid_gate
        act = (silu * up_part).astype(BF16)
        ea_ref[...] = act
        result = dot(act, down_ref[...]).astype(BF16).astype(F32)
        grad = g_ref[...].astype(F32)
        gate = gate_ref[...]
        dg_ref[...] = jnp.sum(grad * result, axis=1, keepdims=True)
        wy_ref[...] = (gate * result).astype(BF16)
        out_grad = (gate * grad).astype(BF16)
        dy_ref[...] = out_grad
        act_grad = dot_nt(out_grad, down_ref[...])
        db_ref[:, :hidden] = (
            act_grad * up_part * sigmoid_gate * (1.0 + gate_part * (1.0 - sigmoid_gate))
        ).astype(BF16)
        db_ref[:, hidden:] = (act_grad * silu).astype(BF16)
        dn_ref[...] = dot_nt(db_ref[...], up_ref[...]).astype(BF16)

    @pl.when(jnp.logical_not(some))
    def _():
        for ref in (wy_ref, dn_ref, ea_ref, dy_ref, db_ref, dg_ref):
            ref[...] = jnp.zeros_like(ref)


def expert(total, rows, grads, gates, ups, downs):
    packed, width = rows.shape
    hidden = sum(part.shape[0] for part, _ in downs)
    tile = 256
    parts = [part for part, _ in ups + downs]
    starts = jnp.stack([start for _, start in ups + downs]).astype(jnp.int32)
    spec = lambda wide: pl.BlockSpec((tile, wide), lambda i, total, starts: (i, 0))
    widths = (width, width, hidden, width, 2 * hidden)
    return pl.pallas_call(
        functools.partial(expert_kernel, len(ups)),
        out_shape=[jax.ShapeDtypeStruct((packed, wide), BF16) for wide in widths]
        + [jax.ShapeDtypeStruct((packed, 1), F32)],
        grid_spec=pltpu.PrefetchScalarGridSpec(
            num_scalar_prefetch=2,
            grid=(packed // tile,),
            in_specs=[spec(width), spec(width), spec(1)]
            + [pl.BlockSpec(memory_space=pl.ANY)] * len(parts),
            out_specs=[spec(wide) for wide in widths] + [spec(1)],
            scratch_shapes=[
                pltpu.VMEM((width, 2 * hidden), BF16),
                pltpu.VMEM((hidden, width), BF16),
                pltpu.SemaphoreType.DMA((len(parts),)),
            ],
        ),
        compiler_params=pltpu.CompilerParams(vmem_limit_bytes=58 * 2**20),
        name="expert",
    )(total, starts, rows, grads, gates, *parts)


def combine_kernel(turned, window, extra, base_ref, order_ref, to_ref, me_ref, pos_ref, rows_ref, dg_ref, act_ref, weight_ref, out_ref):
    mul = dot_nt if turned else dot
    base = pl.multiple_of(base_ref[pl.program_id(0)], 16)
    pick = chosen(pos_ref, base, window)
    at = pl.ds(base, window)
    width = rows_ref.shape[1]
    out_ref[:, :width] = (
        dot_tn(pick.astype(F32).astype(BF16), rows_ref[at, :]) + mul(act_ref[...], weight_ref[...])
    ).astype(BF16)
    if extra:
        count = pick.shape[1]
        line = jnp.sum(jnp.where(pick, dg_ref[at, :], 0.0), axis=0, keepdims=True)
        row = lax.broadcasted_iota(jnp.int32, (count, count), 0)
        lane = lax.broadcasted_iota(jnp.int32, (count, count), 1)
        column = jnp.sum(jnp.where(row == lane, line, 0.0), axis=1, keepdims=True)
        high = column.astype(BF16).astype(F32)
        lane = lax.broadcasted_iota(jnp.int32, (count, extra), 1)
        out_ref[:, width:] = jnp.where(
            lane == me_ref[0], high, jnp.where(lane == me_ref[0] + extra // 2, column - high, 0.0)
        ).astype(BF16)


def combine(packing, order, to, me, rows, dg, act, weight, turned, extra):
    base, pos, _, window, packed = packing
    blocks, _, count = pos.shape
    width = rows.shape[-1]
    whole = lambda ref: pl.BlockSpec(ref.shape, lambda i, *_: (0, 0))
    return pl.pallas_call(
        functools.partial(combine_kernel, turned, window, extra),
        out_shape=jax.ShapeDtypeStruct((blocks * count, width + extra), BF16),
        grid_spec=pltpu.PrefetchScalarGridSpec(
            num_scalar_prefetch=4,
            grid=(blocks,),
            in_specs=[
                pl.BlockSpec((1, 1, count), lambda i, *_: (i, 0, 0)),
                whole(rows),
                whole(dg),
                pl.BlockSpec((count, act.shape[1]), lambda i, base, order, to, me: (order[i], 0)),
                whole(weight),
            ],
            out_specs=pl.BlockSpec(
                (count, width + extra), lambda i, base, order, to, me: (to[i], 0)
            ),
        ),
        compiler_params=pltpu.CompilerParams(vmem_limit_bytes=40 * 2**20),
        name="combine",
    )(base, order, to, me.reshape(1), pos, rows, dg, act, weight)


def gather_all(value):
    return lax.all_gather(value, "expert", axis=0, tiled=True)


def swap(value):
    return lax.all_to_all(value, "expert", split_axis=0, concat_axis=0, tiled=True)


def per_device(
    tokens,
    cotangent,
    segment_ids,
    routes,
    attn_in,
    attn_out,
    gain_attn,
    shared_in,
    shared_out,
    router,
    gain_ffn,
    expert_in,
    expert_out,
):
    n_dp, n_e = lax.axis_size("dp"), lax.axis_size("expert")
    me = lax.axis_index("expert")
    count, width = tokens.shape
    segments = segment_ids[0]
    length = segments.shape[0]
    rows = attn_in.shape[0]
    capacity = min(count, 3 * TOP * count // (2 * n_e))
    shared_rows = shared_out.shape[0]
    shared_width = shared_rows * n_dp
    expert_width = expert_out.shape[1] * n_dp

    order = ring_blocks()
    steady = jnp.arange(n_e, dtype=jnp.int32)
    hidden_in = tokens.astype(F32)
    inverse_one = lax.rsqrt(jnp.mean(hidden_in * hidden_in, axis=-1, keepdims=True) + EPS)
    normed_one = hidden_in * inverse_one
    gain_rows = gain_attn.astype(F32)[:, None]
    head_w = []

    def head_sent(blocks):
        own = (attn_in.astype(F32) * tied(gain_rows, blocks[0][1][0])).astype(BF16)
        own = own.reshape(rows, 3, n_e, HEAD_DIM).transpose(2, 0, 1, 3)
        head_w.append(swap(own.reshape(n_e, rows, 3 * HEAD_DIM)))
        return head_w[0]

    def head_whole(blocks):
        head_w.append(dp_gather(head_w[0]).reshape(width, 3 * HEAD_DIM))
        return head_w[1]

    here = lax.axis_index("dp")

    def pieces_of(size, chunks):
        while size % (16 * chunks):
            chunks -= 1
        return chunks

    def part_of(shard, chunks, j, *after):
        size = shard.shape[0] // chunks
        block = shard[j * size : (j + 1) * size]
        block = tied(block, *after) if after else block
        return [
            (
                lax.ppermute(block, "dp", [(i, (i - step) % n_dp) for i in range(n_dp)]),
                (here + step) % n_dp * shard.shape[0] + j * size,
            )
            for step in range(1, n_dp)
        ]

    first = lambda parts: [part for part, _ in parts]
    up_chunks = pieces_of(expert_in.shape[1], max(1, min(4, expert_in.shape[1] // 256)))
    down_chunks = pieces_of(expert_out.shape[1], 2)
    ups = [(expert_in[0], here * expert_in.shape[1])]
    downs = [(expert_out[0], here * expert_out.shape[1])]
    ups += part_of(expert_in[0], up_chunks, 0)
    up_first = first(ups[1:])

    small = jnp.concatenate([router, gain_ffn[:, None]], axis=1)
    small = dp_gather(small).reshape(-1, n_e + 1)
    extra_rows = 32
    extra = jnp.concatenate([small.T, routes.T.astype(BF16)], axis=0)
    extra = jnp.pad(extra, ((0, extra_rows - extra.shape[0]), (0, 0)))
    extra = jnp.broadcast_to(extra, (n_e,) + extra.shape)
    cos_table, sin_table, first_place = rope_tables(segments)
    share_w = shared_in.reshape(rows, 2, n_dp, n_e, shared_rows).transpose(3, 0, 1, 2, 4)
    share_w = share_w.reshape(n_e, rows, 2 * shared_width)

    half = n_e // 4
    norm_blocks = ring_gather(
        normed_one.astype(BF16),
        {
            half - 1: lambda blocks: [head_sent(blocks)],
            half: lambda blocks: [head_whole(blocks), cos_table, sin_table, extra, share_w],
        },
    )
    head_sent_w, head_w = head_w

    second = part_of(expert_in[0], up_chunks, 1, head_w) if up_chunks > 1 else []
    ups += second

    head_out, query, key, value, lse, norm_all = attend(
        norm_blocks, order, head_w, cos_table, sin_table, first_place
    )
    mixed = jnp.concatenate([head_out.reshape(n_e, count, HEAD_DIM), extra], axis=1)
    share_w = swap(tied(share_w, head_sent_w))
    mixed = swap(tied(mixed, share_w, *up_first))
    third = part_of(expert_in[0], up_chunks, 2, lse) if up_chunks > 2 else []
    fourth = part_of(expert_in[0], up_chunks, 3, lse) if up_chunks > 3 else []
    ups += third + fourth
    downs += part_of(expert_out[0], down_chunks, 0, mixed)
    if down_chunks > 1:
        downs += part_of(expert_out[0], down_chunks, 1, mixed)
    small = mixed[:, count:]
    mixed = mixed[:, :count].transpose(1, 0, 2).reshape(count, n_dp, n_e, rows)
    mixed = mixed.transpose(0, 2, 1, 3).reshape(count, width)
    proj_all = gather_all(dp_gather(attn_out).reshape(n_dp * rows, width))
    routes_all = small[:, n_e + 1 : n_e + 1 + TOP].astype(F32)
    small = small[:, : n_e + 1].reshape(n_e, n_e + 1, n_dp, rows).transpose(1, 2, 0, 3)
    small = small.reshape(n_e + 1, width)
    router_full = small[:n_e]
    gain_second = small[n_e].astype(F32)
    cot_all = gather_all(cotangent)

    share_sent = share_w
    share_w = dp_gather(share_w).reshape(width, 2 * shared_width)
    share_out = dp_gather(shared_out).reshape(shared_width, width)
    resid = hidden_in + dot(mixed, proj_all)
    if second:
        resid = tied(resid, *first(second))

    inverse_two = lax.rsqrt(jnp.mean(resid * resid, axis=-1, keepdims=True) + EPS)
    normed_two = resid * inverse_two
    norm_two = (normed_two * gain_second).astype(BF16)
    logits = dot_nt(norm_two, router_full)
    picked = jnp.any(routes[:, :, None] == jnp.arange(n_e)[None, None, :], axis=1)
    chosen = jnp.where(picked, logits, NEG)
    chosen = jnp.where(picked, jnp.exp(chosen - jnp.max(chosen, axis=-1, keepdims=True)), 0.0)
    gates = chosen / jnp.sum(chosen, axis=-1, keepdims=True)
    gate_high = gates.astype(BF16)
    gate_low = (gates - gate_high.astype(F32)).astype(BF16)
    blank = jnp.zeros((count, 128 - 2 * n_e), BF16)
    payload = jnp.concatenate([norm_two, gate_high, gate_low, blank], axis=1)
    norm_blocks = ring_gather(
        payload,
        {
            half - 1: lambda blocks: [share_sent] + first(third),
            half: lambda blocks: [share_sent] + first(fourth),
        },
    )

    named = jnp.any(routes_all == me.astype(F32), axis=1)
    named = jnp.take(named, order, axis=0)
    ranking = jnp.cumsum(named.astype(jnp.int32), axis=1)
    ends = jnp.cumsum(ranking[:, -1])
    begins = ends - ranking[:, -1]
    pos = jnp.where(named, begins[:, None] + ranking - 1, -1)[:, None, :]
    window = -(-(capacity + 15) // 16) * 16
    packed = -(-(n_e * capacity + 32) // 256) * 256
    packing = (begins // 16 * 16, pos, ends[-1:], window, packed)
    norm_two_all, payload, arrived, _ = dispatch(
        norm_blocks, [width, 128], packing, order, jnp.zeros((n_e, 1, count), F32)
    )
    mine = jnp.arange(n_e) == me
    gate_all = payload[:, : 2 * n_e].astype(F32).reshape(length, 2, n_e)
    gate_all = jnp.sum(jnp.where(mine, gate_all, 0.0), axis=(1, 2)).reshape(n_e, 1, count)
    cot_rows, gate_rows = dispatch(cot_all, None, packing, order, gate_all)
    weighted, row_grad, expert_act, route_grad, pre_grad, gate_grad = expert(
        packing[2],
        arrived,
        cot_rows,
        gate_rows,
        ups,
        downs,
    )

    shared_pre = dot(norm_two_all, share_w)
    shared_act = (
        jax.nn.silu(shared_pre[:, :shared_width]) * shared_pre[:, shared_width:]
    ).astype(BF16)
    shared_act_grad = dot_nt(cot_all, share_out)
    shared_pre_grad = silu_back(
        shared_act_grad, shared_pre[:, :shared_width], shared_pre[:, shared_width:]
    ).astype(BF16)
    norm_two_part = combine(
        packing, order, steady, me, row_grad, gate_grad, shared_pre_grad, share_w, True, 128
    )
    norm_two_grad = ring_scatter(
        lambda n: norm_two_part[n * count : (n + 1) * count]
    )
    gate_grad = norm_two_grad[:, width : width + n_e] + norm_two_grad[:, width + 64 : width + 64 + n_e]
    norm_two_grad = norm_two_grad[:, :width]
    out_part = combine(
        packing, order, order, me, weighted, gate_rows, shared_act, share_out, False, 0
    )
    routed_out = lax.psum_scatter(out_part, "expert", scatter_dimension=0, tiled=True)

    logit_grad = gates * (gate_grad - jnp.sum(gates * gate_grad, axis=-1, keepdims=True))
    router_grad = jnp.dot(
        logit_grad.T, norm_two.astype(F32), precision=HIGHEST, preferred_element_type=F32
    )
    norm_two_grad = norm_two_grad + jnp.dot(
        logit_grad, router_full.astype(F32), precision=HIGHEST, preferred_element_type=F32
    )
    gain_two_grad = jnp.sum(norm_two_grad * normed_two, axis=0)
    upstream = cotangent.astype(F32)
    scaled_two = norm_two_grad * gain_second
    resid_grad = upstream + inverse_two * (
        scaled_two - normed_two * jnp.mean(scaled_two * normed_two, axis=-1, keepdims=True)
    )
    small_grad = jnp.concatenate([router_grad, gain_two_grad[None]], axis=0)

    branch_cot = resid_grad.astype(BF16)
    proj_grad = dot_tn(mixed, branch_cot).astype(BF16)
    mixed_grad = dot_nt(branch_cot, proj_all).astype(BF16)
    after = mixed_grad
    def shard_grads(left, right, chunks):
        size = left.shape[1] // n_dp
        part = size // chunks
        cut = lambda start, wide: tied(lax.dynamic_slice_in_dim(left, start, wide, 1), after)
        got = [
            [
                lax.ppermute(
                    dot_tn(cut((here + step) % n_dp * size + j * part, part), right).astype(BF16),
                    "dp",
                    [(i, (i + step) % n_dp) for i in range(n_dp)],
                )
                for step in range(1, n_dp)
            ]
            for j in range(chunks)
        ]
        return dot_tn(cut(here * size, size), right), got

    def shard_sum(own, got, tokens):
        part = own.shape[0] // len(got)
        own = own[None]
        for j, (parts, token) in enumerate(zip(got, tokens)):
            block = sum(tied(p.astype(F32), token) for p in parts)[None]
            block = own[:, j * part : (j + 1) * part] + block
            own = lax.dynamic_update_slice_in_dim(own, block, j * part, 1)
        return own

    down_own, down_got = shard_grads(expert_act, route_grad, 2)
    up_own, up_got = shard_grads(arrived, pre_grad, up_chunks)

    share_out_grad = dp_scatter(dot_tn(tied(shared_act, after), cot_all).reshape(n_dp, shared_rows, width))
    share_in_grad = dot_tn(norm_two_all, tied(shared_pre_grad, after))
    share_in_grad = dp_scatter(share_in_grad.reshape(n_dp, n_e, rows, 2 * shared_width))
    share_in_grad = swap(share_in_grad.astype(BF16)).astype(F32)
    share_in_grad = (
        share_in_grad.reshape(n_e, rows, 2, n_dp, shared_rows)
        .transpose(1, 2, 3, 0, 4)
        .reshape(rows, -1)
    )

    mixed_grad = mixed_grad.reshape(count, n_e, n_dp, rows).transpose(0, 2, 1, 3)
    mixed_grad = swap(mixed_grad.reshape(count, n_e, HEAD_DIM).transpose(1, 0, 2))
    mixed_grad = mixed_grad.reshape(length, HEAD_DIM)
    proj_grad = lax.psum_scatter(proj_grad, "expert", scatter_dimension=0, tiled=True)
    attn_out_grad = dp_scatter(proj_grad.astype(F32).reshape(n_dp, rows, width))
    qkv_grad = attend_back(
        query, key, value, mixed_grad, lse, first_place, cos_table, sin_table, order
    )
    small_grad = tied(small_grad, qkv_grad).reshape(n_e + 1, n_dp * n_e, rows).transpose(1, 0, 2)
    small_grad = lax.all_to_all(
        small_grad, ("dp", "expert"), split_axis=0, concat_axis=0, tiled=True
    )
    small_grad = jnp.sum(small_grad, axis=0)
    norm_one_part = dot_nt(qkv_grad, head_w).astype(BF16)
    scaled_one = ring_scatter(
        lambda n: norm_one_part[n * count : (n + 1) * count],
        {half - 2: down_got[0], half - 1: down_got[1]},
    )
    expert_out_grad = shard_sum(down_own, down_got, [qkv_grad, scaled_one])
    expert_in_grad = shard_sum(up_own, up_got, ([qkv_grad] + [scaled_one] * 3)[: len(up_got)])
    input_grad = resid_grad + inverse_one * (
        scaled_one - normed_one * jnp.mean(scaled_one * normed_one, axis=-1, keepdims=True)
    )
    head_grad = dot_tn(norm_all, qkv_grad).reshape(n_dp, n_e, rows, 3 * HEAD_DIM)
    head_grad = swap(dp_scatter(head_grad).astype(BF16)).astype(F32)
    head_grad = (
        head_grad.reshape(n_e, rows, 3, HEAD_DIM).transpose(1, 2, 0, 3).reshape(rows, 3 * width)
    )
    gain_attn_grad = jnp.sum(head_grad * attn_in.astype(F32), axis=1)
    attn_in_grad = head_grad * gain_rows
    return (
        (resid + routed_out.astype(F32)).astype(BF16),
        input_grad.astype(BF16),
        attn_in_grad,
        attn_out_grad,
        gain_attn_grad,
        share_in_grad,
        share_out_grad,
        small_grad[:n_e].T,
        small_grad[n_e],
        expert_in_grad,
        expert_out_grad,
    )


def solution(mesh):
    return jax.shard_map(
        per_device,
        mesh=mesh,
        in_specs=(
            P(("dp", "expert"), None),
            P(("dp", "expert"), None),
            P("dp", None),
            P(("dp", "expert"), None),
            P(("dp", "expert"), None),
            P(("dp", "expert"), None),
            P(("dp", "expert")),
            P(("dp", "expert"), None),
            P(("dp", "expert"), None),
            P(("dp", "expert"), None),
            P(("dp", "expert")),
            P("expert", "dp", None),
            P("expert", "dp", None),
        ),
        out_specs=(
            P(("dp", "expert"), None),
            P(("dp", "expert"), None),
            P(("dp", "expert"), None),
            P(("dp", "expert"), None),
            P(("dp", "expert")),
            P(("dp", "expert"), None),
            P(("dp", "expert"), None),
            P(("dp", "expert"), None),
            P(("dp", "expert")),
            P("expert", "dp", None),
            P("expert", "dp", None),
        ),
        check_vma=False,
    )
```

```python
import functools
import math

import jax
import jax.numpy as jnp
from jax import lax
from jax.experimental import pallas as pl
from jax.experimental.pallas import tpu as pltpu
from jax.sharding import PartitionSpec as P

HEADS = 16
HEAD_DIM = 128
TOP = 6


EPS = 1e-06
THETA = 10000.0
NEG = -1e30
HIGHEST = lax.Precision.HIGHEST
BF16 = jnp.bfloat16
F32 = jnp.float32
LOG2E = math.log2(math.e)


def rope_tables(segments):
    length = segments.shape[0]
    places = jnp.arange(length, dtype=jnp.int32)
    starts = jnp.concatenate([jnp.ones((1,), dtype=jnp.bool_), segments[1:] != segments[:-1]])
    first_place = lax.cummax(jnp.where(starts, places, 0), axis=0)
    offset = (places - first_place).astype(jnp.float32)
    half_dim = HEAD_DIM // 2
    freqs = jnp.exp(jnp.arange(half_dim, dtype=jnp.float32) * (-2.0 * math.log(THETA) / HEAD_DIM))
    angles = offset[:, None] * freqs[None, :]
    cos_table, sin_table = jnp.cos(angles), jnp.sin(angles)
    return (
        jnp.concatenate([cos_table, cos_table], axis=1),
        jnp.concatenate([-sin_table, sin_table], axis=1),
        first_place[None, :],
    )


def silu_back(grad_act, gate_part, up_part):
    sigmoid_gate = jax.nn.sigmoid(gate_part)
    gate_grad = grad_act * up_part * sigmoid_gate * (1.0 + gate_part * (1.0 - sigmoid_gate))
    up_grad = grad_act * gate_part * sigmoid_gate
    return jnp.concatenate([gate_grad, up_grad], axis=-1)


def dot(left, right):
    return jnp.dot(left, right, preferred_element_type=F32)


def dot_tn(left, right):
    return lax.dot_general(left, right, (((0,), (0,)), ((), ())), preferred_element_type=F32)


def dot_nt(left, right):
    return lax.dot_general(left, right, (((1,), (1,)), ((), ())), preferred_element_type=F32)


def turn(values, cos_table, sin_table):
    return values * cos_table + pltpu.roll(values, HEAD_DIM // 2, 1) * sin_table


def attend_kernel(sources, block, order_ref, *refs):
    pieces = refs[: sources[-1][-1] + 1]
    weight_ref, cos_ref, sin_ref, start_ref = refs[len(pieces) : len(pieces) + 4]
    o_ref, q_ref, k_ref, v_ref, lse_ref, rows_ref, vt_ref = refs[len(pieces) + 4 :]
    step = pl.program_id(0)
    length = q_ref.shape[0]
    factor = HEAD_DIM ** (-0.5) * LOG2E
    rows = rows_ref.shape[0]

    for n, parts in enumerate(sources):

        @pl.when(step == n)
        def _(parts=parts):
            low = 0
            for part in parts:
                size = pieces[part].shape[0]
                rows_ref[low : low + size, :] = pieces[part][...]
                low += size

    @pl.when(step < len(sources))
    def _():
        qkv = dot(rows_ref[...], weight_ref[...])
        at = pl.ds(pl.multiple_of(order_ref[step] * rows, rows), rows)
        cos_table, sin_table = cos_ref[at, :], sin_ref[at, :]
        q_ref[at, :] = turn(qkv[:, :HEAD_DIM], cos_table, sin_table).astype(BF16)
        k_ref[at, :] = turn(qkv[:, HEAD_DIM : 2 * HEAD_DIM], cos_table, sin_table).astype(BF16)
        value = qkv[:, 2 * HEAD_DIM :]
        v_ref[at, :] = value.astype(BF16)
        vt_ref[:, at] = value.T.astype(BF16)

    for i in range(length // block):

        @pl.when(step == len(sources) + i)
        def _(i=i):
            low, high = i * block, (i + 1) * block
            raw = dot_nt(k_ref[:high, :], q_ref[low:high, :])
            keys = lax.broadcasted_iota(jnp.int32, raw.shape, 0)
            queries = low + lax.broadcasted_iota(jnp.int32, raw.shape, 1)
            allowed = (keys <= queries) & (keys >= start_ref[:, low:high])
            raw = jnp.where(allowed, raw, NEG)
            top = jnp.max(raw, axis=0, keepdims=True)
            shifted = jnp.exp2((raw - top) * factor)
            total = jnp.sum(shifted, axis=0, keepdims=True)
            probs = (shifted * (1.0 / total)).astype(BF16)
            mixed = dot(vt_ref[:, :high], probs)
            o_ref[low:high, :] = mixed.T.astype(BF16)
            lse_ref[:, low:high] = top * factor + jnp.log2(total)


def attend(blocks, order, weight, cos_table, sin_table, first_place):
    pieces, sources = flatten(blocks)
    length = cos_table.shape[0]
    rows = length // len(sources)
    width = weight.shape[0]
    block = min(256, length)
    last = len(sources) - 1
    whole = lambda shape: pl.BlockSpec(shape, lambda i, order: (0, 0))
    head = jax.ShapeDtypeStruct((length, HEAD_DIM), BF16)
    return pl.pallas_call(
        functools.partial(attend_kernel, sources, block),
        out_shape=[head] * 4
        + [jax.ShapeDtypeStruct((1, length), F32), jax.ShapeDtypeStruct((length, width), BF16)],
        grid_spec=pltpu.PrefetchScalarGridSpec(
            num_scalar_prefetch=1,
            grid=(len(sources) + length // block,),
            in_specs=[whole(piece.shape) for piece in pieces]
            + [
                whole(weight.shape),
                whole((length, HEAD_DIM)),
                whole((length, HEAD_DIM)),
                whole((1, length)),
            ],
            out_specs=[whole((length, HEAD_DIM))] * 4
            + [
                whole((1, length)),
                pl.BlockSpec((rows, width), lambda i, order: (jnp.minimum(i, last), 0)),
            ],
            scratch_shapes=[pltpu.VMEM((HEAD_DIM, length), BF16)],
        ),
        compiler_params=pltpu.CompilerParams(vmem_limit_bytes=52 * 2**20),
        name="attend",
    )(order, *pieces, weight, cos_table, sin_table, first_place)


def attend_back_kernel(
    block, rows, order_ref, q_ref, k_ref, v_ref, do_ref, lse_ref, start_ref, cos_ref, sin_ref, out_ref, kt_ref, dq_ref, dk_ref, dv_ref
):
    length = q_ref.shape[0]
    step = pl.program_id(0)
    scale = HEAD_DIM ** (-0.5)
    factor = scale * LOG2E
    count = length // block

    @pl.when(step == 0)
    def _():
        kt_ref[...] = k_ref[...].astype(F32).T.astype(BF16)
        dk_ref[...] = jnp.zeros_like(dk_ref)
        dv_ref[...] = jnp.zeros_like(dv_ref)

    for i in range(count):

        @pl.when(step == i)
        def _(i=i):
            low, high = i * block, (i + 1) * block
            query, grad = q_ref[low:high, :], do_ref[low:high, :]
            raw = dot_nt(k_ref[:high, :], query)
            keys = lax.broadcasted_iota(jnp.int32, raw.shape, 0)
            queries = low + lax.broadcasted_iota(jnp.int32, raw.shape, 1)
            allowed = (keys <= queries) & (keys >= start_ref[:, low:high])
            raw = jnp.where(allowed, raw * factor - lse_ref[:, low:high], NEG)
            probs = jnp.exp2(raw)
            probs_grad = dot_nt(v_ref[:high, :], grad)
            inner = jnp.sum(probs_grad * probs, axis=0, keepdims=True)
            score_grad = (probs * (probs_grad - inner)).astype(BF16)
            dv_ref[:high, :] += dot(probs.astype(BF16), grad)
            dk_ref[:high, :] += dot(score_grad, query)
            dq_ref[low:high, :] = dot(kt_ref[:, :high], score_grad).T

    @pl.when(step == count - 1)
    def _():
        for n in range(length // rows):
            at = pl.ds(pl.multiple_of(order_ref[n] * rows, rows), rows)
            to = slice(n * rows, (n + 1) * rows)
            cos_table, sin_table = cos_ref[at, :], -sin_ref[at, :]
            out_ref[to, :HEAD_DIM] = turn(dq_ref[at, :] * scale, cos_table, sin_table).astype(BF16)
            out_ref[to, HEAD_DIM : 2 * HEAD_DIM] = turn(
                dk_ref[at, :] * scale, cos_table, sin_table
            ).astype(BF16)
            out_ref[to, 2 * HEAD_DIM :] = dv_ref[at, :].astype(BF16)


def attend_back(query, key, value, grad, lse, first_place, cos_table, sin_table, order):
    length = query.shape[0]
    block = min(256, length)
    whole = lambda shape: pl.BlockSpec(shape, lambda i, order: (0, 0))
    head = whole((length, HEAD_DIM))
    return pl.pallas_call(
        functools.partial(attend_back_kernel, block, length // order.shape[0]),
        out_shape=jax.ShapeDtypeStruct((length, 3 * HEAD_DIM), BF16),
        grid_spec=pltpu.PrefetchScalarGridSpec(
            num_scalar_prefetch=1,
            grid=(length // block,),
            in_specs=[head] * 4 + [whole((1, length))] * 2 + [head] * 2,
            out_specs=whole((length, 3 * HEAD_DIM)),
            scratch_shapes=[pltpu.VMEM((HEAD_DIM, length), BF16)]
            + [pltpu.VMEM((length, HEAD_DIM), F32)] * 3,
        ),
        compiler_params=pltpu.CompilerParams(vmem_limit_bytes=48 * 2**20),
        name="attend_back",
    )(order, query, key, value, grad, lse, first_place, cos_table, sin_table)


def dp_gather(value):
    count = lax.axis_size("dp")
    if count == 1:
        return value[None]
    here = lax.axis_index("dp")
    parts = [value] + [
        lax.ppermute(value, "dp", [(i, (i - step) % count) for i in range(count)])
        for step in range(1, count)
    ]
    if count == 2:
        first = here == 0
        return jnp.stack(
            [jnp.where(first, parts[0], parts[1]), jnp.where(first, parts[1], parts[0])]
        )
    whole = jnp.zeros((count,) + value.shape, value.dtype)
    for step, part in enumerate(parts):
        whole = lax.dynamic_update_index_in_dim(whole, part, (here + step) % count, 0)
    return whole


def dp_scatter(value):
    count = lax.axis_size("dp")
    here = lax.axis_index("dp")
    total = lax.dynamic_index_in_dim(value, here, 0, keepdims=False)
    for step in range(1, count):
        block = lax.dynamic_index_in_dim(value, (here + step) % count, 0, keepdims=False)
        got = lax.ppermute(
            block.astype(BF16), "dp", [(i, (i + step) % count) for i in range(count)]
        )
        total = total + got.astype(F32)
    return total


def ring_order():
    pairs = lax.axis_size("expert") // 2
    return list(range(0, pairs, 2)) + list(range(pairs - 1, 0, -2))


def ring_shift(value, step):
    order = ring_order()
    pairs = len(order)
    perm = [
        (order[q] * 2 + c, order[(q + step) % pairs] * 2 + c) for q in range(pairs) for c in range(2)
    ]
    return lax.ppermute(value, "expert", perm)


def core_swap(value):
    count = lax.axis_size("expert")
    return lax.ppermute(value, "expert", [(i, i ^ 1) for i in range(count)])


def ring_offsets():
    half = lax.axis_size("expert") // 4
    return [0] + [o for step in range(1, half) for o in (step, -step)] + [half]


def ring_blocks():
    order = ring_order()
    pairs = len(order)
    table = [[0] * (2 * pairs) for _ in range(2 * pairs)]
    for q in range(pairs):
        for c in range(2):
            for j, offset in enumerate(ring_offsets()):
                for other in range(2):
                    table[order[q] * 2 + c][2 * j + other] = (
                        order[(q - offset) % pairs] * 2 + (c ^ other)
                    )
    return lax.dynamic_index_in_dim(
        jnp.asarray(table, jnp.int32), lax.axis_index("expert"), 0, keepdims=False
    )


def tied(value, *tokens):
    firsts = [lax.slice(t, (0,) * t.ndim, (1,) * t.ndim).reshape(()) for t in tokens]
    token = sum(t.astype(F32) for t in firsts) * 0.0
    return (value.astype(F32) * (1.0 + token)).astype(value.dtype)


def ring_gather(value, gates=None):
    gates = gates or {}
    half_rows = value.shape[0] // 2
    half = lax.axis_size("expert") // 4
    blocks = {}

    def keep(parts, offset):
        blocks[offset] = (parts, [core_swap(part) for part in parts])

    keep([value], 0)
    ahead = back = value
    for step in range(1, half):
        if step in gates:
            token = gates[step](blocks)
            ahead, back = tied(ahead, *token), tied(back, *token)
        ahead, back = ring_shift(ahead, 1), ring_shift(back, -1)
        keep([ahead], step)
        keep([back], -step)
    if half in gates:
        token = gates[half](blocks)
        ahead, back = tied(ahead, *token), tied(back, *token)
    last = [ring_shift(ahead[:half_rows], 1), ring_shift(back[half_rows:], -1)]
    keep(last, half)
    return [parts for offset in ring_offsets() for parts in blocks[offset]]


def flatten(blocks):
    pieces = [piece for parts in blocks for piece in parts]
    sources, n = [], 0
    for parts in blocks:
        sources.append(tuple(range(n, n + len(parts))))
        n += len(parts)
    return pieces, tuple(sources)


def ring_scatter(block, gates=None, marks=None):
    gates = gates or {}
    half = lax.axis_size("expert") // 4
    offsets = ring_offsets()
    spare = {}

    def mine(offset):
        if offset not in spare:
            j = offsets.index(offset)
            spare[offset] = block(2 * j).astype(F32) + core_swap(block(2 * j + 1)).astype(F32)
        return spare[offset]

    far = mine(half).astype(BF16)
    half_rows = far.shape[0] // 2
    ahead = ring_shift(far[:half_rows], 1)
    back = ring_shift(far[half_rows:], -1)
    if marks is not None:
        marks.extend([ahead, back])
    for step in range(half - 1, 0, -1):
        onward, homeward = mine(-step), mine(step)
        if step == half - 1:
            onward = jnp.concatenate(
                [onward[:half_rows] + ahead.astype(F32), onward[half_rows:]], axis=0
            )
            homeward = jnp.concatenate(
                [homeward[:half_rows], homeward[half_rows:] + back.astype(F32)], axis=0
            )
        else:
            onward = onward + ahead.astype(F32)
            homeward = homeward + back.astype(F32)
        if half - step in gates:
            onward, homeward = tied(onward, *gates[half - step]), tied(homeward, *gates[half - step])
        ahead = ring_shift(onward.astype(BF16), 1)
        back = ring_shift(homeward.astype(BF16), -1)
    return mine(0) + ahead.astype(F32) + back.astype(F32)


def chosen(pos_ref, base, window):
    count = pos_ref.shape[-1]
    row = base + lax.broadcasted_iota(jnp.int32, (window, count), 0)
    return row == pos_ref[0]


def dispatch_kernel(sources, widths, window, base_ref, order_ref, pos_ref, gate_ref, *refs):
    outs = refs[-len(widths) - 2 :]
    pieces, blocks, rows_ref, weights_ref = refs[: -len(outs)], outs[:-2], outs[-2], outs[-1]
    step = pl.program_id(0)

    @pl.when(step == 0)
    def _():
        rows_ref[...] = jnp.zeros_like(rows_ref)
        weights_ref[...] = jnp.zeros_like(weights_ref)

    for n, parts in enumerate(sources):

        @pl.when(step == n)
        def _(parts=parts):
            low = 0
            for part in parts:
                size = pieces[part].shape[0]
                left = 0
                for block, wide in zip(blocks, widths):
                    block[low : low + size, :] = pieces[part][:, left : left + wide]
                    left += wide
                low += size

    base = pl.multiple_of(base_ref[step], 16)
    pick = chosen(pos_ref, base, window)
    at = pl.ds(base, window)
    found = dot(pick.astype(F32).astype(BF16), (blocks or pieces)[0][...])
    rows_ref[at, :] = (rows_ref[at, :].astype(F32) + found).astype(BF16)
    weights_ref[at, :] += jnp.sum(jnp.where(pick, gate_ref[0], 0.0), axis=1, keepdims=True)


def dispatch(blocks, widths, packing, order, gates):
    base, pos, _, window, packed = packing
    count, _, rows = pos.shape
    if isinstance(blocks, list):
        pieces, sources = flatten(blocks)
        piece_specs = [pl.BlockSpec(piece.shape, lambda i, base, order: (0, 0)) for piece in pieces]
    else:
        pieces, sources, widths = [blocks], (), []
        piece_specs = [pl.BlockSpec((rows, blocks.shape[1]), lambda i, base, order: (order[i], 0))]
    width = (widths or [pieces[0].shape[1]])[0]
    return pl.pallas_call(
        functools.partial(dispatch_kernel, sources, tuple(widths), window),
        out_shape=[jax.ShapeDtypeStruct((rows * count, wide), BF16) for wide in widths]
        + [
            jax.ShapeDtypeStruct((packed, width), BF16),
            jax.ShapeDtypeStruct((packed, 1), F32),
        ],
        grid_spec=pltpu.PrefetchScalarGridSpec(
            num_scalar_prefetch=2,
            grid=(count,),
            in_specs=[
                pl.BlockSpec((1, 1, rows), lambda i, base, order: (i, 0, 0)),
                pl.BlockSpec((1, 1, rows), lambda i, base, order: (order[i], 0, 0)),
            ]
            + piece_specs,
            out_specs=[
                pl.BlockSpec((rows, wide), lambda i, base, order: (order[i], 0)) for wide in widths
            ]
            + [
                pl.BlockSpec((packed, width), lambda i, base, order: (0, 0)),
                pl.BlockSpec((packed, 1), lambda i, base, order: (0, 0)),
            ],
        ),
        compiler_params=pltpu.CompilerParams(vmem_limit_bytes=52 * 2**20),
        name="dispatch",
    )(base, order, pos, gates, *pieces)


def expert_kernel(ups, total_ref, starts_ref, x_ref, g_ref, gate_ref, *refs):
    parts, refs = refs[:-9], refs[-9:]
    wy_ref, dn_ref, ea_ref, dy_ref, db_ref, dg_ref, up_ref, down_ref, sems = refs
    step = pl.program_id(0)
    rows, hidden = ea_ref.shape
    some = step * rows < total_ref[0]

    @pl.when(step == 0)
    def _():
        copies = []
        for n, part in enumerate(parts):
            at = pl.ds(pl.multiple_of(starts_ref[n], 16), part.shape[0])
            whole = up_ref if n < ups else down_ref
            copies.append(pltpu.make_async_copy(part, whole.at[at, :], sems.at[n]))
        for copy in copies:
            copy.start()
        for copy in copies:
            copy.wait()

    @pl.when(some)
    def _():
        pre = dot(x_ref[...], up_ref[...])
        gate_part, up_part = pre[:, :hidden], pre[:, hidden:]
        sigmoid_gate = 1.0 / (1.0 + jnp.exp(-gate_part))
        silu = gate_part * sigmoid_gate
        act = (silu * up_part).astype(BF16)
        ea_ref[...] = act
        result = dot(act, down_ref[...]).astype(BF16).astype(F32)
        grad = g_ref[...].astype(F32)
        gate = gate_ref[...]
        dg_ref[...] = jnp.sum(grad * result, axis=1, keepdims=True)
        wy_ref[...] = (gate * result).astype(BF16)
        out_grad = (gate * grad).astype(BF16)
        dy_ref[...] = out_grad
        act_grad = dot_nt(out_grad, down_ref[...])
        db_ref[:, :hidden] = (
            act_grad * up_part * sigmoid_gate * (1.0 + gate_part * (1.0 - sigmoid_gate))
        ).astype(BF16)
        db_ref[:, hidden:] = (act_grad * silu).astype(BF16)
        dn_ref[...] = dot_nt(db_ref[...], up_ref[...]).astype(BF16)

    @pl.when(jnp.logical_not(some))
    def _():
        for ref in (wy_ref, dn_ref, ea_ref, dy_ref, db_ref, dg_ref):
            ref[...] = jnp.zeros_like(ref)


def expert(total, rows, grads, gates, ups, downs):
    packed, width = rows.shape
    hidden = sum(part.shape[0] for part, _ in downs)
    tile = 256
    parts = [part for part, _ in ups + downs]
    starts = jnp.stack([start for _, start in ups + downs]).astype(jnp.int32)
    spec = lambda wide: pl.BlockSpec((tile, wide), lambda i, total, starts: (i, 0))
    widths = (width, width, hidden, width, 2 * hidden)
    return pl.pallas_call(
        functools.partial(expert_kernel, len(ups)),
        out_shape=[jax.ShapeDtypeStruct((packed, wide), BF16) for wide in widths]
        + [jax.ShapeDtypeStruct((packed, 1), F32)],
        grid_spec=pltpu.PrefetchScalarGridSpec(
            num_scalar_prefetch=2,
            grid=(packed // tile,),
            in_specs=[spec(width), spec(width), spec(1)]
            + [pl.BlockSpec(memory_space=pl.ANY)] * len(parts),
            out_specs=[spec(wide) for wide in widths] + [spec(1)],
            scratch_shapes=[
                pltpu.VMEM((width, 2 * hidden), BF16),
                pltpu.VMEM((hidden, width), BF16),
                pltpu.SemaphoreType.DMA((len(parts),)),
            ],
        ),
        compiler_params=pltpu.CompilerParams(vmem_limit_bytes=58 * 2**20),
        name="expert",
    )(total, starts, rows, grads, gates, *parts)


def combine_kernel(turned, window, extra, base_ref, order_ref, to_ref, me_ref, pos_ref, rows_ref, dg_ref, act_ref, weight_ref, out_ref):
    mul = dot_nt if turned else dot
    base = pl.multiple_of(base_ref[pl.program_id(0)], 16)
    pick = chosen(pos_ref, base, window)
    at = pl.ds(base, window)
    width = rows_ref.shape[1]
    out_ref[:, :width] = (
        dot_tn(pick.astype(F32).astype(BF16), rows_ref[at, :]) + mul(act_ref[...], weight_ref[...])
    ).astype(BF16)
    if extra:
        count = pick.shape[1]
        line = jnp.sum(jnp.where(pick, dg_ref[at, :], 0.0), axis=0, keepdims=True)
        row = lax.broadcasted_iota(jnp.int32, (count, count), 0)
        lane = lax.broadcasted_iota(jnp.int32, (count, count), 1)
        column = jnp.sum(jnp.where(row == lane, line, 0.0), axis=1, keepdims=True)
        high = column.astype(BF16).astype(F32)
        lane = lax.broadcasted_iota(jnp.int32, (count, extra), 1)
        out_ref[:, width:] = jnp.where(
            lane == me_ref[0], high, jnp.where(lane == me_ref[0] + extra // 2, column - high, 0.0)
        ).astype(BF16)


def combine(packing, order, to, me, rows, dg, act, weight, turned, extra):
    base, pos, _, window, packed = packing
    blocks, _, count = pos.shape
    width = rows.shape[-1]
    whole = lambda ref: pl.BlockSpec(ref.shape, lambda i, *_: (0, 0))
    return pl.pallas_call(
        functools.partial(combine_kernel, turned, window, extra),
        out_shape=jax.ShapeDtypeStruct((blocks * count, width + extra), BF16),
        grid_spec=pltpu.PrefetchScalarGridSpec(
            num_scalar_prefetch=4,
            grid=(blocks,),
            in_specs=[
                pl.BlockSpec((1, 1, count), lambda i, *_: (i, 0, 0)),
                whole(rows),
                whole(dg),
                pl.BlockSpec((count, act.shape[1]), lambda i, base, order, to, me: (order[i], 0)),
                whole(weight),
            ],
            out_specs=pl.BlockSpec(
                (count, width + extra), lambda i, base, order, to, me: (to[i], 0)
            ),
        ),
        compiler_params=pltpu.CompilerParams(vmem_limit_bytes=40 * 2**20),
        name="combine",
    )(base, order, to, me.reshape(1), pos, rows, dg, act, weight)


def gather_all(value):
    return lax.all_gather(value, "expert", axis=0, tiled=True)


def swap(value):
    return lax.all_to_all(value, "expert", split_axis=0, concat_axis=0, tiled=True)


def per_device(
    tokens,
    cotangent,
    segment_ids,
    routes,
    attn_in,
    attn_out,
    gain_attn,
    shared_in,
    shared_out,
    router,
    gain_ffn,
    expert_in,
    expert_out,
):
    n_dp, n_e = lax.axis_size("dp"), lax.axis_size("expert")
    me = lax.axis_index("expert")
    count, width = tokens.shape
    segments = segment_ids[0]
    length = segments.shape[0]
    rows = attn_in.shape[0]
    capacity = min(count, 3 * TOP * count // (2 * n_e))
    shared_rows = shared_out.shape[0]
    shared_width = shared_rows * n_dp
    expert_width = expert_out.shape[1] * n_dp

    order = ring_blocks()
    steady = jnp.arange(n_e, dtype=jnp.int32)
    hidden_in = tokens.astype(F32)
    inverse_one = lax.rsqrt(jnp.mean(hidden_in * hidden_in, axis=-1, keepdims=True) + EPS)
    normed_one = hidden_in * inverse_one
    gain_rows = gain_attn.astype(F32)[:, None]
    head_w = []

    def head_sent(blocks):
        own = (attn_in.astype(F32) * tied(gain_rows, blocks[0][1][0])).astype(BF16)
        own = own.reshape(rows, 3, n_e, HEAD_DIM).transpose(2, 0, 1, 3)
        head_w.append(swap(own.reshape(n_e, rows, 3 * HEAD_DIM)))
        return head_w[0]

    def head_whole(blocks):
        head_w.append(dp_gather(head_w[0]).reshape(width, 3 * HEAD_DIM))
        return head_w[1]

    here = lax.axis_index("dp")

    def spread(shard, chunks):
        while shard.shape[0] % (16 * chunks):
            chunks -= 1
        size = shard.shape[0] // chunks
        parts = [[(shard, here * shard.shape[0])]]
        for j in range(chunks):
            parts.append([])
            for step in range(1, n_dp):
                got = lax.ppermute(
                    shard[j * size : (j + 1) * size],
                    "dp",
                    [(i, (i - step) % n_dp) for i in range(n_dp)],
                )
                parts[-1].append((got, (here + step) % n_dp * shard.shape[0] + j * size))
        return parts

    up_parts = spread(expert_in[0], max(1, min(4, expert_in.shape[1] // 256)))
    down_parts = spread(expert_out[0], 2)
    first = lambda parts: [part for part, _ in parts]
    up_tokens = [first(parts) for parts in up_parts[1:]] + [[]] * 4

    small = jnp.concatenate([router, gain_ffn[:, None]], axis=1)
    small = dp_gather(small).reshape(-1, n_e + 1)
    extra_rows = 32
    extra = jnp.concatenate([small.T, routes.T.astype(BF16)], axis=0)
    extra = jnp.pad(extra, ((0, extra_rows - extra.shape[0]), (0, 0)))
    extra = jnp.broadcast_to(extra, (n_e,) + extra.shape)
    cos_table, sin_table, first_place = rope_tables(segments)
    share_w = shared_in.reshape(rows, 2, n_dp, n_e, shared_rows).transpose(3, 0, 1, 2, 4)
    share_w = share_w.reshape(n_e, rows, 2 * shared_width)

    half = n_e // 4
    norm_blocks = ring_gather(
        normed_one.astype(BF16),
        {
            half - 1: lambda blocks: [head_sent(blocks)] + up_tokens[0],
            half: lambda blocks: [head_whole(blocks), cos_table, sin_table, extra, share_w],
        },
    )
    head_sent_w, head_w = head_w

    head_out, query, key, value, lse, norm_all = attend(
        norm_blocks, order, head_w, cos_table, sin_table, first_place
    )
    mixed = jnp.concatenate([head_out.reshape(n_e, count, HEAD_DIM), extra], axis=1)
    mixed = swap(tied(mixed, *up_tokens[1]) if up_tokens[1] else mixed)
    small = mixed[:, count:]
    mixed = mixed[:, :count].transpose(1, 0, 2).reshape(count, n_dp, n_e, rows)
    mixed = mixed.transpose(0, 2, 1, 3).reshape(count, width)
    share_w = swap(tied(share_w, lse))
    proj_all = gather_all(dp_gather(attn_out).reshape(n_dp * rows, width))
    routes_all = small[:, n_e + 1 : n_e + 1 + TOP].astype(F32)
    small = small[:, : n_e + 1].reshape(n_e, n_e + 1, n_dp, rows).transpose(1, 2, 0, 3)
    small = small.reshape(n_e + 1, width)
    router_full = small[:n_e]
    gain_second = small[n_e].astype(F32)
    cot_all = gather_all(cotangent)

    share_sent = share_w
    share_w = dp_gather(share_w).reshape(width, 2 * shared_width)
    share_out = dp_gather(shared_out).reshape(shared_width, width)
    resid = hidden_in + dot(mixed, proj_all)
    if up_tokens[2]:
        resid = tied(resid, *up_tokens[2])

    inverse_two = lax.rsqrt(jnp.mean(resid * resid, axis=-1, keepdims=True) + EPS)
    normed_two = resid * inverse_two
    norm_two = (normed_two * gain_second).astype(BF16)
    logits = dot_nt(norm_two, router_full)
    picked = jnp.any(routes[:, :, None] == jnp.arange(n_e)[None, None, :], axis=1)
    chosen = jnp.where(picked, logits, NEG)
    chosen = jnp.where(picked, jnp.exp(chosen - jnp.max(chosen, axis=-1, keepdims=True)), 0.0)
    gates = chosen / jnp.sum(chosen, axis=-1, keepdims=True)
    gate_high = gates.astype(BF16)
    gate_low = (gates - gate_high.astype(F32)).astype(BF16)
    blank = jnp.zeros((count, 128 - 2 * n_e), BF16)
    payload = jnp.concatenate([norm_two, gate_high, gate_low, blank], axis=1)
    norm_blocks = ring_gather(
        payload,
        {
            half - 2: lambda blocks: [share_sent] + up_tokens[3],
            half: lambda blocks: first(down_parts[1]),
        },
    )

    named = jnp.any(routes_all == me.astype(F32), axis=1)
    named = jnp.take(named, order, axis=0)
    ranking = jnp.cumsum(named.astype(jnp.int32), axis=1)
    ends = jnp.cumsum(ranking[:, -1])
    begins = ends - ranking[:, -1]
    pos = jnp.where(named, begins[:, None] + ranking - 1, -1)[:, None, :]
    window = -(-(capacity + 15) // 16) * 16
    packed = -(-(n_e * capacity + 32) // 256) * 256
    packing = (begins // 16 * 16, pos, ends[-1:], window, packed)
    norm_two_all, payload, arrived, _ = dispatch(
        norm_blocks, [width, 128], packing, order, jnp.zeros((n_e, 1, count), F32)
    )
    mine = jnp.arange(n_e) == me
    gate_all = payload[:, : 2 * n_e].astype(F32).reshape(length, 2, n_e)
    gate_all = jnp.sum(jnp.where(mine, gate_all, 0.0), axis=(1, 2)).reshape(n_e, 1, count)
    cot_rows, gate_rows = dispatch(cot_all, None, packing, order, gate_all)
    weighted, row_grad, expert_act, route_grad, pre_grad, gate_grad = expert(
        packing[2],
        arrived,
        cot_rows,
        gate_rows,
        [part for parts in up_parts for part in parts],
        [part for parts in down_parts for part in parts],
    )

    shared_pre = dot(norm_two_all, share_w)
    shared_act = (
        jax.nn.silu(shared_pre[:, :shared_width]) * shared_pre[:, shared_width:]
    ).astype(BF16)
    shared_act_grad = dot_nt(cot_all, share_out)
    shared_pre_grad = silu_back(
        shared_act_grad, shared_pre[:, :shared_width], shared_pre[:, shared_width:]
    ).astype(BF16)
    norm_two_part = combine(
        packing, order, steady, me, row_grad, gate_grad, shared_pre_grad, share_w, True, 128
    )
    norm_two_grad = ring_scatter(
        lambda n: norm_two_part[n * count : (n + 1) * count]
    )
    gate_grad = norm_two_grad[:, width : width + n_e] + norm_two_grad[:, width + 64 : width + 64 + n_e]
    norm_two_grad = norm_two_grad[:, :width]
    out_part = combine(
        packing, order, order, me, weighted, gate_rows, shared_act, share_out, False, 0
    )
    routed_out = lax.psum_scatter(out_part, "expert", scatter_dimension=0, tiled=True)

    def shard_grads(left, right, chunks):
        size = left.shape[1] // n_dp
        part = size // chunks
        cut = lambda start, wide: lax.dynamic_slice_in_dim(left, start, wide, 1)
        got = [
            [
                lax.ppermute(
                    dot_tn(cut((here + step) % n_dp * size + j * part, part), right).astype(BF16),
                    "dp",
                    [(i, (i + step) % n_dp) for i in range(n_dp)],
                )
                for step in range(1, n_dp)
            ]
            for j in range(chunks)
        ]
        return dot_tn(cut(here * size, size), right), got

    def shard_sum(own, got, tokens):
        part = own.shape[0] // len(got)
        own = own[None]
        for j, (parts, token) in enumerate(zip(got, tokens)):
            block = sum(tied(p.astype(F32), token) for p in parts)[None]
            block = own[:, j * part : (j + 1) * part] + block
            own = lax.dynamic_update_slice_in_dim(own, block, j * part, 1)
        return own

    down_own, down_got = shard_grads(expert_act, route_grad, 2)
    up_own, up_got = shard_grads(arrived, pre_grad, len(up_parts) - 1)

    share_out_grad = dp_scatter(dot_tn(shared_act, cot_all).reshape(n_dp, shared_rows, width))
    share_in_grad = dot_tn(norm_two_all, shared_pre_grad)
    share_in_grad = dp_scatter(share_in_grad.reshape(n_dp, n_e, rows, 2 * shared_width))
    share_in_grad = swap(share_in_grad.astype(BF16)).astype(F32)
    share_in_grad = (
        share_in_grad.reshape(n_e, rows, 2, n_dp, shared_rows)
        .transpose(1, 2, 3, 0, 4)
        .reshape(rows, -1)
    )

    logit_grad = gates * (gate_grad - jnp.sum(gates * gate_grad, axis=-1, keepdims=True))
    router_grad = jnp.dot(
        logit_grad.T, norm_two.astype(F32), precision=HIGHEST, preferred_element_type=F32
    )
    norm_two_grad = norm_two_grad + jnp.dot(
        logit_grad, router_full.astype(F32), precision=HIGHEST, preferred_element_type=F32
    )
    gain_two_grad = jnp.sum(norm_two_grad * normed_two, axis=0)
    upstream = tied(cotangent.astype(F32), *down_got[0])
    scaled_two = norm_two_grad * gain_second
    resid_grad = upstream + inverse_two * (
        scaled_two - normed_two * jnp.mean(scaled_two * normed_two, axis=-1, keepdims=True)
    )
    small_grad = jnp.concatenate([router_grad, gain_two_grad[None]], axis=0)
    small_grad = jnp.pad(small_grad, ((0, HEAD_DIM - n_e - 1), (0, 0))).T

    branch_cot = resid_grad.astype(BF16)
    proj_grad = dot_tn(mixed, branch_cot).astype(BF16)
    mixed_grad = tied(dot_nt(branch_cot, proj_all), *down_got[1]).astype(BF16)
    mixed_grad = mixed_grad.reshape(count, n_e, n_dp, rows).transpose(0, 2, 1, 3)
    mixed_grad = swap(mixed_grad.reshape(count, n_e, HEAD_DIM).transpose(1, 0, 2))
    mixed_grad = mixed_grad.reshape(length, HEAD_DIM)
    proj_grad = lax.psum_scatter(proj_grad, "expert", scatter_dimension=0, tiled=True)
    attn_out_grad = dp_scatter(proj_grad.astype(F32).reshape(n_dp, rows, width))
    qkv_grad = attend_back(
        query, key, value, mixed_grad, lse, first_place, cos_table, sin_table, order
    )
    norm_one_part = dot_nt(qkv_grad, head_w).astype(BF16)
    scaled_one = ring_scatter(
        lambda n: norm_one_part[n * count : (n + 1) * count],
        {1: up_got[0], half - 1: up_got[min(1, len(up_got) - 1)]},
    )
    expert_out_grad = shard_sum(down_own, down_got, [norm_two_grad, mixed_grad])
    expert_in_grad = shard_sum(up_own, up_got, ([qkv_grad] + [scaled_one] * 3)[: len(up_got)])
    input_grad = resid_grad + inverse_one * (
        scaled_one - normed_one * jnp.mean(scaled_one * normed_one, axis=-1, keepdims=True)
    )
    wide = 3 * HEAD_DIM
    head_grad = jnp.concatenate([dot_tn(norm_all, qkv_grad), small_grad], axis=1)
    head_grad = dp_scatter(head_grad.reshape(n_dp, n_e, rows, wide + small_grad.shape[1]))
    head_grad = swap(head_grad.astype(BF16)).astype(F32)
    small_grad = jnp.sum(head_grad[:, :, wide:], axis=0)
    head_grad = (
        head_grad[:, :, :wide]
        .reshape(n_e, rows, 3, HEAD_DIM)
        .transpose(1, 2, 0, 3)
        .reshape(rows, 3 * width)
    )
    gain_attn_grad = jnp.sum(head_grad * attn_in.astype(F32), axis=1)
    attn_in_grad = head_grad * gain_rows
    return (
        (resid + routed_out.astype(F32)).astype(BF16),
        input_grad.astype(BF16),
        attn_in_grad,
        attn_out_grad,
        gain_attn_grad,
        share_in_grad,
        share_out_grad,
        small_grad[:, :n_e],
        small_grad[:, n_e],
        expert_in_grad,
        expert_out_grad,
    )


def solution(mesh):
    return jax.shard_map(
        per_device,
        mesh=mesh,
        in_specs=(
            P(("dp", "expert"), None),
            P(("dp", "expert"), None),
            P("dp", None),
            P(("dp", "expert"), None),
            P(("dp", "expert"), None),
            P(("dp", "expert"), None),
            P(("dp", "expert")),
            P(("dp", "expert"), None),
            P(("dp", "expert"), None),
            P(("dp", "expert"), None),
            P(("dp", "expert")),
            P("expert", "dp", None),
            P("expert", "dp", None),
        ),
        out_specs=(
            P(("dp", "expert"), None),
            P(("dp", "expert"), None),
            P(("dp", "expert"), None),
            P(("dp", "expert"), None),
            P(("dp", "expert")),
            P(("dp", "expert"), None),
            P(("dp", "expert"), None),
            P(("dp", "expert"), None),
            P(("dp", "expert")),
            P("expert", "dp", None),
            P("expert", "dp", None),
        ),
        check_vma=False,
    )
```

```python
import functools
import math

import jax
import jax.numpy as jnp
from jax import lax
from jax.experimental import pallas as pl
from jax.experimental.pallas import tpu as pltpu
from jax.sharding import PartitionSpec as P

HEADS = 16
HEAD_DIM = 128
TOP = 6


EPS = 1e-06
THETA = 10000.0
NEG = -1e30
HIGHEST = lax.Precision.HIGHEST
BF16 = jnp.bfloat16
F32 = jnp.float32
LOG2E = math.log2(math.e)


def rope_tables(segments):
    length = segments.shape[0]
    places = jnp.arange(length, dtype=jnp.int32)
    starts = jnp.concatenate([jnp.ones((1,), dtype=jnp.bool_), segments[1:] != segments[:-1]])
    first_place = lax.cummax(jnp.where(starts, places, 0), axis=0)
    offset = (places - first_place).astype(jnp.float32)
    half_dim = HEAD_DIM // 2
    freqs = jnp.exp(jnp.arange(half_dim, dtype=jnp.float32) * (-2.0 * math.log(THETA) / HEAD_DIM))
    angles = offset[:, None] * freqs[None, :]
    cos_table, sin_table = jnp.cos(angles), jnp.sin(angles)
    return (
        jnp.concatenate([cos_table, cos_table], axis=1),
        jnp.concatenate([-sin_table, sin_table], axis=1),
        first_place[None, :],
    )


def silu_back(grad_act, gate_part, up_part):
    sigmoid_gate = jax.nn.sigmoid(gate_part)
    gate_grad = grad_act * up_part * sigmoid_gate * (1.0 + gate_part * (1.0 - sigmoid_gate))
    up_grad = grad_act * gate_part * sigmoid_gate
    return jnp.concatenate([gate_grad, up_grad], axis=-1)


def dot(left, right):
    return jnp.dot(left, right, preferred_element_type=F32)


def dot_tn(left, right):
    return lax.dot_general(left, right, (((0,), (0,)), ((), ())), preferred_element_type=F32)


def dot_nt(left, right):
    return lax.dot_general(left, right, (((1,), (1,)), ((), ())), preferred_element_type=F32)


def turn(values, cos_table, sin_table):
    return values * cos_table + pltpu.roll(values, HEAD_DIM // 2, 1) * sin_table


def attend_kernel(sources, block, order_ref, *refs):
    pieces = refs[: sources[-1][-1] + 1]
    weight_ref, cos_ref, sin_ref, start_ref = refs[len(pieces) : len(pieces) + 4]
    o_ref, q_ref, k_ref, v_ref, lse_ref, rows_ref, vt_ref = refs[len(pieces) + 4 :]
    step = pl.program_id(0)
    length = q_ref.shape[0]
    factor = HEAD_DIM ** (-0.5) * LOG2E
    rows = rows_ref.shape[0]

    for n, parts in enumerate(sources):

        @pl.when(step == n)
        def _(parts=parts):
            low = 0
            for part in parts:
                size = pieces[part].shape[0]
                rows_ref[low : low + size, :] = pieces[part][...]
                low += size

    @pl.when(step < len(sources))
    def _():
        qkv = dot(rows_ref[...], weight_ref[...])
        at = pl.ds(pl.multiple_of(order_ref[step] * rows, rows), rows)
        cos_table, sin_table = cos_ref[at, :], sin_ref[at, :]
        q_ref[at, :] = turn(qkv[:, :HEAD_DIM], cos_table, sin_table).astype(BF16)
        k_ref[at, :] = turn(qkv[:, HEAD_DIM : 2 * HEAD_DIM], cos_table, sin_table).astype(BF16)
        value = qkv[:, 2 * HEAD_DIM :]
        v_ref[at, :] = value.astype(BF16)
        vt_ref[:, at] = value.T.astype(BF16)

    for i in range(length // block):

        @pl.when(step == len(sources) + i)
        def _(i=i):
            low, high = i * block, (i + 1) * block
            raw = dot_nt(k_ref[:high, :], q_ref[low:high, :])
            keys = lax.broadcasted_iota(jnp.int32, raw.shape, 0)
            queries = low + lax.broadcasted_iota(jnp.int32, raw.shape, 1)
            allowed = (keys <= queries) & (keys >= start_ref[:, low:high])
            raw = jnp.where(allowed, raw, NEG)
            top = jnp.max(raw, axis=0, keepdims=True)
            shifted = jnp.exp2((raw - top) * factor)
            total = jnp.sum(shifted, axis=0, keepdims=True)
            probs = (shifted * (1.0 / total)).astype(BF16)
            mixed = dot(vt_ref[:, :high], probs)
            o_ref[low:high, :] = mixed.T.astype(BF16)
            lse_ref[:, low:high] = top * factor + jnp.log2(total)


def attend(blocks, order, weight, cos_table, sin_table, first_place):
    pieces, sources = flatten(blocks)
    length = cos_table.shape[0]
    rows = length // len(sources)
    width = weight.shape[0]
    block = min(256, length)
    last = len(sources) - 1
    whole = lambda shape: pl.BlockSpec(shape, lambda i, order: (0, 0))
    head = jax.ShapeDtypeStruct((length, HEAD_DIM), BF16)
    return pl.pallas_call(
        functools.partial(attend_kernel, sources, block),
        out_shape=[head] * 4
        + [jax.ShapeDtypeStruct((1, length), F32), jax.ShapeDtypeStruct((length, width), BF16)],
        grid_spec=pltpu.PrefetchScalarGridSpec(
            num_scalar_prefetch=1,
            grid=(len(sources) + length // block,),
            in_specs=[whole(piece.shape) for piece in pieces]
            + [
                whole(weight.shape),
                whole((length, HEAD_DIM)),
                whole((length, HEAD_DIM)),
                whole((1, length)),
            ],
            out_specs=[whole((length, HEAD_DIM))] * 4
            + [
                whole((1, length)),
                pl.BlockSpec((rows, width), lambda i, order: (jnp.minimum(i, last), 0)),
            ],
            scratch_shapes=[pltpu.VMEM((HEAD_DIM, length), BF16)],
        ),
        compiler_params=pltpu.CompilerParams(vmem_limit_bytes=52 * 2**20),
        name="attend",
    )(order, *pieces, weight, cos_table, sin_table, first_place)


def attend_back_kernel(
    block, rows, order_ref, q_ref, k_ref, v_ref, do_ref, lse_ref, start_ref, cos_ref, sin_ref, out_ref, kt_ref, dq_ref, dk_ref, dv_ref
):
    length = q_ref.shape[0]
    step = pl.program_id(0)
    scale = HEAD_DIM ** (-0.5)
    factor = scale * LOG2E
    count = length // block

    @pl.when(step == 0)
    def _():
        kt_ref[...] = k_ref[...].astype(F32).T.astype(BF16)
        dk_ref[...] = jnp.zeros_like(dk_ref)
        dv_ref[...] = jnp.zeros_like(dv_ref)

    for i in range(count):

        @pl.when(step == i)
        def _(i=i):
            low, high = i * block, (i + 1) * block
            query, grad = q_ref[low:high, :], do_ref[low:high, :]
            raw = dot_nt(k_ref[:high, :], query)
            keys = lax.broadcasted_iota(jnp.int32, raw.shape, 0)
            queries = low + lax.broadcasted_iota(jnp.int32, raw.shape, 1)
            allowed = (keys <= queries) & (keys >= start_ref[:, low:high])
            raw = jnp.where(allowed, raw * factor - lse_ref[:, low:high], NEG)
            probs = jnp.exp2(raw)
            probs_grad = dot_nt(v_ref[:high, :], grad)
            inner = jnp.sum(probs_grad * probs, axis=0, keepdims=True)
            score_grad = (probs * (probs_grad - inner)).astype(BF16)
            dv_ref[:high, :] += dot(probs.astype(BF16), grad)
            dk_ref[:high, :] += dot(score_grad, query)
            dq_ref[low:high, :] = dot(kt_ref[:, :high], score_grad).T

    @pl.when(step == count - 1)
    def _():
        for n in range(length // rows):
            at = pl.ds(pl.multiple_of(order_ref[n] * rows, rows), rows)
            to = slice(n * rows, (n + 1) * rows)
            cos_table, sin_table = cos_ref[at, :], -sin_ref[at, :]
            out_ref[to, :HEAD_DIM] = turn(dq_ref[at, :] * scale, cos_table, sin_table).astype(BF16)
            out_ref[to, HEAD_DIM : 2 * HEAD_DIM] = turn(
                dk_ref[at, :] * scale, cos_table, sin_table
            ).astype(BF16)
            out_ref[to, 2 * HEAD_DIM :] = dv_ref[at, :].astype(BF16)


def attend_back(query, key, value, grad, lse, first_place, cos_table, sin_table, order):
    length = query.shape[0]
    block = min(256, length)
    whole = lambda shape: pl.BlockSpec(shape, lambda i, order: (0, 0))
    head = whole((length, HEAD_DIM))
    return pl.pallas_call(
        functools.partial(attend_back_kernel, block, length // order.shape[0]),
        out_shape=jax.ShapeDtypeStruct((length, 3 * HEAD_DIM), BF16),
        grid_spec=pltpu.PrefetchScalarGridSpec(
            num_scalar_prefetch=1,
            grid=(length // block,),
            in_specs=[head] * 4 + [whole((1, length))] * 2 + [head] * 2,
            out_specs=whole((length, 3 * HEAD_DIM)),
            scratch_shapes=[pltpu.VMEM((HEAD_DIM, length), BF16)]
            + [pltpu.VMEM((length, HEAD_DIM), F32)] * 3,
        ),
        compiler_params=pltpu.CompilerParams(vmem_limit_bytes=48 * 2**20),
        name="attend_back",
    )(order, query, key, value, grad, lse, first_place, cos_table, sin_table)


def dp_gather(value):
    count = lax.axis_size("dp")
    if count == 1:
        return value[None]
    here = lax.axis_index("dp")
    parts = [value] + [
        lax.ppermute(value, "dp", [(i, (i - step) % count) for i in range(count)])
        for step in range(1, count)
    ]
    if count == 2:
        first = here == 0
        return jnp.stack(
            [jnp.where(first, parts[0], parts[1]), jnp.where(first, parts[1], parts[0])]
        )
    whole = jnp.zeros((count,) + value.shape, value.dtype)
    for step, part in enumerate(parts):
        whole = lax.dynamic_update_index_in_dim(whole, part, (here + step) % count, 0)
    return whole


def dp_scatter(value):
    count = lax.axis_size("dp")
    here = lax.axis_index("dp")
    total = lax.dynamic_index_in_dim(value, here, 0, keepdims=False)
    for step in range(1, count):
        block = lax.dynamic_index_in_dim(value, (here + step) % count, 0, keepdims=False)
        got = lax.ppermute(
            block.astype(BF16), "dp", [(i, (i + step) % count) for i in range(count)]
        )
        total = total + got.astype(F32)
    return total


def ring_order():
    pairs = lax.axis_size("expert") // 2
    return list(range(0, pairs, 2)) + list(range(pairs - 1, 0, -2))


def ring_shift(value, step):
    order = ring_order()
    pairs = len(order)
    perm = [
        (order[q] * 2 + c, order[(q + step) % pairs] * 2 + c) for q in range(pairs) for c in range(2)
    ]
    return lax.ppermute(value, "expert", perm)


def core_swap(value):
    count = lax.axis_size("expert")
    return lax.ppermute(value, "expert", [(i, i ^ 1) for i in range(count)])


def ring_offsets():
    half = lax.axis_size("expert") // 4
    return [0] + [o for step in range(1, half) for o in (step, -step)] + [half]


def ring_blocks():
    order = ring_order()
    pairs = len(order)
    table = [[0] * (2 * pairs) for _ in range(2 * pairs)]
    for q in range(pairs):
        for c in range(2):
            for j, offset in enumerate(ring_offsets()):
                for other in range(2):
                    table[order[q] * 2 + c][2 * j + other] = (
                        order[(q - offset) % pairs] * 2 + (c ^ other)
                    )
    return lax.dynamic_index_in_dim(
        jnp.asarray(table, jnp.int32), lax.axis_index("expert"), 0, keepdims=False
    )


def tied(value, *tokens):
    firsts = [lax.slice(t, (0,) * t.ndim, (1,) * t.ndim).reshape(()) for t in tokens]
    token = sum(t.astype(F32) for t in firsts) * 0.0
    return (value.astype(F32) * (1.0 + token)).astype(value.dtype)


def ring_gather(value, gates=None):
    gates = gates or {}
    half_rows = value.shape[0] // 2
    half = lax.axis_size("expert") // 4
    blocks = {}

    def keep(parts, offset):
        blocks[offset] = (parts, [core_swap(part) for part in parts])

    keep([value], 0)
    ahead = back = value
    for step in range(1, half):
        if step in gates:
            token = gates[step](blocks)
            ahead, back = tied(ahead, *token), tied(back, *token)
        ahead, back = ring_shift(ahead, 1), ring_shift(back, -1)
        keep([ahead], step)
        keep([back], -step)
    if half in gates:
        token = gates[half](blocks)
        ahead, back = tied(ahead, *token), tied(back, *token)
    last = [ring_shift(ahead[:half_rows], 1), ring_shift(back[half_rows:], -1)]
    keep(last, half)
    return [parts for offset in ring_offsets() for parts in blocks[offset]]


def flatten(blocks):
    pieces = [piece for parts in blocks for piece in parts]
    sources, n = [], 0
    for parts in blocks:
        sources.append(tuple(range(n, n + len(parts))))
        n += len(parts)
    return pieces, tuple(sources)


def ring_scatter(block, gates=None, marks=None):
    gates = gates or {}
    half = lax.axis_size("expert") // 4
    offsets = ring_offsets()
    spare = {}

    def mine(offset):
        if offset not in spare:
            j = offsets.index(offset)
            spare[offset] = block(2 * j).astype(F32) + core_swap(block(2 * j + 1)).astype(F32)
        return spare[offset]

    far = mine(half).astype(BF16)
    half_rows = far.shape[0] // 2
    ahead = ring_shift(far[:half_rows], 1)
    back = ring_shift(far[half_rows:], -1)
    if marks is not None:
        marks.extend([ahead, back])
    for step in range(half - 1, 0, -1):
        onward, homeward = mine(-step), mine(step)
        if step == half - 1:
            onward = jnp.concatenate(
                [onward[:half_rows] + ahead.astype(F32), onward[half_rows:]], axis=0
            )
            homeward = jnp.concatenate(
                [homeward[:half_rows], homeward[half_rows:] + back.astype(F32)], axis=0
            )
        else:
            onward = onward + ahead.astype(F32)
            homeward = homeward + back.astype(F32)
        if half - step in gates:
            onward, homeward = tied(onward, *gates[half - step]), tied(homeward, *gates[half - step])
        ahead = ring_shift(onward.astype(BF16), 1)
        back = ring_shift(homeward.astype(BF16), -1)
    return mine(0) + ahead.astype(F32) + back.astype(F32)


def chosen(pos_ref, base, window):
    count = pos_ref.shape[-1]
    row = base + lax.broadcasted_iota(jnp.int32, (window, count), 0)
    return row == pos_ref[0]


def dispatch_kernel(sources, widths, window, base_ref, order_ref, pos_ref, gate_ref, *refs):
    outs = refs[-len(widths) - 2 :]
    pieces, blocks, rows_ref, weights_ref = refs[: -len(outs)], outs[:-2], outs[-2], outs[-1]
    step = pl.program_id(0)

    @pl.when(step == 0)
    def _():
        rows_ref[...] = jnp.zeros_like(rows_ref)
        weights_ref[...] = jnp.zeros_like(weights_ref)

    for n, parts in enumerate(sources):

        @pl.when(step == n)
        def _(parts=parts):
            low = 0
            for part in parts:
                size = pieces[part].shape[0]
                left = 0
                for block, wide in zip(blocks, widths):
                    block[low : low + size, :] = pieces[part][:, left : left + wide]
                    left += wide
                low += size

    base = pl.multiple_of(base_ref[step], 16)
    pick = chosen(pos_ref, base, window)
    at = pl.ds(base, window)
    found = dot(pick.astype(F32).astype(BF16), (blocks or pieces)[0][...])
    rows_ref[at, :] = (rows_ref[at, :].astype(F32) + found).astype(BF16)
    weights_ref[at, :] += jnp.sum(jnp.where(pick, gate_ref[0], 0.0), axis=1, keepdims=True)


def dispatch(blocks, widths, packing, order, gates):
    base, pos, _, window, packed = packing
    count, _, rows = pos.shape
    if isinstance(blocks, list):
        pieces, sources = flatten(blocks)
        piece_specs = [pl.BlockSpec(piece.shape, lambda i, base, order: (0, 0)) for piece in pieces]
    else:
        pieces, sources, widths = [blocks], (), []
        piece_specs = [pl.BlockSpec((rows, blocks.shape[1]), lambda i, base, order: (order[i], 0))]
    width = (widths or [pieces[0].shape[1]])[0]
    return pl.pallas_call(
        functools.partial(dispatch_kernel, sources, tuple(widths), window),
        out_shape=[jax.ShapeDtypeStruct((rows * count, wide), BF16) for wide in widths]
        + [
            jax.ShapeDtypeStruct((packed, width), BF16),
            jax.ShapeDtypeStruct((packed, 1), F32),
        ],
        grid_spec=pltpu.PrefetchScalarGridSpec(
            num_scalar_prefetch=2,
            grid=(count,),
            in_specs=[
                pl.BlockSpec((1, 1, rows), lambda i, base, order: (i, 0, 0)),
                pl.BlockSpec((1, 1, rows), lambda i, base, order: (order[i], 0, 0)),
            ]
            + piece_specs,
            out_specs=[
                pl.BlockSpec((rows, wide), lambda i, base, order: (order[i], 0)) for wide in widths
            ]
            + [
                pl.BlockSpec((packed, width), lambda i, base, order: (0, 0)),
                pl.BlockSpec((packed, 1), lambda i, base, order: (0, 0)),
            ],
        ),
        compiler_params=pltpu.CompilerParams(vmem_limit_bytes=52 * 2**20),
        name="dispatch",
    )(base, order, pos, gates, *pieces)


def expert_kernel(ups, total_ref, starts_ref, x_ref, g_ref, gate_ref, *refs):
    parts, refs = refs[:-9], refs[-9:]
    wy_ref, dn_ref, ea_ref, dy_ref, db_ref, dg_ref, up_ref, down_ref, sems = refs
    step = pl.program_id(0)
    rows, hidden = ea_ref.shape
    some = step * rows < total_ref[0]

    @pl.when(step == 0)
    def _():
        copies = []
        for n, part in enumerate(parts):
            at = pl.ds(pl.multiple_of(starts_ref[n], 16), part.shape[0])
            whole = up_ref if n < ups else down_ref
            copies.append(pltpu.make_async_copy(part, whole.at[at, :], sems.at[n]))
        for copy in copies:
            copy.start()
        for copy in copies:
            copy.wait()

    @pl.when(some)
    def _():
        pre = dot(x_ref[...], up_ref[...])
        gate_part, up_part = pre[:, :hidden], pre[:, hidden:]
        sigmoid_gate = 1.0 / (1.0 + jnp.exp(-gate_part))
        silu = gate_part * sigmoid_gate
        act = (silu * up_part).astype(BF16)
        ea_ref[...] = act
        result = dot(act, down_ref[...]).astype(BF16).astype(F32)
        grad = g_ref[...].astype(F32)
        gate = gate_ref[...]
        dg_ref[...] = jnp.sum(grad * result, axis=1, keepdims=True)
        wy_ref[...] = (gate * result).astype(BF16)
        out_grad = (gate * grad).astype(BF16)
        dy_ref[...] = out_grad
        act_grad = dot_nt(out_grad, down_ref[...])
        db_ref[:, :hidden] = (
            act_grad * up_part * sigmoid_gate * (1.0 + gate_part * (1.0 - sigmoid_gate))
        ).astype(BF16)
        db_ref[:, hidden:] = (act_grad * silu).astype(BF16)
        dn_ref[...] = dot_nt(db_ref[...], up_ref[...]).astype(BF16)

    @pl.when(jnp.logical_not(some))
    def _():
        for ref in (wy_ref, dn_ref, ea_ref, dy_ref, db_ref, dg_ref):
            ref[...] = jnp.zeros_like(ref)


def expert(total, rows, grads, gates, ups, downs):
    packed, width = rows.shape
    hidden = sum(part.shape[0] for part, _ in downs)
    tile = 256
    parts = [part for part, _ in ups + downs]
    starts = jnp.stack([start for _, start in ups + downs]).astype(jnp.int32)
    spec = lambda wide: pl.BlockSpec((tile, wide), lambda i, total, starts: (i, 0))
    widths = (width, width, hidden, width, 2 * hidden)
    return pl.pallas_call(
        functools.partial(expert_kernel, len(ups)),
        out_shape=[jax.ShapeDtypeStruct((packed, wide), BF16) for wide in widths]
        + [jax.ShapeDtypeStruct((packed, 1), F32)],
        grid_spec=pltpu.PrefetchScalarGridSpec(
            num_scalar_prefetch=2,
            grid=(packed // tile,),
            in_specs=[spec(width), spec(width), spec(1)]
            + [pl.BlockSpec(memory_space=pl.ANY)] * len(parts),
            out_specs=[spec(wide) for wide in widths] + [spec(1)],
            scratch_shapes=[
                pltpu.VMEM((width, 2 * hidden), BF16),
                pltpu.VMEM((hidden, width), BF16),
                pltpu.SemaphoreType.DMA((len(parts),)),
            ],
        ),
        compiler_params=pltpu.CompilerParams(vmem_limit_bytes=58 * 2**20),
        name="expert",
    )(total, starts, rows, grads, gates, *parts)


def combine_kernel(turned, window, extra, base_ref, order_ref, to_ref, me_ref, pos_ref, rows_ref, dg_ref, act_ref, weight_ref, out_ref):
    mul = dot_nt if turned else dot
    base = pl.multiple_of(base_ref[pl.program_id(0)], 16)
    pick = chosen(pos_ref, base, window)
    at = pl.ds(base, window)
    width = rows_ref.shape[1]
    out_ref[:, :width] = (
        dot_tn(pick.astype(F32).astype(BF16), rows_ref[at, :]) + mul(act_ref[...], weight_ref[...])
    ).astype(BF16)
    if extra:
        count = pick.shape[1]
        line = jnp.sum(jnp.where(pick, dg_ref[at, :], 0.0), axis=0, keepdims=True)
        row = lax.broadcasted_iota(jnp.int32, (count, count), 0)
        lane = lax.broadcasted_iota(jnp.int32, (count, count), 1)
        column = jnp.sum(jnp.where(row == lane, line, 0.0), axis=1, keepdims=True)
        high = column.astype(BF16).astype(F32)
        lane = lax.broadcasted_iota(jnp.int32, (count, extra), 1)
        out_ref[:, width:] = jnp.where(
            lane == me_ref[0], high, jnp.where(lane == me_ref[0] + extra // 2, column - high, 0.0)
        ).astype(BF16)


def combine(packing, order, to, me, rows, dg, act, weight, turned, extra):
    base, pos, _, window, packed = packing
    blocks, _, count = pos.shape
    width = rows.shape[-1]
    whole = lambda ref: pl.BlockSpec(ref.shape, lambda i, *_: (0, 0))
    return pl.pallas_call(
        functools.partial(combine_kernel, turned, window, extra),
        out_shape=jax.ShapeDtypeStruct((blocks * count, width + extra), BF16),
        grid_spec=pltpu.PrefetchScalarGridSpec(
            num_scalar_prefetch=4,
            grid=(blocks,),
            in_specs=[
                pl.BlockSpec((1, 1, count), lambda i, *_: (i, 0, 0)),
                whole(rows),
                whole(dg),
                pl.BlockSpec((count, act.shape[1]), lambda i, base, order, to, me: (order[i], 0)),
                whole(weight),
            ],
            out_specs=pl.BlockSpec(
                (count, width + extra), lambda i, base, order, to, me: (to[i], 0)
            ),
        ),
        compiler_params=pltpu.CompilerParams(vmem_limit_bytes=40 * 2**20),
        name="combine",
    )(base, order, to, me.reshape(1), pos, rows, dg, act, weight)


def gather_all(value):
    return lax.all_gather(value, "expert", axis=0, tiled=True)


def swap(value):
    return lax.all_to_all(value, "expert", split_axis=0, concat_axis=0, tiled=True)


def per_device(
    tokens,
    cotangent,
    segment_ids,
    routes,
    attn_in,
    attn_out,
    gain_attn,
    shared_in,
    shared_out,
    router,
    gain_ffn,
    expert_in,
    expert_out,
):
    n_dp, n_e = lax.axis_size("dp"), lax.axis_size("expert")
    me = lax.axis_index("expert")
    count, width = tokens.shape
    segments = segment_ids[0]
    length = segments.shape[0]
    rows = attn_in.shape[0]
    capacity = min(count, 3 * TOP * count // (2 * n_e))
    shared_rows = shared_out.shape[0]
    shared_width = shared_rows * n_dp
    expert_width = expert_out.shape[1] * n_dp

    order = ring_blocks()
    steady = jnp.arange(n_e, dtype=jnp.int32)
    hidden_in = tokens.astype(F32)
    inverse_one = lax.rsqrt(jnp.mean(hidden_in * hidden_in, axis=-1, keepdims=True) + EPS)
    normed_one = hidden_in * inverse_one
    gain_rows = gain_attn.astype(F32)[:, None]
    head_w = []

    def head_sent(blocks):
        own = (attn_in.astype(F32) * tied(gain_rows, blocks[0][1][0])).astype(BF16)
        own = own.reshape(rows, 3, n_e, HEAD_DIM).transpose(2, 0, 1, 3)
        head_w.append(swap(own.reshape(n_e, rows, 3 * HEAD_DIM)))
        return head_w[0]

    def head_whole(blocks):
        head_w.append(dp_gather(head_w[0]).reshape(width, 3 * HEAD_DIM))
        return head_w[1]

    here = lax.axis_index("dp")

    def pieces_of(size, chunks):
        while size % (16 * chunks):
            chunks -= 1
        return chunks

    def part_of(shard, chunks, j, *after):
        size = shard.shape[0] // chunks
        block = shard[j * size : (j + 1) * size]
        block = tied(block, *after) if after else block
        return [
            (
                lax.ppermute(block, "dp", [(i, (i - step) % n_dp) for i in range(n_dp)]),
                (here + step) % n_dp * shard.shape[0] + j * size,
            )
            for step in range(1, n_dp)
        ]

    first = lambda parts: [part for part, _ in parts]
    up_chunks = pieces_of(expert_in.shape[1], max(1, min(4, expert_in.shape[1] // 256)))
    down_chunks = pieces_of(expert_out.shape[1], 2)
    ups = [(expert_in[0], here * expert_in.shape[1])]
    downs = [(expert_out[0], here * expert_out.shape[1])]
    ups += part_of(expert_in[0], up_chunks, 0)
    up_first = first(ups[1:])

    small = jnp.concatenate([router, gain_ffn[:, None]], axis=1)
    small = dp_gather(small).reshape(-1, n_e + 1)
    extra_rows = 32
    extra = jnp.concatenate([small.T, routes.T.astype(BF16)], axis=0)
    extra = jnp.pad(extra, ((0, extra_rows - extra.shape[0]), (0, 0)))
    extra = jnp.broadcast_to(extra, (n_e,) + extra.shape)
    cos_table, sin_table, first_place = rope_tables(segments)
    share_w = shared_in.reshape(rows, 2, n_dp, n_e, shared_rows).transpose(3, 0, 1, 2, 4)
    share_w = share_w.reshape(n_e, rows, 2 * shared_width)

    half = n_e // 4
    norm_blocks = ring_gather(
        normed_one.astype(BF16),
        {
            half - 1: lambda blocks: [head_sent(blocks)] + up_first,
            half: lambda blocks: [head_whole(blocks), cos_table, sin_table, extra, share_w],
        },
    )
    head_sent_w, head_w = head_w

    second = part_of(expert_in[0], up_chunks, 1, head_w) if up_chunks > 1 else []
    ups += second

    head_out, query, key, value, lse, norm_all = attend(
        norm_blocks, order, head_w, cos_table, sin_table, first_place
    )
    mixed = jnp.concatenate([head_out.reshape(n_e, count, HEAD_DIM), extra], axis=1)
    share_w = swap(tied(share_w, head_sent_w))
    third = part_of(expert_in[0], up_chunks, 2, lse) if up_chunks > 2 else []
    mixed = swap(tied(mixed, share_w, *first(second)))
    fourth = part_of(expert_in[0], up_chunks, 3, mixed) if up_chunks > 3 else []
    ups += third + fourth
    small = mixed[:, count:]
    mixed = mixed[:, :count].transpose(1, 0, 2).reshape(count, n_dp, n_e, rows)
    mixed = mixed.transpose(0, 2, 1, 3).reshape(count, width)
    proj_all = dp_gather(attn_out).reshape(n_dp * rows, width)
    proj_all = gather_all(tied(proj_all, norm_blocks[-3][0], norm_blocks[-5][0]))
    routes_all = small[:, n_e + 1 : n_e + 1 + TOP].astype(F32)
    small = small[:, : n_e + 1].reshape(n_e, n_e + 1, n_dp, rows).transpose(1, 2, 0, 3)
    small = small.reshape(n_e + 1, width)
    router_full = small[:n_e]
    gain_second = small[n_e].astype(F32)
    cot_all = gather_all(tied(cotangent, lse))

    share_sent = share_w
    share_w = dp_gather(share_w).reshape(width, 2 * shared_width)
    share_out = dp_gather(shared_out).reshape(shared_width, width)
    resid = hidden_in + dot(mixed, proj_all)
    if third:
        resid = tied(resid, *first(third))
    down_first = part_of(expert_out[0], down_chunks, 0, resid)
    downs += down_first
    if down_chunks > 1:
        downs += part_of(expert_out[0], down_chunks, 1, resid)

    inverse_two = lax.rsqrt(jnp.mean(resid * resid, axis=-1, keepdims=True) + EPS)
    normed_two = resid * inverse_two
    norm_two = (normed_two * gain_second).astype(BF16)
    logits = dot_nt(norm_two, router_full)
    picked = jnp.any(routes[:, :, None] == jnp.arange(n_e)[None, None, :], axis=1)
    chosen = jnp.where(picked, logits, NEG)
    chosen = jnp.where(picked, jnp.exp(chosen - jnp.max(chosen, axis=-1, keepdims=True)), 0.0)
    gates = chosen / jnp.sum(chosen, axis=-1, keepdims=True)
    gate_high = gates.astype(BF16)
    gate_low = (gates - gate_high.astype(F32)).astype(BF16)
    blank = jnp.zeros((count, 128 - 2 * n_e), BF16)
    payload = jnp.concatenate([norm_two, gate_high, gate_low, blank], axis=1)
    norm_blocks = ring_gather(
        payload,
        {
            half - 1: lambda blocks: [share_sent] + first(fourth),
        },
    )

    named = jnp.any(routes_all == me.astype(F32), axis=1)
    named = jnp.take(named, order, axis=0)
    ranking = jnp.cumsum(named.astype(jnp.int32), axis=1)
    ends = jnp.cumsum(ranking[:, -1])
    begins = ends - ranking[:, -1]
    pos = jnp.where(named, begins[:, None] + ranking - 1, -1)[:, None, :]
    window = -(-(capacity + 15) // 16) * 16
    packed = -(-(n_e * capacity + 32) // 256) * 256
    packing = (begins // 16 * 16, pos, ends[-1:], window, packed)
    norm_two_all, payload, arrived, _ = dispatch(
        norm_blocks, [width, 128], packing, order, jnp.zeros((n_e, 1, count), F32)
    )
    mine = jnp.arange(n_e) == me
    gate_all = payload[:, : 2 * n_e].astype(F32).reshape(length, 2, n_e)
    gate_all = jnp.sum(jnp.where(mine, gate_all, 0.0), axis=(1, 2)).reshape(n_e, 1, count)
    cot_rows, gate_rows = dispatch(cot_all, None, packing, order, gate_all)
    weighted, row_grad, expert_act, route_grad, pre_grad, gate_grad = expert(
        packing[2],
        arrived,
        cot_rows,
        gate_rows,
        ups,
        downs,
    )

    shared_pre = dot(norm_two_all, share_w)
    shared_act = (
        jax.nn.silu(shared_pre[:, :shared_width]) * shared_pre[:, shared_width:]
    ).astype(BF16)
    shared_act_grad = dot_nt(cot_all, share_out)
    shared_pre_grad = silu_back(
        shared_act_grad, shared_pre[:, :shared_width], shared_pre[:, shared_width:]
    ).astype(BF16)
    norm_two_part = combine(
        packing, order, steady, me, row_grad, gate_grad, shared_pre_grad, share_w, True, 128
    )
    norm_two_grad = ring_scatter(
        lambda n: norm_two_part[n * count : (n + 1) * count]
    )
    gate_grad = norm_two_grad[:, width : width + n_e] + norm_two_grad[:, width + 64 : width + 64 + n_e]
    norm_two_grad = norm_two_grad[:, :width]
    out_part = combine(
        packing, order, order, me, weighted, gate_rows, shared_act, share_out, False, 0
    )
    routed_out = lax.psum_scatter(out_part, "expert", scatter_dimension=0, tiled=True)

    def shard_grads(left, right, chunks):
        size = left.shape[1] // n_dp
        part = size // chunks
        cut = lambda start, wide: lax.dynamic_slice_in_dim(left, start, wide, 1)
        got = [
            [
                lax.ppermute(
                    dot_tn(cut((here + step) % n_dp * size + j * part, part), right).astype(BF16),
                    "dp",
                    [(i, (i + step) % n_dp) for i in range(n_dp)],
                )
                for step in range(1, n_dp)
            ]
            for j in range(chunks)
        ]
        return dot_tn(cut(here * size, size), right), got

    def shard_sum(own, got, tokens):
        part = own.shape[0] // len(got)
        own = own[None]
        for j, (parts, token) in enumerate(zip(got, tokens)):
            block = sum(tied(p.astype(F32), token) for p in parts)[None]
            block = own[:, j * part : (j + 1) * part] + block
            own = lax.dynamic_update_slice_in_dim(own, block, j * part, 1)
        return own

    down_own, down_got = shard_grads(expert_act, route_grad, 2)
    up_own, up_got = shard_grads(arrived, pre_grad, up_chunks)

    share_out_grad = dp_scatter(dot_tn(shared_act, cot_all).reshape(n_dp, shared_rows, width))
    share_in_grad = dot_tn(norm_two_all, shared_pre_grad)
    share_in_grad = dp_scatter(share_in_grad.reshape(n_dp, n_e, rows, 2 * shared_width))
    share_in_grad = swap(share_in_grad.astype(BF16)).astype(F32)
    share_in_grad = (
        share_in_grad.reshape(n_e, rows, 2, n_dp, shared_rows)
        .transpose(1, 2, 3, 0, 4)
        .reshape(rows, -1)
    )

    logit_grad = gates * (gate_grad - jnp.sum(gates * gate_grad, axis=-1, keepdims=True))
    router_grad = jnp.dot(
        logit_grad.T, norm_two.astype(F32), precision=HIGHEST, preferred_element_type=F32
    )
    norm_two_grad = norm_two_grad + jnp.dot(
        logit_grad, router_full.astype(F32), precision=HIGHEST, preferred_element_type=F32
    )
    gain_two_grad = jnp.sum(norm_two_grad * normed_two, axis=0)
    upstream = tied(cotangent.astype(F32), *down_got[0])
    scaled_two = norm_two_grad * gain_second
    resid_grad = upstream + inverse_two * (
        scaled_two - normed_two * jnp.mean(scaled_two * normed_two, axis=-1, keepdims=True)
    )
    small_grad = jnp.concatenate([router_grad, gain_two_grad[None]], axis=0)
    small_grad = jnp.pad(small_grad, ((0, HEAD_DIM - n_e - 1), (0, 0))).T

    branch_cot = resid_grad.astype(BF16)
    proj_grad = dot_tn(mixed, branch_cot).astype(BF16)
    mixed_grad = tied(dot_nt(branch_cot, proj_all), *down_got[1]).astype(BF16)
    mixed_grad = mixed_grad.reshape(count, n_e, n_dp, rows).transpose(0, 2, 1, 3)
    mixed_grad = swap(mixed_grad.reshape(count, n_e, HEAD_DIM).transpose(1, 0, 2))
    mixed_grad = mixed_grad.reshape(length, HEAD_DIM)
    proj_grad = lax.psum_scatter(proj_grad, "expert", scatter_dimension=0, tiled=True)
    attn_out_grad = dp_scatter(proj_grad.astype(F32).reshape(n_dp, rows, width))
    qkv_grad = attend_back(
        query, key, value, mixed_grad, lse, first_place, cos_table, sin_table, order
    )
    norm_one_part = dot_nt(qkv_grad, head_w).astype(BF16)
    scaled_one = ring_scatter(
        lambda n: norm_one_part[n * count : (n + 1) * count],
        {1: up_got[0], half - 1: [proj_grad] + up_got[min(1, len(up_got) - 1)]},
    )
    expert_out_grad = shard_sum(down_own, down_got, [norm_two_grad, mixed_grad])
    expert_in_grad = shard_sum(up_own, up_got, ([qkv_grad] + [scaled_one] * 3)[: len(up_got)])
    input_grad = resid_grad + inverse_one * (
        scaled_one - normed_one * jnp.mean(scaled_one * normed_one, axis=-1, keepdims=True)
    )
    wide = 3 * HEAD_DIM
    head_grad = jnp.concatenate([dot_tn(norm_all, qkv_grad), small_grad], axis=1)
    head_grad = dp_scatter(head_grad.reshape(n_dp, n_e, rows, wide + small_grad.shape[1]))
    head_grad = swap(head_grad.astype(BF16)).astype(F32)
    small_grad = jnp.sum(head_grad[:, :, wide:], axis=0)
    head_grad = (
        head_grad[:, :, :wide]
        .reshape(n_e, rows, 3, HEAD_DIM)
        .transpose(1, 2, 0, 3)
        .reshape(rows, 3 * width)
    )
    gain_attn_grad = jnp.sum(head_grad * attn_in.astype(F32), axis=1)
    attn_in_grad = head_grad * gain_rows
    return (
        (resid + routed_out.astype(F32)).astype(BF16),
        input_grad.astype(BF16),
        attn_in_grad,
        attn_out_grad,
        gain_attn_grad,
        share_in_grad,
        share_out_grad,
        small_grad[:, :n_e],
        small_grad[:, n_e],
        expert_in_grad,
        expert_out_grad,
    )


def solution(mesh):
    return jax.shard_map(
        per_device,
        mesh=mesh,
        in_specs=(
            P(("dp", "expert"), None),
            P(("dp", "expert"), None),
            P("dp", None),
            P(("dp", "expert"), None),
            P(("dp", "expert"), None),
            P(("dp", "expert"), None),
            P(("dp", "expert")),
            P(("dp", "expert"), None),
            P(("dp", "expert"), None),
            P(("dp", "expert"), None),
            P(("dp", "expert")),
            P("expert", "dp", None),
            P("expert", "dp", None),
        ),
        out_specs=(
            P(("dp", "expert"), None),
            P(("dp", "expert"), None),
            P(("dp", "expert"), None),
            P(("dp", "expert"), None),
            P(("dp", "expert")),
            P(("dp", "expert"), None),
            P(("dp", "expert"), None),
            P(("dp", "expert"), None),
            P(("dp", "expert")),
            P("expert", "dp", None),
            P("expert", "dp", None),
        ),
        check_vma=False,
    )
```

```python
import functools
import math

import jax
import jax.numpy as jnp
from jax import lax
from jax.experimental import pallas as pl
from jax.experimental.pallas import tpu as pltpu
from jax.sharding import PartitionSpec as P

HEADS = 16
HEAD_DIM = 128
TOP = 6


EPS = 1e-06
THETA = 10000.0
NEG = -1e30
HIGHEST = lax.Precision.HIGHEST
BF16 = jnp.bfloat16
F32 = jnp.float32
LOG2E = math.log2(math.e)


def rope_tables(segments):
    length = segments.shape[0]
    places = jnp.arange(length, dtype=jnp.int32)
    starts = jnp.concatenate([jnp.ones((1,), dtype=jnp.bool_), segments[1:] != segments[:-1]])
    first_place = lax.cummax(jnp.where(starts, places, 0), axis=0)
    offset = (places - first_place).astype(jnp.float32)
    half_dim = HEAD_DIM // 2
    freqs = jnp.exp(jnp.arange(half_dim, dtype=jnp.float32) * (-2.0 * math.log(THETA) / HEAD_DIM))
    angles = offset[:, None] * freqs[None, :]
    cos_table, sin_table = jnp.cos(angles), jnp.sin(angles)
    return (
        jnp.concatenate([cos_table, cos_table], axis=1),
        jnp.concatenate([-sin_table, sin_table], axis=1),
        first_place[None, :],
    )


def silu_back(grad_act, gate_part, up_part):
    sigmoid_gate = jax.nn.sigmoid(gate_part)
    gate_grad = grad_act * up_part * sigmoid_gate * (1.0 + gate_part * (1.0 - sigmoid_gate))
    up_grad = grad_act * gate_part * sigmoid_gate
    return jnp.concatenate([gate_grad, up_grad], axis=-1)


def dot(left, right):
    return jnp.dot(left, right, preferred_element_type=F32)


def dot_tn(left, right):
    return lax.dot_general(left, right, (((0,), (0,)), ((), ())), preferred_element_type=F32)


def dot_nt(left, right):
    return lax.dot_general(left, right, (((1,), (1,)), ((), ())), preferred_element_type=F32)


def turn(values, cos_table, sin_table):
    return values * cos_table + pltpu.roll(values, HEAD_DIM // 2, 1) * sin_table


def attend_kernel(sources, block, order_ref, *refs):
    pieces = refs[: sources[-1][-1] + 1]
    weight_ref, cos_ref, sin_ref, start_ref = refs[len(pieces) : len(pieces) + 4]
    o_ref, q_ref, k_ref, v_ref, lse_ref, rows_ref, vt_ref = refs[len(pieces) + 4 :]
    step = pl.program_id(0)
    length = q_ref.shape[0]
    factor = HEAD_DIM ** (-0.5) * LOG2E
    rows = rows_ref.shape[0]

    for n, parts in enumerate(sources):

        @pl.when(step == n)
        def _(parts=parts):
            low = 0
            for part in parts:
                size = pieces[part].shape[0]
                rows_ref[low : low + size, :] = pieces[part][...]
                low += size

    @pl.when(step < len(sources))
    def _():
        qkv = dot(rows_ref[...], weight_ref[...])
        at = pl.ds(pl.multiple_of(order_ref[step] * rows, rows), rows)
        cos_table, sin_table = cos_ref[at, :], sin_ref[at, :]
        q_ref[at, :] = turn(qkv[:, :HEAD_DIM], cos_table, sin_table).astype(BF16)
        k_ref[at, :] = turn(qkv[:, HEAD_DIM : 2 * HEAD_DIM], cos_table, sin_table).astype(BF16)
        value = qkv[:, 2 * HEAD_DIM :]
        v_ref[at, :] = value.astype(BF16)
        vt_ref[:, at] = value.T.astype(BF16)

    for i in range(length // block):

        @pl.when(step == len(sources) + i)
        def _(i=i):
            low, high = i * block, (i + 1) * block
            raw = dot_nt(k_ref[:high, :], q_ref[low:high, :])
            keys = lax.broadcasted_iota(jnp.int32, raw.shape, 0)
            queries = low + lax.broadcasted_iota(jnp.int32, raw.shape, 1)
            allowed = (keys <= queries) & (keys >= start_ref[:, low:high])
            raw = jnp.where(allowed, raw, NEG)
            top = jnp.max(raw, axis=0, keepdims=True)
            shifted = jnp.exp2((raw - top) * factor)
            total = jnp.sum(shifted, axis=0, keepdims=True)
            probs = (shifted * (1.0 / total)).astype(BF16)
            mixed = dot(vt_ref[:, :high], probs)
            o_ref[low:high, :] = mixed.T.astype(BF16)
            lse_ref[:, low:high] = top * factor + jnp.log2(total)


def attend(blocks, order, weight, cos_table, sin_table, first_place):
    pieces, sources = flatten(blocks)
    length = cos_table.shape[0]
    rows = length // len(sources)
    width = weight.shape[0]
    block = min(256, length)
    last = len(sources) - 1
    whole = lambda shape: pl.BlockSpec(shape, lambda i, order: (0, 0))
    head = jax.ShapeDtypeStruct((length, HEAD_DIM), BF16)
    return pl.pallas_call(
        functools.partial(attend_kernel, sources, block),
        out_shape=[head] * 4
        + [jax.ShapeDtypeStruct((1, length), F32), jax.ShapeDtypeStruct((length, width), BF16)],
        grid_spec=pltpu.PrefetchScalarGridSpec(
            num_scalar_prefetch=1,
            grid=(len(sources) + length // block,),
            in_specs=[whole(piece.shape) for piece in pieces]
            + [
                whole(weight.shape),
                whole((length, HEAD_DIM)),
                whole((length, HEAD_DIM)),
                whole((1, length)),
            ],
            out_specs=[whole((length, HEAD_DIM))] * 4
            + [
                whole((1, length)),
                pl.BlockSpec((rows, width), lambda i, order: (jnp.minimum(i, last), 0)),
            ],
            scratch_shapes=[pltpu.VMEM((HEAD_DIM, length), BF16)],
        ),
        compiler_params=pltpu.CompilerParams(vmem_limit_bytes=52 * 2**20),
        name="attend",
    )(order, *pieces, weight, cos_table, sin_table, first_place)


def attend_back_kernel(
    block, rows, order_ref, q_ref, k_ref, v_ref, do_ref, lse_ref, start_ref, cos_ref, sin_ref, out_ref, kt_ref, dq_ref, dk_ref, dv_ref
):
    length = q_ref.shape[0]
    step = pl.program_id(0)
    scale = HEAD_DIM ** (-0.5)
    factor = scale * LOG2E
    count = length // block

    @pl.when(step == 0)
    def _():
        kt_ref[...] = k_ref[...].astype(F32).T.astype(BF16)
        dk_ref[...] = jnp.zeros_like(dk_ref)
        dv_ref[...] = jnp.zeros_like(dv_ref)

    for i in range(count):

        @pl.when(step == i)
        def _(i=i):
            low, high = i * block, (i + 1) * block
            query, grad = q_ref[low:high, :], do_ref[low:high, :]
            raw = dot_nt(k_ref[:high, :], query)
            keys = lax.broadcasted_iota(jnp.int32, raw.shape, 0)
            queries = low + lax.broadcasted_iota(jnp.int32, raw.shape, 1)
            allowed = (keys <= queries) & (keys >= start_ref[:, low:high])
            raw = jnp.where(allowed, raw * factor - lse_ref[:, low:high], NEG)
            probs = jnp.exp2(raw)
            probs_grad = dot_nt(v_ref[:high, :], grad)
            inner = jnp.sum(probs_grad * probs, axis=0, keepdims=True)
            score_grad = (probs * (probs_grad - inner)).astype(BF16)
            dv_ref[:high, :] += dot(probs.astype(BF16), grad)
            dk_ref[:high, :] += dot(score_grad, query)
            dq_ref[low:high, :] = dot(kt_ref[:, :high], score_grad).T

    @pl.when(step == count - 1)
    def _():
        for n in range(length // rows):
            at = pl.ds(pl.multiple_of(order_ref[n] * rows, rows), rows)
            to = slice(n * rows, (n + 1) * rows)
            cos_table, sin_table = cos_ref[at, :], -sin_ref[at, :]
            out_ref[to, :HEAD_DIM] = turn(dq_ref[at, :] * scale, cos_table, sin_table).astype(BF16)
            out_ref[to, HEAD_DIM : 2 * HEAD_DIM] = turn(
                dk_ref[at, :] * scale, cos_table, sin_table
            ).astype(BF16)
            out_ref[to, 2 * HEAD_DIM :] = dv_ref[at, :].astype(BF16)


def attend_back(query, key, value, grad, lse, first_place, cos_table, sin_table, order):
    length = query.shape[0]
    block = min(256, length)
    whole = lambda shape: pl.BlockSpec(shape, lambda i, order: (0, 0))
    head = whole((length, HEAD_DIM))
    return pl.pallas_call(
        functools.partial(attend_back_kernel, block, length // order.shape[0]),
        out_shape=jax.ShapeDtypeStruct((length, 3 * HEAD_DIM), BF16),
        grid_spec=pltpu.PrefetchScalarGridSpec(
            num_scalar_prefetch=1,
            grid=(length // block,),
            in_specs=[head] * 4 + [whole((1, length))] * 2 + [head] * 2,
            out_specs=whole((length, 3 * HEAD_DIM)),
            scratch_shapes=[pltpu.VMEM((HEAD_DIM, length), BF16)]
            + [pltpu.VMEM((length, HEAD_DIM), F32)] * 3,
        ),
        compiler_params=pltpu.CompilerParams(vmem_limit_bytes=48 * 2**20),
        name="attend_back",
    )(order, query, key, value, grad, lse, first_place, cos_table, sin_table)


def dp_gather(value):
    count = lax.axis_size("dp")
    if count == 1:
        return value[None]
    here = lax.axis_index("dp")
    parts = [value] + [
        lax.ppermute(value, "dp", [(i, (i - step) % count) for i in range(count)])
        for step in range(1, count)
    ]
    if count == 2:
        first = here == 0
        return jnp.stack(
            [jnp.where(first, parts[0], parts[1]), jnp.where(first, parts[1], parts[0])]
        )
    whole = jnp.zeros((count,) + value.shape, value.dtype)
    for step, part in enumerate(parts):
        whole = lax.dynamic_update_index_in_dim(whole, part, (here + step) % count, 0)
    return whole


def dp_scatter(value):
    count = lax.axis_size("dp")
    here = lax.axis_index("dp")
    total = lax.dynamic_index_in_dim(value, here, 0, keepdims=False)
    for step in range(1, count):
        block = lax.dynamic_index_in_dim(value, (here + step) % count, 0, keepdims=False)
        got = lax.ppermute(
            block.astype(BF16), "dp", [(i, (i + step) % count) for i in range(count)]
        )
        total = total + got.astype(F32)
    return total


def ring_order():
    pairs = lax.axis_size("expert") // 2
    return list(range(0, pairs, 2)) + list(range(pairs - 1, 0, -2))


def ring_shift(value, step):
    order = ring_order()
    pairs = len(order)
    perm = [
        (order[q] * 2 + c, order[(q + step) % pairs] * 2 + c) for q in range(pairs) for c in range(2)
    ]
    return lax.ppermute(value, "expert", perm)


def core_swap(value):
    count = lax.axis_size("expert")
    return lax.ppermute(value, "expert", [(i, i ^ 1) for i in range(count)])


def ring_offsets():
    half = lax.axis_size("expert") // 4
    return [0] + [o for step in range(1, half) for o in (step, -step)] + [half]


def ring_blocks():
    order = ring_order()
    pairs = len(order)
    table = [[0] * (2 * pairs) for _ in range(2 * pairs)]
    for q in range(pairs):
        for c in range(2):
            for j, offset in enumerate(ring_offsets()):
                for other in range(2):
                    table[order[q] * 2 + c][2 * j + other] = (
                        order[(q - offset) % pairs] * 2 + (c ^ other)
                    )
    return lax.dynamic_index_in_dim(
        jnp.asarray(table, jnp.int32), lax.axis_index("expert"), 0, keepdims=False
    )


def tied(value, *tokens):
    firsts = [lax.slice(t, (0,) * t.ndim, (1,) * t.ndim).reshape(()) for t in tokens]
    token = sum(t.astype(F32) for t in firsts) * 0.0
    return (value.astype(F32) * (1.0 + token)).astype(value.dtype)


def ring_gather(value, gates=None):
    gates = gates or {}
    half_rows = value.shape[0] // 2
    half = lax.axis_size("expert") // 4
    blocks = {}

    def keep(parts, offset):
        blocks[offset] = (parts, [core_swap(part) for part in parts])

    keep([value], 0)
    ahead = back = value
    for step in range(1, half):
        if step in gates:
            token = gates[step](blocks)
            ahead, back = tied(ahead, *token), tied(back, *token)
        ahead, back = ring_shift(ahead, 1), ring_shift(back, -1)
        keep([ahead], step)
        keep([back], -step)
    if half in gates:
        token = gates[half](blocks)
        ahead, back = tied(ahead, *token), tied(back, *token)
    last = [ring_shift(ahead[:half_rows], 1), ring_shift(back[half_rows:], -1)]
    keep(last, half)
    return [parts for offset in ring_offsets() for parts in blocks[offset]]


def flatten(blocks):
    pieces = [piece for parts in blocks for piece in parts]
    sources, n = [], 0
    for parts in blocks:
        sources.append(tuple(range(n, n + len(parts))))
        n += len(parts)
    return pieces, tuple(sources)


def ring_scatter(block, gates=None, marks=None):
    gates = gates or {}
    half = lax.axis_size("expert") // 4
    offsets = ring_offsets()
    spare = {}

    def mine(offset):
        if offset not in spare:
            j = offsets.index(offset)
            spare[offset] = block(2 * j).astype(F32) + core_swap(block(2 * j + 1)).astype(F32)
        return spare[offset]

    far = mine(half).astype(BF16)
    half_rows = far.shape[0] // 2
    ahead = ring_shift(far[:half_rows], 1)
    back = ring_shift(far[half_rows:], -1)
    if marks is not None:
        marks.extend([ahead, back])
    for step in range(half - 1, 0, -1):
        onward, homeward = mine(-step), mine(step)
        if step == half - 1:
            onward = jnp.concatenate(
                [onward[:half_rows] + ahead.astype(F32), onward[half_rows:]], axis=0
            )
            homeward = jnp.concatenate(
                [homeward[:half_rows], homeward[half_rows:] + back.astype(F32)], axis=0
            )
        else:
            onward = onward + ahead.astype(F32)
            homeward = homeward + back.astype(F32)
        if half - step in gates:
            onward, homeward = tied(onward, *gates[half - step]), tied(homeward, *gates[half - step])
        ahead = ring_shift(onward.astype(BF16), 1)
        back = ring_shift(homeward.astype(BF16), -1)
    return mine(0) + ahead.astype(F32) + back.astype(F32)


def chosen(pos_ref, base, window):
    count = pos_ref.shape[-1]
    row = base + lax.broadcasted_iota(jnp.int32, (window, count), 0)
    return row == pos_ref[0]


def dispatch_kernel(sources, widths, window, base_ref, order_ref, pos_ref, gate_ref, *refs):
    outs = refs[-len(widths) - 2 :]
    pieces, blocks, rows_ref, weights_ref = refs[: -len(outs)], outs[:-2], outs[-2], outs[-1]
    step = pl.program_id(0)

    @pl.when(step == 0)
    def _():
        rows_ref[...] = jnp.zeros_like(rows_ref)
        weights_ref[...] = jnp.zeros_like(weights_ref)

    for n, parts in enumerate(sources):

        @pl.when(step == n)
        def _(parts=parts):
            low = 0
            for part in parts:
                size = pieces[part].shape[0]
                left = 0
                for block, wide in zip(blocks, widths):
                    block[low : low + size, :] = pieces[part][:, left : left + wide]
                    left += wide
                low += size

    base = pl.multiple_of(base_ref[step], 16)
    pick = chosen(pos_ref, base, window)
    at = pl.ds(base, window)
    found = dot(pick.astype(F32).astype(BF16), (blocks or pieces)[0][...])
    rows_ref[at, :] = (rows_ref[at, :].astype(F32) + found).astype(BF16)
    weights_ref[at, :] += jnp.sum(jnp.where(pick, gate_ref[0], 0.0), axis=1, keepdims=True)


def dispatch(blocks, widths, packing, order, gates):
    base, pos, _, window, packed = packing
    count, _, rows = pos.shape
    if isinstance(blocks, list):
        pieces, sources = flatten(blocks)
        piece_specs = [pl.BlockSpec(piece.shape, lambda i, base, order: (0, 0)) for piece in pieces]
    else:
        pieces, sources, widths = [blocks], (), []
        piece_specs = [pl.BlockSpec((rows, blocks.shape[1]), lambda i, base, order: (order[i], 0))]
    width = (widths or [pieces[0].shape[1]])[0]
    return pl.pallas_call(
        functools.partial(dispatch_kernel, sources, tuple(widths), window),
        out_shape=[jax.ShapeDtypeStruct((rows * count, wide), BF16) for wide in widths]
        + [
            jax.ShapeDtypeStruct((packed, width), BF16),
            jax.ShapeDtypeStruct((packed, 1), F32),
        ],
        grid_spec=pltpu.PrefetchScalarGridSpec(
            num_scalar_prefetch=2,
            grid=(count,),
            in_specs=[
                pl.BlockSpec((1, 1, rows), lambda i, base, order: (i, 0, 0)),
                pl.BlockSpec((1, 1, rows), lambda i, base, order: (order[i], 0, 0)),
            ]
            + piece_specs,
            out_specs=[
                pl.BlockSpec((rows, wide), lambda i, base, order: (order[i], 0)) for wide in widths
            ]
            + [
                pl.BlockSpec((packed, width), lambda i, base, order: (0, 0)),
                pl.BlockSpec((packed, 1), lambda i, base, order: (0, 0)),
            ],
        ),
        compiler_params=pltpu.CompilerParams(vmem_limit_bytes=52 * 2**20),
        name="dispatch",
    )(base, order, pos, gates, *pieces)


def expert_kernel(ups, total_ref, starts_ref, x_ref, g_ref, gate_ref, *refs):
    parts, refs = refs[:-9], refs[-9:]
    wy_ref, dn_ref, ea_ref, dy_ref, db_ref, dg_ref, up_ref, down_ref, sems = refs
    step = pl.program_id(0)
    rows, hidden = ea_ref.shape
    some = step * rows < total_ref[0]

    @pl.when(step == 0)
    def _():
        copies = []
        for n, part in enumerate(parts):
            at = pl.ds(pl.multiple_of(starts_ref[n], 16), part.shape[0])
            whole = up_ref if n < ups else down_ref
            copies.append(pltpu.make_async_copy(part, whole.at[at, :], sems.at[n]))
        for copy in copies:
            copy.start()
        for copy in copies:
            copy.wait()

    @pl.when(some)
    def _():
        pre = dot(x_ref[...], up_ref[...])
        gate_part, up_part = pre[:, :hidden], pre[:, hidden:]
        sigmoid_gate = 1.0 / (1.0 + jnp.exp(-gate_part))
        silu = gate_part * sigmoid_gate
        act = (silu * up_part).astype(BF16)
        ea_ref[...] = act
        result = dot(act, down_ref[...]).astype(BF16).astype(F32)
        grad = g_ref[...].astype(F32)
        gate = gate_ref[...]
        dg_ref[...] = jnp.sum(grad * result, axis=1, keepdims=True)
        wy_ref[...] = (gate * result).astype(BF16)
        out_grad = (gate * grad).astype(BF16)
        dy_ref[...] = out_grad
        act_grad = dot_nt(out_grad, down_ref[...])
        db_ref[:, :hidden] = (
            act_grad * up_part * sigmoid_gate * (1.0 + gate_part * (1.0 - sigmoid_gate))
        ).astype(BF16)
        db_ref[:, hidden:] = (act_grad * silu).astype(BF16)
        dn_ref[...] = dot_nt(db_ref[...], up_ref[...]).astype(BF16)

    @pl.when(jnp.logical_not(some))
    def _():
        for ref in (wy_ref, dn_ref, ea_ref, dy_ref, db_ref, dg_ref):
            ref[...] = jnp.zeros_like(ref)


def expert(total, rows, grads, gates, ups, downs):
    packed, width = rows.shape
    hidden = sum(part.shape[0] for part, _ in downs)
    tile = 256
    parts = [part for part, _ in ups + downs]
    starts = jnp.stack([start for _, start in ups + downs]).astype(jnp.int32)
    spec = lambda wide: pl.BlockSpec((tile, wide), lambda i, total, starts: (i, 0))
    widths = (width, width, hidden, width, 2 * hidden)
    return pl.pallas_call(
        functools.partial(expert_kernel, len(ups)),
        out_shape=[jax.ShapeDtypeStruct((packed, wide), BF16) for wide in widths]
        + [jax.ShapeDtypeStruct((packed, 1), F32)],
        grid_spec=pltpu.PrefetchScalarGridSpec(
            num_scalar_prefetch=2,
            grid=(packed // tile,),
            in_specs=[spec(width), spec(width), spec(1)]
            + [pl.BlockSpec(memory_space=pl.ANY)] * len(parts),
            out_specs=[spec(wide) for wide in widths] + [spec(1)],
            scratch_shapes=[
                pltpu.VMEM((width, 2 * hidden), BF16),
                pltpu.VMEM((hidden, width), BF16),
                pltpu.SemaphoreType.DMA((len(parts),)),
            ],
        ),
        compiler_params=pltpu.CompilerParams(vmem_limit_bytes=58 * 2**20),
        name="expert",
    )(total, starts, rows, grads, gates, *parts)


def combine_kernel(turned, window, extra, base_ref, order_ref, to_ref, me_ref, pos_ref, rows_ref, dg_ref, act_ref, weight_ref, out_ref):
    mul = dot_nt if turned else dot
    base = pl.multiple_of(base_ref[pl.program_id(0)], 16)
    pick = chosen(pos_ref, base, window)
    at = pl.ds(base, window)
    width = rows_ref.shape[1]
    out_ref[:, :width] = (
        dot_tn(pick.astype(F32).astype(BF16), rows_ref[at, :]) + mul(act_ref[...], weight_ref[...])
    ).astype(BF16)
    if extra:
        count = pick.shape[1]
        line = jnp.sum(jnp.where(pick, dg_ref[at, :], 0.0), axis=0, keepdims=True)
        row = lax.broadcasted_iota(jnp.int32, (count, count), 0)
        lane = lax.broadcasted_iota(jnp.int32, (count, count), 1)
        column = jnp.sum(jnp.where(row == lane, line, 0.0), axis=1, keepdims=True)
        high = column.astype(BF16).astype(F32)
        lane = lax.broadcasted_iota(jnp.int32, (count, extra), 1)
        out_ref[:, width:] = jnp.where(
            lane == me_ref[0], high, jnp.where(lane == me_ref[0] + extra // 2, column - high, 0.0)
        ).astype(BF16)


def combine(packing, order, to, me, rows, dg, act, weight, turned, extra):
    base, pos, _, window, packed = packing
    blocks, _, count = pos.shape
    width = rows.shape[-1]
    whole = lambda ref: pl.BlockSpec(ref.shape, lambda i, *_: (0, 0))
    return pl.pallas_call(
        functools.partial(combine_kernel, turned, window, extra),
        out_shape=jax.ShapeDtypeStruct((blocks * count, width + extra), BF16),
        grid_spec=pltpu.PrefetchScalarGridSpec(
            num_scalar_prefetch=4,
            grid=(blocks,),
            in_specs=[
                pl.BlockSpec((1, 1, count), lambda i, *_: (i, 0, 0)),
                whole(rows),
                whole(dg),
                pl.BlockSpec((count, act.shape[1]), lambda i, base, order, to, me: (order[i], 0)),
                whole(weight),
            ],
            out_specs=pl.BlockSpec(
                (count, width + extra), lambda i, base, order, to, me: (to[i], 0)
            ),
        ),
        compiler_params=pltpu.CompilerParams(vmem_limit_bytes=40 * 2**20),
        name="combine",
    )(base, order, to, me.reshape(1), pos, rows, dg, act, weight)


def gather_all(value):
    return lax.all_gather(value, "expert", axis=0, tiled=True)


def swap(value):
    return lax.all_to_all(value, "expert", split_axis=0, concat_axis=0, tiled=True)


def per_device(
    tokens,
    cotangent,
    segment_ids,
    routes,
    attn_in,
    attn_out,
    gain_attn,
    shared_in,
    shared_out,
    router,
    gain_ffn,
    expert_in,
    expert_out,
):
    n_dp, n_e = lax.axis_size("dp"), lax.axis_size("expert")
    me = lax.axis_index("expert")
    count, width = tokens.shape
    segments = segment_ids[0]
    length = segments.shape[0]
    rows = attn_in.shape[0]
    capacity = min(count, 3 * TOP * count // (2 * n_e))
    shared_rows = shared_out.shape[0]
    shared_width = shared_rows * n_dp
    expert_width = expert_out.shape[1] * n_dp

    order = ring_blocks()
    steady = jnp.arange(n_e, dtype=jnp.int32)
    hidden_in = tokens.astype(F32)
    inverse_one = lax.rsqrt(jnp.mean(hidden_in * hidden_in, axis=-1, keepdims=True) + EPS)
    normed_one = hidden_in * inverse_one
    gain_rows = gain_attn.astype(F32)[:, None]
    head_w = []

    def head_sent(blocks):
        own = (attn_in.astype(F32) * tied(gain_rows, blocks[0][1][0])).astype(BF16)
        own = own.reshape(rows, 3, n_e, HEAD_DIM).transpose(2, 0, 1, 3)
        head_w.append(swap(own.reshape(n_e, rows, 3 * HEAD_DIM)))
        return head_w[0]

    def head_whole(blocks):
        head_w.append(dp_gather(head_w[0]).reshape(width, 3 * HEAD_DIM))
        return head_w[1]

    here = lax.axis_index("dp")

    def spread(shard, chunks):
        while shard.shape[0] % (16 * chunks):
            chunks -= 1
        size = shard.shape[0] // chunks
        parts = [[(shard, here * shard.shape[0])]]
        for j in range(chunks):
            parts.append([])
            for step in range(1, n_dp):
                got = lax.ppermute(
                    shard[j * size : (j + 1) * size],
                    "dp",
                    [(i, (i - step) % n_dp) for i in range(n_dp)],
                )
                parts[-1].append((got, (here + step) % n_dp * shard.shape[0] + j * size))
        return parts

    up_parts = spread(expert_in[0], max(1, min(4, expert_in.shape[1] // 256)))
    down_parts = spread(expert_out[0], 2)
    first = lambda parts: [part for part, _ in parts]
    up_tokens = [first(parts) for parts in up_parts[1:]] + [[]] * 4

    small = jnp.concatenate([router, gain_ffn[:, None]], axis=1)
    small = dp_gather(small).reshape(-1, n_e + 1)
    extra_rows = 32
    extra = jnp.concatenate([small.T, routes.T.astype(BF16)], axis=0)
    extra = jnp.pad(extra, ((0, extra_rows - extra.shape[0]), (0, 0)))
    extra = jnp.broadcast_to(extra, (n_e,) + extra.shape)
    cos_table, sin_table, first_place = rope_tables(segments)
    share_w = shared_in.reshape(rows, 2, n_dp, n_e, shared_rows).transpose(3, 0, 1, 2, 4)
    share_w = share_w.reshape(n_e, rows, 2 * shared_width)

    half = n_e // 4
    norm_blocks = ring_gather(
        normed_one.astype(BF16),
        {
            half - 1: lambda blocks: [head_sent(blocks)] + up_tokens[0],
            half: lambda blocks: [head_whole(blocks), cos_table, sin_table, extra, share_w],
        },
    )
    head_sent_w, head_w = head_w

    head_out, query, key, value, lse, norm_all = attend(
        norm_blocks, order, head_w, cos_table, sin_table, first_place
    )
    mixed = jnp.concatenate([head_out.reshape(n_e, count, HEAD_DIM), extra], axis=1)
    mixed = swap(tied(mixed, *up_tokens[1]) if up_tokens[1] else mixed)
    small = mixed[:, count:]
    mixed = mixed[:, :count].transpose(1, 0, 2).reshape(count, n_dp, n_e, rows)
    mixed = mixed.transpose(0, 2, 1, 3).reshape(count, width)
    share_w = swap(tied(share_w, lse))
    proj_all = dp_gather(attn_out).reshape(n_dp * rows, width)
    proj_all = gather_all(tied(proj_all, norm_blocks[-3][0], norm_blocks[-5][0]))
    routes_all = small[:, n_e + 1 : n_e + 1 + TOP].astype(F32)
    small = small[:, : n_e + 1].reshape(n_e, n_e + 1, n_dp, rows).transpose(1, 2, 0, 3)
    small = small.reshape(n_e + 1, width)
    router_full = small[:n_e]
    gain_second = small[n_e].astype(F32)
    cot_all = gather_all(tied(cotangent, lse))

    share_sent = share_w
    share_w = dp_gather(share_w).reshape(width, 2 * shared_width)
    share_out = dp_gather(shared_out).reshape(shared_width, width)
    resid = hidden_in + dot(mixed, proj_all)
    if up_tokens[2]:
        resid = tied(resid, *up_tokens[2])

    inverse_two = lax.rsqrt(jnp.mean(resid * resid, axis=-1, keepdims=True) + EPS)
    normed_two = resid * inverse_two
    norm_two = (normed_two * gain_second).astype(BF16)
    logits = dot_nt(norm_two, router_full)
    picked = jnp.any(routes[:, :, None] == jnp.arange(n_e)[None, None, :], axis=1)
    chosen = jnp.where(picked, logits, NEG)
    chosen = jnp.where(picked, jnp.exp(chosen - jnp.max(chosen, axis=-1, keepdims=True)), 0.0)
    gates = chosen / jnp.sum(chosen, axis=-1, keepdims=True)
    gate_high = gates.astype(BF16)
    gate_low = (gates - gate_high.astype(F32)).astype(BF16)
    blank = jnp.zeros((count, 128 - 2 * n_e), BF16)
    payload = jnp.concatenate([norm_two, gate_high, gate_low, blank], axis=1)
    norm_blocks = ring_gather(
        payload,
        {
            half - 2: lambda blocks: [share_sent] + up_tokens[3],
            half: lambda blocks: first(down_parts[1]),
        },
    )

    named = jnp.any(routes_all == me.astype(F32), axis=1)
    named = jnp.take(named, order, axis=0)
    ranking = jnp.cumsum(named.astype(jnp.int32), axis=1)
    ends = jnp.cumsum(ranking[:, -1])
    begins = ends - ranking[:, -1]
    pos = jnp.where(named, begins[:, None] + ranking - 1, -1)[:, None, :]
    window = -(-(capacity + 15) // 16) * 16
    packed = -(-(n_e * capacity + 32) // 256) * 256
    packing = (begins // 16 * 16, pos, ends[-1:], window, packed)
    norm_two_all, payload, arrived, _ = dispatch(
        norm_blocks, [width, 128], packing, order, jnp.zeros((n_e, 1, count), F32)
    )
    mine = jnp.arange(n_e) == me
    gate_all = payload[:, : 2 * n_e].astype(F32).reshape(length, 2, n_e)
    gate_all = jnp.sum(jnp.where(mine, gate_all, 0.0), axis=(1, 2)).reshape(n_e, 1, count)
    cot_rows, gate_rows = dispatch(cot_all, None, packing, order, gate_all)
    weighted, row_grad, expert_act, route_grad, pre_grad, gate_grad = expert(
        packing[2],
        arrived,
        cot_rows,
        gate_rows,
        [part for parts in up_parts for part in parts],
        [part for parts in down_parts for part in parts],
    )

    shared_pre = dot(norm_two_all, share_w)
    shared_act = (
        jax.nn.silu(shared_pre[:, :shared_width]) * shared_pre[:, shared_width:]
    ).astype(BF16)
    shared_act_grad = dot_nt(cot_all, share_out)
    shared_pre_grad = silu_back(
        shared_act_grad, shared_pre[:, :shared_width], shared_pre[:, shared_width:]
    ).astype(BF16)
    norm_two_part = combine(
        packing, order, steady, me, row_grad, gate_grad, shared_pre_grad, share_w, True, 128
    )
    norm_two_grad = ring_scatter(
        lambda n: norm_two_part[n * count : (n + 1) * count]
    )
    gate_grad = norm_two_grad[:, width : width + n_e] + norm_two_grad[:, width + 64 : width + 64 + n_e]
    norm_two_grad = norm_two_grad[:, :width]
    out_part = combine(
        packing, order, order, me, weighted, gate_rows, shared_act, share_out, False, 0
    )
    routed_out = lax.psum_scatter(out_part, "expert", scatter_dimension=0, tiled=True)

    def shard_grads(left, right, chunks):
        size = left.shape[1] // n_dp
        part = size // chunks
        cut = lambda start, wide: lax.dynamic_slice_in_dim(left, start, wide, 1)
        got = [
            [
                lax.ppermute(
                    dot_tn(cut((here + step) % n_dp * size + j * part, part), right).astype(BF16),
                    "dp",
                    [(i, (i + step) % n_dp) for i in range(n_dp)],
                )
                for step in range(1, n_dp)
            ]
            for j in range(chunks)
        ]
        return dot_tn(cut(here * size, size), right), got

    def shard_sum(own, got, tokens):
        part = own.shape[0] // len(got)
        own = own[None]
        for j, (parts, token) in enumerate(zip(got, tokens)):
            block = sum(tied(p.astype(F32), token) for p in parts)[None]
            block = own[:, j * part : (j + 1) * part] + block
            own = lax.dynamic_update_slice_in_dim(own, block, j * part, 1)
        return own

    down_own, down_got = shard_grads(expert_act, route_grad, 2)
    up_own, up_got = shard_grads(arrived, pre_grad, len(up_parts) - 1)

    share_out_grad = dp_scatter(dot_tn(shared_act, cot_all).reshape(n_dp, shared_rows, width))
    share_in_grad = dot_tn(norm_two_all, shared_pre_grad)
    share_in_grad = dp_scatter(share_in_grad.reshape(n_dp, n_e, rows, 2 * shared_width))
    share_in_grad = swap(share_in_grad.astype(BF16)).astype(F32)
    share_in_grad = (
        share_in_grad.reshape(n_e, rows, 2, n_dp, shared_rows)
        .transpose(1, 2, 3, 0, 4)
        .reshape(rows, -1)
    )

    logit_grad = gates * (gate_grad - jnp.sum(gates * gate_grad, axis=-1, keepdims=True))
    router_grad = jnp.dot(
        logit_grad.T, norm_two.astype(F32), precision=HIGHEST, preferred_element_type=F32
    )
    norm_two_grad = norm_two_grad + jnp.dot(
        logit_grad, router_full.astype(F32), precision=HIGHEST, preferred_element_type=F32
    )
    gain_two_grad = jnp.sum(norm_two_grad * normed_two, axis=0)
    upstream = tied(cotangent.astype(F32), *down_got[0])
    scaled_two = norm_two_grad * gain_second
    resid_grad = upstream + inverse_two * (
        scaled_two - normed_two * jnp.mean(scaled_two * normed_two, axis=-1, keepdims=True)
    )
    small_grad = jnp.concatenate([router_grad, gain_two_grad[None]], axis=0)
    small_grad = jnp.pad(small_grad, ((0, HEAD_DIM - n_e - 1), (0, 0))).T

    branch_cot = resid_grad.astype(BF16)
    proj_grad = dot_tn(mixed, branch_cot).astype(BF16)
    mixed_grad = tied(dot_nt(branch_cot, proj_all), *down_got[1]).astype(BF16)
    mixed_grad = mixed_grad.reshape(count, n_e, n_dp, rows).transpose(0, 2, 1, 3)
    mixed_grad = swap(mixed_grad.reshape(count, n_e, HEAD_DIM).transpose(1, 0, 2))
    mixed_grad = mixed_grad.reshape(length, HEAD_DIM)
    proj_grad = lax.psum_scatter(proj_grad, "expert", scatter_dimension=0, tiled=True)
    attn_out_grad = dp_scatter(proj_grad.astype(F32).reshape(n_dp, rows, width))
    qkv_grad = attend_back(
        query, key, value, mixed_grad, lse, first_place, cos_table, sin_table, order
    )
    norm_one_part = dot_nt(qkv_grad, head_w).astype(BF16)
    scaled_one = ring_scatter(
        lambda n: norm_one_part[n * count : (n + 1) * count],
        {1: up_got[0], half - 1: up_got[min(1, len(up_got) - 1)]},
    )
    expert_out_grad = shard_sum(down_own, down_got, [norm_two_grad, mixed_grad])
    expert_in_grad = shard_sum(up_own, up_got, ([qkv_grad] + [scaled_one] * 3)[: len(up_got)])
    input_grad = resid_grad + inverse_one * (
        scaled_one - normed_one * jnp.mean(scaled_one * normed_one, axis=-1, keepdims=True)
    )
    wide = 3 * HEAD_DIM
    head_grad = jnp.concatenate([dot_tn(norm_all, qkv_grad), small_grad], axis=1)
    head_grad = dp_scatter(head_grad.reshape(n_dp, n_e, rows, wide + small_grad.shape[1]))
    head_grad = swap(head_grad.astype(BF16)).astype(F32)
    small_grad = jnp.sum(head_grad[:, :, wide:], axis=0)
    head_grad = (
        head_grad[:, :, :wide]
        .reshape(n_e, rows, 3, HEAD_DIM)
        .transpose(1, 2, 0, 3)
        .reshape(rows, 3 * width)
    )
    gain_attn_grad = jnp.sum(head_grad * attn_in.astype(F32), axis=1)
    attn_in_grad = head_grad * gain_rows
    return (
        (resid + routed_out.astype(F32)).astype(BF16),
        input_grad.astype(BF16),
        attn_in_grad,
        attn_out_grad,
        gain_attn_grad,
        share_in_grad,
        share_out_grad,
        small_grad[:, :n_e],
        small_grad[:, n_e],
        expert_in_grad,
        expert_out_grad,
    )


def solution(mesh):
    return jax.shard_map(
        per_device,
        mesh=mesh,
        in_specs=(
            P(("dp", "expert"), None),
            P(("dp", "expert"), None),
            P("dp", None),
            P(("dp", "expert"), None),
            P(("dp", "expert"), None),
            P(("dp", "expert"), None),
            P(("dp", "expert")),
            P(("dp", "expert"), None),
            P(("dp", "expert"), None),
            P(("dp", "expert"), None),
            P(("dp", "expert")),
            P("expert", "dp", None),
            P("expert", "dp", None),
        ),
        out_specs=(
            P(("dp", "expert"), None),
            P(("dp", "expert"), None),
            P(("dp", "expert"), None),
            P(("dp", "expert"), None),
            P(("dp", "expert")),
            P(("dp", "expert"), None),
            P(("dp", "expert"), None),
            P(("dp", "expert"), None),
            P(("dp", "expert")),
            P("expert", "dp", None),
            P("expert", "dp", None),
        ),
        check_vma=False,
    )
```

```python
import functools
import math

import jax
import jax.numpy as jnp
from jax import lax
from jax.experimental import pallas as pl
from jax.experimental.pallas import tpu as pltpu
from jax.sharding import PartitionSpec as P

HEADS = 16
HEAD_DIM = 128
TOP = 6


EPS = 1e-06
THETA = 10000.0
NEG = -1e30
HIGHEST = lax.Precision.HIGHEST
BF16 = jnp.bfloat16
F32 = jnp.float32
LOG2E = math.log2(math.e)


def rope_tables(segments):
    length = segments.shape[0]
    places = jnp.arange(length, dtype=jnp.int32)
    starts = jnp.concatenate([jnp.ones((1,), dtype=jnp.bool_), segments[1:] != segments[:-1]])
    first_place = lax.cummax(jnp.where(starts, places, 0), axis=0)
    offset = (places - first_place).astype(jnp.float32)
    half_dim = HEAD_DIM // 2
    freqs = jnp.exp(jnp.arange(half_dim, dtype=jnp.float32) * (-2.0 * math.log(THETA) / HEAD_DIM))
    angles = offset[:, None] * freqs[None, :]
    cos_table, sin_table = jnp.cos(angles), jnp.sin(angles)
    return (
        jnp.concatenate([cos_table, cos_table], axis=1),
        jnp.concatenate([-sin_table, sin_table], axis=1),
        first_place[None, :],
    )


def silu_back(grad_act, gate_part, up_part):
    sigmoid_gate = jax.nn.sigmoid(gate_part)
    gate_grad = grad_act * up_part * sigmoid_gate * (1.0 + gate_part * (1.0 - sigmoid_gate))
    up_grad = grad_act * gate_part * sigmoid_gate
    return jnp.concatenate([gate_grad, up_grad], axis=-1)


def dot(left, right):
    return jnp.dot(left, right, preferred_element_type=F32)


def dot_tn(left, right):
    return lax.dot_general(left, right, (((0,), (0,)), ((), ())), preferred_element_type=F32)


def dot_nt(left, right):
    return lax.dot_general(left, right, (((1,), (1,)), ((), ())), preferred_element_type=F32)


def turn(values, cos_table, sin_table):
    return values * cos_table + pltpu.roll(values, HEAD_DIM // 2, 1) * sin_table


def attend_kernel(sources, block, order_ref, *refs):
    pieces = refs[: sources[-1][-1] + 1]
    weight_ref, cos_ref, sin_ref, start_ref = refs[len(pieces) : len(pieces) + 4]
    o_ref, q_ref, k_ref, v_ref, lse_ref, rows_ref, vt_ref = refs[len(pieces) + 4 :]
    step = pl.program_id(0)
    length = q_ref.shape[0]
    factor = HEAD_DIM ** (-0.5) * LOG2E
    rows = rows_ref.shape[0]

    for n, parts in enumerate(sources):

        @pl.when(step == n)
        def _(parts=parts):
            low = 0
            for part in parts:
                size = pieces[part].shape[0]
                rows_ref[low : low + size, :] = pieces[part][...]
                low += size

    @pl.when(step < len(sources))
    def _():
        qkv = dot(rows_ref[...], weight_ref[...])
        at = pl.ds(pl.multiple_of(order_ref[step] * rows, rows), rows)
        cos_table, sin_table = cos_ref[at, :], sin_ref[at, :]
        q_ref[at, :] = turn(qkv[:, :HEAD_DIM], cos_table, sin_table).astype(BF16)
        k_ref[at, :] = turn(qkv[:, HEAD_DIM : 2 * HEAD_DIM], cos_table, sin_table).astype(BF16)
        value = qkv[:, 2 * HEAD_DIM :]
        v_ref[at, :] = value.astype(BF16)
        vt_ref[:, at] = value.T.astype(BF16)

    for i in range(length // block):

        @pl.when(step == len(sources) + i)
        def _(i=i):
            low, high = i * block, (i + 1) * block
            raw = dot_nt(k_ref[:high, :], q_ref[low:high, :])
            keys = lax.broadcasted_iota(jnp.int32, raw.shape, 0)
            queries = low + lax.broadcasted_iota(jnp.int32, raw.shape, 1)
            allowed = (keys <= queries) & (keys >= start_ref[:, low:high])
            raw = jnp.where(allowed, raw, NEG)
            top = jnp.max(raw, axis=0, keepdims=True)
            shifted = jnp.exp2((raw - top) * factor)
            total = jnp.sum(shifted, axis=0, keepdims=True)
            probs = (shifted * (1.0 / total)).astype(BF16)
            mixed = dot(vt_ref[:, :high], probs)
            o_ref[low:high, :] = mixed.T.astype(BF16)
            lse_ref[:, low:high] = top * factor + jnp.log2(total)


def attend(blocks, order, weight, cos_table, sin_table, first_place):
    pieces, sources = flatten(blocks)
    length = cos_table.shape[0]
    rows = length // len(sources)
    width = weight.shape[0]
    block = min(256, length)
    last = len(sources) - 1
    whole = lambda shape: pl.BlockSpec(shape, lambda i, order: (0, 0))
    head = jax.ShapeDtypeStruct((length, HEAD_DIM), BF16)
    return pl.pallas_call(
        functools.partial(attend_kernel, sources, block),
        out_shape=[head] * 4
        + [jax.ShapeDtypeStruct((1, length), F32), jax.ShapeDtypeStruct((length, width), BF16)],
        grid_spec=pltpu.PrefetchScalarGridSpec(
            num_scalar_prefetch=1,
            grid=(len(sources) + length // block,),
            in_specs=[whole(piece.shape) for piece in pieces]
            + [
                whole(weight.shape),
                whole((length, HEAD_DIM)),
                whole((length, HEAD_DIM)),
                whole((1, length)),
            ],
            out_specs=[whole((length, HEAD_DIM))] * 4
            + [
                whole((1, length)),
                pl.BlockSpec((rows, width), lambda i, order: (jnp.minimum(i, last), 0)),
            ],
            scratch_shapes=[pltpu.VMEM((HEAD_DIM, length), BF16)],
        ),
        compiler_params=pltpu.CompilerParams(vmem_limit_bytes=52 * 2**20),
        name="attend",
    )(order, *pieces, weight, cos_table, sin_table, first_place)


def attend_back_kernel(
    block, rows, order_ref, q_ref, k_ref, v_ref, do_ref, lse_ref, start_ref, cos_ref, sin_ref, out_ref, kt_ref, dq_ref, dk_ref, dv_ref
):
    length = q_ref.shape[0]
    step = pl.program_id(0)
    scale = HEAD_DIM ** (-0.5)
    factor = scale * LOG2E
    count = length // block

    @pl.when(step == 0)
    def _():
        kt_ref[...] = k_ref[...].astype(F32).T.astype(BF16)
        dk_ref[...] = jnp.zeros_like(dk_ref)
        dv_ref[...] = jnp.zeros_like(dv_ref)

    for i in range(count):

        @pl.when(step == i)
        def _(i=i):
            low, high = i * block, (i + 1) * block
            query, grad = q_ref[low:high, :], do_ref[low:high, :]
            raw = dot_nt(k_ref[:high, :], query)
            keys = lax.broadcasted_iota(jnp.int32, raw.shape, 0)
            queries = low + lax.broadcasted_iota(jnp.int32, raw.shape, 1)
            allowed = (keys <= queries) & (keys >= start_ref[:, low:high])
            raw = jnp.where(allowed, raw * factor - lse_ref[:, low:high], NEG)
            probs = jnp.exp2(raw)
            probs_grad = dot_nt(v_ref[:high, :], grad)
            inner = jnp.sum(probs_grad * probs, axis=0, keepdims=True)
            score_grad = (probs * (probs_grad - inner)).astype(BF16)
            dv_ref[:high, :] += dot(probs.astype(BF16), grad)
            dk_ref[:high, :] += dot(score_grad, query)
            dq_ref[low:high, :] = dot(kt_ref[:, :high], score_grad).T

    @pl.when(step == count - 1)
    def _():
        for n in range(length // rows):
            at = pl.ds(pl.multiple_of(order_ref[n] * rows, rows), rows)
            to = slice(n * rows, (n + 1) * rows)
            cos_table, sin_table = cos_ref[at, :], -sin_ref[at, :]
            out_ref[to, :HEAD_DIM] = turn(dq_ref[at, :] * scale, cos_table, sin_table).astype(BF16)
            out_ref[to, HEAD_DIM : 2 * HEAD_DIM] = turn(
                dk_ref[at, :] * scale, cos_table, sin_table
            ).astype(BF16)
            out_ref[to, 2 * HEAD_DIM :] = dv_ref[at, :].astype(BF16)


def attend_back(query, key, value, grad, lse, first_place, cos_table, sin_table, order):
    length = query.shape[0]
    block = min(256, length)
    whole = lambda shape: pl.BlockSpec(shape, lambda i, order: (0, 0))
    head = whole((length, HEAD_DIM))
    return pl.pallas_call(
        functools.partial(attend_back_kernel, block, length // order.shape[0]),
        out_shape=jax.ShapeDtypeStruct((length, 3 * HEAD_DIM), BF16),
        grid_spec=pltpu.PrefetchScalarGridSpec(
            num_scalar_prefetch=1,
            grid=(length // block,),
            in_specs=[head] * 4 + [whole((1, length))] * 2 + [head] * 2,
            out_specs=whole((length, 3 * HEAD_DIM)),
            scratch_shapes=[pltpu.VMEM((HEAD_DIM, length), BF16)]
            + [pltpu.VMEM((length, HEAD_DIM), F32)] * 3,
        ),
        compiler_params=pltpu.CompilerParams(vmem_limit_bytes=48 * 2**20),
        name="attend_back",
    )(order, query, key, value, grad, lse, first_place, cos_table, sin_table)


def dp_gather(value):
    count = lax.axis_size("dp")
    if count == 1:
        return value[None]
    here = lax.axis_index("dp")
    parts = [value] + [
        lax.ppermute(value, "dp", [(i, (i - step) % count) for i in range(count)])
        for step in range(1, count)
    ]
    if count == 2:
        first = here == 0
        return jnp.stack(
            [jnp.where(first, parts[0], parts[1]), jnp.where(first, parts[1], parts[0])]
        )
    whole = jnp.zeros((count,) + value.shape, value.dtype)
    for step, part in enumerate(parts):
        whole = lax.dynamic_update_index_in_dim(whole, part, (here + step) % count, 0)
    return whole


def dp_scatter(value):
    count = lax.axis_size("dp")
    here = lax.axis_index("dp")
    total = lax.dynamic_index_in_dim(value, here, 0, keepdims=False)
    for step in range(1, count):
        block = lax.dynamic_index_in_dim(value, (here + step) % count, 0, keepdims=False)
        got = lax.ppermute(
            block.astype(BF16), "dp", [(i, (i + step) % count) for i in range(count)]
        )
        total = total + got.astype(F32)
    return total


def ring_order():
    pairs = lax.axis_size("expert") // 2
    return list(range(0, pairs, 2)) + list(range(pairs - 1, 0, -2))


def ring_shift(value, step):
    order = ring_order()
    pairs = len(order)
    perm = [
        (order[q] * 2 + c, order[(q + step) % pairs] * 2 + c) for q in range(pairs) for c in range(2)
    ]
    return lax.ppermute(value, "expert", perm)


def core_swap(value):
    count = lax.axis_size("expert")
    return lax.ppermute(value, "expert", [(i, i ^ 1) for i in range(count)])


def ring_offsets():
    half = lax.axis_size("expert") // 4
    return [0] + [o for step in range(1, half) for o in (step, -step)] + [half]


def ring_blocks():
    order = ring_order()
    pairs = len(order)
    table = [[0] * (2 * pairs) for _ in range(2 * pairs)]
    for q in range(pairs):
        for c in range(2):
            for j, offset in enumerate(ring_offsets()):
                for other in range(2):
                    table[order[q] * 2 + c][2 * j + other] = (
                        order[(q - offset) % pairs] * 2 + (c ^ other)
                    )
    return lax.dynamic_index_in_dim(
        jnp.asarray(table, jnp.int32), lax.axis_index("expert"), 0, keepdims=False
    )


def tied(value, *tokens):
    firsts = [lax.slice(t, (0,) * t.ndim, (1,) * t.ndim).reshape(()) for t in tokens]
    token = sum(t.astype(F32) for t in firsts) * 0.0
    return (value.astype(F32) * (1.0 + token)).astype(value.dtype)


def ring_gather(value, gates=None):
    gates = gates or {}
    half_rows = value.shape[0] // 2
    half = lax.axis_size("expert") // 4
    blocks = {}

    def keep(parts, offset):
        blocks[offset] = (parts, [core_swap(part) for part in parts])

    keep([value], 0)
    ahead = back = value
    for step in range(1, half):
        if step in gates:
            token = gates[step](blocks)
            ahead, back = tied(ahead, *token), tied(back, *token)
        ahead, back = ring_shift(ahead, 1), ring_shift(back, -1)
        keep([ahead], step)
        keep([back], -step)
    if half in gates:
        token = gates[half](blocks)
        ahead, back = tied(ahead, *token), tied(back, *token)
    last = [ring_shift(ahead[:half_rows], 1), ring_shift(back[half_rows:], -1)]
    keep(last, half)
    return [parts for offset in ring_offsets() for parts in blocks[offset]]


def flatten(blocks):
    pieces = [piece for parts in blocks for piece in parts]
    sources, n = [], 0
    for parts in blocks:
        sources.append(tuple(range(n, n + len(parts))))
        n += len(parts)
    return pieces, tuple(sources)


def ring_scatter(block, gates=None, marks=None):
    gates = gates or {}
    half = lax.axis_size("expert") // 4
    offsets = ring_offsets()
    spare = {}

    def mine(offset):
        if offset not in spare:
            j = offsets.index(offset)
            spare[offset] = block(2 * j).astype(F32) + core_swap(block(2 * j + 1)).astype(F32)
        return spare[offset]

    far = mine(half).astype(BF16)
    half_rows = far.shape[0] // 2
    ahead = ring_shift(far[:half_rows], 1)
    back = ring_shift(far[half_rows:], -1)
    if marks is not None:
        marks.extend([ahead, back])
    for step in range(half - 1, 0, -1):
        onward, homeward = mine(-step), mine(step)
        if step == half - 1:
            onward = jnp.concatenate(
                [onward[:half_rows] + ahead.astype(F32), onward[half_rows:]], axis=0
            )
            homeward = jnp.concatenate(
                [homeward[:half_rows], homeward[half_rows:] + back.astype(F32)], axis=0
            )
        else:
            onward = onward + ahead.astype(F32)
            homeward = homeward + back.astype(F32)
        if half - step in gates:
            onward, homeward = tied(onward, *gates[half - step]), tied(homeward, *gates[half - step])
        ahead = ring_shift(onward.astype(BF16), 1)
        back = ring_shift(homeward.astype(BF16), -1)
    return mine(0) + ahead.astype(F32) + back.astype(F32)


def chosen(pos_ref, base, window):
    count = pos_ref.shape[-1]
    row = base + lax.broadcasted_iota(jnp.int32, (window, count), 0)
    return row == pos_ref[0]


def dispatch_kernel(sources, widths, window, base_ref, order_ref, pos_ref, gate_ref, *refs):
    outs = refs[-len(widths) - 2 :]
    pieces, blocks, rows_ref, weights_ref = refs[: -len(outs)], outs[:-2], outs[-2], outs[-1]
    step = pl.program_id(0)

    @pl.when(step == 0)
    def _():
        rows_ref[...] = jnp.zeros_like(rows_ref)
        weights_ref[...] = jnp.zeros_like(weights_ref)

    for n, parts in enumerate(sources):

        @pl.when(step == n)
        def _(parts=parts):
            low = 0
            for part in parts:
                size = pieces[part].shape[0]
                left = 0
                for block, wide in zip(blocks, widths):
                    block[low : low + size, :] = pieces[part][:, left : left + wide]
                    left += wide
                low += size

    base = pl.multiple_of(base_ref[step], 16)
    pick = chosen(pos_ref, base, window)
    at = pl.ds(base, window)
    found = dot(pick.astype(F32).astype(BF16), (blocks or pieces)[0][...])
    rows_ref[at, :] = (rows_ref[at, :].astype(F32) + found).astype(BF16)
    weights_ref[at, :] += jnp.sum(jnp.where(pick, gate_ref[0], 0.0), axis=1, keepdims=True)


def dispatch(blocks, widths, packing, order, gates):
    base, pos, _, window, packed = packing
    count, _, rows = pos.shape
    if isinstance(blocks, list):
        pieces, sources = flatten(blocks)
        piece_specs = [pl.BlockSpec(piece.shape, lambda i, base, order: (0, 0)) for piece in pieces]
    else:
        pieces, sources, widths = [blocks], (), []
        piece_specs = [pl.BlockSpec((rows, blocks.shape[1]), lambda i, base, order: (order[i], 0))]
    width = (widths or [pieces[0].shape[1]])[0]
    return pl.pallas_call(
        functools.partial(dispatch_kernel, sources, tuple(widths), window),
        out_shape=[jax.ShapeDtypeStruct((rows * count, wide), BF16) for wide in widths]
        + [
            jax.ShapeDtypeStruct((packed, width), BF16),
            jax.ShapeDtypeStruct((packed, 1), F32),
        ],
        grid_spec=pltpu.PrefetchScalarGridSpec(
            num_scalar_prefetch=2,
            grid=(count,),
            in_specs=[
                pl.BlockSpec((1, 1, rows), lambda i, base, order: (i, 0, 0)),
                pl.BlockSpec((1, 1, rows), lambda i, base, order: (order[i], 0, 0)),
            ]
            + piece_specs,
            out_specs=[
                pl.BlockSpec((rows, wide), lambda i, base, order: (order[i], 0)) for wide in widths
            ]
            + [
                pl.BlockSpec((packed, width), lambda i, base, order: (0, 0)),
                pl.BlockSpec((packed, 1), lambda i, base, order: (0, 0)),
            ],
        ),
        compiler_params=pltpu.CompilerParams(vmem_limit_bytes=52 * 2**20),
        name="dispatch",
    )(base, order, pos, gates, *pieces)


def expert_kernel(ups, total_ref, starts_ref, x_ref, g_ref, gate_ref, *refs):
    parts, refs = refs[:-9], refs[-9:]
    wy_ref, dn_ref, ea_ref, dy_ref, db_ref, dg_ref, up_ref, down_ref, sems = refs
    step = pl.program_id(0)
    rows, hidden = ea_ref.shape
    some = step * rows < total_ref[0]

    @pl.when(step == 0)
    def _():
        copies = []
        for n, part in enumerate(parts):
            at = pl.ds(pl.multiple_of(starts_ref[n], 16), part.shape[0])
            whole = up_ref if n < ups else down_ref
            copies.append(pltpu.make_async_copy(part, whole.at[at, :], sems.at[n]))
        for copy in copies:
            copy.start()
        for copy in copies:
            copy.wait()

    @pl.when(some)
    def _():
        pre = dot(x_ref[...], up_ref[...])
        gate_part, up_part = pre[:, :hidden], pre[:, hidden:]
        sigmoid_gate = 1.0 / (1.0 + jnp.exp(-gate_part))
        silu = gate_part * sigmoid_gate
        act = (silu * up_part).astype(BF16)
        ea_ref[...] = act
        result = dot(act, down_ref[...]).astype(BF16).astype(F32)
        grad = g_ref[...].astype(F32)
        gate = gate_ref[...]
        dg_ref[...] = jnp.sum(grad * result, axis=1, keepdims=True)
        wy_ref[...] = (gate * result).astype(BF16)
        out_grad = (gate * grad).astype(BF16)
        dy_ref[...] = out_grad
        act_grad = dot_nt(out_grad, down_ref[...])
        db_ref[:, :hidden] = (
            act_grad * up_part * sigmoid_gate * (1.0 + gate_part * (1.0 - sigmoid_gate))
        ).astype(BF16)
        db_ref[:, hidden:] = (act_grad * silu).astype(BF16)
        dn_ref[...] = dot_nt(db_ref[...], up_ref[...]).astype(BF16)

    @pl.when(jnp.logical_not(some))
    def _():
        for ref in (wy_ref, dn_ref, ea_ref, dy_ref, db_ref, dg_ref):
            ref[...] = jnp.zeros_like(ref)


def expert(total, rows, grads, gates, ups, downs):
    packed, width = rows.shape
    hidden = sum(part.shape[0] for part, _ in downs)
    tile = 256
    parts = [part for part, _ in ups + downs]
    starts = jnp.stack([start for _, start in ups + downs]).astype(jnp.int32)
    spec = lambda wide: pl.BlockSpec((tile, wide), lambda i, total, starts: (i, 0))
    widths = (width, width, hidden, width, 2 * hidden)
    return pl.pallas_call(
        functools.partial(expert_kernel, len(ups)),
        out_shape=[jax.ShapeDtypeStruct((packed, wide), BF16) for wide in widths]
        + [jax.ShapeDtypeStruct((packed, 1), F32)],
        grid_spec=pltpu.PrefetchScalarGridSpec(
            num_scalar_prefetch=2,
            grid=(packed // tile,),
            in_specs=[spec(width), spec(width), spec(1)]
            + [pl.BlockSpec(memory_space=pl.ANY)] * len(parts),
            out_specs=[spec(wide) for wide in widths] + [spec(1)],
            scratch_shapes=[
                pltpu.VMEM((width, 2 * hidden), BF16),
                pltpu.VMEM((hidden, width), BF16),
                pltpu.SemaphoreType.DMA((len(parts),)),
            ],
        ),
        compiler_params=pltpu.CompilerParams(vmem_limit_bytes=58 * 2**20),
        name="expert",
    )(total, starts, rows, grads, gates, *parts)


def combine_kernel(turned, window, extra, base_ref, order_ref, to_ref, me_ref, pos_ref, rows_ref, dg_ref, act_ref, weight_ref, out_ref):
    mul = dot_nt if turned else dot
    base = pl.multiple_of(base_ref[pl.program_id(0)], 16)
    pick = chosen(pos_ref, base, window)
    at = pl.ds(base, window)
    width = rows_ref.shape[1]
    out_ref[:, :width] = (
        dot_tn(pick.astype(F32).astype(BF16), rows_ref[at, :]) + mul(act_ref[...], weight_ref[...])
    ).astype(BF16)
    if extra:
        count = pick.shape[1]
        line = jnp.sum(jnp.where(pick, dg_ref[at, :], 0.0), axis=0, keepdims=True)
        row = lax.broadcasted_iota(jnp.int32, (count, count), 0)
        lane = lax.broadcasted_iota(jnp.int32, (count, count), 1)
        column = jnp.sum(jnp.where(row == lane, line, 0.0), axis=1, keepdims=True)
        high = column.astype(BF16).astype(F32)
        lane = lax.broadcasted_iota(jnp.int32, (count, extra), 1)
        out_ref[:, width:] = jnp.where(
            lane == me_ref[0], high, jnp.where(lane == me_ref[0] + extra // 2, column - high, 0.0)
        ).astype(BF16)


def combine(packing, order, to, me, rows, dg, act, weight, turned, extra):
    base, pos, _, window, packed = packing
    blocks, _, count = pos.shape
    width = rows.shape[-1]
    whole = lambda ref: pl.BlockSpec(ref.shape, lambda i, *_: (0, 0))
    return pl.pallas_call(
        functools.partial(combine_kernel, turned, window, extra),
        out_shape=jax.ShapeDtypeStruct((blocks * count, width + extra), BF16),
        grid_spec=pltpu.PrefetchScalarGridSpec(
            num_scalar_prefetch=4,
            grid=(blocks,),
            in_specs=[
                pl.BlockSpec((1, 1, count), lambda i, *_: (i, 0, 0)),
                whole(rows),
                whole(dg),
                pl.BlockSpec((count, act.shape[1]), lambda i, base, order, to, me: (order[i], 0)),
                whole(weight),
            ],
            out_specs=pl.BlockSpec(
                (count, width + extra), lambda i, base, order, to, me: (to[i], 0)
            ),
        ),
        compiler_params=pltpu.CompilerParams(vmem_limit_bytes=40 * 2**20),
        name="combine",
    )(base, order, to, me.reshape(1), pos, rows, dg, act, weight)


def gather_all(value):
    return lax.all_gather(value, "expert", axis=0, tiled=True)


def swap(value):
    return lax.all_to_all(value, "expert", split_axis=0, concat_axis=0, tiled=True)


def per_device(
    tokens,
    cotangent,
    segment_ids,
    routes,
    attn_in,
    attn_out,
    gain_attn,
    shared_in,
    shared_out,
    router,
    gain_ffn,
    expert_in,
    expert_out,
):
    n_dp, n_e = lax.axis_size("dp"), lax.axis_size("expert")
    me = lax.axis_index("expert")
    count, width = tokens.shape
    segments = segment_ids[0]
    length = segments.shape[0]
    rows = attn_in.shape[0]
    capacity = min(count, 3 * TOP * count // (2 * n_e))
    shared_rows = shared_out.shape[0]
    shared_width = shared_rows * n_dp
    expert_width = expert_out.shape[1] * n_dp

    order = ring_blocks()
    steady = jnp.arange(n_e, dtype=jnp.int32)
    hidden_in = tokens.astype(F32)
    inverse_one = lax.rsqrt(jnp.mean(hidden_in * hidden_in, axis=-1, keepdims=True) + EPS)
    normed_one = hidden_in * inverse_one
    gain_rows = gain_attn.astype(F32)[:, None]
    head_w = []

    def head_sent(blocks):
        own = (attn_in.astype(F32) * tied(gain_rows, blocks[0][1][0])).astype(BF16)
        own = own.reshape(rows, 3, n_e, HEAD_DIM).transpose(2, 0, 1, 3)
        head_w.append(swap(own.reshape(n_e, rows, 3 * HEAD_DIM)))
        return head_w[0]

    def head_whole(blocks):
        head_w.append(dp_gather(head_w[0]).reshape(width, 3 * HEAD_DIM))
        return head_w[1]

    here = lax.axis_index("dp")

    def spread(shard, chunks):
        while shard.shape[0] % (16 * chunks):
            chunks -= 1
        size = shard.shape[0] // chunks
        parts = [[(shard, here * shard.shape[0])]]
        for j in range(chunks):
            parts.append([])
            for step in range(1, n_dp):
                got = lax.ppermute(
                    shard[j * size : (j + 1) * size],
                    "dp",
                    [(i, (i - step) % n_dp) for i in range(n_dp)],
                )
                parts[-1].append((got, (here + step) % n_dp * shard.shape[0] + j * size))
        return parts

    up_parts = spread(expert_in[0], max(1, min(4, expert_in.shape[1] // 256)))
    down_parts = spread(expert_out[0], 2)
    first = lambda parts: [part for part, _ in parts]
    up_tokens = [first(parts) for parts in up_parts[1:]] + [[]] * 4

    small = jnp.concatenate([router, gain_ffn[:, None]], axis=1)
    small = dp_gather(small).reshape(-1, n_e + 1)
    extra_rows = 32
    extra = jnp.concatenate([small.T, routes.T.astype(BF16)], axis=0)
    extra = jnp.pad(extra, ((0, extra_rows - extra.shape[0]), (0, 0)))
    extra = jnp.broadcast_to(extra, (n_e,) + extra.shape)
    cos_table, sin_table, first_place = rope_tables(segments)
    share_w = shared_in.reshape(rows, 2, n_dp, n_e, shared_rows).transpose(3, 0, 1, 2, 4)
    share_w = share_w.reshape(n_e, rows, 2 * shared_width)

    half = n_e // 4
    norm_blocks = ring_gather(
        normed_one.astype(BF16),
        {
            half - 1: lambda blocks: [head_sent(blocks)],
            half: lambda blocks: [head_whole(blocks), cos_table, sin_table, extra, share_w],
        },
    )
    head_sent_w, head_w = head_w

    head_out, query, key, value, lse, norm_all = attend(
        norm_blocks, order, head_w, cos_table, sin_table, first_place
    )
    mixed = jnp.concatenate([head_out.reshape(n_e, count, HEAD_DIM), extra], axis=1)
    mixed = swap(tied(mixed, *up_tokens[0], *up_tokens[1]) if up_tokens[0] else mixed)
    small = mixed[:, count:]
    mixed = mixed[:, :count].transpose(1, 0, 2).reshape(count, n_dp, n_e, rows)
    mixed = mixed.transpose(0, 2, 1, 3).reshape(count, width)
    share_w = swap(tied(share_w, lse))
    proj_all = gather_all(dp_gather(attn_out).reshape(n_dp * rows, width))
    routes_all = small[:, n_e + 1 : n_e + 1 + TOP].astype(F32)
    small = small[:, : n_e + 1].reshape(n_e, n_e + 1, n_dp, rows).transpose(1, 2, 0, 3)
    small = small.reshape(n_e + 1, width)
    router_full = small[:n_e]
    gain_second = small[n_e].astype(F32)
    cot_all = gather_all(cotangent)

    share_sent = share_w
    share_w = dp_gather(share_w).reshape(width, 2 * shared_width)
    share_out = dp_gather(shared_out).reshape(shared_width, width)
    resid = hidden_in + dot(mixed, proj_all)
    if up_tokens[2]:
        resid = tied(resid, *up_tokens[2])

    inverse_two = lax.rsqrt(jnp.mean(resid * resid, axis=-1, keepdims=True) + EPS)
    normed_two = resid * inverse_two
    norm_two = (normed_two * gain_second).astype(BF16)
    logits = dot_nt(norm_two, router_full)
    picked = jnp.any(routes[:, :, None] == jnp.arange(n_e)[None, None, :], axis=1)
    chosen = jnp.where(picked, logits, NEG)
    chosen = jnp.where(picked, jnp.exp(chosen - jnp.max(chosen, axis=-1, keepdims=True)), 0.0)
    gates = chosen / jnp.sum(chosen, axis=-1, keepdims=True)
    gate_high = gates.astype(BF16)
    gate_low = (gates - gate_high.astype(F32)).astype(BF16)
    blank = jnp.zeros((count, 128 - 2 * n_e), BF16)
    payload = jnp.concatenate([norm_two, gate_high, gate_low, blank], axis=1)
    norm_blocks = ring_gather(
        payload,
        {
            half - 1: lambda blocks: [share_sent],
            half: lambda blocks: up_tokens[3] + [share_sent],
        },
    )

    named = jnp.any(routes_all == me.astype(F32), axis=1)
    named = jnp.take(named, order, axis=0)
    ranking = jnp.cumsum(named.astype(jnp.int32), axis=1)
    ends = jnp.cumsum(ranking[:, -1])
    begins = ends - ranking[:, -1]
    pos = jnp.where(named, begins[:, None] + ranking - 1, -1)[:, None, :]
    window = -(-(capacity + 15) // 16) * 16
    packed = -(-(n_e * capacity + 32) // 256) * 256
    packing = (begins // 16 * 16, pos, ends[-1:], window, packed)
    norm_two_all, payload, arrived, _ = dispatch(
        norm_blocks, [width, 128], packing, order, jnp.zeros((n_e, 1, count), F32)
    )
    mine = jnp.arange(n_e) == me
    gate_all = payload[:, : 2 * n_e].astype(F32).reshape(length, 2, n_e)
    gate_all = jnp.sum(jnp.where(mine, gate_all, 0.0), axis=(1, 2)).reshape(n_e, 1, count)
    cot_rows, gate_rows = dispatch(cot_all, None, packing, order, gate_all)
    weighted, row_grad, expert_act, route_grad, pre_grad, gate_grad = expert(
        packing[2],
        arrived,
        cot_rows,
        gate_rows,
        [part for parts in up_parts for part in parts],
        [part for parts in down_parts for part in parts],
    )

    shared_pre = dot(norm_two_all, share_w)
    shared_act = (
        jax.nn.silu(shared_pre[:, :shared_width]) * shared_pre[:, shared_width:]
    ).astype(BF16)
    shared_act_grad = dot_nt(cot_all, share_out)
    shared_pre_grad = silu_back(
        shared_act_grad, shared_pre[:, :shared_width], shared_pre[:, shared_width:]
    ).astype(BF16)
    norm_two_part = combine(
        packing, order, steady, me, row_grad, gate_grad, shared_pre_grad, share_w, True, 128
    )
    norm_two_grad = ring_scatter(
        lambda n: norm_two_part[n * count : (n + 1) * count]
    )
    gate_grad = norm_two_grad[:, width : width + n_e] + norm_two_grad[:, width + 64 : width + 64 + n_e]
    norm_two_grad = norm_two_grad[:, :width]
    out_part = combine(
        packing, order, order, me, weighted, gate_rows, shared_act, share_out, False, 0
    )
    routed_out = lax.psum_scatter(out_part, "expert", scatter_dimension=0, tiled=True)

    def shard_grads(left, right, chunks):
        size = left.shape[1] // n_dp
        part = size // chunks
        cut = lambda start, wide: lax.dynamic_slice_in_dim(left, start, wide, 1)
        got = [
            [
                lax.ppermute(
                    dot_tn(cut((here + step) % n_dp * size + j * part, part), right).astype(BF16),
                    "dp",
                    [(i, (i + step) % n_dp) for i in range(n_dp)],
                )
                for step in range(1, n_dp)
            ]
            for j in range(chunks)
        ]
        return dot_tn(cut(here * size, size), right), got

    def shard_sum(own, got, tokens):
        part = own.shape[0] // len(got)
        own = own[None]
        for j, (parts, token) in enumerate(zip(got, tokens)):
            block = sum(tied(p.astype(F32), token) for p in parts)[None]
            block = own[:, j * part : (j + 1) * part] + block
            own = lax.dynamic_update_slice_in_dim(own, block, j * part, 1)
        return own

    down_own, down_got = shard_grads(expert_act, route_grad, 2)
    up_own, up_got = shard_grads(arrived, pre_grad, len(up_parts) - 1)

    share_out_grad = dp_scatter(dot_tn(shared_act, cot_all).reshape(n_dp, shared_rows, width))
    share_in_grad = dot_tn(norm_two_all, shared_pre_grad)
    share_in_grad = dp_scatter(share_in_grad.reshape(n_dp, n_e, rows, 2 * shared_width))
    share_in_grad = swap(share_in_grad.astype(BF16)).astype(F32)
    share_in_grad = (
        share_in_grad.reshape(n_e, rows, 2, n_dp, shared_rows)
        .transpose(1, 2, 3, 0, 4)
        .reshape(rows, -1)
    )

    logit_grad = gates * (gate_grad - jnp.sum(gates * gate_grad, axis=-1, keepdims=True))
    router_grad = jnp.dot(
        logit_grad.T, norm_two.astype(F32), precision=HIGHEST, preferred_element_type=F32
    )
    norm_two_grad = norm_two_grad + jnp.dot(
        logit_grad, router_full.astype(F32), precision=HIGHEST, preferred_element_type=F32
    )
    gain_two_grad = jnp.sum(norm_two_grad * normed_two, axis=0)
    upstream = tied(cotangent.astype(F32), *down_got[0])
    scaled_two = norm_two_grad * gain_second
    resid_grad = upstream + inverse_two * (
        scaled_two - normed_two * jnp.mean(scaled_two * normed_two, axis=-1, keepdims=True)
    )
    small_grad = jnp.concatenate([router_grad, gain_two_grad[None]], axis=0)
    small_grad = jnp.pad(small_grad, ((0, HEAD_DIM - n_e - 1), (0, 0))).T

    branch_cot = resid_grad.astype(BF16)
    proj_grad = dot_tn(mixed, branch_cot).astype(BF16)
    mixed_grad = tied(dot_nt(branch_cot, proj_all), *down_got[1]).astype(BF16)
    mixed_grad = mixed_grad.reshape(count, n_e, n_dp, rows).transpose(0, 2, 1, 3)
    mixed_grad = swap(mixed_grad.reshape(count, n_e, HEAD_DIM).transpose(1, 0, 2))
    mixed_grad = mixed_grad.reshape(length, HEAD_DIM)
    proj_grad = lax.psum_scatter(proj_grad, "expert", scatter_dimension=0, tiled=True)
    attn_out_grad = dp_scatter(proj_grad.astype(F32).reshape(n_dp, rows, width))
    qkv_grad = attend_back(
        query, key, value, mixed_grad, lse, first_place, cos_table, sin_table, order
    )
    norm_one_part = dot_nt(qkv_grad, head_w).astype(BF16)
    scaled_one = ring_scatter(
        lambda n: norm_one_part[n * count : (n + 1) * count],
        {1: up_got[0], half - 1: up_got[min(1, len(up_got) - 1)]},
    )
    expert_out_grad = shard_sum(down_own, down_got, [norm_two_grad, mixed_grad])
    expert_in_grad = shard_sum(up_own, up_got, ([qkv_grad] + [scaled_one] * 3)[: len(up_got)])
    input_grad = resid_grad + inverse_one * (
        scaled_one - normed_one * jnp.mean(scaled_one * normed_one, axis=-1, keepdims=True)
    )
    wide = 3 * HEAD_DIM
    head_grad = jnp.concatenate([dot_tn(norm_all, qkv_grad), small_grad], axis=1)
    head_grad = dp_scatter(head_grad.reshape(n_dp, n_e, rows, wide + small_grad.shape[1]))
    head_grad = swap(head_grad.astype(BF16)).astype(F32)
    small_grad = jnp.sum(head_grad[:, :, wide:], axis=0)
    head_grad = (
        head_grad[:, :, :wide]
        .reshape(n_e, rows, 3, HEAD_DIM)
        .transpose(1, 2, 0, 3)
        .reshape(rows, 3 * width)
    )
    gain_attn_grad = jnp.sum(head_grad * attn_in.astype(F32), axis=1)
    attn_in_grad = head_grad * gain_rows
    return (
        (resid + routed_out.astype(F32)).astype(BF16),
        input_grad.astype(BF16),
        attn_in_grad,
        attn_out_grad,
        gain_attn_grad,
        share_in_grad,
        share_out_grad,
        small_grad[:, :n_e],
        small_grad[:, n_e],
        expert_in_grad,
        expert_out_grad,
    )


def solution(mesh):
    return jax.shard_map(
        per_device,
        mesh=mesh,
        in_specs=(
            P(("dp", "expert"), None),
            P(("dp", "expert"), None),
            P("dp", None),
            P(("dp", "expert"), None),
            P(("dp", "expert"), None),
            P(("dp", "expert"), None),
            P(("dp", "expert")),
            P(("dp", "expert"), None),
            P(("dp", "expert"), None),
            P(("dp", "expert"), None),
            P(("dp", "expert")),
            P("expert", "dp", None),
            P("expert", "dp", None),
        ),
        out_specs=(
            P(("dp", "expert"), None),
            P(("dp", "expert"), None),
            P(("dp", "expert"), None),
            P(("dp", "expert"), None),
            P(("dp", "expert")),
            P(("dp", "expert"), None),
            P(("dp", "expert"), None),
            P(("dp", "expert"), None),
            P(("dp", "expert")),
            P("expert", "dp", None),
            P("expert", "dp", None),
        ),
        check_vma=False,
    )
```

```python
import functools
import math

import jax
import jax.numpy as jnp
from jax import lax
from jax.experimental import pallas as pl
from jax.experimental.pallas import tpu as pltpu
from jax.sharding import PartitionSpec as P

HEADS = 16
HEAD_DIM = 128
TOP = 6


EPS = 1e-06
THETA = 10000.0
NEG = -1e30
HIGHEST = lax.Precision.HIGHEST
BF16 = jnp.bfloat16
F32 = jnp.float32
LOG2E = math.log2(math.e)


def rope_tables(segments):
    length = segments.shape[0]
    places = jnp.arange(length, dtype=jnp.int32)
    starts = jnp.concatenate([jnp.ones((1,), dtype=jnp.bool_), segments[1:] != segments[:-1]])
    first_place = lax.cummax(jnp.where(starts, places, 0), axis=0)
    offset = (places - first_place).astype(jnp.float32)
    half_dim = HEAD_DIM // 2
    freqs = jnp.exp(jnp.arange(half_dim, dtype=jnp.float32) * (-2.0 * math.log(THETA) / HEAD_DIM))
    angles = offset[:, None] * freqs[None, :]
    cos_table, sin_table = jnp.cos(angles), jnp.sin(angles)
    return (
        jnp.concatenate([cos_table, cos_table], axis=1),
        jnp.concatenate([-sin_table, sin_table], axis=1),
        first_place[None, :],
    )


def silu_back(grad_act, gate_part, up_part):
    sigmoid_gate = jax.nn.sigmoid(gate_part)
    gate_grad = grad_act * up_part * sigmoid_gate * (1.0 + gate_part * (1.0 - sigmoid_gate))
    up_grad = grad_act * gate_part * sigmoid_gate
    return jnp.concatenate([gate_grad, up_grad], axis=-1)


def dot(left, right):
    return jnp.dot(left, right, preferred_element_type=F32)


def dot_tn(left, right):
    return lax.dot_general(left, right, (((0,), (0,)), ((), ())), preferred_element_type=F32)


def dot_nt(left, right):
    return lax.dot_general(left, right, (((1,), (1,)), ((), ())), preferred_element_type=F32)


def turn(values, cos_table, sin_table):
    return values * cos_table + pltpu.roll(values, HEAD_DIM // 2, 1) * sin_table


def attend_kernel(sources, block, order_ref, *refs):
    pieces = refs[: sources[-1][-1] + 1]
    weight_ref, cos_ref, sin_ref, start_ref = refs[len(pieces) : len(pieces) + 4]
    o_ref, q_ref, k_ref, v_ref, lse_ref, rows_ref, vt_ref = refs[len(pieces) + 4 :]
    step = pl.program_id(0)
    length = q_ref.shape[0]
    factor = HEAD_DIM ** (-0.5) * LOG2E
    rows = rows_ref.shape[0]

    for n, parts in enumerate(sources):

        @pl.when(step == n)
        def _(parts=parts):
            low = 0
            for part in parts:
                size = pieces[part].shape[0]
                rows_ref[low : low + size, :] = pieces[part][...]
                low += size

    @pl.when(step < len(sources))
    def _():
        qkv = dot(rows_ref[...], weight_ref[...])
        at = pl.ds(pl.multiple_of(order_ref[step] * rows, rows), rows)
        cos_table, sin_table = cos_ref[at, :], sin_ref[at, :]
        q_ref[at, :] = turn(qkv[:, :HEAD_DIM], cos_table, sin_table).astype(BF16)
        k_ref[at, :] = turn(qkv[:, HEAD_DIM : 2 * HEAD_DIM], cos_table, sin_table).astype(BF16)
        value = qkv[:, 2 * HEAD_DIM :]
        v_ref[at, :] = value.astype(BF16)
        vt_ref[:, at] = value.T.astype(BF16)

    for i in range(length // block):

        @pl.when(step == len(sources) + i)
        def _(i=i):
            low, high = i * block, (i + 1) * block
            raw = dot_nt(k_ref[:high, :], q_ref[low:high, :])
            keys = lax.broadcasted_iota(jnp.int32, raw.shape, 0)
            queries = low + lax.broadcasted_iota(jnp.int32, raw.shape, 1)
            allowed = (keys <= queries) & (keys >= start_ref[:, low:high])
            raw = jnp.where(allowed, raw, NEG)
            top = jnp.max(raw, axis=0, keepdims=True)
            shifted = jnp.exp2((raw - top) * factor)
            total = jnp.sum(shifted, axis=0, keepdims=True)
            probs = (shifted * (1.0 / total)).astype(BF16)
            mixed = dot(vt_ref[:, :high], probs)
            o_ref[low:high, :] = mixed.T.astype(BF16)
            lse_ref[:, low:high] = top * factor + jnp.log2(total)


def attend(blocks, order, weight, cos_table, sin_table, first_place):
    pieces, sources = flatten(blocks)
    length = cos_table.shape[0]
    rows = length // len(sources)
    width = weight.shape[0]
    block = min(256, length)
    last = len(sources) - 1
    whole = lambda shape: pl.BlockSpec(shape, lambda i, order: (0, 0))
    head = jax.ShapeDtypeStruct((length, HEAD_DIM), BF16)
    return pl.pallas_call(
        functools.partial(attend_kernel, sources, block),
        out_shape=[head] * 4
        + [jax.ShapeDtypeStruct((1, length), F32), jax.ShapeDtypeStruct((length, width), BF16)],
        grid_spec=pltpu.PrefetchScalarGridSpec(
            num_scalar_prefetch=1,
            grid=(len(sources) + length // block,),
            in_specs=[whole(piece.shape) for piece in pieces]
            + [
                whole(weight.shape),
                whole((length, HEAD_DIM)),
                whole((length, HEAD_DIM)),
                whole((1, length)),
            ],
            out_specs=[whole((length, HEAD_DIM))] * 4
            + [
                whole((1, length)),
                pl.BlockSpec((rows, width), lambda i, order: (jnp.minimum(i, last), 0)),
            ],
            scratch_shapes=[pltpu.VMEM((HEAD_DIM, length), BF16)],
        ),
        compiler_params=pltpu.CompilerParams(vmem_limit_bytes=52 * 2**20),
        name="attend",
    )(order, *pieces, weight, cos_table, sin_table, first_place)


def attend_back_kernel(
    block, rows, order_ref, q_ref, k_ref, v_ref, do_ref, lse_ref, start_ref, cos_ref, sin_ref, out_ref, kt_ref, dq_ref, dk_ref, dv_ref
):
    length = q_ref.shape[0]
    step = pl.program_id(0)
    scale = HEAD_DIM ** (-0.5)
    factor = scale * LOG2E
    count = length // block

    @pl.when(step == 0)
    def _():
        kt_ref[...] = k_ref[...].astype(F32).T.astype(BF16)
        dk_ref[...] = jnp.zeros_like(dk_ref)
        dv_ref[...] = jnp.zeros_like(dv_ref)

    for i in range(count):

        @pl.when(step == i)
        def _(i=i):
            low, high = i * block, (i + 1) * block
            query, grad = q_ref[low:high, :], do_ref[low:high, :]
            raw = dot_nt(k_ref[:high, :], query)
            keys = lax.broadcasted_iota(jnp.int32, raw.shape, 0)
            queries = low + lax.broadcasted_iota(jnp.int32, raw.shape, 1)
            allowed = (keys <= queries) & (keys >= start_ref[:, low:high])
            raw = jnp.where(allowed, raw * factor - lse_ref[:, low:high], NEG)
            probs = jnp.exp2(raw)
            probs_grad = dot_nt(v_ref[:high, :], grad)
            inner = jnp.sum(probs_grad * probs, axis=0, keepdims=True)
            score_grad = (probs * (probs_grad - inner)).astype(BF16)
            dv_ref[:high, :] += dot(probs.astype(BF16), grad)
            dk_ref[:high, :] += dot(score_grad, query)
            dq_ref[low:high, :] = dot(kt_ref[:, :high], score_grad).T

    @pl.when(step == count - 1)
    def _():
        for n in range(length // rows):
            at = pl.ds(pl.multiple_of(order_ref[n] * rows, rows), rows)
            to = slice(n * rows, (n + 1) * rows)
            cos_table, sin_table = cos_ref[at, :], -sin_ref[at, :]
            out_ref[to, :HEAD_DIM] = turn(dq_ref[at, :] * scale, cos_table, sin_table).astype(BF16)
            out_ref[to, HEAD_DIM : 2 * HEAD_DIM] = turn(
                dk_ref[at, :] * scale, cos_table, sin_table
            ).astype(BF16)
            out_ref[to, 2 * HEAD_DIM :] = dv_ref[at, :].astype(BF16)


def attend_back(query, key, value, grad, lse, first_place, cos_table, sin_table, order):
    length = query.shape[0]
    block = min(256, length)
    whole = lambda shape: pl.BlockSpec(shape, lambda i, order: (0, 0))
    head = whole((length, HEAD_DIM))
    return pl.pallas_call(
        functools.partial(attend_back_kernel, block, length // order.shape[0]),
        out_shape=jax.ShapeDtypeStruct((length, 3 * HEAD_DIM), BF16),
        grid_spec=pltpu.PrefetchScalarGridSpec(
            num_scalar_prefetch=1,
            grid=(length // block,),
            in_specs=[head] * 4 + [whole((1, length))] * 2 + [head] * 2,
            out_specs=whole((length, 3 * HEAD_DIM)),
            scratch_shapes=[pltpu.VMEM((HEAD_DIM, length), BF16)]
            + [pltpu.VMEM((length, HEAD_DIM), F32)] * 3,
        ),
        compiler_params=pltpu.CompilerParams(vmem_limit_bytes=48 * 2**20),
        name="attend_back",
    )(order, query, key, value, grad, lse, first_place, cos_table, sin_table)


def dp_gather(value):
    count = lax.axis_size("dp")
    if count == 1:
        return value[None]
    here = lax.axis_index("dp")
    parts = [value] + [
        lax.ppermute(value, "dp", [(i, (i - step) % count) for i in range(count)])
        for step in range(1, count)
    ]
    if count == 2:
        first = here == 0
        return jnp.stack(
            [jnp.where(first, parts[0], parts[1]), jnp.where(first, parts[1], parts[0])]
        )
    whole = jnp.zeros((count,) + value.shape, value.dtype)
    for step, part in enumerate(parts):
        whole = lax.dynamic_update_index_in_dim(whole, part, (here + step) % count, 0)
    return whole


def dp_scatter(value):
    count = lax.axis_size("dp")
    here = lax.axis_index("dp")
    total = lax.dynamic_index_in_dim(value, here, 0, keepdims=False)
    for step in range(1, count):
        block = lax.dynamic_index_in_dim(value, (here + step) % count, 0, keepdims=False)
        got = lax.ppermute(
            block.astype(BF16), "dp", [(i, (i + step) % count) for i in range(count)]
        )
        total = total + got.astype(F32)
    return total


def ring_order():
    pairs = lax.axis_size("expert") // 2
    return list(range(0, pairs, 2)) + list(range(pairs - 1, 0, -2))


def ring_shift(value, step):
    order = ring_order()
    pairs = len(order)
    perm = [
        (order[q] * 2 + c, order[(q + step) % pairs] * 2 + c) for q in range(pairs) for c in range(2)
    ]
    return lax.ppermute(value, "expert", perm)


def core_swap(value):
    count = lax.axis_size("expert")
    return lax.ppermute(value, "expert", [(i, i ^ 1) for i in range(count)])


def ring_offsets():
    half = lax.axis_size("expert") // 4
    return [0] + [o for step in range(1, half) for o in (step, -step)] + [half]


def ring_blocks():
    order = ring_order()
    pairs = len(order)
    table = [[0] * (2 * pairs) for _ in range(2 * pairs)]
    for q in range(pairs):
        for c in range(2):
            for j, offset in enumerate(ring_offsets()):
                for other in range(2):
                    table[order[q] * 2 + c][2 * j + other] = (
                        order[(q - offset) % pairs] * 2 + (c ^ other)
                    )
    return lax.dynamic_index_in_dim(
        jnp.asarray(table, jnp.int32), lax.axis_index("expert"), 0, keepdims=False
    )


def tied(value, *tokens):
    firsts = [lax.slice(t, (0,) * t.ndim, (1,) * t.ndim).reshape(()) for t in tokens]
    token = sum(t.astype(F32) for t in firsts) * 0.0
    return (value.astype(F32) * (1.0 + token)).astype(value.dtype)


def ring_gather(value, gates=None):
    gates = gates or {}
    half_rows = value.shape[0] // 2
    half = lax.axis_size("expert") // 4
    blocks = {}

    def keep(parts, offset):
        blocks[offset] = (parts, [core_swap(part) for part in parts])

    keep([value], 0)
    ahead = back = value
    for step in range(1, half):
        if step in gates:
            token = gates[step](blocks)
            ahead, back = tied(ahead, *token), tied(back, *token)
        ahead, back = ring_shift(ahead, 1), ring_shift(back, -1)
        keep([ahead], step)
        keep([back], -step)
    if half in gates:
        token = gates[half](blocks)
        ahead, back = tied(ahead, *token), tied(back, *token)
    last = [ring_shift(ahead[:half_rows], 1), ring_shift(back[half_rows:], -1)]
    keep(last, half)
    return [parts for offset in ring_offsets() for parts in blocks[offset]]


def flatten(blocks):
    pieces = [piece for parts in blocks for piece in parts]
    sources, n = [], 0
    for parts in blocks:
        sources.append(tuple(range(n, n + len(parts))))
        n += len(parts)
    return pieces, tuple(sources)


def ring_scatter(block, gates=None, marks=None):
    gates = gates or {}
    half = lax.axis_size("expert") // 4
    offsets = ring_offsets()
    spare = {}

    def mine(offset):
        if offset not in spare:
            j = offsets.index(offset)
            spare[offset] = block(2 * j).astype(F32) + core_swap(block(2 * j + 1)).astype(F32)
        return spare[offset]

    far = mine(half).astype(BF16)
    half_rows = far.shape[0] // 2
    ahead = ring_shift(far[:half_rows], 1)
    back = ring_shift(far[half_rows:], -1)
    if marks is not None:
        marks.extend([ahead, back])
    for step in range(half - 1, 0, -1):
        onward, homeward = mine(-step), mine(step)
        if step == half - 1:
            onward = jnp.concatenate(
                [onward[:half_rows] + ahead.astype(F32), onward[half_rows:]], axis=0
            )
            homeward = jnp.concatenate(
                [homeward[:half_rows], homeward[half_rows:] + back.astype(F32)], axis=0
            )
        else:
            onward = onward + ahead.astype(F32)
            homeward = homeward + back.astype(F32)
        if half - step in gates:
            onward, homeward = tied(onward, *gates[half - step]), tied(homeward, *gates[half - step])
        ahead = ring_shift(onward.astype(BF16), 1)
        back = ring_shift(homeward.astype(BF16), -1)
    return mine(0) + ahead.astype(F32) + back.astype(F32)


def chosen(pos_ref, base, window):
    count = pos_ref.shape[-1]
    row = base + lax.broadcasted_iota(jnp.int32, (window, count), 0)
    return row == pos_ref[0]


def dispatch_kernel(sources, widths, window, base_ref, order_ref, pos_ref, gate_ref, *refs):
    outs = refs[-len(widths) - 2 :]
    pieces, blocks, rows_ref, weights_ref = refs[: -len(outs)], outs[:-2], outs[-2], outs[-1]
    step = pl.program_id(0)

    @pl.when(step == 0)
    def _():
        rows_ref[...] = jnp.zeros_like(rows_ref)
        weights_ref[...] = jnp.zeros_like(weights_ref)

    for n, parts in enumerate(sources):

        @pl.when(step == n)
        def _(parts=parts):
            low = 0
            for part in parts:
                size = pieces[part].shape[0]
                left = 0
                for block, wide in zip(blocks, widths):
                    block[low : low + size, :] = pieces[part][:, left : left + wide]
                    left += wide
                low += size

    base = pl.multiple_of(base_ref[step], 16)
    pick = chosen(pos_ref, base, window)
    at = pl.ds(base, window)
    found = dot(pick.astype(F32).astype(BF16), (blocks or pieces)[0][...])
    rows_ref[at, :] = (rows_ref[at, :].astype(F32) + found).astype(BF16)
    weights_ref[at, :] += jnp.sum(jnp.where(pick, gate_ref[0], 0.0), axis=1, keepdims=True)


def dispatch(blocks, widths, packing, order, gates):
    base, pos, _, window, packed = packing
    count, _, rows = pos.shape
    if isinstance(blocks, list):
        pieces, sources = flatten(blocks)
        piece_specs = [pl.BlockSpec(piece.shape, lambda i, base, order: (0, 0)) for piece in pieces]
    else:
        pieces, sources, widths = [blocks], (), []
        piece_specs = [pl.BlockSpec((rows, blocks.shape[1]), lambda i, base, order: (order[i], 0))]
    width = (widths or [pieces[0].shape[1]])[0]
    return pl.pallas_call(
        functools.partial(dispatch_kernel, sources, tuple(widths), window),
        out_shape=[jax.ShapeDtypeStruct((rows * count, wide), BF16) for wide in widths]
        + [
            jax.ShapeDtypeStruct((packed, width), BF16),
            jax.ShapeDtypeStruct((packed, 1), F32),
        ],
        grid_spec=pltpu.PrefetchScalarGridSpec(
            num_scalar_prefetch=2,
            grid=(count,),
            in_specs=[
                pl.BlockSpec((1, 1, rows), lambda i, base, order: (i, 0, 0)),
                pl.BlockSpec((1, 1, rows), lambda i, base, order: (order[i], 0, 0)),
            ]
            + piece_specs,
            out_specs=[
                pl.BlockSpec((rows, wide), lambda i, base, order: (order[i], 0)) for wide in widths
            ]
            + [
                pl.BlockSpec((packed, width), lambda i, base, order: (0, 0)),
                pl.BlockSpec((packed, 1), lambda i, base, order: (0, 0)),
            ],
        ),
        compiler_params=pltpu.CompilerParams(vmem_limit_bytes=52 * 2**20),
        name="dispatch",
    )(base, order, pos, gates, *pieces)


def expert_kernel(ups, total_ref, starts_ref, x_ref, g_ref, gate_ref, *refs):
    parts, refs = refs[:-9], refs[-9:]
    wy_ref, dn_ref, ea_ref, dy_ref, db_ref, dg_ref, up_ref, down_ref, sems = refs
    step = pl.program_id(0)
    rows, hidden = ea_ref.shape
    some = step * rows < total_ref[0]

    @pl.when(step == 0)
    def _():
        copies = []
        for n, part in enumerate(parts):
            at = pl.ds(pl.multiple_of(starts_ref[n], 16), part.shape[0])
            whole = up_ref if n < ups else down_ref
            copies.append(pltpu.make_async_copy(part, whole.at[at, :], sems.at[n]))
        for copy in copies:
            copy.start()
        for copy in copies:
            copy.wait()

    @pl.when(some)
    def _():
        pre = dot(x_ref[...], up_ref[...])
        gate_part, up_part = pre[:, :hidden], pre[:, hidden:]
        sigmoid_gate = 1.0 / (1.0 + jnp.exp(-gate_part))
        silu = gate_part * sigmoid_gate
        act = (silu * up_part).astype(BF16)
        ea_ref[...] = act
        result = dot(act, down_ref[...]).astype(BF16).astype(F32)
        grad = g_ref[...].astype(F32)
        gate = gate_ref[...]
        dg_ref[...] = jnp.sum(grad * result, axis=1, keepdims=True)
        wy_ref[...] = (gate * result).astype(BF16)
        out_grad = (gate * grad).astype(BF16)
        dy_ref[...] = out_grad
        act_grad = dot_nt(out_grad, down_ref[...])
        db_ref[:, :hidden] = (
            act_grad * up_part * sigmoid_gate * (1.0 + gate_part * (1.0 - sigmoid_gate))
        ).astype(BF16)
        db_ref[:, hidden:] = (act_grad * silu).astype(BF16)
        dn_ref[...] = dot_nt(db_ref[...], up_ref[...]).astype(BF16)

    @pl.when(jnp.logical_not(some))
    def _():
        for ref in (wy_ref, dn_ref, ea_ref, dy_ref, db_ref, dg_ref):
            ref[...] = jnp.zeros_like(ref)


def expert(total, rows, grads, gates, ups, downs):
    packed, width = rows.shape
    hidden = sum(part.shape[0] for part, _ in downs)
    tile = 256
    parts = [part for part, _ in ups + downs]
    starts = jnp.stack([start for _, start in ups + downs]).astype(jnp.int32)
    spec = lambda wide: pl.BlockSpec((tile, wide), lambda i, total, starts: (i, 0))
    widths = (width, width, hidden, width, 2 * hidden)
    return pl.pallas_call(
        functools.partial(expert_kernel, len(ups)),
        out_shape=[jax.ShapeDtypeStruct((packed, wide), BF16) for wide in widths]
        + [jax.ShapeDtypeStruct((packed, 1), F32)],
        grid_spec=pltpu.PrefetchScalarGridSpec(
            num_scalar_prefetch=2,
            grid=(packed // tile,),
            in_specs=[spec(width), spec(width), spec(1)]
            + [pl.BlockSpec(memory_space=pl.ANY)] * len(parts),
            out_specs=[spec(wide) for wide in widths] + [spec(1)],
            scratch_shapes=[
                pltpu.VMEM((width, 2 * hidden), BF16),
                pltpu.VMEM((hidden, width), BF16),
                pltpu.SemaphoreType.DMA((len(parts),)),
            ],
        ),
        compiler_params=pltpu.CompilerParams(vmem_limit_bytes=58 * 2**20),
        name="expert",
    )(total, starts, rows, grads, gates, *parts)


def combine_kernel(turned, window, extra, base_ref, order_ref, to_ref, me_ref, pos_ref, rows_ref, dg_ref, act_ref, weight_ref, out_ref):
    mul = dot_nt if turned else dot
    base = pl.multiple_of(base_ref[pl.program_id(0)], 16)
    pick = chosen(pos_ref, base, window)
    at = pl.ds(base, window)
    width = rows_ref.shape[1]
    out_ref[:, :width] = (
        dot_tn(pick.astype(F32).astype(BF16), rows_ref[at, :]) + mul(act_ref[...], weight_ref[...])
    ).astype(BF16)
    if extra:
        count = pick.shape[1]
        line = jnp.sum(jnp.where(pick, dg_ref[at, :], 0.0), axis=0, keepdims=True)
        row = lax.broadcasted_iota(jnp.int32, (count, count), 0)
        lane = lax.broadcasted_iota(jnp.int32, (count, count), 1)
        column = jnp.sum(jnp.where(row == lane, line, 0.0), axis=1, keepdims=True)
        high = column.astype(BF16).astype(F32)
        lane = lax.broadcasted_iota(jnp.int32, (count, extra), 1)
        out_ref[:, width:] = jnp.where(
            lane == me_ref[0], high, jnp.where(lane == me_ref[0] + extra // 2, column - high, 0.0)
        ).astype(BF16)


def combine(packing, order, to, me, rows, dg, act, weight, turned, extra):
    base, pos, _, window, packed = packing
    blocks, _, count = pos.shape
    width = rows.shape[-1]
    whole = lambda ref: pl.BlockSpec(ref.shape, lambda i, *_: (0, 0))
    return pl.pallas_call(
        functools.partial(combine_kernel, turned, window, extra),
        out_shape=jax.ShapeDtypeStruct((blocks * count, width + extra), BF16),
        grid_spec=pltpu.PrefetchScalarGridSpec(
            num_scalar_prefetch=4,
            grid=(blocks,),
            in_specs=[
                pl.BlockSpec((1, 1, count), lambda i, *_: (i, 0, 0)),
                whole(rows),
                whole(dg),
                pl.BlockSpec((count, act.shape[1]), lambda i, base, order, to, me: (order[i], 0)),
                whole(weight),
            ],
            out_specs=pl.BlockSpec(
                (count, width + extra), lambda i, base, order, to, me: (to[i], 0)
            ),
        ),
        compiler_params=pltpu.CompilerParams(vmem_limit_bytes=40 * 2**20),
        name="combine",
    )(base, order, to, me.reshape(1), pos, rows, dg, act, weight)


def gather_all(value):
    return lax.all_gather(value, "expert", axis=0, tiled=True)


def swap(value):
    return lax.all_to_all(value, "expert", split_axis=0, concat_axis=0, tiled=True)


def per_device(
    tokens,
    cotangent,
    segment_ids,
    routes,
    attn_in,
    attn_out,
    gain_attn,
    shared_in,
    shared_out,
    router,
    gain_ffn,
    expert_in,
    expert_out,
):
    n_dp, n_e = lax.axis_size("dp"), lax.axis_size("expert")
    me = lax.axis_index("expert")
    count, width = tokens.shape
    segments = segment_ids[0]
    length = segments.shape[0]
    rows = attn_in.shape[0]
    capacity = min(count, 3 * TOP * count // (2 * n_e))
    shared_rows = shared_out.shape[0]
    shared_width = shared_rows * n_dp
    expert_width = expert_out.shape[1] * n_dp

    order = ring_blocks()
    steady = jnp.arange(n_e, dtype=jnp.int32)
    hidden_in = tokens.astype(F32)
    inverse_one = lax.rsqrt(jnp.mean(hidden_in * hidden_in, axis=-1, keepdims=True) + EPS)
    normed_one = hidden_in * inverse_one
    gain_rows = gain_attn.astype(F32)[:, None]
    head_w = []

    def head_sent(blocks):
        own = (attn_in.astype(F32) * tied(gain_rows, blocks[0][1][0])).astype(BF16)
        own = own.reshape(rows, 3, n_e, HEAD_DIM).transpose(2, 0, 1, 3)
        head_w.append(swap(own.reshape(n_e, rows, 3 * HEAD_DIM)))
        return head_w[0]

    def head_whole(blocks):
        head_w.append(dp_gather(head_w[0]).reshape(width, 3 * HEAD_DIM))
        return head_w[1]

    here = lax.axis_index("dp")

    def spread(shard, chunks):
        while shard.shape[0] % (16 * chunks):
            chunks -= 1
        size = shard.shape[0] // chunks
        parts = [[(shard, here * shard.shape[0])]]
        for j in range(chunks):
            parts.append([])
            for step in range(1, n_dp):
                got = lax.ppermute(
                    shard[j * size : (j + 1) * size],
                    "dp",
                    [(i, (i - step) % n_dp) for i in range(n_dp)],
                )
                parts[-1].append((got, (here + step) % n_dp * shard.shape[0] + j * size))
        return parts

    up_parts = spread(expert_in[0], max(1, min(4, expert_in.shape[1] // 256)))
    down_parts = spread(expert_out[0], 2)
    first = lambda parts: [part for part, _ in parts]
    up_tokens = [first(parts) for parts in up_parts[1:]] + [[]] * 4

    small = jnp.concatenate([router, gain_ffn[:, None]], axis=1)
    small = dp_gather(small).reshape(-1, n_e + 1)
    extra_rows = 32
    extra = jnp.concatenate([small.T, routes.T.astype(BF16)], axis=0)
    extra = jnp.pad(extra, ((0, extra_rows - extra.shape[0]), (0, 0)))
    extra = jnp.broadcast_to(extra, (n_e,) + extra.shape)
    cos_table, sin_table, first_place = rope_tables(segments)
    share_w = shared_in.reshape(rows, 2, n_dp, n_e, shared_rows).transpose(3, 0, 1, 2, 4)
    share_w = share_w.reshape(n_e, rows, 2 * shared_width)

    half = n_e // 4
    norm_blocks = ring_gather(
        normed_one.astype(BF16),
        {
            half - 1: lambda blocks: [head_sent(blocks)],
            half: lambda blocks: [head_whole(blocks), cos_table, sin_table, extra, share_w],
        },
    )
    head_sent_w, head_w = head_w

    head_out, query, key, value, lse, norm_all = attend(
        norm_blocks, order, head_w, cos_table, sin_table, first_place
    )
    mixed = jnp.concatenate([head_out.reshape(n_e, count, HEAD_DIM), extra], axis=1)
    mixed = swap(tied(mixed, *up_tokens[0], *up_tokens[1]) if up_tokens[0] else mixed)
    small = mixed[:, count:]
    mixed = mixed[:, :count].transpose(1, 0, 2).reshape(count, n_dp, n_e, rows)
    mixed = mixed.transpose(0, 2, 1, 3).reshape(count, width)
    share_w = swap(tied(share_w, lse))
    proj_all = gather_all(dp_gather(attn_out).reshape(n_dp * rows, width))
    routes_all = small[:, n_e + 1 : n_e + 1 + TOP].astype(F32)
    small = small[:, : n_e + 1].reshape(n_e, n_e + 1, n_dp, rows).transpose(1, 2, 0, 3)
    small = small.reshape(n_e + 1, width)
    router_full = small[:n_e]
    gain_second = small[n_e].astype(F32)
    cot_all = gather_all(cotangent)

    share_sent = share_w
    share_w = dp_gather(share_w).reshape(width, 2 * shared_width)
    share_out = dp_gather(shared_out).reshape(shared_width, width)
    resid = hidden_in + dot(mixed, proj_all)
    if up_tokens[2]:
        resid = tied(resid, *up_tokens[2])

    inverse_two = lax.rsqrt(jnp.mean(resid * resid, axis=-1, keepdims=True) + EPS)
    normed_two = resid * inverse_two
    norm_two = (normed_two * gain_second).astype(BF16)
    logits = dot_nt(norm_two, router_full)
    picked = jnp.any(routes[:, :, None] == jnp.arange(n_e)[None, None, :], axis=1)
    chosen = jnp.where(picked, logits, NEG)
    chosen = jnp.where(picked, jnp.exp(chosen - jnp.max(chosen, axis=-1, keepdims=True)), 0.0)
    gates = chosen / jnp.sum(chosen, axis=-1, keepdims=True)
    gate_high = gates.astype(BF16)
    gate_low = (gates - gate_high.astype(F32)).astype(BF16)
    blank = jnp.zeros((count, 128 - 2 * n_e), BF16)
    payload = jnp.concatenate([norm_two, gate_high, gate_low, blank], axis=1)
    norm_blocks = ring_gather(
        payload,
        {
            half - 1: lambda blocks: [share_sent],
            half: lambda blocks: up_tokens[3] + first(down_parts[1]) + [share_sent],
        },
    )

    named = jnp.any(routes_all == me.astype(F32), axis=1)
    named = jnp.take(named, order, axis=0)
    ranking = jnp.cumsum(named.astype(jnp.int32), axis=1)
    ends = jnp.cumsum(ranking[:, -1])
    begins = ends - ranking[:, -1]
    pos = jnp.where(named, begins[:, None] + ranking - 1, -1)[:, None, :]
    window = -(-(capacity + 15) // 16) * 16
    packed = -(-(n_e * capacity + 32) // 256) * 256
    packing = (begins // 16 * 16, pos, ends[-1:], window, packed)
    norm_two_all, payload, arrived, _ = dispatch(
        norm_blocks, [width, 128], packing, order, jnp.zeros((n_e, 1, count), F32)
    )
    mine = jnp.arange(n_e) == me
    gate_all = payload[:, : 2 * n_e].astype(F32).reshape(length, 2, n_e)
    gate_all = jnp.sum(jnp.where(mine, gate_all, 0.0), axis=(1, 2)).reshape(n_e, 1, count)
    cot_rows, gate_rows = dispatch(cot_all, None, packing, order, gate_all)
    weighted, row_grad, expert_act, route_grad, pre_grad, gate_grad = expert(
        packing[2],
        arrived,
        cot_rows,
        gate_rows,
        [part for parts in up_parts for part in parts],
        [part for parts in down_parts for part in parts],
    )

    shared_pre = dot(norm_two_all, share_w)
    shared_act = (
        jax.nn.silu(shared_pre[:, :shared_width]) * shared_pre[:, shared_width:]
    ).astype(BF16)
    shared_act_grad = dot_nt(cot_all, share_out)
    shared_pre_grad = silu_back(
        shared_act_grad, shared_pre[:, :shared_width], shared_pre[:, shared_width:]
    ).astype(BF16)
    norm_two_part = combine(
        packing, order, steady, me, row_grad, gate_grad, shared_pre_grad, share_w, True, 128
    )
    norm_two_grad = ring_scatter(
        lambda n: norm_two_part[n * count : (n + 1) * count]
    )
    gate_grad = norm_two_grad[:, width : width + n_e] + norm_two_grad[:, width + 64 : width + 64 + n_e]
    norm_two_grad = norm_two_grad[:, :width]
    out_part = combine(
        packing, order, order, me, weighted, gate_rows, shared_act, share_out, False, 0
    )
    routed_out = lax.psum_scatter(out_part, "expert", scatter_dimension=0, tiled=True)

    def shard_grads(left, right, chunks):
        size = left.shape[1] // n_dp
        part = size // chunks
        cut = lambda start, wide: lax.dynamic_slice_in_dim(left, start, wide, 1)
        got = [
            [
                lax.ppermute(
                    dot_tn(cut((here + step) % n_dp * size + j * part, part), right).astype(BF16),
                    "dp",
                    [(i, (i + step) % n_dp) for i in range(n_dp)],
                )
                for step in range(1, n_dp)
            ]
            for j in range(chunks)
        ]
        return dot_tn(cut(here * size, size), right), got

    def shard_sum(own, got, tokens):
        part = own.shape[0] // len(got)
        own = own[None]
        for j, (parts, token) in enumerate(zip(got, tokens)):
            block = sum(tied(p.astype(F32), token) for p in parts)[None]
            block = own[:, j * part : (j + 1) * part] + block
            own = lax.dynamic_update_slice_in_dim(own, block, j * part, 1)
        return own

    down_own, down_got = shard_grads(expert_act, route_grad, 2)
    up_own, up_got = shard_grads(arrived, pre_grad, len(up_parts) - 1)

    share_out_grad = dp_scatter(dot_tn(shared_act, cot_all).reshape(n_dp, shared_rows, width))
    share_in_grad = dot_tn(norm_two_all, shared_pre_grad)
    share_in_grad = dp_scatter(share_in_grad.reshape(n_dp, n_e, rows, 2 * shared_width))
    share_in_grad = swap(share_in_grad.astype(BF16)).astype(F32)
    share_in_grad = (
        share_in_grad.reshape(n_e, rows, 2, n_dp, shared_rows)
        .transpose(1, 2, 3, 0, 4)
        .reshape(rows, -1)
    )

    logit_grad = gates * (gate_grad - jnp.sum(gates * gate_grad, axis=-1, keepdims=True))
    router_grad = jnp.dot(
        logit_grad.T, norm_two.astype(F32), precision=HIGHEST, preferred_element_type=F32
    )
    norm_two_grad = norm_two_grad + jnp.dot(
        logit_grad, router_full.astype(F32), precision=HIGHEST, preferred_element_type=F32
    )
    gain_two_grad = jnp.sum(norm_two_grad * normed_two, axis=0)
    upstream = tied(cotangent.astype(F32), *down_got[0])
    scaled_two = norm_two_grad * gain_second
    resid_grad = upstream + inverse_two * (
        scaled_two - normed_two * jnp.mean(scaled_two * normed_two, axis=-1, keepdims=True)
    )
    small_grad = jnp.concatenate([router_grad, gain_two_grad[None]], axis=0)
    small_grad = jnp.pad(small_grad, ((0, HEAD_DIM - n_e - 1), (0, 0))).T

    branch_cot = resid_grad.astype(BF16)
    proj_grad = dot_tn(mixed, branch_cot).astype(BF16)
    mixed_grad = tied(dot_nt(branch_cot, proj_all), *down_got[1]).astype(BF16)
    mixed_grad = mixed_grad.reshape(count, n_e, n_dp, rows).transpose(0, 2, 1, 3)
    mixed_grad = swap(mixed_grad.reshape(count, n_e, HEAD_DIM).transpose(1, 0, 2))
    mixed_grad = mixed_grad.reshape(length, HEAD_DIM)
    proj_grad = lax.psum_scatter(proj_grad, "expert", scatter_dimension=0, tiled=True)
    attn_out_grad = dp_scatter(proj_grad.astype(F32).reshape(n_dp, rows, width))
    qkv_grad = attend_back(
        query, key, value, mixed_grad, lse, first_place, cos_table, sin_table, order
    )
    norm_one_part = dot_nt(qkv_grad, head_w).astype(BF16)
    scaled_one = ring_scatter(
        lambda n: norm_one_part[n * count : (n + 1) * count],
        {1: up_got[0], half - 1: up_got[min(1, len(up_got) - 1)]},
    )
    expert_out_grad = shard_sum(down_own, down_got, [norm_two_grad, mixed_grad])
    expert_in_grad = shard_sum(up_own, up_got, ([qkv_grad] * 3 + [scaled_one])[: len(up_got)])
    input_grad = resid_grad + inverse_one * (
        scaled_one - normed_one * jnp.mean(scaled_one * normed_one, axis=-1, keepdims=True)
    )
    wide = 3 * HEAD_DIM
    head_grad = jnp.concatenate([dot_tn(norm_all, qkv_grad), small_grad], axis=1)
    head_grad = dp_scatter(head_grad.reshape(n_dp, n_e, rows, wide + small_grad.shape[1]))
    head_grad = swap(head_grad.astype(BF16)).astype(F32)
    small_grad = jnp.sum(head_grad[:, :, wide:], axis=0)
    head_grad = (
        head_grad[:, :, :wide]
        .reshape(n_e, rows, 3, HEAD_DIM)
        .transpose(1, 2, 0, 3)
        .reshape(rows, 3 * width)
    )
    gain_attn_grad = jnp.sum(head_grad * attn_in.astype(F32), axis=1)
    attn_in_grad = head_grad * gain_rows
    return (
        (resid + routed_out.astype(F32)).astype(BF16),
        input_grad.astype(BF16),
        attn_in_grad,
        attn_out_grad,
        gain_attn_grad,
        share_in_grad,
        share_out_grad,
        small_grad[:, :n_e],
        small_grad[:, n_e],
        expert_in_grad,
        expert_out_grad,
    )


def solution(mesh):
    return jax.shard_map(
        per_device,
        mesh=mesh,
        in_specs=(
            P(("dp", "expert"), None),
            P(("dp", "expert"), None),
            P("dp", None),
            P(("dp", "expert"), None),
            P(("dp", "expert"), None),
            P(("dp", "expert"), None),
            P(("dp", "expert")),
            P(("dp", "expert"), None),
            P(("dp", "expert"), None),
            P(("dp", "expert"), None),
            P(("dp", "expert")),
            P("expert", "dp", None),
            P("expert", "dp", None),
        ),
        out_specs=(
            P(("dp", "expert"), None),
            P(("dp", "expert"), None),
            P(("dp", "expert"), None),
            P(("dp", "expert"), None),
            P(("dp", "expert")),
            P(("dp", "expert"), None),
            P(("dp", "expert"), None),
            P(("dp", "expert"), None),
            P(("dp", "expert")),
            P("expert", "dp", None),
            P("expert", "dp", None),
        ),
        check_vma=False,
    )
```
